32 devices in a mesh: rows: 16 (over z, x, core), cols: 2 (over y).
Axes of the slice: x: 2, y: 2, z: 4, core: 2. Of those that a mesh axis runs over, the one named last changes fastest.
Arguments:
- tokens: bfloat16 [49152, 1024], P('rows', 'cols'), may hold values from -6 to 6
- doc_lengths: int32 [16, 2, 4], replicated, may hold values from 1 to 512, 1024 in all within a row
- match_picks: int32 [512, 128, 32], P('rows', 'cols'), may hold values from 0 to 4095
- labels: int32 [512], P('rows'), may hold values from 0 to 127
- w_qkv: bfloat16 [3, 1024, 1024], P(None, None, 'cols'), may hold values from -0.1875 to 0.1875
- b_qkv: float32 [3, 1024], P(None, 'cols'), may hold values from -3 to 3
- w_out: bfloat16 [1024, 1024], P('cols'), may hold values from -1.5 to 1.5
- b_out: float32 [1024], P('cols'), may hold values from -3 to 3
- ln1_gain: float32 [1024], P('cols'), may hold values from 0.5 to 1.5
- ln1_bias: float32 [1024], P('cols'), may hold values from -3 to 3
- w_up: bfloat16 [1024, 4096], P(None, 'cols'), may hold values from -0.1875 to 0.1875
- b_up: float32 [4096], P('cols'), may hold values from -3 to 3
- w_down: bfloat16 [4096, 1024], P('cols'), may hold values from -0.125 to 0.125
- b_down: float32 [1024], P('cols'), may hold values from -3 to 3
- ln2_gain: float32 [1024], P('cols'), may hold values from 0.5 to 1.5
- ln2_bias: float32 [1024], P('cols'), may hold values from -3 to 3
- w_proj: bfloat16 [1024, 128], P('cols'), may hold values from -0.1875 to 0.1875
- log_scale: float32 [1], replicated, may hold values from 1 to 1.8
Outputs:
- scores: float32 [512, 128], P('rows', 'cols')
- contrastive_loss: float32 [512], P('rows')
- tokens_grad: float32 [49152, 1024], P('rows', 'cols')
- w_qkv_grad: float32 [3, 1024, 1024], P(None, 'rows', 'cols')
- b_qkv_grad: float32 [3, 1024], P(None, ('cols', 'rows'))
- w_out_grad: float32 [1024, 1024], P('cols', 'rows')
- b_out_grad: float32 [1024], P(('cols', 'rows'))
- ln1_gain_grad: float32 [1024], P(('cols', 'rows'))
- ln1_bias_grad: float32 [1024], P(('cols', 'rows'))
- w_up_grad: float32 [1024, 4096], P('rows', 'cols')
- b_up_grad: float32 [4096], P(('cols', 'rows'))
- w_down_grad: float32 [4096, 1024], P('cols', 'rows')
- b_down_grad: float32 [1024], P(('cols', 'rows'))
- ln2_gain_grad: float32 [1024], P(('cols', 'rows'))
- ln2_bias_grad: float32 [1024], P(('cols', 'rows'))
- w_proj_grad: float32 [1024, 128], P('cols', 'rows')
- log_scale_grad: float32 [1], replicated
The draws below stay inside these ranges and needn't reach their ends.
Inputs may be any that keep to these rules, and one draw needn't show every extreme that they name: `doc_lengths`: in each block the 4 lengths sum to 1024, and the largest of them is exactly 512.
All inputs are finite; a program needn't handle non-finite values.
Results may differ from the reference program's by a relative error of at most 0.018.
The reference program's roundings to bfloat16 on the way count: a program that leaves them out, or rounds other values in their place, can miss the bound.
Values may be sent and summed in bfloat16 or wider, within the bound.
A program may use at most 384 MiB of HBM per device.

```python
import math
import jax
import jax.numpy as jnp
import numpy as np
from jax import lax

D = 1024
H = 16
DH = 64
FF = 4096
PROJ = 128
QLEN = 32
ROW_LEN = 1024
DPS = 4
ABLK = 512
GROUPS = 16
BLOCKS = 2
DPACK = 2048
GT = 3072
TOKENS = 49152
DSHARD = 1024
DMOST = 512
NQ = 512
ND = 128


def with_ends(array, key, low, top_value):
    extent = array.shape
    spot = [jax.random.randint(jax.random.fold_in(key, axis), (), 0, extent[axis]) for axis in range(len(extent))]
    array = array.at[tuple(spot)].set(low)
    longest = extent.index(max(extent))
    spot[longest] = (spot[longest] + 1) % extent[longest]
    return array.at[tuple(spot)].set(top_value)


def levels(key, extent, shards, least, high):
    loudness, own = 1.0, jax.random.fold_in(key, 6)
    for dim, blocks in shards:
        heights = jnp.exp(jax.random.uniform(jax.random.fold_in(own, dim), (blocks,), jnp.float32, least / len(shards), high / len(shards)))
        loudness = loudness * jnp.repeat(heights, extent[dim] // blocks).reshape([-1 if axis == dim else 1 for axis in range(len(extent))])
    return loudness


def length_profile(number_of, total, limit, skew):
    weights = [(1 << 20) // math.isqrt(grade ** skew) + 1 for grade in range(2, number_of + 1)]
    rest, holding = total - limit - (number_of - 1), [1] * (number_of - 1)
    while rest > 0:
        candidates = [i for i in range(number_of - 1) if holding[i] < limit]
        mass, remaining = sum([weights[i] for i in candidates]), rest
        for i in candidates:
            addition = min(limit - holding[i], max(1, remaining * weights[i] // mass), rest)
            holding[i] = holding[i] + addition
            rest = rest - addition
    return np.array([limit] + holding)


def uneven_parts(own_key, count, total, reach, slope):
    if count == 2:
        one = jax.random.randint(own_key, (), max(1, total - reach), min(reach, total - 1) + 1)
        return jnp.stack([one, total - one])
    tallies = jnp.asarray(length_profile(count, total, reach, slope), jnp.int32)
    twos = (count - 1) // 2
    donor, sink = tallies[1:1 + 2 * twos:2], tallies[2:2 + 2 * twos:2]
    margin = jnp.minimum(donor - 1, reach - sink)
    moved = jax.random.randint(jax.random.fold_in(own_key, 1), (twos,), 0, 1 << 20) % (margin + 1)
    tallies = tallies.at[1:1 + 2 * twos:2].set(donor - moved).at[2:2 + 2 * twos:2].set(sink + moved)
    return tallies[jax.random.permutation(jax.random.fold_in(own_key, 2), count)]


def scatter_about(key, dims, width, reach, pieces=(), kind=jnp.bfloat16):
    entries = jax.random.normal(key, dims, jnp.float32) * width
    if len(pieces) > 0:
        entries = levels(key, dims, pieces, -0.22, 0.18) * entries
    return jnp.clip(entries, min=-reach, max=reach).astype(kind)


def setup_inputs(seed: int = 0) -> dict:
    streams_of = jax.random.split(jax.random.key(seed), 19)
    tokens = scatter_about(streams_of[0], (TOKENS, D), 1.0, 6.0, ((0, 16), (1, 2)))
    doc_lengths = jax.vmap(lambda own: uneven_parts(own, DPS, DSHARD, DMOST, 2))(jax.random.split(streams_of[1], GROUPS * BLOCKS)).reshape((GROUPS, BLOCKS, DPS)).astype(jnp.int32)
    match_picks = with_ends(jax.random.randint(streams_of[2], (NQ, ND, QLEN), 0, 4096), jax.random.fold_in(streams_of[2], 1), 0, 4095).astype(jnp.int32)
    labels = with_ends(jax.random.randint(streams_of[3], (NQ,), 0, ND), jax.random.fold_in(streams_of[3], 1), 0, ND - 1).astype(jnp.int32)
    w_qkv = scatter_about(streams_of[4], (3, D, D), D ** -0.5, 0.1875, ((2, 2),))
    b_qkv = scatter_about(streams_of[5], (3, D), 0.5, 3.0, ((1, 2),), jnp.float32)
    w_out = scatter_about(streams_of[6], (D, D), (D // 64) ** -0.5, 1.5, ((0, 2),))
    b_out = scatter_about(streams_of[7], (D,), 0.5, 3.0, ((0, 2),), jnp.float32)
    ln1_gain = jnp.clip(1.0 + 0.1 * jax.random.normal(streams_of[8], (D,), jnp.float32), 0.5, 1.5)
    ln1_bias = scatter_about(streams_of[9], (D,), 0.5, 3.0, ((0, 2),), jnp.float32)
    w_up = scatter_about(streams_of[10], (D, FF), D ** -0.5, 0.1875, ((1, 2),))
    b_up = scatter_about(streams_of[11], (FF,), 0.5, 3.0, ((0, 2),), jnp.float32)
    w_down = scatter_about(streams_of[12], (FF, D), (FF // 2) ** -0.5, 0.125, ((0, 2),))
    b_down = scatter_about(streams_of[13], (D,), 0.5, 3.0, ((0, 2),), jnp.float32)
    ln2_gain = jnp.clip(1.0 + 0.1 * jax.random.normal(streams_of[14], (D,), jnp.float32), 0.5, 1.5)
    ln2_bias = scatter_about(streams_of[15], (D,), 0.5, 3.0, ((0, 2),), jnp.float32)
    w_proj = scatter_about(streams_of[16], (D, PROJ), D ** -0.5, 0.1875, ((0, 2),))
    log_scale = jnp.clip(jax.random.uniform(streams_of[17], (1,), jnp.float32, 1.0, 1.8), 1.0, 1.8)
    return dict(tokens=tokens, doc_lengths=doc_lengths, match_picks=match_picks, labels=labels, w_qkv=w_qkv, b_qkv=b_qkv, w_out=w_out, b_out=b_out, ln1_gain=ln1_gain, ln1_bias=ln1_bias, w_up=w_up, b_up=b_up, w_down=w_down, b_down=b_down, ln2_gain=ln2_gain, ln2_bias=ln2_bias, w_proj=w_proj, log_scale=log_scale)


@jax.custom_vjp
def low(v):
    return lax.optimization_barrier(v.astype(jnp.bfloat16)).astype(jnp.float32)

@jax.custom_vjp
def low_back(v):
    return v

def low_keep(v):
    return (low(v), None)

def low_pass(kept, grad):
    return (grad,)

def back_keep(v):
    return (v, None)

def back_low(kept, grad):
    return (low(grad),)
low.defvjp(low_keep, low_pass)
low_back.defvjp(back_keep, back_low)
precise = lax.Precision.HIGHEST

def rotary_tables(positions, head_size):
    half_size = head_size // 2
    frequency = jnp.exp(jnp.arange(half_size, dtype=jnp.float32) * (-2.0 * math.log(10000.0) / head_size))
    angles = positions.astype(jnp.float32)[:, None] * frequency[None, :]
    return (jnp.cos(angles), jnp.sin(angles))

def rotate(values, cosine, sine_table, turn_sign):
    half_size = values.shape[-1] // 2
    first_half = values[..., :half_size]
    second = values[..., half_size:]
    cos_rows = cosine[:, None, :]
    sin_rows = turn_sign * sine_table[:, None, :]
    return jnp.concatenate([first_half * cos_rows - second * sin_rows, second * cos_rows + first_half * sin_rows], axis=-1)

def group_layout(lengths_group, row_length, query_length, shard_rows):
    query_places = jnp.arange(row_length, dtype=jnp.int32)
    doc_ends = jnp.cumsum(lengths_group, axis=1, dtype=jnp.int32)
    places = jnp.arange(shard_rows, dtype=jnp.int32)
    passed = places[None, :, None] >= doc_ends[:, None, :]
    doc_slot = lax.optimization_barrier(jnp.sum(passed.astype(jnp.int32), axis=2, dtype=jnp.int32))
    doc_begin = lax.optimization_barrier(jnp.sum(jnp.where(passed, lengths_group[:, None, :], 0), axis=2, dtype=jnp.int32))
    block_count = lengths_group.shape[0]
    doc_count = lengths_group.shape[1]
    doc_segment = row_length // query_length + jnp.arange(block_count, dtype=jnp.int32)[:, None] * doc_count + doc_slot
    segment = jnp.concatenate([query_places // query_length, doc_segment.reshape(-1)]).astype(jnp.int32)
    position = jnp.concatenate([query_places % query_length, (places[None, :] - doc_begin).reshape(-1)]).astype(jnp.int32)
    return (segment, position)

def attend(queries, keys, values, segment):
    row_count = queries.shape[0]
    padding = jnp.zeros((ABLK,) + keys.shape[1:], keys.dtype)
    key_pad = jnp.concatenate([padding, keys, padding])
    value_pad = jnp.concatenate([padding, values, padding])
    nothing = jnp.full((ABLK,), -1, jnp.int32)
    segment_pad = jnp.concatenate([nothing, segment, nothing])

    def one_block(block_index):
        first_row = block_index * ABLK
        query_block = lax.dynamic_slice_in_dim(queries, first_row, ABLK, 0)
        query_segment = lax.dynamic_slice_in_dim(segment, first_row, ABLK, 0)
        key_window = lax.dynamic_slice_in_dim(key_pad, first_row, 3 * ABLK, 0)
        value_window = lax.dynamic_slice_in_dim(value_pad, first_row, 3 * ABLK, 0)
        key_segment = lax.dynamic_slice_in_dim(segment_pad, first_row, 3 * ABLK, 0)
        logits = low_back(jnp.einsum('qhd,khd->hqk', query_block, key_window, precision=precise) * DH ** (-0.5))
        logits = jnp.where((query_segment[:, None] == key_segment[None, :])[None], logits, -1e+30)
        row_top = lax.optimization_barrier(jnp.max(logits, axis=2, keepdims=True))
        weights = jnp.exp(logits - row_top)
        weights = weights / lax.optimization_barrier(jnp.sum(weights, axis=2, keepdims=True))
        return jnp.einsum('hqk,khd->qhd', low(weights), value_window, precision=precise)
    result = lax.map(jax.checkpoint(one_block), jnp.arange(row_count // ABLK, dtype=jnp.int32))
    return result.reshape(row_count, -1)

def layer_norm(residual, norm_gain, norm_bias):
    row_mean = lax.optimization_barrier(jnp.mean(residual, axis=1, keepdims=True))
    row_var = lax.optimization_barrier(jnp.mean((residual - row_mean) ** 2, axis=1, keepdims=True))
    return (residual - row_mean) * lax.rsqrt(row_var + 1e-05) * norm_gain + norm_bias

def layer_group(params, inputs, segment, position):
    w_qkv, b_qkv, w_out, b_out, gain_one, bias_one, w_up, b_up, w_down, b_down, gain_two, bias_two, w_proj = params
    row_count = inputs.shape[0]
    mixed_qkv = low_back(jnp.einsum('nd,tde->tne', inputs, w_qkv, precision=precise) + b_qkv[:, None, :])
    cosine, sine_table = rotary_tables(position, DH)
    queries = low(rotate(mixed_qkv[0].reshape(row_count, H, DH), cosine, sine_table, 1.0))
    keys = low(rotate(mixed_qkv[1].reshape(row_count, H, DH), cosine, sine_table, 1.0))
    values = low(mixed_qkv[2].reshape(row_count, H, DH))
    attended = low(low_back(attend(queries, keys, values, segment)))
    residual = inputs + low_back(jnp.dot(attended, w_out, precision=precise)) + b_out
    hidden = layer_norm(residual, gain_one, bias_one)
    pre_act = low_back(jnp.dot(low(hidden), w_up, precision=precise) + b_up)
    branch = low_back(jnp.dot(low(jax.nn.gelu(pre_act, approximate=False)), w_down, precision=precise)) + b_down
    normed_out = layer_norm(hidden + branch, gain_two, bias_two)
    embedding = low_back(jnp.dot(low(normed_out), w_proj, precision=precise))
    unit_rows = embedding * lax.rsqrt(lax.optimization_barrier(jnp.sum(embedding * embedding, axis=1, keepdims=True)) + 1e-06)
    return low(unit_rows)

def doc_places(doc_lengths, match_picks):
    doc_sizes = jnp.transpose(doc_lengths, (1, 0, 2))
    offsets = (jnp.arange(GROUPS, dtype=jnp.int32) * DSHARD)[None, :, None]
    begins = jnp.cumsum(doc_sizes, axis=2, dtype=jnp.int32) - doc_sizes + offsets
    return (begins.reshape(-1)[None, :, None] + match_picks % doc_sizes.reshape(-1)[None, :, None]).astype(jnp.int32)

def score_all(queries, doc_tiles, places):

    def per_query(block_item):
        vectors, matched = block_item
        sim = low_back(jnp.einsum('tp,bjp->btj', vectors, doc_tiles, precision=precise))
        matched = jnp.transpose(matched.reshape(BLOCKS, GROUPS * DPS, QLEN), (0, 2, 1))
        return lax.optimization_barrier(jnp.sum(jnp.take_along_axis(sim, matched, axis=2), axis=1)).reshape(-1)
    return lax.map(jax.checkpoint(per_query), (queries, places))

def contrast(scores, log_scale, labels):
    scaled = jnp.exp(log_scale[0]) * scores
    row_top = lax.optimization_barrier(jnp.max(scaled, axis=1, keepdims=True))
    row_total = row_top[:, 0] + jnp.log(lax.optimization_barrier(jnp.sum(jnp.exp(scaled - row_top), axis=1)))
    chosen = jnp.take_along_axis(scaled, labels[:, None], axis=1)[:, 0]
    return row_total - chosen

def reference(tokens, doc_lengths, match_picks, labels, w_qkv, b_qkv, w_out, b_out, ln1_gain, ln1_bias, w_up, b_up, w_down, b_down, ln2_gain, ln2_bias, w_proj, log_scale):
    params = tuple((weight.astype(jnp.float32) for weight in (w_qkv, b_qkv, w_out, b_out, ln1_gain, ln1_bias, w_up, b_up, w_down, b_down, ln2_gain, ln2_bias, w_proj)))
    group_inputs = tokens.astype(jnp.float32).reshape(GROUPS, GT, D)
    segments, positions = lax.map(lambda sizes: group_layout(sizes, ROW_LEN, QLEN, DSHARD), doc_lengths)

    def encode(group_item):
        return layer_group(params, group_item[0], group_item[1], group_item[2])
    embedded = lax.map(encode, (group_inputs, segments, positions))
    queries = embedded[:, :ROW_LEN].reshape(NQ, QLEN, PROJ)
    doc_tiles = jnp.transpose(embedded[:, ROW_LEN:].reshape(GROUPS, BLOCKS, DSHARD, PROJ), (1, 0, 2, 3)).reshape(BLOCKS, GROUPS * DSHARD, PROJ)
    places = doc_places(doc_lengths, match_picks)

    def loss_head(query_vectors, doc_vectors, scale_log):
        scores = score_all(query_vectors, doc_vectors, places)
        row_losses = contrast(scores, scale_log, labels)
        return (jnp.mean(row_losses), (scores, row_losses))
    loss_value, pull_head, extras = jax.vjp(loss_head, queries, doc_tiles, log_scale.astype(jnp.float32), has_aux=True)
    scores, row_losses = extras
    query_grad, doc_grad, scale_grad = pull_head(jnp.ones_like(loss_value))
    doc_grad = jnp.transpose(doc_grad.reshape(BLOCKS, GROUPS, DSHARD, PROJ), (1, 0, 2, 3)).reshape(GROUPS, DPACK, PROJ)
    embed_grad = jnp.concatenate([query_grad.reshape(GROUPS, ROW_LEN, PROJ), doc_grad], axis=1)

    def group_step(running, group_item):
        inputs, segment, position, grad_rows = group_item
        unused, pull_layer = jax.vjp(lambda weights, rows: layer_group(weights, rows, segment, position), params, inputs)
        weight_grads, input_grad = pull_layer(grad_rows)
        return (jax.tree.map(jnp.add, running, weight_grads), input_grad)
    zeros = jax.tree.map(jnp.zeros_like, params)
    weight_grads, input_grads = lax.scan(group_step, zeros, (group_inputs, segments, positions, embed_grad))
    return (scores, row_losses, input_grads.reshape(TOKENS, D)) + tuple(weight_grads) + (scale_grad.reshape(1),)
```

```python
import functools
import math

import jax
import jax.numpy as jnp
from jax import lax
from jax.experimental import pallas as pl
from jax.experimental.pallas import tpu as pltpu
from jax.sharding import PartitionSpec as P

DH = 64
QLEN = 32
ROW_LEN = 1024
F32 = jnp.float32
BF16 = jnp.bfloat16
VMEM_LIMIT = 56 * 1024 * 1024
NT = (((1,), (1,)), ((), ()))
NN = (((1,), (0,)), ((), ()))
TN = (((0,), (0,)), ((), ()))


def mm(left, right, dims=NN):
    return lax.dot_general(left, right, dims, preferred_element_type=F32)


def swap_halves(block):
    lane = lax.broadcasted_iota(jnp.int32, block.shape, 1)
    return jnp.where((lane & 32) == 0, pltpu.roll(block, 96, 1), pltpu.roll(block, 32, 1))


def half_lanes(block, head):
    lane = lax.broadcasted_iota(jnp.int32, block.shape, 1)
    return jnp.where((lane >= 64) == (head == 1), block, jnp.zeros_like(block))


def scaled(block):
    return (block.astype(F32) * DH**-0.5).astype(BF16)


def query_mask(size):
    down = lax.broadcasted_iota(jnp.int32, (size, size), 0) // QLEN
    across = lax.broadcasted_iota(jnp.int32, (size, size), 1) // QLEN
    return down == across


def attend_tile(keys, values_t, query_tile, mask):
    outs, masses = [], []
    for head in range(2):
        logits = mm(keys, half_lanes(query_tile, head), NT)
        logits = jnp.where(mask, logits, -1e30)
        top = jnp.max(logits, axis=0, keepdims=True)
        weights = jnp.exp(logits - top)
        mass = jnp.sum(weights, axis=0, keepdims=True)
        probs = (weights * (1.0 / mass)).astype(BF16)
        outs.append(mm(values_t[head * DH : (head + 1) * DH], probs))
        masses.append(top + jnp.log(mass))
    return jnp.concatenate(outs, axis=0).T.astype(BF16), masses


def attention_forward_kernel(
    q_ref, k_ref, v_ref, cos_ref, sin_ref, segc_ref, segr_ref,
    qo_ref, ko_ref, out_ref, qlse_ref, dlse_ref, *, q_rows, q_tile, d_tile,
):
    rows = q_ref.shape[0]
    d_rows = rows - q_rows

    @pl.loop(0, rows // q_tile)
    def _(step):
        at = pl.ds(pl.multiple_of(step * q_tile, q_tile), q_tile)
        for src, dst in ((q_ref, qo_ref), (k_ref, ko_ref)):
            block = src[at, :]
            dst[at, :] = (block * cos_ref[at, :] + swap_halves(block) * sin_ref[at, :]).astype(BF16)

    @pl.loop(0, q_rows // q_tile)
    def _(step):
        at = pl.ds(pl.multiple_of(step * q_tile, q_tile), q_tile)
        values_t = v_ref[at, :].astype(F32).T.astype(BF16)
        out, masses = attend_tile(ko_ref[at, :], values_t, scaled(qo_ref[at, :]), query_mask(q_tile))
        out_ref[at, :] = out
        for head in range(2):
            qlse_ref[0, step, head : head + 1, :] = masses[head]

    keys = ko_ref[q_rows:, :]
    values_t = v_ref[q_rows:, :].astype(F32).T.astype(BF16)
    seg_keys = segc_ref[...]

    @pl.loop(0, d_rows // d_tile)
    def _(step):
        at = pl.ds(pl.multiple_of(q_rows + step * d_tile, q_tile), d_tile)
        mask = seg_keys == segr_ref[step]
        out, masses = attend_tile(keys, values_t, scaled(qo_ref[at, :]), mask)
        out_ref[at, :] = out
        for head in range(2):
            dlse_ref[0, step, head : head + 1, :] = masses[head]


def grad_tile(keys, keys_t, values, query_tile, grad_out, mask, masses):
    probs, flows, query_heads, grad_heads, dq = [], [], [], [], []
    for head in range(2):
        query_head = half_lanes(query_tile, head)
        grad_head = half_lanes(grad_out, head)
        logits = jnp.where(mask, mm(keys, query_head, NT), -1e30)
        weights = jnp.exp(logits - masses[head])
        flow = mm(values, grad_head, NT)
        inner = jnp.sum(weights * flow, axis=0, keepdims=True)
        slope = (weights * (flow - inner)).astype(BF16)
        dq.append(mm(keys_t[head * DH : (head + 1) * DH], slope))
        probs.append(weights.astype(BF16))
        flows.append(slope)
        query_heads.append(query_head)
        grad_heads.append(grad_head)
    dv = mm(jnp.concatenate(probs, axis=1), jnp.concatenate(grad_heads, axis=0))
    dk = mm(jnp.concatenate(flows, axis=1), jnp.concatenate(query_heads, axis=0))
    return jnp.concatenate(dq, axis=0).T, dk, dv


def attention_backward_kernel(
    q_ref, k_ref, v_ref, g_ref, cos_ref, sin_ref, segc_ref, segr_ref, qlse_ref, dlse_ref,
    out_ref, sum_ref, dq_ref, dk_ref, dv_ref, *, q_rows, q_tile, d_tile,
):
    rows = q_ref.shape[0]
    d_rows = rows - q_rows

    @pl.loop(0, q_rows // q_tile)
    def _(step):
        at = pl.ds(pl.multiple_of(step * q_tile, q_tile), q_tile)
        keys = k_ref[at, :]
        keys_t = scaled(keys).astype(F32).T.astype(BF16)
        masses = [qlse_ref[0, step, head : head + 1, :] for head in range(2)]
        dq, dk, dv = grad_tile(
            keys, keys_t, v_ref[at, :], scaled(q_ref[at, :]), g_ref[at, :],
            query_mask(q_tile), masses,
        )
        dq_ref[at, :] = dq
        dk_ref[at, :] = dk
        dv_ref[at, :] = dv

    keys = k_ref[q_rows:, :]
    keys_t = scaled(keys).astype(F32).T.astype(BF16)
    values = v_ref[q_rows:, :]
    seg_keys = segc_ref[...]
    dk_ref[q_rows:, :] = jnp.zeros((d_rows, 128), F32)
    dv_ref[q_rows:, :] = jnp.zeros((d_rows, 128), F32)

    @pl.loop(0, d_rows // d_tile)
    def _(step):
        at = pl.ds(pl.multiple_of(q_rows + step * d_tile, q_tile), d_tile)
        mask = seg_keys == segr_ref[step]
        masses = [dlse_ref[0, step, head : head + 1, :] for head in range(2)]
        dq, dk, dv = grad_tile(
            keys, keys_t, values, scaled(q_ref[at, :]), g_ref[at, :], mask, masses
        )
        dq_ref[at, :] = dq
        dk_ref[q_rows:, :] += dk
        dv_ref[q_rows:, :] += dv

    def finish(step, sums):
        at = pl.ds(pl.multiple_of(step * q_tile, q_tile), q_tile)
        cosine, sine = cos_ref[at, :], sin_ref[at, :]
        added = []
        for which, src in enumerate((dq_ref, dk_ref, dv_ref)):
            block = src[at, :]
            if which < 2:
                block = block * cosine - swap_halves(block) * sine
            low = block.astype(BF16)
            out_ref[which, at, :] = low
            added.append(sums[which] + jnp.sum(low.astype(F32), axis=0, keepdims=True))
        return tuple(added)

    zero = jnp.zeros((1, 128), F32)
    sums = lax.fori_loop(0, rows // q_tile, finish, (zero, zero, zero))
    sum_ref[0] = jnp.concatenate(sums + (jnp.zeros((5, 128), F32),), axis=0)


def attention_sizes(rows, q_rows):
    q_tile = min(128, q_rows)
    return dict(q_rows=q_rows, q_tile=q_tile, d_tile=min(256, rows - q_rows))


def attention_forward(q_mixed, k_mixed, values, cosine, sine, seg_col, seg_row, q_rows):
    rows, width = q_mixed.shape
    sizes = attention_sizes(rows, q_rows)
    pairs = width // 128
    q_steps, d_steps = q_rows // sizes["q_tile"], (rows - q_rows) // sizes["d_tile"]
    wide = pl.BlockSpec((rows, 128), lambda i: (0, i))
    fixed = pl.BlockSpec((rows, 128), lambda i: (0, 0))
    q_mass = pl.BlockSpec((1, q_steps, 2, sizes["q_tile"]), lambda i: (i, 0, 0, 0))
    d_mass = pl.BlockSpec((1, d_steps, 2, sizes["d_tile"]), lambda i: (i, 0, 0, 0))
    low = jax.ShapeDtypeStruct((rows, width), BF16)
    return pl.pallas_call(
        functools.partial(attention_forward_kernel, **sizes),
        grid=(pairs,),
        in_specs=[
            wide, wide, wide, fixed, fixed,
            pl.BlockSpec(seg_col.shape, lambda i: (0, 0)),
            pl.BlockSpec(seg_row.shape, lambda i: (0, 0, 0)),
        ],
        out_specs=[wide, wide, wide, q_mass, d_mass],
        out_shape=[
            low, low, low,
            jax.ShapeDtypeStruct((pairs, q_steps, 2, sizes["q_tile"]), F32),
            jax.ShapeDtypeStruct((pairs, d_steps, 2, sizes["d_tile"]), F32),
        ],
        compiler_params=pltpu.CompilerParams(vmem_limit_bytes=VMEM_LIMIT),
        cost_estimate=pl.CostEstimate(
            flops=20_000_000_000, bytes_accessed=30_000_000, transcendentals=0
        ),
        name="attention_forward",
    )(q_mixed, k_mixed, values, cosine, sine, seg_col, seg_row)


def attention_backward(queries, keys, values, grads, cosine, sine, seg_col, seg_row, masses, q_rows):
    rows, width = queries.shape
    sizes = attention_sizes(rows, q_rows)
    pairs = width // 128
    q_steps, d_steps = q_rows // sizes["q_tile"], (rows - q_rows) // sizes["d_tile"]
    wide = pl.BlockSpec((rows, 128), lambda i: (0, i))
    fixed = pl.BlockSpec((rows, 128), lambda i: (0, 0))
    q_mass = pl.BlockSpec((1, q_steps, 2, sizes["q_tile"]), lambda i: (i, 0, 0, 0))
    d_mass = pl.BlockSpec((1, d_steps, 2, sizes["d_tile"]), lambda i: (i, 0, 0, 0))
    return pl.pallas_call(
        functools.partial(attention_backward_kernel, **sizes),
        grid=(pairs,),
        in_specs=[
            wide, wide, wide, wide, fixed, fixed,
            pl.BlockSpec(seg_col.shape, lambda i: (0, 0)),
            pl.BlockSpec(seg_row.shape, lambda i: (0, 0, 0)),
            q_mass, d_mass,
        ],
        out_specs=[
            pl.BlockSpec((3, rows, 128), lambda i: (0, 0, i)),
            pl.BlockSpec((1, 8, 128), lambda i: (i, 0, 0)),
        ],
        out_shape=[
            jax.ShapeDtypeStruct((3, rows, width), BF16),
            jax.ShapeDtypeStruct((pairs, 8, 128), F32),
        ],
        scratch_shapes=[pltpu.VMEM((rows, 128), F32)] * 3,
        compiler_params=pltpu.CompilerParams(vmem_limit_bytes=VMEM_LIMIT),
        cost_estimate=pl.CostEstimate(
            flops=60_000_000_000, bytes_accessed=30_000_000, transcendentals=0
        ),
        name="attention_backward",
    )(queries, keys, values, grads, cosine, sine, seg_col, seg_row, *masses)


STRIP = 32


def score_kernel(begin_ref, size_ref, doc_ref, query_ref, pick_ref, out_ref, sim_ref):
    group = pl.program_id(0)
    docs, width = pick_ref.shape[1:]
    chunk = min(256, doc_ref.shape[0])

    @pl.loop(0, doc_ref.shape[0] // chunk)
    def _(step):
        at = pl.ds(pl.multiple_of(step * chunk, chunk), chunk)
        sim_ref[at, :] = mm(doc_ref[at, :], query_ref[...], NT)

    for doc in range(docs):
        begin = begin_ref[group * docs + doc]
        end = begin + size_ref[group * docs + doc]
        pick = pick_ref[0, doc : doc + 1, :]

        def strip(step, total):
            first = pl.multiple_of(step * STRIP, STRIP)
            row = lax.broadcasted_iota(jnp.int32, (STRIP, width), 0) + first
            held = jnp.where(row == pick, sim_ref[pl.ds(first, STRIP), :], 0.0)
            return total + jnp.sum(held.reshape(STRIP // 8, 8, width), axis=0)

        total = lax.fori_loop(
            begin // STRIP, (end + STRIP - 1) // STRIP, strip, jnp.zeros((8, width), F32)
        )
        out_ref[0, doc : doc + 1, :] = jnp.sum(total, axis=0, keepdims=True)


def score_grad_kernel(
    begin_ref, size_ref, doc_ref, query_ref, pick_ref, weight_ref, doc_out, query_out, sparse_ref
):
    group = pl.program_id(0)
    docs, width = pick_ref.shape[1:]
    doc_rows = doc_ref.shape[0]

    @pl.loop(0, doc_rows // STRIP)
    def _(step):
        first = pl.multiple_of(step * STRIP, STRIP)
        row = lax.broadcasted_iota(jnp.int32, (STRIP, width), 0) + first
        low = jnp.int32(0)
        high = jnp.int32(0)
        for doc in range(docs):
            begin = begin_ref[group * docs + doc]
            end = begin + size_ref[group * docs + doc]
            low += (end <= first).astype(jnp.int32)
            high += (begin < first + STRIP).astype(jnp.int32)

        def one_doc(doc, held):
            pick = pick_ref[0, pl.ds(doc, 1), :]
            return jnp.where(row == pick, weight_ref[0, pl.ds(doc, 1), :], held)

        held = lax.fori_loop(low, high, one_doc, jnp.zeros((STRIP, width), F32))
        sparse_ref[pl.ds(first, STRIP), :] = held.astype(BF16)

    docs_t = doc_ref[...].astype(F32).T.astype(BF16)
    doc_out[...] = mm(sparse_ref[...], query_ref[...])

    @pl.when(group == 0)
    def _():
        query_out[...] = jnp.zeros_like(query_out)

    query_out[...] += mm(docs_t, sparse_ref[...])


def score_specs(doc_tile, query_tile, picks):
    groups, docs, width = picks.shape
    doc_rows = doc_tile.shape[0] // groups
    return (
        pl.BlockSpec((doc_rows, 128), lambda i, *_: (i, 0)),
        pl.BlockSpec(query_tile.shape, lambda i, *_: (0, 0)),
        pl.BlockSpec((1, docs, width), lambda i, *_: (i, 0, 0)),
    )


def score_forward(begins, sizes, doc_tile, query_tile, picks):
    groups, docs, width = picks.shape
    doc_spec, query_spec, pick_spec = score_specs(doc_tile, query_tile, picks)
    return pl.pallas_call(
        score_kernel,
        grid_spec=pltpu.PrefetchScalarGridSpec(
            num_scalar_prefetch=2,
            grid=(groups,),
            in_specs=[doc_spec, query_spec, pick_spec],
            out_specs=pick_spec,
            scratch_shapes=[pltpu.VMEM((doc_tile.shape[0] // groups, width), F32)],
        ),
        out_shape=jax.ShapeDtypeStruct((groups, docs, width), F32),
        compiler_params=pltpu.CompilerParams(vmem_limit_bytes=VMEM_LIMIT),
        name="score_forward",
    )(begins, sizes, doc_tile, query_tile, picks)


def score_backward(begins, sizes, doc_tile, query_tile, picks, weights):
    groups, docs, width = picks.shape
    doc_spec, query_spec, pick_spec = score_specs(doc_tile, query_tile, picks)
    return pl.pallas_call(
        score_grad_kernel,
        grid_spec=pltpu.PrefetchScalarGridSpec(
            num_scalar_prefetch=2,
            grid=(groups,),
            in_specs=[doc_spec, query_spec, pick_spec, pick_spec],
            out_specs=[doc_spec, pl.BlockSpec((128, width), lambda i, *_: (0, 0))],
            scratch_shapes=[pltpu.VMEM((doc_tile.shape[0] // groups, width), BF16)],
        ),
        out_shape=[
            jax.ShapeDtypeStruct(doc_tile.shape, F32),
            jax.ShapeDtypeStruct((128, width), F32),
        ],
        compiler_params=pltpu.CompilerParams(vmem_limit_bytes=VMEM_LIMIT),
        name="score_backward",
    )(begins, sizes, doc_tile, query_tile, picks, weights)


def rotary_tables(position):
    half_size = DH // 2
    frequency = jnp.exp(
        jnp.arange(half_size, dtype=F32) * (-2.0 * math.log(10000.0) / DH)
    )
    angles = position.astype(F32)[:, None] * frequency[None, :]
    cosine, sine = jnp.cos(angles), jnp.sin(angles)
    return (
        jnp.concatenate([cosine] * 4, axis=1),
        jnp.concatenate([-sine, sine, -sine, sine], axis=1),
    )


def norm_forward(residual, gain, bias):
    mean = jnp.mean(residual, axis=1, keepdims=True)
    centred = residual - mean
    inverse = lax.rsqrt(jnp.mean(centred * centred, axis=1, keepdims=True) + 1e-05)
    normed = centred * inverse
    return normed * gain + bias, normed, inverse


def norm_backward(grad_rows, normed, inverse, gain):
    spread = grad_rows * gain
    grad = inverse * (
        spread
        - jnp.mean(spread, axis=1, keepdims=True)
        - normed * jnp.mean(spread * normed, axis=1, keepdims=True)
    )
    return grad, jnp.sum(grad_rows * normed, axis=0), jnp.sum(grad_rows, axis=0)


def on_device(
    tokens,
    doc_lengths,
    match_picks,
    labels,
    w_qkv,
    b_qkv,
    w_out,
    b_out,
    ln1_gain,
    ln1_bias,
    w_up,
    b_up,
    w_down,
    b_down,
    ln2_gain,
    ln2_bias,
    w_proj,
    log_scale,
):
    C = lax.axis_size("cols")
    R = lax.axis_size("rows")
    c = lax.axis_index("cols")
    r = lax.axis_index("rows")
    width = tokens.shape[1]
    D = width * C
    Q = ROW_LEN // C
    DS = (tokens.shape[0] - ROW_LEN) // C
    n = Q + DS

    def shift_cols(value, k):
        return lax.ppermute(value, "cols", [(i, (i + k) % C) for i in range(C)])

    def swap_rows(value, bit):
        return lax.ppermute(value, "rows", [(i, i ^ bit) for i in range(R)])

    def in_order(slots):
        if len(slots) == 1:
            return slots
        if len(slots) == 2:
            return [lax.select(c == 0, slots[0], slots[1]), lax.select(c == 0, slots[1], slots[0])]
        stacked = jnp.stack(slots)
        return [
            lax.dynamic_index_in_dim(stacked, (c - j) % C, 0, keepdims=False) for j in range(C)
        ]

    parts = jnp.concatenate(
        [tokens[:ROW_LEN].reshape(C, Q, width), tokens[ROW_LEN:].reshape(C, DS, width)], axis=1
    )

    def part(k):
        return lax.dynamic_index_in_dim(parts, (c + k) % C, 0, keepdims=False)

    slots = [part(0)] + [shift_cols(part(k), k) for k in range(1, C)]
    x = jnp.concatenate(in_order(slots), axis=1)

    def gather_slots(shard):
        flat = shard.reshape(-1, shard.shape[-1])
        piece = lax.dynamic_index_in_dim(
            flat.reshape(R, flat.shape[0] // R, flat.shape[1]), r, 0, keepdims=False
        )
        others = [
            lax.all_gather(shift_cols(piece, k), "rows", axis=0, tiled=True).reshape(shard.shape)
            for k in range(1, C)
        ]
        return [shard] + others

    wqkv_slots = gather_slots(w_qkv)
    wout_slots = gather_slots(w_out)
    wup_slots = gather_slots(w_up)
    wdown_slots = gather_slots(w_down)
    wproj = lax.all_gather(w_proj, "cols", axis=0, tiled=True)

    vectors = [b_qkv.reshape(-1), b_up, b_out, ln1_gain, ln1_bias, b_down, ln2_gain, ln2_bias]
    spread = lax.all_gather(jnp.concatenate(vectors), "cols", axis=0)
    ends = [0]
    for vector in vectors:
        ends.append(ends[-1] + vector.shape[0])

    def of_slot(which, k):
        row = lax.dynamic_index_in_dim(spread, (c - k) % C, 0, keepdims=False)
        return row[ends[which] : ends[which + 1]]

    def whole(which):
        return spread[:, ends[which] : ends[which + 1]].reshape(-1)

    bqkv_slots = [of_slot(0, k).reshape(b_qkv.shape) for k in range(C)]
    bup_slots = [of_slot(1, k) for k in range(C)]
    bout, gain1, bias1, bdown, gain2, bias2 = [whole(which) for which in range(2, 8)]

    own_sizes = lax.dynamic_index_in_dim(
        lax.dynamic_index_in_dim(doc_lengths, r, 0, keepdims=False), c, 0, keepdims=False
    )
    own_ends = jnp.cumsum(own_sizes)
    places = jnp.arange(DS, dtype=jnp.int32)
    passed = places[:, None] >= own_ends[None, :]
    slot_id = jnp.sum(passed.astype(jnp.int32), axis=1)
    slot_begin = jnp.sum(jnp.where(passed, own_sizes[None, :], 0), axis=1)
    position = jnp.concatenate([jnp.arange(Q, dtype=jnp.int32) % QLEN, places - slot_begin])
    cosine, sine = rotary_tables(position)
    d_tile = attention_sizes(n, Q)["d_tile"]
    seg_col = slot_id[:, None]
    seg_row = slot_id.reshape(DS // d_tile, 1, d_tile)

    def project(which):
        return jnp.concatenate(
            [mm(x, wqkv_slots[k][which]) + bqkv_slots[k][which] for k in range(C)], axis=1
        )

    values = project(2).astype(BF16)
    queries, keys, attended, *masses = attention_forward(
        project(0), project(1), values, cosine, sine, seg_col, seg_row, Q
    )

    def slot_of(array, k):
        size = array.shape[1] // C
        return array[:, k * size : (k + 1) * size]

    resid_one = x.astype(F32) + bout
    for k in range(C):
        resid_one = resid_one + mm(slot_of(attended, k), wout_slots[k])
    hidden, normed_one, inverse_one = norm_forward(resid_one, gain1, bias1)
    hidden_low = hidden.astype(BF16)
    pre = [mm(hidden_low, wup_slots[k]) + bup_slots[k] for k in range(C)]
    active = [jax.nn.gelu(p, approximate=False).astype(BF16) for p in pre]
    resid_two = hidden + bdown
    for k in range(C):
        resid_two = resid_two + mm(active[k], wdown_slots[k])
    normed_out, normed_two, inverse_two = norm_forward(resid_two, gain2, bias2)
    output_low = normed_out.astype(BF16)
    embedding = mm(output_low, wproj)
    inverse_unit = lax.rsqrt(jnp.sum(embedding * embedding, axis=1, keepdims=True) + 1e-06)
    unit = embedding * inverse_unit
    unit_low = unit.astype(BF16)

    doc_tile = lax.all_gather(unit_low[Q:], "rows", axis=0, tiled=True)
    query_tile = lax.all_gather(unit_low[:Q], "cols", axis=0, tiled=True)
    queries_here, tile_docs, _ = match_picks.shape
    docs = own_sizes.shape[0]
    sizes = lax.dynamic_index_in_dim(doc_lengths, c, 1, keepdims=False)
    begins = jnp.cumsum(sizes, axis=1) - sizes
    sizes_flat, begins_flat = sizes.reshape(-1), begins.reshape(-1)
    picks = jnp.transpose(match_picks, (1, 0, 2)).reshape(tile_docs, queries_here * QLEN)
    picks = begins_flat[:, None] + picks % sizes_flat[:, None]
    picks = picks.reshape(R, docs, queries_here * QLEN)
    sims = score_forward(begins_flat, sizes_flat, doc_tile, query_tile, picks)
    scores = jnp.sum(sims.reshape(tile_docs, queries_here, QLEN), axis=2).T

    scale = jnp.exp(log_scale[0])
    z = scale * scores
    row_top = jnp.max(z, axis=1)
    row_mass = jnp.sum(jnp.exp(z - row_top[:, None]), axis=1)
    is_label = (
        jnp.arange(tile_docs, dtype=jnp.int32)[None, :] == (labels - c * tile_docs)[:, None]
    )
    chosen = jnp.sum(jnp.where(is_label, z, 0.0), axis=1)
    stats = lax.all_gather(jnp.stack([row_top, row_mass, chosen]), "cols", axis=0)
    top_all = jnp.max(stats[:, 0], axis=0)
    mass_all = jnp.sum(stats[:, 1] * jnp.exp(stats[:, 0] - top_all), axis=0)
    log_total = top_all + jnp.log(mass_all)
    loss = log_total - jnp.sum(stats[:, 2], axis=0)
    dz = (jnp.exp(z - log_total[:, None]) - is_label.astype(F32)) / (queries_here * R)
    scale_sum = lax.psum(jnp.sum(dz * z), ("rows", "cols"))
    dscores = (scale * dz).astype(BF16).astype(F32)
    weights = jnp.broadcast_to(
        dscores.T[:, :, None], (tile_docs, queries_here, QLEN)
    ).reshape(R, docs, queries_here * QLEN)
    doc_grad, query_grad_t = score_backward(
        begins_flat, sizes_flat, doc_tile, query_tile, picks, weights
    )
    query_grad = lax.psum_scatter(query_grad_t.T, "cols", scatter_dimension=0, tiled=True)

    def halve(total, bit):
        size = total.shape[0] // 2
        pairs = total.reshape((size, 2) + total.shape[1:])
        mine = (r // bit) % 2
        send = lax.dynamic_index_in_dim(pairs, 1 - mine, 1, keepdims=False).astype(BF16)
        keep = lax.dynamic_index_in_dim(pairs, mine, 1, keepdims=False)
        return keep + swap_rows(send, bit).astype(F32)

    doc_sum = doc_grad.reshape(R, DS, 128)
    bit = 1
    while bit < R:
        doc_sum = halve(doc_sum, bit)
        bit *= 2
    unit_grad = jnp.concatenate([query_grad, doc_sum[0]], axis=0)
    embed_grad = (
        inverse_unit * (unit_grad - unit * jnp.sum(unit_grad * unit, axis=1, keepdims=True))
    ).astype(BF16)

    def weight_grad(left, right_slots):
        share = left.shape[1] // R
        split = left.reshape(n, R // 2, 2, share)
        own = lax.dynamic_index_in_dim(split, r % 2, 2, keepdims=False).reshape(n, -1)
        other = lax.dynamic_index_in_dim(split, 1 - r % 2, 2, keepdims=False).reshape(n, -1)
        arrived = [swap_rows(mm(other, right, TN).astype(BF16), 1) for right in right_slots]
        sums = [
            mm(own, right, TN) + came.astype(F32) for right, came in zip(right_slots, arrived)
        ]
        total = sums[0]
        for k in range(1, C):
            total = total + shift_cols(sums[k].astype(BF16), C - k).astype(F32)
        total = total.reshape(R // 2, share, -1)
        bit = 2
        while bit < R:
            total = halve(total, bit)
            bit *= 2
        return total[0]

    proj_grad = mm(output_low, embed_grad, TN)
    proj_grad = proj_grad.reshape(C, width, R, -1).transpose(0, 2, 1, 3).reshape(C * R, -1)
    proj_grad = lax.psum_scatter(proj_grad, ("cols", "rows"), scatter_dimension=0, tiled=True)
    output_grad = mm(embed_grad, wproj, NT)
    resid_two_grad, gain2_grad, bias2_grad = norm_backward(
        output_grad, normed_two, inverse_two, gain2
    )
    bdown_grad = jnp.sum(resid_two_grad, axis=0)
    branch = resid_two_grad.astype(BF16)
    down_grad = weight_grad(branch, active)
    pre_grad = []
    for k in range(C):
        _, pull = jax.vjp(functools.partial(jax.nn.gelu, approximate=False), pre[k])
        pre_grad.append(pull(mm(branch, wdown_slots[k], NT))[0].astype(BF16))
    bup_grad = [jnp.sum(g.astype(F32), axis=0) for g in pre_grad]
    up_grad = weight_grad(hidden_low, pre_grad)
    hidden_grad = resid_two_grad
    for k in range(C):
        hidden_grad = hidden_grad + mm(pre_grad[k], wup_slots[k], NT)
    resid_one_grad, gain1_grad, bias1_grad = norm_backward(
        hidden_grad, normed_one, inverse_one, gain1
    )
    bout_grad = jnp.sum(resid_one_grad, axis=0)
    branch_one = resid_one_grad.astype(BF16)
    out_grad = weight_grad(branch_one, [slot_of(attended, k) for k in range(C)])
    attended_grad = jnp.concatenate(
        [mm(branch_one, wout_slots[k], NT).astype(BF16) for k in range(C)], axis=1
    )
    mixed_grad, mixed_sums = attention_backward(
        queries, keys, values, attended_grad, cosine, sine, seg_col, seg_row, masses, Q
    )
    tokens_part = resid_one_grad
    for k in range(C):
        for which in range(3):
            tokens_part = tokens_part + mm(
                slot_of(mixed_grad[which], k), wqkv_slots[k][which], NT
            )
    blocks = tokens_part.reshape(n, C, width)

    def block(k):
        return lax.dynamic_index_in_dim(blocks, (c + k) % C, 1, keepdims=False)

    slots = [block(0)] + [
        shift_cols(block(k).astype(BF16), k).astype(F32) for k in range(1, C)
    ]
    ordered = in_order(slots)
    tokens_grad = jnp.concatenate([s[:Q] for s in ordered] + [s[Q:] for s in ordered], axis=0)
    qkv_grad = jnp.stack(
        [
            weight_grad(x, [slot_of(mixed_grad[which], k) for k in range(C)])
            for which in range(3)
        ]
    )

    def canonical(slot_list):
        return jnp.concatenate(in_order(slot_list), axis=-1)

    bqkv_sums = mixed_sums[:, :3].transpose(1, 0, 2).reshape(3, D)
    bqkv_grad = canonical([slot_of(bqkv_sums, k) for k in range(C)])
    small = jnp.concatenate(
        [g.reshape(C * R, -1) for g in bqkv_grad]
        + [
            g.reshape(C * R, -1)
            for g in (
                canonical(bup_grad), bout_grad, gain1_grad, bias1_grad,
                bdown_grad, gain2_grad, bias2_grad,
            )
        ],
        axis=1,
    )
    small = lax.psum_scatter(small, ("cols", "rows"), scatter_dimension=0, tiled=True)[0]
    one = D // (C * R)
    up_part = bup_grad[0].shape[0] // R
    bounds = [3 * one, 3 * one + up_part]
    for _ in range(6):
        bounds.append(bounds[-1] + one)
    pieces = [small[: bounds[0]].reshape(3, one)] + [
        small[a:b] for a, b in zip(bounds[:-1], bounds[1:])
    ]
    (bqkv_out, bup_out, bout_out, gain1_out, bias1_out, bdown_out, gain2_out, bias2_out) = pieces
    return (
        scores,
        loss,
        tokens_grad,
        qkv_grad,
        bqkv_out,
        out_grad.T,
        bout_out,
        gain1_out,
        bias1_out,
        up_grad,
        bup_out,
        down_grad.T,
        bdown_out,
        gain2_out,
        bias2_out,
        proj_grad.reshape(width, -1),
        scale_sum.reshape(1),
    )


def solution(mesh):
    in_specs = (
        P("rows", "cols"),
        P(),
        P("rows", "cols", None),
        P("rows"),
        P(None, None, "cols"),
        P(None, "cols"),
        P("cols", None),
        P("cols"),
        P("cols"),
        P("cols"),
        P(None, "cols"),
        P("cols"),
        P("cols", None),
        P("cols"),
        P("cols"),
        P("cols"),
        P("cols", None),
        P(),
    )
    out_specs = (
        P("rows", "cols"),
        P("rows"),
        P("rows", "cols"),
        P(None, "rows", "cols"),
        P(None, ("cols", "rows")),
        P("cols", "rows"),
        P(("cols", "rows")),
        P(("cols", "rows")),
        P(("cols", "rows")),
        P("rows", "cols"),
        P(("cols", "rows")),
        P("cols", "rows"),
        P(("cols", "rows")),
        P(("cols", "rows")),
        P(("cols", "rows")),
        P("cols", "rows"),
        P(),
    )
    return jax.shard_map(
        on_device, mesh=mesh, in_specs=in_specs, out_specs=out_specs, check_vma=False
    )
```

```python
import functools
import math

import jax
import jax.numpy as jnp
from jax import lax
from jax.experimental import pallas as pl
from jax.experimental.pallas import tpu as pltpu
from jax.sharding import PartitionSpec as P

DH = 64
QLEN = 32
ROW_LEN = 1024
F32 = jnp.float32
BF16 = jnp.bfloat16
VMEM_LIMIT = 56 * 1024 * 1024
NT = (((1,), (1,)), ((), ()))
NN = (((1,), (0,)), ((), ()))
TN = (((0,), (0,)), ((), ()))


def mm(left, right, dims=NN):
    return lax.dot_general(left, right, dims, preferred_element_type=F32)


def row_step(rows):
    return 512 if rows % 512 == 0 else 128


def held(shape):
    return pl.BlockSpec(shape, lambda *_: (0,) * len(shape), pipeline_mode=pl.Buffered(1))


def shaped(dtype, *shape):
    return jax.ShapeDtypeStruct(shape, dtype)


def call(body, name, grid, in_specs, out_specs, out_shape, operands, flops, scratch=(), prefetch=0):
    size = sum(math.prod(o.shape) * o.dtype.itemsize for o in list(operands) + list(out_shape))
    return pl.pallas_call(
        body,
        grid_spec=pltpu.PrefetchScalarGridSpec(
            num_scalar_prefetch=prefetch,
            grid=grid,
            in_specs=in_specs,
            out_specs=out_specs,
            scratch_shapes=list(scratch),
        ),
        out_shape=out_shape,
        compiler_params=pltpu.CompilerParams(vmem_limit_bytes=VMEM_LIMIT),
        cost_estimate=pl.CostEstimate(flops=flops, bytes_accessed=size, transcendentals=0),
        name=name,
    )(*operands)


def row_spec(step, width):
    return pl.BlockSpec((step, width), lambda i, *_: (i, 0))


def column_spec(width, step):
    return pl.BlockSpec((width, step), lambda i, *_: (0, i))


def swap_halves(block):
    lane = lax.broadcasted_iota(jnp.int32, block.shape, 1)
    width = block.shape[1]
    return jnp.where((lane & 32) == 0, pltpu.roll(block, width - 32, 1), pltpu.roll(block, 32, 1))


def wide_table(table, width):
    return jnp.concatenate([table] * (width // 128), axis=1)


def qkv_kernel(x_ref, w_ref, b_ref, cos_ref, sin_ref, out_ref):
    which = pl.program_id(0)
    mixed = mm(x_ref[...], w_ref[0]) + b_ref[pl.ds(which, 1), :]
    width = mixed.shape[1]

    @pl.when(which < 2)
    def _():
        turned = mixed * wide_table(cos_ref[...], width)
        turned = turned + swap_halves(mixed) * wide_table(sin_ref[...], width)
        out_ref[0] = turned.astype(BF16)

    @pl.when(which == 2)
    def _():
        out_ref[0] = mixed.astype(BF16)


def project_qkv(x, weight, bias, cosine, sine):
    n, D = x.shape
    width = weight.shape[2]
    step = row_step(n)
    return call(
        qkv_kernel, "project_qkv", (3, n // step),
        [
            pl.BlockSpec((step, D), lambda j, i: (i, 0)),
            pl.BlockSpec((1, D, width), lambda j, i: (j, 0, 0)),
            held(bias.shape),
            pl.BlockSpec((step, 128), lambda j, i: (i, 0)),
            pl.BlockSpec((step, 128), lambda j, i: (i, 0)),
        ],
        [pl.BlockSpec((1, step, width), lambda j, i: (j, i, 0))],
        [shaped(BF16, 3, n, width)],
        (x, weight, bias, cosine, sine), 6 * n * D * width,
    )[0]


def normed_rows(residual):
    mean = jnp.mean(residual, axis=1, keepdims=True)
    centred = residual - mean
    inverse = lax.rsqrt(jnp.mean(centred * centred, axis=1, keepdims=True) + 1e-05)
    return centred * inverse, inverse


def norm_pull(grad_rows, normed, inverse, gain):
    spread = grad_rows * gain
    return inverse * (
        spread
        - jnp.mean(spread, axis=1, keepdims=True)
        - normed * jnp.mean(spread * normed, axis=1, keepdims=True)
    )


def column_sums(*arrays):
    rows = [jnp.sum(array, axis=0, keepdims=True) for array in arrays]
    rows.append(jnp.zeros((8 - len(rows), rows[0].shape[1]), F32))
    return jnp.concatenate(rows, axis=0)


def add_over_steps(ref, value):
    first = pl.program_id(0) == 0

    @pl.when(first)
    def _():
        ref[...] = value

    @pl.when(jnp.logical_not(first))
    def _():
        ref[...] += value


def out_norm_kernel(slots, *refs):
    x_ref, vec_ref = refs[:2]
    att_refs, w_refs = refs[2 : 2 + slots], refs[2 + slots : 2 + 2 * slots]
    normed_ref, inverse_ref, low_ref, turned_ref = refs[2 + 2 * slots :]
    residual = x_ref[...].astype(F32) + vec_ref[0:1, :]
    for att_ref, w_ref in zip(att_refs, w_refs):
        residual = residual + mm(att_ref[...], w_ref[...])
    normed, inverse = normed_rows(residual)
    hidden = normed * vec_ref[1:2, :] + vec_ref[2:3, :]
    normed_ref[...] = normed
    inverse_ref[...] = inverse
    low_ref[...] = hidden.astype(BF16)
    turned_ref[...] = hidden.T.astype(BF16)


def out_and_norm(x, vectors, attended, weights):
    n, D = x.shape
    step = row_step(n)
    slots = len(attended)
    width = attended[0].shape[1]
    return call(
        functools.partial(out_norm_kernel, slots), "out_and_norm", (n // step,),
        [row_spec(step, D), held(vectors.shape)]
        + [row_spec(step, width)] * slots + [held((width, D))] * slots,
        [row_spec(step, D), row_spec(step, 1), row_spec(step, D), column_spec(D, step)],
        [shaped(F32, n, D), shaped(F32, n, 1), shaped(BF16, n, D), shaped(BF16, D, n)],
        (x, vectors, *attended, *weights), 2 * n * D * D,
    )


GELU_TERMS = (
    0.23532527933595032, 0.09138803439798156, 0.6495603483388861,
    -0.6354014529895687, 0.8866650885491606, -0.22753729931242958,
)


def gelu_parts(values):
    size = jnp.abs(values)
    part = pl.reciprocal(1.0 + (0.39 / math.sqrt(2.0)) * size)
    bell = jnp.exp(-0.5 * (values * values))
    series = 0.5 * GELU_TERMS[-1]
    for term in GELU_TERMS[-2::-1]:
        series = series * part + 0.5 * term
    tail = series * part * bell
    below = jnp.where(values >= 0.0, 1.0 - tail, tail)
    return values * below, below + values * bell * (1.0 / math.sqrt(2.0 * math.pi))


def up_kernel(x_ref, w_ref, b_ref, active_ref, slope_ref):
    width = w_ref.shape[1]
    chunk = min(512, width)
    for first in range(0, width, chunk):
        at = slice(first, first + chunk)
        active, slope = gelu_parts(mm(x_ref[...], w_ref[:, at]) + b_ref[:, at])
        active_ref[:, at] = active.astype(BF16)
        slope_ref[:, at] = slope


def up_and_gelu(x, weight, bias):
    n, D = x.shape
    width = weight.shape[1]
    step = row_step(n)
    return call(
        up_kernel, "up_and_gelu", (n // step,),
        [row_spec(step, D), held(weight.shape), held(bias.shape)],
        [row_spec(step, width)] * 2,
        [shaped(BF16, n, width), shaped(F32, n, width)],
        (x, weight, bias), 5 * n * D * width,
    )


def down_norm_kernel(slots, *refs):
    normed_ref, vec_ref, proj_ref = refs[:3]
    act_refs, w_refs = refs[3 : 3 + slots], refs[3 + slots : 3 + 2 * slots]
    normed_out, inverse_ref, low_ref, unit_ref, unit_low_ref, unit_inverse_ref = refs[3 + 2 * slots :]
    residual = normed_ref[...] * vec_ref[1:2, :] + vec_ref[2:3, :] + vec_ref[3:4, :]
    for act_ref, w_ref in zip(act_refs, w_refs):
        residual = residual + mm(act_ref[...], w_ref[...])
    normed, inverse = normed_rows(residual)
    normed_out[...] = normed
    inverse_ref[...] = inverse
    low = (normed * vec_ref[4:5, :] + vec_ref[5:6, :]).astype(BF16)
    low_ref[...] = low
    embedding = mm(low, proj_ref[...])
    unit_inverse = lax.rsqrt(jnp.sum(embedding * embedding, axis=1, keepdims=True) + 1e-06)
    unit = embedding * unit_inverse
    unit_ref[...] = unit
    unit_low_ref[...] = unit.astype(BF16)
    unit_inverse_ref[...] = unit_inverse


def down_and_norm(normed, vectors, proj, active, weights):
    n, D = normed.shape
    step = row_step(n)
    slots = len(active)
    width = active[0].shape[1]
    return call(
        functools.partial(down_norm_kernel, slots), "down_and_norm", (n // step,),
        [row_spec(step, D), held(vectors.shape), held(proj.shape)]
        + [row_spec(step, width)] * slots + [held((width, D))] * slots,
        [
            row_spec(step, D), row_spec(step, 1), row_spec(step, D),
            row_spec(step, 128), row_spec(step, 128), row_spec(step, 1),
        ],
        [
            shaped(F32, n, D), shaped(F32, n, 1), shaped(BF16, n, D),
            shaped(F32, n, 128), shaped(BF16, n, 128), shaped(F32, n, 1),
        ],
        (normed, vectors, proj, *active, *weights), 2 * n * D * width * slots,
    )


def head_pull_kernel(
    grad_ref, unit_ref, unit_inverse_ref, proj_ref, normed_ref, inverse_ref, vec_ref,
    embed_ref, residual_ref, low_ref, turned_ref, sum_ref,
):
    grad, unit = grad_ref[...], unit_ref[...]
    embed = unit_inverse_ref[...] * (grad - unit * jnp.sum(grad * unit, axis=1, keepdims=True))
    embed = embed.astype(BF16)
    embed_ref[...] = embed
    output_grad = mm(embed, proj_ref[...], NT)
    normed = normed_ref[...]
    residual = norm_pull(output_grad, normed, inverse_ref[...], vec_ref[4:5, :])
    residual_ref[...] = residual
    low_ref[...] = residual.astype(BF16)
    turned_ref[...] = residual.T.astype(BF16)
    add_over_steps(sum_ref, column_sums(residual, output_grad * normed, output_grad))


def head_pull(unit_grad, unit, unit_inverse, proj, normed, inverse, vectors):
    n, D = normed.shape
    step = row_step(n)
    return call(
        head_pull_kernel, "head_pull", (n // step,),
        [
            row_spec(step, 128), row_spec(step, 128), row_spec(step, 1), held(proj.shape),
            row_spec(step, D), row_spec(step, 1), held(vectors.shape),
        ],
        [
            row_spec(step, 128), row_spec(step, D), row_spec(step, D),
            column_spec(D, step), pl.BlockSpec((8, D), lambda i: (0, 0)),
        ],
        [
            shaped(BF16, n, 128), shaped(F32, n, D), shaped(BF16, n, D),
            shaped(BF16, D, n), shaped(F32, 8, D),
        ],
        (unit_grad, unit, unit_inverse, proj, normed, inverse, vectors), 4 * n * D * 128,
    )


def up_pull_kernel(branch_ref, w_ref, slope_ref, out_ref, sum_ref):
    width = w_ref.shape[0]
    chunk = min(512, width)
    sums = []
    for first in range(0, width, chunk):
        at = slice(first, first + chunk)
        low = (mm(branch_ref[...], w_ref[at, :], NT) * slope_ref[:, at]).astype(BF16)
        out_ref[:, at] = low
        sums.append(column_sums(low.astype(F32)))
    add_over_steps(sum_ref, jnp.concatenate(sums, axis=1))


def up_pull(branch, weight, slope):
    n, D = branch.shape
    width = weight.shape[0]
    step = row_step(n)
    return call(
        up_pull_kernel, "up_pull", (n // step,),
        [row_spec(step, D), held(weight.shape), row_spec(step, width)],
        [row_spec(step, width), pl.BlockSpec((8, width), lambda i: (0, 0))],
        [shaped(BF16, n, width), shaped(F32, 8, width)],
        (branch, weight, slope), 2 * n * D * width,
    )


def hidden_pull_kernel(slots, *refs):
    residual_ref, normed_ref, inverse_ref, vec_ref = refs[:4]
    pre_refs, up_refs, out_refs = (refs[4 + j * slots : 4 + (j + 1) * slots] for j in range(3))
    rest = refs[4 + 3 * slots :]
    grad_ref, turned_ref, sum_ref = rest[:3]
    att_refs = rest[3:]
    hidden_grad = residual_ref[...]
    for pre_ref, up_ref in zip(pre_refs, up_refs):
        hidden_grad = hidden_grad + mm(pre_ref[...], up_ref[...], NT)
    normed = normed_ref[...]
    residual = norm_pull(hidden_grad, normed, inverse_ref[...], vec_ref[1:2, :])
    grad_ref[...] = residual
    low = residual.astype(BF16)
    turned_ref[...] = residual.T.astype(BF16)
    add_over_steps(sum_ref, column_sums(residual, hidden_grad * normed, hidden_grad))
    for att_ref, out_ref in zip(att_refs, out_refs):
        att_ref[...] = mm(low, out_ref[...], NT).astype(BF16)


def hidden_pull(residual, normed, inverse, vectors, pre_grads, ups, outs):
    n, D = residual.shape
    step = row_step(n)
    slots = len(ups)
    wide, width = ups[0].shape[1], outs[0].shape[0]
    return call(
        functools.partial(hidden_pull_kernel, slots), "hidden_pull", (n // step,),
        [row_spec(step, D), row_spec(step, D), row_spec(step, 1), held(vectors.shape)]
        + [row_spec(step, wide)] * slots + [held((D, wide))] * slots
        + [held((width, D))] * slots,
        [row_spec(step, D), column_spec(D, step), pl.BlockSpec((8, D), lambda i: (0, 0))]
        + [row_spec(step, width)] * slots,
        [shaped(F32, n, D), shaped(BF16, D, n), shaped(F32, 8, D)]
        + [shaped(BF16, n, width)] * slots,
        (residual, normed, inverse, vectors, *pre_grads, *ups, *outs),
        2 * n * D * (wide + width) * slots,
    )


def token_pull_kernel(slots, place_ref, *refs):
    residual_ref = refs[0]
    mixed_refs, w_refs = refs[1 : 1 + slots], refs[1 + slots : 1 + 2 * slots]
    out_ref = refs[-1]
    width = out_ref.shape[1]
    at = pl.ds(pl.multiple_of(place_ref[0] * width, width), width)
    total = residual_ref[...]
    for mixed_ref, w_ref in zip(mixed_refs, w_refs):
        for which in range(3):
            total = total + mm(mixed_ref[which], w_ref[which, at, :], NT)
    out_ref[...] = total.astype(out_ref.dtype)


def token_pull(place, residual, mixed_grads, weights, dtype):
    n, D = residual.shape
    step = row_step(n)
    slots = len(weights)
    width = weights[0].shape[2]
    return call(
        functools.partial(token_pull_kernel, slots), "token_pull", (n // step,),
        [pl.BlockSpec((step, width), lambda i, p: (i, p[0]))]
        + [pl.BlockSpec((3, step, width), lambda i, p: (0, i, 0))] * slots
        + [held((3, D, width))] * slots,
        [row_spec(step, width)],
        [shaped(dtype, n, width)],
        (place.reshape(1), residual, *mixed_grads, *weights), 6 * n * D * width, prefetch=1,
    )[0]


def weight_pull_kernel(place_ref, left_ref, right_ref, *refs):
    out_ref = refs[-1]
    total = mm(left_ref[:, 0].reshape(-1, left_ref.shape[-1]), right_ref[0])
    if len(refs) > 1:
        total = total + refs[0][0].astype(F32)
    out_ref[0] = total.astype(out_ref.dtype)


def weight_pull(place, left, right, arrived, dtype):
    pairs, _, share, n = left.shape
    count, _, m = right.shape
    rows = pairs * share
    chunk = min(512, m)
    spec = pl.BlockSpec((1, rows, chunk), lambda j, i, p: (j, 0, i))
    return call(
        weight_pull_kernel, "weight_pull", (count, m // chunk),
        [
            pl.BlockSpec((pairs, 1, share, n), lambda j, i, p: (0, p[0], 0, 0)),
            pl.BlockSpec((1, n, chunk), lambda j, i, p: (j, 0, i)),
        ] + ([] if arrived is None else [spec]),
        [spec],
        [shaped(dtype, count, rows, m)],
        (place.reshape(1), left, right) + (() if arrived is None else (arrived,)),
        2 * count * rows * n * m, prefetch=1,
    )[0]


def row_step(rows):
    return 512 if rows % 512 == 0 else 128


def held(shape):
    return pl.BlockSpec(shape, lambda *_: (0,) * len(shape), pipeline_mode=pl.Buffered(1))


def shaped(dtype, *shape):
    return jax.ShapeDtypeStruct(shape, dtype)


def call(body, name, grid, in_specs, out_specs, out_shape, operands, flops, scratch=(), prefetch=0):
    size = sum(math.prod(o.shape) * o.dtype.itemsize for o in list(operands) + list(out_shape))
    return pl.pallas_call(
        body,
        grid_spec=pltpu.PrefetchScalarGridSpec(
            num_scalar_prefetch=prefetch,
            grid=grid,
            in_specs=in_specs,
            out_specs=out_specs,
            scratch_shapes=list(scratch),
        ),
        out_shape=out_shape,
        compiler_params=pltpu.CompilerParams(vmem_limit_bytes=VMEM_LIMIT),
        cost_estimate=pl.CostEstimate(flops=flops, bytes_accessed=size, transcendentals=0),
        name=name,
    )(*operands)


def row_spec(step, width):
    return pl.BlockSpec((step, width), lambda i, *_: (i, 0))


def column_spec(width, step):
    return pl.BlockSpec((width, step), lambda i, *_: (0, i))


def swap_halves(block):
    lane = lax.broadcasted_iota(jnp.int32, block.shape, 1)
    width = block.shape[1]
    return jnp.where((lane & 32) == 0, pltpu.roll(block, width - 32, 1), pltpu.roll(block, 32, 1))


def wide_table(table, width):
    return jnp.concatenate([table] * (width // 128), axis=1)


def qkv_kernel(x_ref, w_ref, b_ref, cos_ref, sin_ref, out_ref):
    which = pl.program_id(0)
    mixed = mm(x_ref[...], w_ref[0]) + b_ref[pl.ds(which, 1), :]
    width = mixed.shape[1]

    @pl.when(which < 2)
    def _():
        turned = mixed * wide_table(cos_ref[...], width)
        turned = turned + swap_halves(mixed) * wide_table(sin_ref[...], width)
        out_ref[0] = turned.astype(BF16)

    @pl.when(which == 2)
    def _():
        out_ref[0] = mixed.astype(BF16)


def project_qkv(x, weight, bias, cosine, sine):
    n, D = x.shape
    width = weight.shape[2]
    step = row_step(n)
    return call(
        qkv_kernel, "project_qkv", (3, n // step),
        [
            pl.BlockSpec((step, D), lambda j, i: (i, 0)),
            pl.BlockSpec((1, D, width), lambda j, i: (j, 0, 0)),
            held(bias.shape),
            pl.BlockSpec((step, 128), lambda j, i: (i, 0)),
            pl.BlockSpec((step, 128), lambda j, i: (i, 0)),
        ],
        [pl.BlockSpec((1, step, width), lambda j, i: (j, i, 0))],
        [shaped(BF16, 3, n, width)],
        (x, weight, bias, cosine, sine), 6 * n * D * width,
    )[0]


def normed_rows(residual):
    mean = jnp.mean(residual, axis=1, keepdims=True)
    centred = residual - mean
    inverse = lax.rsqrt(jnp.mean(centred * centred, axis=1, keepdims=True) + 1e-05)
    return centred * inverse, inverse


def norm_pull(grad_rows, normed, inverse, gain):
    spread = grad_rows * gain
    return inverse * (
        spread
        - jnp.mean(spread, axis=1, keepdims=True)
        - normed * jnp.mean(spread * normed, axis=1, keepdims=True)
    )


def column_sums(*arrays):
    rows = [jnp.sum(array, axis=0, keepdims=True) for array in arrays]
    rows.append(jnp.zeros((8 - len(rows), rows[0].shape[1]), F32))
    return jnp.concatenate(rows, axis=0)


def add_over_steps(ref, value):
    first = pl.program_id(0) == 0

    @pl.when(first)
    def _():
        ref[...] = value

    @pl.when(jnp.logical_not(first))
    def _():
        ref[...] += value


def out_norm_kernel(slots, *refs):
    x_ref, vec_ref = refs[:2]
    att_refs, w_refs = refs[2 : 2 + slots], refs[2 + slots : 2 + 2 * slots]
    normed_ref, inverse_ref, low_ref, turned_ref = refs[2 + 2 * slots :]
    residual = x_ref[...].astype(F32) + vec_ref[0:1, :]
    for att_ref, w_ref in zip(att_refs, w_refs):
        residual = residual + mm(att_ref[...], w_ref[...])
    normed, inverse = normed_rows(residual)
    hidden = normed * vec_ref[1:2, :] + vec_ref[2:3, :]
    normed_ref[...] = normed
    inverse_ref[...] = inverse
    low_ref[...] = hidden.astype(BF16)
    turned_ref[...] = hidden.T.astype(BF16)


def out_and_norm(x, vectors, attended, weights):
    n, D = x.shape
    step = row_step(n)
    slots = len(attended)
    width = attended[0].shape[1]
    return call(
        functools.partial(out_norm_kernel, slots), "out_and_norm", (n // step,),
        [row_spec(step, D), held(vectors.shape)]
        + [row_spec(step, width)] * slots + [held((width, D))] * slots,
        [row_spec(step, D), row_spec(step, 1), row_spec(step, D), column_spec(D, step)],
        [shaped(F32, n, D), shaped(F32, n, 1), shaped(BF16, n, D), shaped(BF16, D, n)],
        (x, vectors, *attended, *weights), 2 * n * D * D,
    )


GELU_TERMS = (
    0.23532527933595032, 0.09138803439798156, 0.6495603483388861,
    -0.6354014529895687, 0.8866650885491606, -0.22753729931242958,
)


def gelu_parts(values):
    size = jnp.abs(values)
    part = pl.reciprocal(1.0 + (0.39 / math.sqrt(2.0)) * size)
    bell = jnp.exp(-0.5 * (values * values))
    series = 0.5 * GELU_TERMS[-1]
    for term in GELU_TERMS[-2::-1]:
        series = series * part + 0.5 * term
    tail = series * part * bell
    below = jnp.where(values >= 0.0, 1.0 - tail, tail)
    return values * below, below + values * bell * (1.0 / math.sqrt(2.0 * math.pi))


def up_kernel(x_ref, w_ref, b_ref, active_ref, slope_ref):
    width = w_ref.shape[1]
    chunk = min(512, width)
    for first in range(0, width, chunk):
        at = slice(first, first + chunk)
        active, slope = gelu_parts(mm(x_ref[...], w_ref[:, at]) + b_ref[:, at])
        active_ref[:, at] = active.astype(BF16)
        slope_ref[:, at] = slope


def up_and_gelu(x, weight, bias):
    n, D = x.shape
    width = weight.shape[1]
    step = row_step(n)
    return call(
        up_kernel, "up_and_gelu", (n // step,),
        [row_spec(step, D), held(weight.shape), held(bias.shape)],
        [row_spec(step, width)] * 2,
        [shaped(BF16, n, width), shaped(F32, n, width)],
        (x, weight, bias), 5 * n * D * width,
    )


def down_norm_kernel(slots, *refs):
    normed_ref, vec_ref, proj_ref = refs[:3]
    act_refs, w_refs = refs[3 : 3 + slots], refs[3 + slots : 3 + 2 * slots]
    normed_out, inverse_ref, low_ref, unit_ref, unit_low_ref, unit_inverse_ref = refs[3 + 2 * slots :]
    residual = normed_ref[...] * vec_ref[1:2, :] + vec_ref[2:3, :] + vec_ref[3:4, :]
    for act_ref, w_ref in zip(act_refs, w_refs):
        residual = residual + mm(act_ref[...], w_ref[...])
    normed, inverse = normed_rows(residual)
    normed_out[...] = normed
    inverse_ref[...] = inverse
    low = (normed * vec_ref[4:5, :] + vec_ref[5:6, :]).astype(BF16)
    low_ref[...] = low
    embedding = mm(low, proj_ref[...])
    unit_inverse = lax.rsqrt(jnp.sum(embedding * embedding, axis=1, keepdims=True) + 1e-06)
    unit = embedding * unit_inverse
    unit_ref[...] = unit
    unit_low_ref[...] = unit.astype(BF16)
    unit_inverse_ref[...] = unit_inverse


def down_and_norm(normed, vectors, proj, active, weights):
    n, D = normed.shape
    step = row_step(n)
    slots = len(active)
    width = active[0].shape[1]
    return call(
        functools.partial(down_norm_kernel, slots), "down_and_norm", (n // step,),
        [row_spec(step, D), held(vectors.shape), held(proj.shape)]
        + [row_spec(step, width)] * slots + [held((width, D))] * slots,
        [
            row_spec(step, D), row_spec(step, 1), row_spec(step, D),
            row_spec(step, 128), row_spec(step, 128), row_spec(step, 1),
        ],
        [
            shaped(F32, n, D), shaped(F32, n, 1), shaped(BF16, n, D),
            shaped(F32, n, 128), shaped(BF16, n, 128), shaped(F32, n, 1),
        ],
        (normed, vectors, proj, *active, *weights), 2 * n * D * width * slots,
    )


def head_pull_kernel(
    grad_ref, unit_ref, unit_inverse_ref, proj_ref, normed_ref, inverse_ref, vec_ref,
    embed_ref, residual_ref, low_ref, turned_ref, sum_ref,
):
    grad, unit = grad_ref[...], unit_ref[...]
    embed = unit_inverse_ref[...] * (grad - unit * jnp.sum(grad * unit, axis=1, keepdims=True))
    embed = embed.astype(BF16)
    embed_ref[...] = embed
    output_grad = mm(embed, proj_ref[...], NT)
    normed = normed_ref[...]
    residual = norm_pull(output_grad, normed, inverse_ref[...], vec_ref[4:5, :])
    residual_ref[...] = residual
    low_ref[...] = residual.astype(BF16)
    turned_ref[...] = residual.T.astype(BF16)
    add_over_steps(sum_ref, column_sums(residual, output_grad * normed, output_grad))


def head_pull(unit_grad, unit, unit_inverse, proj, normed, inverse, vectors):
    n, D = normed.shape
    step = row_step(n)
    return call(
        head_pull_kernel, "head_pull", (n // step,),
        [
            row_spec(step, 128), row_spec(step, 128), row_spec(step, 1), held(proj.shape),
            row_spec(step, D), row_spec(step, 1), held(vectors.shape),
        ],
        [
            row_spec(step, 128), row_spec(step, D), row_spec(step, D),
            column_spec(D, step), pl.BlockSpec((8, D), lambda i: (0, 0)),
        ],
        [
            shaped(BF16, n, 128), shaped(F32, n, D), shaped(BF16, n, D),
            shaped(BF16, D, n), shaped(F32, 8, D),
        ],
        (unit_grad, unit, unit_inverse, proj, normed, inverse, vectors), 4 * n * D * 128,
    )


def up_pull_kernel(branch_ref, w_ref, slope_ref, out_ref, sum_ref):
    width = w_ref.shape[0]
    chunk = min(512, width)
    sums = []
    for first in range(0, width, chunk):
        at = slice(first, first + chunk)
        low = (mm(branch_ref[...], w_ref[at, :], NT) * slope_ref[:, at]).astype(BF16)
        out_ref[:, at] = low
        sums.append(column_sums(low.astype(F32)))
    add_over_steps(sum_ref, jnp.concatenate(sums, axis=1))


def up_pull(branch, weight, slope):
    n, D = branch.shape
    width = weight.shape[0]
    step = row_step(n)
    return call(
        up_pull_kernel, "up_pull", (n // step,),
        [row_spec(step, D), held(weight.shape), row_spec(step, width)],
        [row_spec(step, width), pl.BlockSpec((8, width), lambda i: (0, 0))],
        [shaped(BF16, n, width), shaped(F32, 8, width)],
        (branch, weight, slope), 2 * n * D * width,
    )


def hidden_pull_kernel(slots, *refs):
    residual_ref, normed_ref, inverse_ref, vec_ref = refs[:4]
    pre_refs, up_refs, out_refs = (refs[4 + j * slots : 4 + (j + 1) * slots] for j in range(3))
    rest = refs[4 + 3 * slots :]
    grad_ref, turned_ref, sum_ref = rest[:3]
    att_refs = rest[3:]
    hidden_grad = residual_ref[...]
    for pre_ref, up_ref in zip(pre_refs, up_refs):
        hidden_grad = hidden_grad + mm(pre_ref[...], up_ref[...], NT)
    normed = normed_ref[...]
    residual = norm_pull(hidden_grad, normed, inverse_ref[...], vec_ref[1:2, :])
    grad_ref[...] = residual
    low = residual.astype(BF16)
    turned_ref[...] = residual.T.astype(BF16)
    add_over_steps(sum_ref, column_sums(residual, hidden_grad * normed, hidden_grad))
    for att_ref, out_ref in zip(att_refs, out_refs):
        att_ref[...] = mm(low, out_ref[...], NT).astype(BF16)


def hidden_pull(residual, normed, inverse, vectors, pre_grads, ups, outs):
    n, D = residual.shape
    step = row_step(n)
    slots = len(ups)
    wide, width = ups[0].shape[1], outs[0].shape[0]
    return call(
        functools.partial(hidden_pull_kernel, slots), "hidden_pull", (n // step,),
        [row_spec(step, D), row_spec(step, D), row_spec(step, 1), held(vectors.shape)]
        + [row_spec(step, wide)] * slots + [held((D, wide))] * slots
        + [held((width, D))] * slots,
        [row_spec(step, D), column_spec(D, step), pl.BlockSpec((8, D), lambda i: (0, 0))]
        + [row_spec(step, width)] * slots,
        [shaped(F32, n, D), shaped(BF16, D, n), shaped(F32, 8, D)]
        + [shaped(BF16, n, width)] * slots,
        (residual, normed, inverse, vectors, *pre_grads, *ups, *outs),
        2 * n * D * (wide + width) * slots,
    )


def token_pull_kernel(slots, place_ref, *refs):
    residual_ref = refs[0]
    mixed_refs, w_refs = refs[1 : 1 + slots], refs[1 + slots : 1 + 2 * slots]
    out_ref = refs[-1]
    width = out_ref.shape[1]
    at = pl.ds(pl.multiple_of(place_ref[0] * width, width), width)
    total = residual_ref[...]
    for mixed_ref, w_ref in zip(mixed_refs, w_refs):
        for which in range(3):
            total = total + mm(mixed_ref[which], w_ref[which, at, :], NT)
    out_ref[...] = total.astype(out_ref.dtype)


def token_pull(place, residual, mixed_grads, weights, dtype):
    n, D = residual.shape
    step = row_step(n)
    slots = len(weights)
    width = weights[0].shape[2]
    return call(
        functools.partial(token_pull_kernel, slots), "token_pull", (n // step,),
        [pl.BlockSpec((step, width), lambda i, p: (i, p[0]))]
        + [pl.BlockSpec((3, step, width), lambda i, p: (0, i, 0))] * slots
        + [held((3, D, width))] * slots,
        [row_spec(step, width)],
        [shaped(dtype, n, width)],
        (place.reshape(1), residual, *mixed_grads, *weights), 6 * n * D * width, prefetch=1,
    )[0]


def weight_pull_kernel(place_ref, left_ref, right_ref, *refs):
    out_ref = refs[-1]
    total = mm(left_ref[:, 0].reshape(-1, left_ref.shape[-1]), right_ref[0])
    if len(refs) > 1:
        total = total + refs[0][0].astype(F32)
    out_ref[0] = total.astype(out_ref.dtype)


def weight_pull(place, left, right, arrived, dtype):
    pairs, _, share, n = left.shape
    count, _, m = right.shape
    rows = pairs * share
    chunk = min(512, m)
    spec = pl.BlockSpec((1, rows, chunk), lambda j, i, p: (j, 0, i))
    return call(
        weight_pull_kernel, "weight_pull", (count, m // chunk),
        [
            pl.BlockSpec((pairs, 1, share, n), lambda j, i, p: (0, p[0], 0, 0)),
            pl.BlockSpec((1, n, chunk), lambda j, i, p: (j, 0, i)),
        ] + ([] if arrived is None else [spec]),
        [spec],
        [shaped(dtype, count, rows, m)],
        (place.reshape(1), left, right) + (() if arrived is None else (arrived,)),
        2 * count * rows * n * m, prefetch=1,
    )[0]


def row_step(rows):
    return 512 if rows % 512 == 0 else 128


def held(shape):
    return pl.BlockSpec(shape, lambda *_: (0,) * len(shape), pipeline_mode=pl.Buffered(1))


def shaped(dtype, *shape):
    return jax.ShapeDtypeStruct(shape, dtype)


def call(body, name, grid, in_specs, out_specs, out_shape, operands, flops, scratch=(), prefetch=0):
    size = sum(math.prod(o.shape) * o.dtype.itemsize for o in list(operands) + list(out_shape))
    return pl.pallas_call(
        body,
        grid_spec=pltpu.PrefetchScalarGridSpec(
            num_scalar_prefetch=prefetch,
            grid=grid,
            in_specs=in_specs,
            out_specs=out_specs,
            scratch_shapes=list(scratch),
        ),
        out_shape=out_shape,
        compiler_params=pltpu.CompilerParams(vmem_limit_bytes=VMEM_LIMIT),
        cost_estimate=pl.CostEstimate(flops=flops, bytes_accessed=size, transcendentals=0),
        name=name,
    )(*operands)


def row_spec(step, width):
    return pl.BlockSpec((step, width), lambda i, *_: (i, 0))


def column_spec(width, step):
    return pl.BlockSpec((width, step), lambda i, *_: (0, i))


def swap_halves(block):
    lane = lax.broadcasted_iota(jnp.int32, block.shape, 1)
    width = block.shape[1]
    return jnp.where((lane & 32) == 0, pltpu.roll(block, width - 32, 1), pltpu.roll(block, 32, 1))


def wide_table(table, width):
    return jnp.concatenate([table] * (width // 128), axis=1)


def qkv_kernel(x_ref, w_ref, b_ref, cos_ref, sin_ref, out_ref):
    which = pl.program_id(0)
    mixed = mm(x_ref[...], w_ref[0]) + b_ref[pl.ds(which, 1), :]
    width = mixed.shape[1]

    @pl.when(which < 2)
    def _():
        turned = mixed * wide_table(cos_ref[...], width)
        turned = turned + swap_halves(mixed) * wide_table(sin_ref[...], width)
        out_ref[0] = turned.astype(BF16)

    @pl.when(which == 2)
    def _():
        out_ref[0] = mixed.astype(BF16)


def project_qkv(x, weight, bias, cosine, sine):
    n, D = x.shape
    width = weight.shape[2]
    step = row_step(n)
    return call(
        qkv_kernel, "project_qkv", (3, n // step),
        [
            pl.BlockSpec((step, D), lambda j, i: (i, 0)),
            pl.BlockSpec((1, D, width), lambda j, i: (j, 0, 0)),
            held(bias.shape),
            pl.BlockSpec((step, 128), lambda j, i: (i, 0)),
            pl.BlockSpec((step, 128), lambda j, i: (i, 0)),
        ],
        [pl.BlockSpec((1, step, width), lambda j, i: (j, i, 0))],
        [shaped(BF16, 3, n, width)],
        (x, weight, bias, cosine, sine), 6 * n * D * width,
    )[0]


def normed_rows(residual):
    mean = jnp.mean(residual, axis=1, keepdims=True)
    centred = residual - mean
    inverse = lax.rsqrt(jnp.mean(centred * centred, axis=1, keepdims=True) + 1e-05)
    return centred * inverse, inverse


def norm_pull(grad_rows, normed, inverse, gain):
    spread = grad_rows * gain
    return inverse * (
        spread
        - jnp.mean(spread, axis=1, keepdims=True)
        - normed * jnp.mean(spread * normed, axis=1, keepdims=True)
    )


def column_sums(*arrays):
    rows = [jnp.sum(array, axis=0, keepdims=True) for array in arrays]
    rows.append(jnp.zeros((8 - len(rows), rows[0].shape[1]), F32))
    return jnp.concatenate(rows, axis=0)


def add_over_steps(ref, value):
    first = pl.program_id(0) == 0

    @pl.when(first)
    def _():
        ref[...] = value

    @pl.when(jnp.logical_not(first))
    def _():
        ref[...] += value


def out_norm_kernel(slots, *refs):
    x_ref, vec_ref = refs[:2]
    att_refs, w_refs = refs[2 : 2 + slots], refs[2 + slots : 2 + 2 * slots]
    normed_ref, inverse_ref, low_ref, turned_ref = refs[2 + 2 * slots :]
    residual = x_ref[...].astype(F32) + vec_ref[0:1, :]
    for att_ref, w_ref in zip(att_refs, w_refs):
        residual = residual + mm(att_ref[...], w_ref[...])
    normed, inverse = normed_rows(residual)
    hidden = normed * vec_ref[1:2, :] + vec_ref[2:3, :]
    normed_ref[...] = normed
    inverse_ref[...] = inverse
    low_ref[...] = hidden.astype(BF16)
    turned_ref[...] = hidden.T.astype(BF16)


def out_and_norm(x, vectors, attended, weights):
    n, D = x.shape
    step = row_step(n)
    slots = len(attended)
    width = attended[0].shape[1]
    return call(
        functools.partial(out_norm_kernel, slots), "out_and_norm", (n // step,),
        [row_spec(step, D), held(vectors.shape)]
        + [row_spec(step, width)] * slots + [held((width, D))] * slots,
        [row_spec(step, D), row_spec(step, 1), row_spec(step, D), column_spec(D, step)],
        [shaped(F32, n, D), shaped(F32, n, 1), shaped(BF16, n, D), shaped(BF16, D, n)],
        (x, vectors, *attended, *weights), 2 * n * D * D,
    )


GELU_TERMS = (
    0.23532527933595032, 0.09138803439798156, 0.6495603483388861,
    -0.6354014529895687, 0.8866650885491606, -0.22753729931242958,
)


def gelu_parts(values):
    size = jnp.abs(values)
    part = pl.reciprocal(1.0 + (0.39 / math.sqrt(2.0)) * size)
    bell = jnp.exp(-0.5 * (values * values))
    series = 0.5 * GELU_TERMS[-1]
    for term in GELU_TERMS[-2::-1]:
        series = series * part + 0.5 * term
    tail = series * part * bell
    below = jnp.where(values >= 0.0, 1.0 - tail, tail)
    return values * below, below + values * bell * (1.0 / math.sqrt(2.0 * math.pi))


def up_kernel(x_ref, w_ref, b_ref, active_ref, slope_ref):
    width = w_ref.shape[1]
    chunk = min(512, width)
    for first in range(0, width, chunk):
        at = slice(first, first + chunk)
        active, slope = gelu_parts(mm(x_ref[...], w_ref[:, at]) + b_ref[:, at])
        active_ref[:, at] = active.astype(BF16)
        slope_ref[:, at] = slope


def up_and_gelu(x, weight, bias):
    n, D = x.shape
    width = weight.shape[1]
    step = row_step(n)
    return call(
        up_kernel, "up_and_gelu", (n // step,),
        [row_spec(step, D), held(weight.shape), held(bias.shape)],
        [row_spec(step, width)] * 2,
        [shaped(BF16, n, width), shaped(F32, n, width)],
        (x, weight, bias), 5 * n * D * width,
    )


def down_norm_kernel(slots, *refs):
    normed_ref, vec_ref, proj_ref = refs[:3]
    act_refs, w_refs = refs[3 : 3 + slots], refs[3 + slots : 3 + 2 * slots]
    normed_out, inverse_ref, low_ref, unit_ref, unit_low_ref, unit_inverse_ref = refs[3 + 2 * slots :]
    residual = normed_ref[...] * vec_ref[1:2, :] + vec_ref[2:3, :] + vec_ref[3:4, :]
    for act_ref, w_ref in zip(act_refs, w_refs):
        residual = residual + mm(act_ref[...], w_ref[...])
    normed, inverse = normed_rows(residual)
    normed_out[...] = normed
    inverse_ref[...] = inverse
    low = (normed * vec_ref[4:5, :] + vec_ref[5:6, :]).astype(BF16)
    low_ref[...] = low
    embedding = mm(low, proj_ref[...])
    unit_inverse = lax.rsqrt(jnp.sum(embedding * embedding, axis=1, keepdims=True) + 1e-06)
    unit = embedding * unit_inverse
    unit_ref[...] = unit
    unit_low_ref[...] = unit.astype(BF16)
    unit_inverse_ref[...] = unit_inverse


def down_and_norm(normed, vectors, proj, active, weights):
    n, D = normed.shape
    step = row_step(n)
    slots = len(active)
    width = active[0].shape[1]
    return call(
        functools.partial(down_norm_kernel, slots), "down_and_norm", (n // step,),
        [row_spec(step, D), held(vectors.shape), held(proj.shape)]
        + [row_spec(step, width)] * slots + [held((width, D))] * slots,
        [
            row_spec(step, D), row_spec(step, 1), row_spec(step, D),
            row_spec(step, 128), row_spec(step, 128), row_spec(step, 1),
        ],
        [
            shaped(F32, n, D), shaped(F32, n, 1), shaped(BF16, n, D),
            shaped(F32, n, 128), shaped(BF16, n, 128), shaped(F32, n, 1),
        ],
        (normed, vectors, proj, *active, *weights), 2 * n * D * width * slots,
    )


def head_pull_kernel(
    grad_ref, unit_ref, unit_inverse_ref, proj_ref, normed_ref, inverse_ref, vec_ref,
    embed_ref, residual_ref, low_ref, turned_ref, sum_ref,
):
    grad, unit = grad_ref[...], unit_ref[...]
    embed = unit_inverse_ref[...] * (grad - unit * jnp.sum(grad * unit, axis=1, keepdims=True))
    embed = embed.astype(BF16)
    embed_ref[...] = embed
    output_grad = mm(embed, proj_ref[...], NT)
    normed = normed_ref[...]
    residual = norm_pull(output_grad, normed, inverse_ref[...], vec_ref[4:5, :])
    residual_ref[...] = residual
    low_ref[...] = residual.astype(BF16)
    turned_ref[...] = residual.T.astype(BF16)
    add_over_steps(sum_ref, column_sums(residual, output_grad * normed, output_grad))


def head_pull(unit_grad, unit, unit_inverse, proj, normed, inverse, vectors):
    n, D = normed.shape
    step = row_step(n)
    return call(
        head_pull_kernel, "head_pull", (n // step,),
        [
            row_spec(step, 128), row_spec(step, 128), row_spec(step, 1), held(proj.shape),
            row_spec(step, D), row_spec(step, 1), held(vectors.shape),
        ],
        [
            row_spec(step, 128), row_spec(step, D), row_spec(step, D),
            column_spec(D, step), pl.BlockSpec((8, D), lambda i: (0, 0)),
        ],
        [
            shaped(BF16, n, 128), shaped(F32, n, D), shaped(BF16, n, D),
            shaped(BF16, D, n), shaped(F32, 8, D),
        ],
        (unit_grad, unit, unit_inverse, proj, normed, inverse, vectors), 4 * n * D * 128,
    )


def up_pull_kernel(branch_ref, w_ref, slope_ref, out_ref, sum_ref):
    width = w_ref.shape[0]
    chunk = min(512, width)
    sums = []
    for first in range(0, width, chunk):
        at = slice(first, first + chunk)
        low = (mm(branch_ref[...], w_ref[at, :], NT) * slope_ref[:, at]).astype(BF16)
        out_ref[:, at] = low
        sums.append(column_sums(low.astype(F32)))
    add_over_steps(sum_ref, jnp.concatenate(sums, axis=1))


def up_pull(branch, weight, slope):
    n, D = branch.shape
    width = weight.shape[0]
    step = row_step(n)
    return call(
        up_pull_kernel, "up_pull", (n // step,),
        [row_spec(step, D), held(weight.shape), row_spec(step, width)],
        [row_spec(step, width), pl.BlockSpec((8, width), lambda i: (0, 0))],
        [shaped(BF16, n, width), shaped(F32, 8, width)],
        (branch, weight, slope), 2 * n * D * width,
    )


def hidden_pull_kernel(slots, *refs):
    residual_ref, normed_ref, inverse_ref, vec_ref = refs[:4]
    pre_refs, up_refs, out_refs = (refs[4 + j * slots : 4 + (j + 1) * slots] for j in range(3))
    rest = refs[4 + 3 * slots :]
    grad_ref, turned_ref, sum_ref = rest[:3]
    att_refs = rest[3:]
    hidden_grad = residual_ref[...]
    for pre_ref, up_ref in zip(pre_refs, up_refs):
        hidden_grad = hidden_grad + mm(pre_ref[...], up_ref[...], NT)
    normed = normed_ref[...]
    residual = norm_pull(hidden_grad, normed, inverse_ref[...], vec_ref[1:2, :])
    grad_ref[...] = residual
    low = residual.astype(BF16)
    turned_ref[...] = residual.T.astype(BF16)
    add_over_steps(sum_ref, column_sums(residual, hidden_grad * normed, hidden_grad))
    for att_ref, out_ref in zip(att_refs, out_refs):
        att_ref[...] = mm(low, out_ref[...], NT).astype(BF16)


def hidden_pull(residual, normed, inverse, vectors, pre_grads, ups, outs):
    n, D = residual.shape
    step = row_step(n)
    slots = len(ups)
    wide, width = ups[0].shape[1], outs[0].shape[0]
    return call(
        functools.partial(hidden_pull_kernel, slots), "hidden_pull", (n // step,),
        [row_spec(step, D), row_spec(step, D), row_spec(step, 1), held(vectors.shape)]
        + [row_spec(step, wide)] * slots + [held((D, wide))] * slots
        + [held((width, D))] * slots,
        [row_spec(step, D), column_spec(D, step), pl.BlockSpec((8, D), lambda i: (0, 0))]
        + [row_spec(step, width)] * slots,
        [shaped(F32, n, D), shaped(BF16, D, n), shaped(F32, 8, D)]
        + [shaped(BF16, n, width)] * slots,
        (residual, normed, inverse, vectors, *pre_grads, *ups, *outs),
        2 * n * D * (wide + width) * slots,
    )


def token_pull_kernel(slots, place_ref, *refs):
    residual_ref = refs[0]
    mixed_refs, w_refs = refs[1 : 1 + slots], refs[1 + slots : 1 + 2 * slots]
    out_ref = refs[-1]
    width = out_ref.shape[1]
    at = pl.ds(pl.multiple_of(place_ref[0] * width, width), width)
    total = residual_ref[...]
    for mixed_ref, w_ref in zip(mixed_refs, w_refs):
        for which in range(3):
            total = total + mm(mixed_ref[which], w_ref[which, at, :], NT)
    out_ref[...] = total.astype(out_ref.dtype)


def token_pull(place, residual, mixed_grads, weights, dtype):
    n, D = residual.shape
    step = row_step(n)
    slots = len(weights)
    width = weights[0].shape[2]
    return call(
        functools.partial(token_pull_kernel, slots), "token_pull", (n // step,),
        [pl.BlockSpec((step, width), lambda i, p: (i, p[0]))]
        + [pl.BlockSpec((3, step, width), lambda i, p: (0, i, 0))] * slots
        + [held((3, D, width))] * slots,
        [row_spec(step, width)],
        [shaped(dtype, n, width)],
        (place.reshape(1), residual, *mixed_grads, *weights), 6 * n * D * width, prefetch=1,
    )[0]


def weight_pull_kernel(place_ref, left_ref, right_ref, *refs):
    out_ref = refs[-1]
    total = mm(left_ref[:, 0].reshape(-1, left_ref.shape[-1]), right_ref[0])
    if len(refs) > 1:
        total = total + refs[0][0].astype(F32)
    out_ref[0] = total.astype(out_ref.dtype)


def weight_pull(place, left, right, arrived, dtype):
    pairs, _, share, n = left.shape
    count, _, m = right.shape
    rows = pairs * share
    chunk = min(512, m)
    spec = pl.BlockSpec((1, rows, chunk), lambda j, i, p: (j, 0, i))
    return call(
        weight_pull_kernel, "weight_pull", (count, m // chunk),
        [
            pl.BlockSpec((pairs, 1, share, n), lambda j, i, p: (0, p[0], 0, 0)),
            pl.BlockSpec((1, n, chunk), lambda j, i, p: (j, 0, i)),
        ] + ([] if arrived is None else [spec]),
        [spec],
        [shaped(dtype, count, rows, m)],
        (place.reshape(1), left, right) + (() if arrived is None else (arrived,)),
        2 * count * rows * n * m, prefetch=1,
    )[0]


SEGMENTS = 8


def half_lanes(block, head, other):
    lane = lax.broadcasted_iota(jnp.int32, block.shape, 1)
    return jnp.where((lane >= DH) == (head == 1), block, other)


def scaled(block):
    return (block.astype(F32) * DH**-0.5).astype(BF16)


def three_terms(value):
    high = value.astype(BF16).astype(F32)
    middle = (value - high).astype(BF16).astype(F32)
    return high, middle, value - high - middle


def attention_forward_kernel(
    span_ref, qkv_ref, ext_k_ref, ext_q_ref, out_ref, rest_ref, ext_ref,
    keys_ref, queries_ref, values_ref, logits_ref, *, tile,
):
    n = ext_k_ref.shape[0]
    tiles = n // tile
    for head in range(2):
        keys_ref[head] = half_lanes(qkv_ref[1], head, ext_k_ref[...])
        queries_ref[head] = half_lanes(scaled(qkv_ref[0]), head, ext_q_ref[...])
    for step in range(tiles):
        block = qkv_ref[2, step * tile : (step + 1) * tile, :]
        values_ref[step] = block.astype(F32).T.astype(BF16)

    def rows(step):
        return pl.ds(pl.multiple_of(step * tile, tile), tile)

    def by_eight(block):
        return block.reshape(tile // 8, 8, tile)

    @pl.loop(0, tiles)
    def _(step):
        low, high = span_ref[step], span_ref[tiles + step]
        queries = [queries_ref[head, rows(step), :] for head in range(2)]

        def find_top(block, tops):
            found = []
            for head in range(2):
                logits = mm(keys_ref[head, rows(block), :], queries[head], NT)
                logits_ref[head, block] = logits
                found.append(jnp.maximum(tops[head], jnp.max(by_eight(logits), axis=0)))
            return tuple(found)

        start = jnp.full((8, tile), -3e38, F32)
        tops = lax.fori_loop(low, high, find_top, (start, start))
        tops = [jnp.max(top, axis=0, keepdims=True) for top in tops]

        def add_mass(block, masses):
            after = []
            for head in range(2):
                weights = jnp.exp(logits_ref[head, block] - tops[head])
                logits_ref[head, block] = weights
                after.append(masses[head] + jnp.sum(by_eight(weights), axis=0))
            return tuple(after)

        start = jnp.zeros((8, tile), F32)
        masses = lax.fori_loop(low, high, add_mass, (start, start))
        masses = [jnp.sum(mass, axis=0, keepdims=True) for mass in masses]
        shares = [1.0 / mass for mass in masses]

        def add_values(block, totals):
            after = []
            for head in range(2):
                probs = (logits_ref[head, block] * shares[head]).astype(BF16)
                values = values_ref[block, head * DH : (head + 1) * DH, :]
                after.append(totals[head] + mm(values, probs))
            return tuple(after)

        zero = jnp.zeros((DH, tile), F32)
        outs = lax.fori_loop(low, high, add_values, (zero, zero))
        extras = []
        for head in range(2):
            terms = three_terms(-(tops[head] + jnp.log(masses[head])))
            extras.append(
                jnp.concatenate(
                    [jnp.zeros((8, tile), F32), *terms, jnp.zeros((DH - 11, tile), F32)], axis=0
                )
            )
        out = jnp.concatenate(outs, axis=0).T
        out_ref[rows(step), :] = out.astype(BF16)
        rest_ref[rows(step), :] = (out - out.astype(BF16).astype(F32)).astype(BF16)
        extra = jnp.concatenate(extras[::-1], axis=0).T
        ext_ref[rows(step), :] = (extra + ext_q_ref[rows(step), :].astype(F32)).astype(BF16)


def attention_forward(spans, qkv, ext_k, ext_q, tile):
    _, n, width = qkv.shape
    wide = pl.BlockSpec((n, 128), lambda i, *_: (0, i))
    tiles = n // tile
    return call(
        functools.partial(attention_forward_kernel, tile=tile), "attention_forward",
        (width // 128,),
        [pl.BlockSpec((3, n, 128), lambda i, *_: (0, 0, i)), held((n, 128)), held((n, 128))],
        [wide, wide, wide],
        [shaped(BF16, n, width)] * 3,
        (spans, qkv, ext_k, ext_q), 6_000_000_000, prefetch=1,
        scratch=[
            pltpu.VMEM((2, n, 128), BF16), pltpu.VMEM((2, n, 128), BF16),
            pltpu.VMEM((tiles, 128, tile), BF16), pltpu.VMEM((2, tiles, tile, tile), F32),
        ],
    )


def attention_backward_kernel(
    span_ref, qkv_ref, ext_ref, att_ref, rest_ref, grad_ref, ext_k_ref, cos_ref, sin_ref,
    out_ref, sum_ref,
    keys_ref, turned_ref, values_ref, queries_ref, plain_ref, grads_ref, plain_grads_ref,
    dq_ref, dk_ref, dv_ref, *, tile,
):
    n = ext_k_ref.shape[0]
    tiles = n // tile
    zeros = jnp.zeros((n, 128), BF16)
    lane = lax.broadcasted_iota(jnp.int32, (n, 128), 1)
    product = grad_ref[...].astype(F32) * (att_ref[...].astype(F32) + rest_ref[...].astype(F32))
    query = scaled(qkv_ref[0])
    for head in range(2):
        keys_ref[head] = half_lanes(qkv_ref[1], head, ext_k_ref[...])
        values_ref[head] = half_lanes(qkv_ref[2], head, ext_k_ref[...])
        queries_ref[head] = half_lanes(query, head, ext_ref[...])
        plain_ref[head] = half_lanes(query, head, zeros)
        plain_grads_ref[head] = half_lanes(grad_ref[...], head, zeros)
        inner = jnp.sum(half_lanes(product, head, 0.0), axis=1, keepdims=True)
        extra = jnp.zeros((n, 128), F32)
        for place, term in enumerate(three_terms(-inner)):
            extra = jnp.where((lane & (DH - 1)) == SEGMENTS + place, term, extra)
        grads_ref[head] = half_lanes(grad_ref[...], head, extra.astype(BF16))
    for step in range(tiles):
        block = scaled(qkv_ref[1, step * tile : (step + 1) * tile, :])
        turned_ref[step] = block.astype(F32).T.astype(BF16)
    dk_ref[...] = jnp.zeros((n, 128), F32)
    dv_ref[...] = jnp.zeros((n, 128), F32)

    def rows(step):
        return pl.ds(pl.multiple_of(step * tile, tile), tile)

    @pl.loop(0, tiles)
    def _(step):
        queries = [queries_ref[head, rows(step), :] for head in range(2)]
        grads = [grads_ref[head, rows(step), :] for head in range(2)]
        plain = jnp.concatenate([plain_ref[head, rows(step), :] for head in range(2)], axis=0)
        plain_grads = jnp.concatenate(
            [plain_grads_ref[head, rows(step), :] for head in range(2)], axis=0
        )

        def one_block(block, totals):
            probs, slopes, after = [], [], []
            for head in range(2):
                weights = jnp.exp(mm(keys_ref[head, rows(block), :], queries[head], NT))
                flow = mm(values_ref[head, rows(block), :], grads[head], NT)
                slope = (weights * flow).astype(BF16)
                probs.append(weights.astype(BF16))
                slopes.append(slope)
                turned = turned_ref[block, head * DH : (head + 1) * DH, :]
                after.append(totals[head] + mm(turned, slope))
            dv_ref[rows(block), :] += mm(jnp.concatenate(probs, axis=1), plain_grads)
            dk_ref[rows(block), :] += mm(jnp.concatenate(slopes, axis=1), plain)
            return tuple(after)

        zero = jnp.zeros((DH, tile), F32)
        totals = lax.fori_loop(span_ref[step], span_ref[tiles + step], one_block, (zero, zero))
        dq_ref[rows(step), :] = jnp.concatenate(totals, axis=0).T

    def finish(step, sums):
        cosine, sine = cos_ref[rows(step), :], sin_ref[rows(step), :]
        added = []
        for which, src in enumerate((dq_ref, dk_ref, dv_ref)):
            block = src[rows(step), :]
            if which < 2:
                block = block * cosine - swap_halves(block) * sine
            low = block.astype(BF16)
            out_ref[which, rows(step), :] = low
            added.append(sums[which] + jnp.sum(low.astype(F32), axis=0, keepdims=True))
        return tuple(added)

    zero = jnp.zeros((1, 128), F32)
    sums = lax.fori_loop(0, tiles, finish, (zero, zero, zero))
    sum_ref[...] = jnp.concatenate(sums + (jnp.zeros((5, 128), F32),), axis=0)


def attention_backward(spans, qkv, ext, attended, rest, grads, ext_k, cosine, sine, tile):
    _, n, width = qkv.shape
    wide = pl.BlockSpec((n, 128), lambda i, *_: (0, i))
    three = pl.BlockSpec((3, n, 128), lambda i, *_: (0, 0, i))
    tiles = n // tile
    two = pltpu.VMEM((2, n, 128), BF16)
    return call(
        functools.partial(attention_backward_kernel, tile=tile), "attention_backward",
        (width // 128,),
        [three, wide, wide, wide, wide, held((n, 128)), held((n, 128)), held((n, 128))],
        [three, pl.BlockSpec((8, 128), lambda i, *_: (0, i))],
        [shaped(BF16, 3, n, width), shaped(F32, 8, width)],
        (spans, qkv, ext, attended, rest, grads, ext_k, cosine, sine), 15_000_000_000, prefetch=1,
        scratch=[two, pltpu.VMEM((tiles, 128, tile), BF16)] + [two] * 5
        + [pltpu.VMEM((n, 128), F32)] * 3,
    )


STRIP = 32


def score_kernel(begin_ref, size_ref, doc_ref, query_ref, pick_ref, out_ref, sim_ref):
    group = pl.program_id(0)
    docs, width = pick_ref.shape[1:]
    chunk = min(256, doc_ref.shape[0])

    @pl.loop(0, doc_ref.shape[0] // chunk)
    def _(step):
        at = pl.ds(pl.multiple_of(step * chunk, chunk), chunk)
        sim_ref[at, :] = mm(doc_ref[at, :], query_ref[...], NT)

    for doc in range(docs):
        begin = begin_ref[group * docs + doc]
        end = begin + size_ref[group * docs + doc]
        pick = pick_ref[0, doc : doc + 1, :]

        def strip(step, total):
            first = pl.multiple_of(step * STRIP, STRIP)
            row = lax.broadcasted_iota(jnp.int32, (STRIP, width), 0) + first
            held = jnp.where(row == pick, sim_ref[pl.ds(first, STRIP), :], 0.0)
            return total + jnp.sum(held.reshape(STRIP // 8, 8, width), axis=0)

        total = lax.fori_loop(
            begin // STRIP, (end + STRIP - 1) // STRIP, strip, jnp.zeros((8, width), F32)
        )
        out_ref[0, doc : doc + 1, :] = jnp.sum(total, axis=0, keepdims=True)


def score_grad_kernel(
    begin_ref, size_ref, doc_ref, query_ref, pick_ref, weight_ref, doc_out, query_out, sparse_ref
):
    group = pl.program_id(0)
    docs, width = pick_ref.shape[1:]
    doc_rows = doc_ref.shape[0]

    @pl.loop(0, doc_rows // STRIP)
    def _(step):
        first = pl.multiple_of(step * STRIP, STRIP)
        row = lax.broadcasted_iota(jnp.int32, (STRIP, width), 0) + first
        low = jnp.int32(0)
        high = jnp.int32(0)
        for doc in range(docs):
            begin = begin_ref[group * docs + doc]
            end = begin + size_ref[group * docs + doc]
            low += (end <= first).astype(jnp.int32)
            high += (begin < first + STRIP).astype(jnp.int32)

        def one_doc(doc, held):
            pick = pick_ref[0, pl.ds(doc, 1), :]
            return jnp.where(row == pick, weight_ref[0, pl.ds(doc, 1), :], held)

        held = lax.fori_loop(low, high, one_doc, jnp.zeros((STRIP, width), F32))
        sparse_ref[pl.ds(first, STRIP), :] = held.astype(BF16)

    docs_t = doc_ref[...].astype(F32).T.astype(BF16)
    doc_out[...] = mm(sparse_ref[...], query_ref[...])

    @pl.when(group == 0)
    def _():
        query_out[...] = jnp.zeros_like(query_out)

    query_out[...] += mm(docs_t, sparse_ref[...])


def score_specs(doc_tile, query_tile, picks):
    groups, docs, width = picks.shape
    doc_rows = doc_tile.shape[0] // groups
    return (
        pl.BlockSpec((doc_rows, 128), lambda i, *_: (i, 0)),
        pl.BlockSpec(query_tile.shape, lambda i, *_: (0, 0)),
        pl.BlockSpec((1, docs, width), lambda i, *_: (i, 0, 0)),
    )


def score_forward(begins, sizes, doc_tile, query_tile, picks):
    groups, docs, width = picks.shape
    doc_spec, query_spec, pick_spec = score_specs(doc_tile, query_tile, picks)
    return pl.pallas_call(
        score_kernel,
        grid_spec=pltpu.PrefetchScalarGridSpec(
            num_scalar_prefetch=2,
            grid=(groups,),
            in_specs=[doc_spec, query_spec, pick_spec],
            out_specs=pick_spec,
            scratch_shapes=[pltpu.VMEM((doc_tile.shape[0] // groups, width), F32)],
        ),
        out_shape=jax.ShapeDtypeStruct((groups, docs, width), F32),
        compiler_params=pltpu.CompilerParams(vmem_limit_bytes=VMEM_LIMIT),
        name="score_forward",
    )(begins, sizes, doc_tile, query_tile, picks)


def score_backward(begins, sizes, doc_tile, query_tile, picks, weights):
    groups, docs, width = picks.shape
    doc_spec, query_spec, pick_spec = score_specs(doc_tile, query_tile, picks)
    return pl.pallas_call(
        score_grad_kernel,
        grid_spec=pltpu.PrefetchScalarGridSpec(
            num_scalar_prefetch=2,
            grid=(groups,),
            in_specs=[doc_spec, query_spec, pick_spec, pick_spec],
            out_specs=[doc_spec, pl.BlockSpec((128, width), lambda i, *_: (0, 0))],
            scratch_shapes=[pltpu.VMEM((doc_tile.shape[0] // groups, width), BF16)],
        ),
        out_shape=[
            jax.ShapeDtypeStruct(doc_tile.shape, F32),
            jax.ShapeDtypeStruct((128, width), F32),
        ],
        compiler_params=pltpu.CompilerParams(vmem_limit_bytes=VMEM_LIMIT),
        name="score_backward",
    )(begins, sizes, doc_tile, query_tile, picks, weights)


def rotary_tables(position):
    half_size = DH // 2
    frequency = jnp.exp(
        jnp.arange(half_size, dtype=F32) * (-2.0 * math.log(10000.0) / DH)
    )
    angles = position.astype(F32)[:, None] * frequency[None, :]
    cosine, sine = jnp.cos(angles), jnp.sin(angles)
    return (
        jnp.concatenate([cosine] * 4, axis=1),
        jnp.concatenate([-sine, sine, -sine, sine], axis=1),
    )


def on_device(
    tokens,
    doc_lengths,
    match_picks,
    labels,
    w_qkv,
    b_qkv,
    w_out,
    b_out,
    ln1_gain,
    ln1_bias,
    w_up,
    b_up,
    w_down,
    b_down,
    ln2_gain,
    ln2_bias,
    w_proj,
    log_scale,
):
    C = lax.axis_size("cols")
    R = lax.axis_size("rows")
    c = lax.axis_index("cols")
    r = lax.axis_index("rows")
    width = tokens.shape[1]
    D = width * C
    Q = ROW_LEN // C
    DS = (tokens.shape[0] - ROW_LEN) // C
    n = Q + DS
    tile = math.gcd(256, math.gcd(Q, DS))

    def shift_cols(value, k):
        return lax.ppermute(value, "cols", [(i, (i + k) % C) for i in range(C)])

    def swap_rows(value, bit):
        return lax.ppermute(value, "rows", [(i, i ^ bit) for i in range(R)])

    def in_order(slots):
        if len(slots) == 1:
            return slots
        if len(slots) == 2:
            return [lax.select(c == 0, slots[0], slots[1]), lax.select(c == 0, slots[1], slots[0])]
        stacked = jnp.stack(slots)
        return [
            lax.dynamic_index_in_dim(stacked, (c - j) % C, 0, keepdims=False) for j in range(C)
        ]

    parts = jnp.concatenate(
        [tokens[:ROW_LEN].reshape(C, Q, width), tokens[ROW_LEN:].reshape(C, DS, width)], axis=1
    )

    def part(k):
        return lax.dynamic_index_in_dim(parts, (c + k) % C, 0, keepdims=False)

    slots = [part(0)] + [shift_cols(part(k), k) for k in range(1, C)]
    x = jnp.concatenate(in_order(slots), axis=1)

    def gather_slots(shard):
        flat = shard.reshape(-1, shard.shape[-1])
        piece = lax.dynamic_index_in_dim(
            flat.reshape(R, flat.shape[0] // R, flat.shape[1]), r, 0, keepdims=False
        )
        others = [
            lax.all_gather(shift_cols(piece, k), "rows", axis=0, tiled=True).reshape(shard.shape)
            for k in range(1, C)
        ]
        return [shard] + others

    wqkv_slots = gather_slots(w_qkv)
    wout_slots = gather_slots(w_out)
    wup_slots = gather_slots(w_up)
    wdown_slots = gather_slots(w_down)
    wproj = jnp.concatenate(
        in_order([w_proj] + [shift_cols(w_proj, k) for k in range(1, C)]), axis=0
    )

    pack = [b_qkv.reshape(-1), b_up, b_out, ln1_gain, ln1_bias, b_down, ln2_gain, ln2_bias]
    ends = [0]
    for vector in pack:
        ends.append(ends[-1] + vector.shape[0])
    packed = jnp.concatenate(pack)
    packs = [packed] + [shift_cols(packed, k) for k in range(1, C)]
    ordered_packs = in_order(packs)

    def of_slot(which, k):
        return packs[k][ends[which] : ends[which + 1]]

    def whole(which):
        return jnp.concatenate([p[ends[which] : ends[which + 1]] for p in ordered_packs])

    bqkv_slots = [of_slot(0, k).reshape(b_qkv.shape) for k in range(C)]
    bup_slots = [of_slot(1, k)[None, :] for k in range(C)]
    bout, gain1, bias1, bdown, gain2, bias2 = [whole(which) for which in range(2, 8)]
    zero_row = jnp.zeros_like(bout)
    vectors = jnp.stack([bout, gain1, bias1, bdown, gain2, bias2, zero_row, zero_row])

    own_sizes = lax.dynamic_index_in_dim(
        lax.dynamic_index_in_dim(doc_lengths, r, 0, keepdims=False), c, 0, keepdims=False
    )
    own_ends = jnp.cumsum(own_sizes)
    places = jnp.arange(DS, dtype=jnp.int32)
    passed = places[:, None] >= own_ends[None, :]
    slot_id = jnp.sum(passed.astype(jnp.int32), axis=1)
    slot_begin = jnp.sum(jnp.where(passed, own_sizes[None, :], 0), axis=1)
    query_places = jnp.arange(Q, dtype=jnp.int32)
    position = jnp.concatenate([query_places % QLEN, places - slot_begin])
    cosine, sine = rotary_tables(position)
    segment = jnp.concatenate([(query_places // QLEN) % SEGMENTS, slot_id])
    lane = jnp.arange(128, dtype=jnp.int32)[None, :] % DH
    same = segment[:, None] == lane
    ext_k = (same | ((lane >= SEGMENTS) & (lane < SEGMENTS + 3))).astype(BF16)
    ext_q = jnp.where((lane < SEGMENTS) & ~same, -1e30, 0.0).astype(BF16)
    q_tiles, d_tiles = Q // tile, DS // tile
    steps = jnp.arange(q_tiles, dtype=jnp.int32)
    first_rows = jnp.arange(d_tiles, dtype=jnp.int32) * tile
    is_passed = first_rows[:, None] >= own_ends[None, :]
    low_rows = jnp.sum(jnp.where(is_passed, own_sizes[None, :], 0), axis=1)
    last_passed = (first_rows + tile - 1)[:, None] >= own_ends[None, :]
    high_rows = jnp.min(jnp.where(last_passed, DS, own_ends[None, :]), axis=1)
    spans = jnp.concatenate(
        [steps, q_tiles + low_rows // tile, steps + 1, q_tiles + (high_rows + tile - 1) // tile]
    ).astype(jnp.int32)

    qkv, attended, rests, exts = [], [], [], []
    for k in range(C):
        qkv.append(project_qkv(x, wqkv_slots[k], bqkv_slots[k], cosine, sine))
        out, rest, ext = attention_forward(spans, qkv[k], ext_k, ext_q, tile)
        attended.append(out)
        rests.append(rest)
        exts.append(ext)
    normed_one, inverse_one, hidden_low, hidden_t = out_and_norm(x, vectors, attended, wout_slots)
    active, slopes = zip(*[up_and_gelu(hidden_low, wup_slots[k], bup_slots[k]) for k in range(C)])
    normed_two, inverse_two, output_low, unit, unit_low, unit_inverse = down_and_norm(
        normed_one, vectors, wproj, active, wdown_slots
    )

    doc_tile = lax.all_gather(unit_low[Q:], "rows", axis=0, tiled=True)
    query_tile = jnp.concatenate(
        in_order([unit_low[:Q]] + [shift_cols(unit_low[:Q], k) for k in range(1, C)]), axis=0
    )
    queries_here, tile_docs, _ = match_picks.shape
    docs = own_sizes.shape[0]
    sizes = lax.dynamic_index_in_dim(doc_lengths, c, 1, keepdims=False)
    begins = jnp.cumsum(sizes, axis=1) - sizes
    sizes_flat, begins_flat = sizes.reshape(-1), begins.reshape(-1)
    picks = jnp.transpose(match_picks, (1, 0, 2)).reshape(tile_docs, queries_here * QLEN)
    picks = begins_flat[:, None] + picks % sizes_flat[:, None]
    picks = picks.reshape(R, docs, queries_here * QLEN)
    sims = score_forward(begins_flat, sizes_flat, doc_tile, query_tile, picks)
    scores = jnp.sum(sims.reshape(tile_docs, queries_here, QLEN), axis=2).T

    scale = jnp.exp(log_scale[0])
    z = scale * scores
    row_top = jnp.max(z, axis=1)
    row_mass = jnp.sum(jnp.exp(z - row_top[:, None]), axis=1)
    is_label = (
        jnp.arange(tile_docs, dtype=jnp.int32)[None, :] == (labels - c * tile_docs)[:, None]
    )
    chosen = jnp.sum(jnp.where(is_label, z, 0.0), axis=1)
    own_stats = jnp.stack([row_top, row_mass, chosen])
    stats = jnp.stack([own_stats] + [shift_cols(own_stats, k) for k in range(1, C)])
    top_all = jnp.max(stats[:, 0], axis=0)
    mass_all = jnp.sum(stats[:, 1] * jnp.exp(stats[:, 0] - top_all), axis=0)
    log_total = top_all + jnp.log(mass_all)
    loss = log_total - jnp.sum(stats[:, 2], axis=0)
    dz = (jnp.exp(z - log_total[:, None]) - is_label.astype(F32)) / (queries_here * R)
    scale_part = jnp.sum(dz * z)
    dscores = (scale * dz).astype(BF16).astype(F32)
    weights = jnp.broadcast_to(
        dscores.T[:, :, None], (tile_docs, queries_here, QLEN)
    ).reshape(R, docs, queries_here * QLEN)
    doc_grad, query_grad_t = score_backward(
        begins_flat, sizes_flat, doc_tile, query_tile, picks, weights
    )
    query_parts = query_grad_t.T.reshape(C, Q, 128)

    def query_part(k):
        return lax.dynamic_index_in_dim(query_parts, (c + k) % C, 0, keepdims=False)

    query_grad = query_part(0)
    for k in range(1, C):
        query_grad = query_grad + shift_cols(query_part(k), k)

    def halve(total, bit, wire):
        size = total.shape[0] // 2
        pairs = total.reshape((size, 2) + total.shape[1:])
        mine = (r // bit) % 2
        send = lax.dynamic_index_in_dim(pairs, 1 - mine, 1, keepdims=False).astype(wire)
        keep = lax.dynamic_index_in_dim(pairs, mine, 1, keepdims=False)
        return keep + swap_rows(send, bit).astype(F32)

    doc_sum = doc_grad.reshape(R, DS, 128)
    bit = 1
    while bit < R:
        doc_sum = halve(doc_sum, bit, BF16)
        bit *= 2
    unit_grad = jnp.concatenate([query_grad, doc_sum[0]], axis=0)

    core = r % 2

    def weight_grad(left_t, right_slots):
        left = left_t.reshape(R // 2, 2, -1, n)
        arrived = [
            swap_rows(weight_pull(1 - core, left, right, None, BF16), 1)
            for right in right_slots[::-1]
        ][::-1]
        total = None
        for k in range(C - 1, 0, -1):
            part = weight_pull(core, left, right_slots[k], arrived[k], BF16)
            part = shift_cols(part, C - k).astype(F32)
            total = part if total is None else total + part
        own = weight_pull(core, left, right_slots[0], arrived[0], F32)
        total = own if total is None else own + total
        total = jnp.moveaxis(total.reshape(total.shape[0], R // 2, -1, total.shape[2]), 1, 0)
        bit = 2
        while bit < R:
            total = halve(total, bit, BF16)
            bit *= 2
        return total[0]

    embed_grad, resid_two_grad, branch, branch_t, head_sums = head_pull(
        unit_grad, unit, unit_inverse, wproj, normed_two, inverse_two, vectors
    )
    down_grad = weight_grad(branch_t, [a[None] for a in active])
    pre_grads, up_sums = zip(
        *[up_pull(branch, wdown_slots[k], slopes[k]) for k in range(C)]
    )
    up_grad = weight_grad(hidden_t, [g[None] for g in pre_grads])
    resid_one_grad, branch_one_t, hidden_sums, *attended_grads = hidden_pull(
        resid_two_grad, normed_one, inverse_one, vectors, pre_grads, wup_slots, wout_slots
    )
    out_grad = weight_grad(branch_one_t, [a[None] for a in attended])
    output_slots = [
        lax.dynamic_slice_in_dim(output_low, ((c - k) % C) * width, width, 1)[None]
        for k in range(C)
    ]
    proj_grad = weight_grad(embed_grad.T, output_slots)
    mixed_grads, mixed_sums = [None] * C, [None] * C
    for k in range(C - 1, -1, -1):
        mixed_grads[k], mixed_sums[k] = attention_backward(
            spans, qkv[k], exts[k], attended[k], rests[k], attended_grads[k], ext_k, cosine, sine,
            tile,
        )
    sent = [
        shift_cols(token_pull((c + k) % C, resid_one_grad, mixed_grads, wqkv_slots, BF16), k)
        for k in range(1, C)
    ]
    kept = token_pull(c, resid_one_grad, mixed_grads, wqkv_slots, F32)
    ordered = in_order([kept] + [s.astype(F32) for s in sent])
    tokens_grad = jnp.concatenate([s[:Q] for s in ordered] + [s[Q:] for s in ordered], axis=0)
    qkv_grad = weight_grad(x.T, mixed_grads)

    def cut(values, slot_rows):
        return values.reshape(slot_rows, R, -1)

    own_order = [(c - k) % C for k in range(C)]
    canonical = jnp.stack(
        [hidden_sums[0], hidden_sums[1], hidden_sums[2], head_sums[0], head_sums[1], head_sums[2]]
    ).reshape(6, C, R, -1)
    slots_small = []
    for k in range(C):
        rows = [mixed_sums[k][j].reshape(R, -1) for j in range(3)]
        rows.append(up_sums[k][0].reshape(R, -1))
        rows += [
            lax.dynamic_index_in_dim(canonical[j], own_order[k], 0, keepdims=False)
            for j in range(6)
        ]
        rows.append(jnp.broadcast_to(scale_part, (R, 1)))
        slots_small.append(jnp.concatenate(rows, axis=1))
    small = halve(jnp.stack(slots_small, axis=1), 1, F32)
    own_small = small[:, 0]
    for k in range(1, C):
        own_small = own_small + shift_cols(small[:, k], C - k)
    bit = 2
    while bit < R:
        own_small = halve(own_small, bit, F32)
        bit *= 2
    small = own_small[0]
    one = D // (C * R)
    up_part = bup_slots[0].shape[1] // R
    bounds = [3 * one, 3 * one + up_part]
    for _ in range(6):
        bounds.append(bounds[-1] + one)
    pieces = [small[a:b] for a, b in zip(bounds[:-1], bounds[1:])]
    bup_out, bout_out, gain1_out, bias1_out, bdown_out, gain2_out, bias2_out = pieces
    return (
        scores,
        loss,
        tokens_grad,
        qkv_grad,
        small[: bounds[0]].reshape(3, one),
        out_grad[0].T,
        bout_out,
        gain1_out,
        bias1_out,
        up_grad[0],
        bup_out,
        down_grad[0].T,
        bdown_out,
        gain2_out,
        bias2_out,
        proj_grad[0].T,
        small[-1:],
    )


def solution(mesh):
    in_specs = (
        P("rows", "cols"),
        P(),
        P("rows", "cols", None),
        P("rows"),
        P(None, None, "cols"),
        P(None, "cols"),
        P("cols", None),
        P("cols"),
        P("cols"),
        P("cols"),
        P(None, "cols"),
        P("cols"),
        P("cols", None),
        P("cols"),
        P("cols"),
        P("cols"),
        P("cols", None),
        P(),
    )
    out_specs = (
        P("rows", "cols"),
        P("rows"),
        P("rows", "cols"),
        P(None, "rows", "cols"),
        P(None, ("cols", "rows")),
        P("cols", "rows"),
        P(("cols", "rows")),
        P(("cols", "rows")),
        P(("cols", "rows")),
        P("rows", "cols"),
        P(("cols", "rows")),
        P("cols", "rows"),
        P(("cols", "rows")),
        P(("cols", "rows")),
        P(("cols", "rows")),
        P("cols", "rows"),
        P(),
    )
    return jax.shard_map(
        on_device, mesh=mesh, in_specs=in_specs, out_specs=out_specs, check_vma=False
    )
```

```python
import functools
import math

import jax
import jax.numpy as jnp
from jax import lax
from jax.experimental import pallas as pl
from jax.experimental.pallas import tpu as pltpu
from jax.sharding import PartitionSpec as P

DH = 64
QLEN = 32
ROW_LEN = 1024
F32 = jnp.float32
BF16 = jnp.bfloat16
VMEM_LIMIT = 56 * 1024 * 1024
NT = (((1,), (1,)), ((), ()))
NN = (((1,), (0,)), ((), ()))
TN = (((0,), (0,)), ((), ()))


def mm(left, right, dims=NN):
    return lax.dot_general(left, right, dims, preferred_element_type=F32)


def row_step(rows):
    return 512 if rows % 512 == 0 else 128


def parts_of(step):
    size = min(step, 256)
    return [slice(first, first + size) for first in range(0, step, size)]


def held(shape):
    return pl.BlockSpec(shape, lambda *_: (0,) * len(shape), pipeline_mode=pl.Buffered(1))


def shaped(dtype, *shape):
    return jax.ShapeDtypeStruct(shape, dtype)


class Order:
    last = ()


def call(
    body, name, grid, in_specs, out_specs, out_shape, operands, flops, scratch=(), prefetch=0, after=()
):
    count = len(operands)
    after = tuple(after) + Order.last

    def wrapped(*refs):
        body(*refs[:count], *refs[count + len(after) :])

    size = sum(math.prod(o.shape) * o.dtype.itemsize for o in list(operands) + list(out_shape))
    if flops == 0:
        size = 1024
    outs = pl.pallas_call(
        wrapped,
        grid_spec=pltpu.PrefetchScalarGridSpec(
            num_scalar_prefetch=prefetch,
            grid=grid,
            in_specs=list(in_specs) + [pl.BlockSpec(memory_space=pl.ANY)] * len(after),
            out_specs=out_specs,
            scratch_shapes=list(scratch),
        ),
        out_shape=out_shape,
        compiler_params=pltpu.CompilerParams(vmem_limit_bytes=VMEM_LIMIT),
        cost_estimate=pl.CostEstimate(flops=flops, bytes_accessed=size, transcendentals=0),
        name=name,
    )(*operands, *after)
    Order.last = (min(outs, key=lambda out: out.size * out.dtype.itemsize),)
    return outs


def row_spec(step, width):
    return pl.BlockSpec((step, width), lambda i, *_: (i, 0))


def column_spec(width, step):
    return pl.BlockSpec((width, step), lambda i, *_: (0, i))


def swap_halves(block):
    lane = lax.broadcasted_iota(jnp.int32, block.shape, 1)
    return jnp.where((lane & 32) == 0, pltpu.roll(block, 96, 1), pltpu.roll(block, 32, 1))


def qkv_kernel(x_ref, w_ref, b_ref, cos_ref, sin_ref, out_ref):
    which = pl.program_id(0)
    bias = b_ref[pl.ds(which, 1), :]

    @pl.when(which < 2)
    def _():
        for at in parts_of(x_ref.shape[0]):
            mixed = mm(x_ref[at, :], w_ref[0]) + bias
            for first in range(0, mixed.shape[1], 128):
                block = mixed[:, first : first + 128]
                turned = block * cos_ref[at, :] + swap_halves(block) * sin_ref[at, :]
                out_ref[0, at, first : first + 128] = turned.astype(BF16)

    @pl.when(which == 2)
    def _():
        for at in parts_of(x_ref.shape[0]):
            out_ref[0, at, :] = (mm(x_ref[at, :], w_ref[0]) + bias).astype(BF16)


def project_qkv(x, weight, bias, cosine, sine, after=()):
    n, D = x.shape
    width = weight.shape[2]
    step = row_step(n)
    return call(
        qkv_kernel, "project_qkv", (3, n // step),
        [
            pl.BlockSpec((step, D), lambda j, i: (i, 0)),
            pl.BlockSpec((1, D, width), lambda j, i: (j, 0, 0)),
            held(bias.shape),
            pl.BlockSpec((step, 128), lambda j, i: (i, 0)),
            pl.BlockSpec((step, 128), lambda j, i: (i, 0)),
        ],
        [pl.BlockSpec((1, step, width), lambda j, i: (j, i, 0))],
        [shaped(BF16, 3, n, width)],
        (x, weight, bias, cosine, sine), 6 * n * D * width, after=after,
    )[0]


def normed_rows(residual):
    mean = jnp.mean(residual, axis=1, keepdims=True)
    centred = residual - mean
    inverse = lax.rsqrt(jnp.mean(centred * centred, axis=1, keepdims=True) + 1e-05)
    return centred * inverse, inverse


def norm_pull(grad_rows, normed, inverse, gain):
    spread = grad_rows * gain
    return inverse * (
        spread
        - jnp.mean(spread, axis=1, keepdims=True)
        - normed * jnp.mean(spread * normed, axis=1, keepdims=True)
    )


def column_sums(*arrays):
    rows = [jnp.sum(array, axis=0, keepdims=True) for array in arrays]
    rows.append(jnp.zeros((8 - len(rows), rows[0].shape[1]), F32))
    return jnp.concatenate(rows, axis=0)


def add_over_steps(ref, value):
    first = pl.program_id(0) == 0

    @pl.when(first)
    def _():
        ref[...] = value

    @pl.when(jnp.logical_not(first))
    def _():
        ref[...] += value


def out_norm_kernel(slots, *refs):
    x_ref, vec_ref = refs[:2]
    att_refs, w_refs = refs[2 : 2 + slots], refs[2 + slots : 2 + 2 * slots]
    normed_ref, inverse_ref, low_ref, turned_ref = refs[2 + 2 * slots :]
    for at in parts_of(x_ref.shape[0]):
        residual = x_ref[at, :].astype(F32) + vec_ref[0:1, :]
        for att_ref, w_ref in zip(att_refs, w_refs):
            residual = residual + mm(att_ref[at, :], w_ref[...])
        normed, inverse = normed_rows(residual)
        hidden = normed * vec_ref[1:2, :] + vec_ref[2:3, :]
        normed_ref[at, :] = normed
        inverse_ref[at, :] = inverse
        low_ref[at, :] = hidden.astype(BF16)
        turned_ref[:, at] = hidden.T.astype(BF16)


def out_and_norm(x, vectors, attended, weights):
    n, D = x.shape
    step = row_step(n)
    slots = len(attended)
    width = attended[0].shape[1]
    return call(
        functools.partial(out_norm_kernel, slots), "out_and_norm", (n // step,),
        [row_spec(step, D), held(vectors.shape)]
        + [row_spec(step, width)] * slots + [held((width, D))] * slots,
        [row_spec(step, D), row_spec(step, 1), row_spec(step, D), column_spec(D, step)],
        [shaped(F32, n, D), shaped(F32, n, 1), shaped(BF16, n, D), shaped(BF16, D, n)],
        (x, vectors, *attended, *weights), 2 * n * D * D,
    )


GELU_TERMS = (
    0.23532527933595032, 0.09138803439798156, 0.6495603483388861,
    -0.6354014529895687, 0.8866650885491606, -0.22753729931242958,
)


def gelu_parts(values):
    size = jnp.abs(values)
    part = pl.reciprocal(1.0 + (0.39 / math.sqrt(2.0)) * size)
    bell = jnp.exp(-0.5 * (values * values))
    series = 0.5 * GELU_TERMS[-1]
    for term in GELU_TERMS[-2::-1]:
        series = series * part + 0.5 * term
    tail = series * part * bell
    below = jnp.where(values >= 0.0, 1.0 - tail, tail)
    return values * below, below + values * bell * (1.0 / math.sqrt(2.0 * math.pi))


def up_kernel(x_ref, w_ref, b_ref, active_ref, slope_ref):
    width = w_ref.shape[1]
    chunk = min(256, width)
    for first in range(0, width, chunk):
        at = slice(first, first + chunk)
        active, slope = gelu_parts(mm(x_ref[...], w_ref[:, at]) + b_ref[:, at])
        active_ref[:, at] = active.astype(BF16)
        slope_ref[:, at] = slope


def up_and_gelu(x, weight, bias):
    n, D = x.shape
    width = weight.shape[1]
    step = row_step(n)
    return call(
        up_kernel, "up_and_gelu", (n // step,),
        [row_spec(step, D), held(weight.shape), held(bias.shape)],
        [row_spec(step, width)] * 2,
        [shaped(BF16, n, width), shaped(F32, n, width)],
        (x, weight, bias), 5 * n * D * width,
    )


def down_norm_kernel(slots, *refs):
    normed_ref, vec_ref, proj_ref = refs[:3]
    act_refs, w_refs = refs[3 : 3 + slots], refs[3 + slots : 3 + 2 * slots]
    normed_out, inverse_ref, low_ref, unit_ref, unit_low_ref, unit_inverse_ref = refs[3 + 2 * slots :]
    for at in parts_of(normed_ref.shape[0]):
        residual = normed_ref[at, :] * vec_ref[1:2, :] + vec_ref[2:3, :] + vec_ref[3:4, :]
        for act_ref, w_ref in zip(act_refs, w_refs):
            residual = residual + mm(act_ref[at, :], w_ref[...])
        normed, inverse = normed_rows(residual)
        normed_out[at, :] = normed
        inverse_ref[at, :] = inverse
        low = (normed * vec_ref[4:5, :] + vec_ref[5:6, :]).astype(BF16)
        low_ref[at, :] = low
        embedding = mm(low, proj_ref[...])
        unit_inverse = lax.rsqrt(jnp.sum(embedding * embedding, axis=1, keepdims=True) + 1e-06)
        unit = embedding * unit_inverse
        unit_ref[at, :] = unit
        unit_low_ref[at, :] = unit.astype(BF16)
        unit_inverse_ref[at, :] = unit_inverse


def down_and_norm(normed, vectors, proj, active, weights):
    n, D = normed.shape
    step = row_step(n)
    slots = len(active)
    width = active[0].shape[1]
    return call(
        functools.partial(down_norm_kernel, slots), "down_and_norm", (n // step,),
        [row_spec(step, D), held(vectors.shape), held(proj.shape)]
        + [row_spec(step, width)] * slots + [held((width, D))] * slots,
        [
            row_spec(step, D), row_spec(step, 1), row_spec(step, D),
            row_spec(step, 128), row_spec(step, 128), row_spec(step, 1),
        ],
        [
            shaped(F32, n, D), shaped(F32, n, 1), shaped(BF16, n, D),
            shaped(F32, n, 128), shaped(BF16, n, 128), shaped(F32, n, 1),
        ],
        (normed, vectors, proj, *active, *weights), 2 * n * D * width * slots,
    )


def head_pull_kernel(
    grad_ref, unit_ref, unit_inverse_ref, proj_ref, normed_ref, inverse_ref, vec_ref,
    embed_ref, residual_ref, low_ref, turned_ref, sum_ref,
):
    sums = []
    for at in parts_of(grad_ref.shape[0]):
        grad, unit = grad_ref[at, :], unit_ref[at, :]
        embed = grad - unit * jnp.sum(grad * unit, axis=1, keepdims=True)
        embed = (unit_inverse_ref[at, :] * embed).astype(BF16)
        embed_ref[at, :] = embed
        output_grad = mm(embed, proj_ref[...], NT)
        normed = normed_ref[at, :]
        residual = norm_pull(output_grad, normed, inverse_ref[at, :], vec_ref[4:5, :])
        residual_ref[at, :] = residual
        low_ref[at, :] = residual.astype(BF16)
        turned_ref[:, at] = residual.T.astype(BF16)
        sums.append(column_sums(residual, output_grad * normed, output_grad))
    add_over_steps(sum_ref, sum(sums))


def head_pull(unit_grad, unit, unit_inverse, proj, normed, inverse, vectors):
    n, D = normed.shape
    step = row_step(n)
    return call(
        head_pull_kernel, "head_pull", (n // step,),
        [
            row_spec(step, 128), row_spec(step, 128), row_spec(step, 1), held(proj.shape),
            row_spec(step, D), row_spec(step, 1), held(vectors.shape),
        ],
        [
            row_spec(step, 128), row_spec(step, D), row_spec(step, D),
            column_spec(D, step), pl.BlockSpec((8, D), lambda i: (0, 0)),
        ],
        [
            shaped(BF16, n, 128), shaped(F32, n, D), shaped(BF16, n, D),
            shaped(BF16, D, n), shaped(F32, 8, D),
        ],
        (unit_grad, unit, unit_inverse, proj, normed, inverse, vectors), 4 * n * D * 128,
    )


def up_pull_kernel(branch_ref, w_ref, slope_ref, out_ref, sum_ref):
    width = w_ref.shape[0]
    chunk = min(512, width)
    sums = []
    for first in range(0, width, chunk):
        at = slice(first, first + chunk)
        low = (mm(branch_ref[...], w_ref[at, :], NT) * slope_ref[:, at]).astype(BF16)
        out_ref[:, at] = low
        sums.append(column_sums(low.astype(F32)))
    add_over_steps(sum_ref, jnp.concatenate(sums, axis=1))


def up_pull(branch, weight, slope):
    n, D = branch.shape
    width = weight.shape[0]
    step = row_step(n)
    return call(
        up_pull_kernel, "up_pull", (n // step,),
        [row_spec(step, D), held(weight.shape), row_spec(step, width)],
        [row_spec(step, width), pl.BlockSpec((8, width), lambda i: (0, 0))],
        [shaped(BF16, n, width), shaped(F32, 8, width)],
        (branch, weight, slope), 2 * n * D * width,
    )


def hidden_pull_kernel(slots, *refs):
    residual_ref, normed_ref, inverse_ref, vec_ref = refs[:4]
    pre_refs, up_refs, out_refs = (refs[4 + j * slots : 4 + (j + 1) * slots] for j in range(3))
    rest = refs[4 + 3 * slots :]
    grad_ref, turned_ref, sum_ref = rest[:3]
    att_refs = rest[3:]
    sums = []
    for at in parts_of(residual_ref.shape[0]):
        hidden_grad = residual_ref[at, :]
        for pre_ref, up_ref in zip(pre_refs, up_refs):
            hidden_grad = hidden_grad + mm(pre_ref[at, :], up_ref[...], NT)
        normed = normed_ref[at, :]
        residual = norm_pull(hidden_grad, normed, inverse_ref[at, :], vec_ref[1:2, :])
        grad_ref[at, :] = residual
        low = residual.astype(BF16)
        turned_ref[:, at] = residual.T.astype(BF16)
        sums.append(column_sums(residual, hidden_grad * normed, hidden_grad))
        for att_ref, out_ref in zip(att_refs, out_refs):
            att_ref[at, :] = mm(low, out_ref[...], NT).astype(BF16)
    add_over_steps(sum_ref, sum(sums))


def hidden_pull(residual, normed, inverse, vectors, pre_grads, ups, outs):
    n, D = residual.shape
    step = row_step(n)
    slots = len(ups)
    wide, width = ups[0].shape[1], outs[0].shape[0]
    return call(
        functools.partial(hidden_pull_kernel, slots), "hidden_pull", (n // step,),
        [row_spec(step, D), row_spec(step, D), row_spec(step, 1), held(vectors.shape)]
        + [row_spec(step, wide)] * slots + [held((D, wide))] * slots
        + [held((width, D))] * slots,
        [row_spec(step, D), column_spec(D, step), pl.BlockSpec((8, D), lambda i: (0, 0))]
        + [row_spec(step, width)] * slots,
        [shaped(F32, n, D), shaped(BF16, D, n), shaped(F32, 8, D)]
        + [shaped(BF16, n, width)] * slots,
        (residual, normed, inverse, vectors, *pre_grads, *ups, *outs),
        0,
    )


def token_pull_kernel(slots, place_ref, *refs):
    residual_ref = refs[0]
    mixed_refs, w_refs = refs[1 : 1 + slots], refs[1 + slots : 1 + 2 * slots]
    out_ref = refs[-1]
    width = out_ref.shape[1]
    at = pl.ds(pl.multiple_of(place_ref[0] * width, width), width)
    total = residual_ref[...]
    for mixed_ref, w_ref in zip(mixed_refs, w_refs):
        for which in range(3):
            total = total + mm(mixed_ref[which], w_ref[which, at, :], NT)
    out_ref[...] = total.astype(out_ref.dtype)


def token_pull(place, residual, mixed_grads, weights, dtype):
    n, D = residual.shape
    step = row_step(n)
    slots = len(weights)
    width = weights[0].shape[2]
    return call(
        functools.partial(token_pull_kernel, slots), "token_pull", (n // step,),
        [pl.BlockSpec((step, width), lambda i, p: (i, p[0]))]
        + [pl.BlockSpec((3, step, width), lambda i, p: (0, i, 0))] * slots
        + [held((3, D, width))] * slots,
        [row_spec(step, width)],
        [shaped(dtype, n, width)],
        (place.reshape(1), residual, *mixed_grads, *weights), 6 * n * D * width, prefetch=1,
    )[0]


def put_halves(total, inner, side, refs):
    pairs = total.reshape(-1, 2, inner, total.shape[1])
    keep = jnp.where(side == 0, pairs[:, 0], pairs[:, 1]).reshape(-1, total.shape[1])
    send = jnp.where(side == 0, pairs[:, 1], pairs[:, 0]).reshape(-1, total.shape[1])
    refs[0][0] = send.astype(BF16)
    refs[1][0] = keep


def grouped_index(starts, place, count):
    def index(j, i, *_):
        inside = (j >= starts[place]) & (j < starts[place + 1])
        row = jnp.clip(j - starts[place], 0, starts[place + 1] - starts[place] - 1)
        rest = jnp.where(j < starts[place], 0, count - 1)
        return row, 0, jnp.where(inside, i, rest)

    return index


def for_group(starts, body):
    for place in range(len(starts) - 1):

        @pl.when((pl.program_id(0) >= starts[place]) & (pl.program_id(0) < starts[place + 1]))
        def _(place=place):
            body(place)


def weight_pull_kernel(starts, added, inner, place_ref, *refs):
    groups = len(starts) - 1
    lefts, rights, refs = refs[:groups], refs[groups : 2 * groups], refs[2 * groups :]

    def one_group(place):
        left = lefts[place]
        total = mm(left[:, 0].reshape(-1, left.shape[-1]), rights[place][0])
        outs = refs
        if added:
            total = total + refs[0][0].astype(F32)
            outs = refs[1:]
        if inner:
            put_halves(total, inner, place_ref[1], outs)
        else:
            outs[0][0] = total.astype(outs[0].dtype)

    for_group(starts, one_group)


def weight_pull(places, lefts, rights, arrived=None, dtype=BF16, inner=0):
    pairs, _, share, n = lefts[0].shape
    m = rights[0].shape[2]
    rows = pairs * share
    chunk = min(512, m)
    starts = [0]
    for right in rights:
        starts.append(starts[-1] + right.shape[0])

    def spec(size):
        return pl.BlockSpec((1, size, chunk), lambda j, i, p: (j, 0, i))

    half = rows // 2
    outs = [(BF16, half), (F32, half)] if inner else [(dtype, rows)]
    return call(
        functools.partial(weight_pull_kernel, starts, arrived is not None, inner), "weight_pull",
        (starts[-1], m // chunk),
        [pl.BlockSpec((pairs, 1, share, n), lambda j, i, p: (0, p[0], 0, 0)) for _ in lefts]
        + [
            pl.BlockSpec((1, n, chunk), grouped_index(starts, place, m // chunk))
            for place in range(len(rights))
        ] + ([] if arrived is None else [spec(rows)]),
        [spec(size) for _, size in outs],
        [shaped(kind, starts[-1], size, m) for kind, size in outs],
        (places, *lefts, *rights) + (() if arrived is None else (arrived,)),
        2 * starts[-1] * rows * n * m, prefetch=1,
    )


def fold_kernel(starts, inner, place_ref, *refs):
    groups = len(starts) - 1

    def one_group(place):
        total = refs[place][0] + refs[groups + place][0].astype(F32)
        put_halves(total, inner, place_ref[0], refs[2 * groups :])

    for_group(starts, one_group)


def fold(side, owns, arrived, inner):
    _, rows, m = owns[0].shape
    chunk = min(1024, m)
    starts = [0]
    for own in owns:
        starts.append(starts[-1] + own.shape[0])

    def spec(size):
        return pl.BlockSpec((1, size, chunk), lambda j, i, p: (j, 0, i))

    half = rows // 2
    specs = [
        pl.BlockSpec((1, rows, chunk), grouped_index(starts, place, m // chunk))
        for place in range(len(owns))
    ]
    return call(
        functools.partial(fold_kernel, starts, inner), "fold", (starts[-1], m // chunk),
        specs + specs, [spec(half), spec(half)],
        [shaped(BF16, starts[-1], half, m), shaped(F32, starts[-1], half, m)],
        (side.reshape(1), *owns, *arrived), 0, prefetch=1,
    )


SEGMENTS = 8
ATTENTION_LANES = 256


def half_lanes(block, head, other):
    lane = lax.broadcasted_iota(jnp.int32, block.shape, 1)
    return jnp.where((lane >= DH) == (head == 1), block, other)


def scaled(block):
    return (block.astype(F32) * DH**-0.5).astype(BF16)


def three_terms(value):
    high = value.astype(BF16).astype(F32)
    middle = (value - high).astype(BF16).astype(F32)
    return high, middle, value - high - middle


def attention_forward_kernel(
    span_ref, qkv_ref, ext_k_ref, ext_q_ref, out_ref, rest_ref, ext_ref,
    keys_ref, queries_ref, values_ref, logits_ref, *, tile,
):
    n = ext_k_ref.shape[0]
    tiles = n // tile
    pairs = qkv_ref.shape[2] // 128
    heads = range(2 * pairs)

    def lanes(head):
        return slice(head // 2 * 128, head // 2 * 128 + 128)

    def own_rows(head):
        return slice(head % 2 * DH, head % 2 * DH + DH)

    for head in heads:
        keys_ref[head] = half_lanes(qkv_ref[1, :, lanes(head)], head % 2, ext_k_ref[...])
        queries_ref[head] = half_lanes(
            scaled(qkv_ref[0, :, lanes(head)]), head % 2, ext_q_ref[...]
        )
    for pair in range(pairs):
        for step in range(tiles):
            block = qkv_ref[2, step * tile : (step + 1) * tile, lanes(2 * pair)]
            values_ref[pair, step] = block.astype(F32).T.astype(BF16)

    def rows(step):
        return pl.ds(pl.multiple_of(step * tile, tile), tile)

    def by_eight(block):
        return block.reshape(tile // 8, 8, tile)

    @pl.loop(0, tiles)
    def _(step):
        low, high = span_ref[step], span_ref[tiles + step]

        def find_top(block, tops):
            found = []
            for head in heads:
                logits = mm(
                    keys_ref[head, rows(block), :], queries_ref[head, rows(step), :], NT
                )
                logits_ref[head, block] = logits
                found.append(jnp.maximum(tops[head], jnp.max(by_eight(logits), axis=0)))
            return tuple(found)

        start = jnp.full((8, tile), -3e38, F32)
        tops = lax.fori_loop(low, high, find_top, tuple(start for _ in heads))
        tops = [jnp.max(top, axis=0, keepdims=True) for top in tops]

        def add_mass(block, masses):
            after = []
            for head in heads:
                weights = jnp.exp(logits_ref[head, block] - tops[head])
                logits_ref[head, block] = weights
                after.append(masses[head] + jnp.sum(by_eight(weights), axis=0))
            return tuple(after)

        start = jnp.zeros((8, tile), F32)
        masses = lax.fori_loop(low, high, add_mass, tuple(start for _ in heads))
        masses = [jnp.sum(mass, axis=0, keepdims=True) for mass in masses]
        shares = [1.0 / mass for mass in masses]

        def add_values(block, totals):
            after = []
            for head in heads:
                probs = (logits_ref[head, block] * shares[head]).astype(BF16)
                after.append(totals[head] + mm(values_ref[head // 2, block, own_rows(head), :], probs))
            return tuple(after)

        zero = jnp.zeros((DH, tile), F32)
        outs = lax.fori_loop(low, high, add_values, tuple(zero for _ in heads))
        for pair in range(pairs):
            extras = []
            for head in (2 * pair + 1, 2 * pair):
                terms = three_terms(-(tops[head] + jnp.log(masses[head])))
                extras += [
                    jnp.zeros((8, tile), F32), *terms, jnp.zeros((DH - 11, tile), F32)
                ]
            at = lanes(2 * pair)
            out = jnp.concatenate(outs[2 * pair : 2 * pair + 2], axis=0).T
            out_ref[rows(step), at] = out.astype(BF16)
            rest_ref[rows(step), at] = (out - out.astype(BF16).astype(F32)).astype(BF16)
            extra = jnp.concatenate(extras, axis=0).T
            ext_ref[rows(step), at] = (extra + ext_q_ref[rows(step), :].astype(F32)).astype(BF16)


def attention_forward(spans, qkv, ext_k, ext_q, tile):
    _, n, width = qkv.shape
    span = min(width, ATTENTION_LANES)
    wide = pl.BlockSpec((n, span), lambda i, *_: (0, i))
    tiles, pairs = n // tile, span // 128
    return call(
        functools.partial(attention_forward_kernel, tile=tile), "attention_forward",
        (width // span,),
        [pl.BlockSpec((3, n, span), lambda i, *_: (0, 0, i)), held((n, 128)), held((n, 128))],
        [wide, wide, wide],
        [shaped(BF16, n, width)] * 3,
        (spans, qkv, ext_k, ext_q), 0, prefetch=1,
        scratch=[
            pltpu.VMEM((2 * pairs, n, 128), BF16), pltpu.VMEM((2 * pairs, n, 128), BF16),
            pltpu.VMEM((pairs, tiles, 128, tile), BF16),
            pltpu.VMEM((2 * pairs, tiles, tile, tile), F32),
        ],
    )


def attention_backward_kernel(
    span_ref, qkv_ref, ext_ref, att_ref, rest_ref, grad_ref, ext_k_ref, cos_ref, sin_ref,
    out_ref, sum_ref,
    keys_ref, turned_ref, values_ref, queries_ref, plain_ref, grads_ref, plain_grads_ref,
    dq_ref, dk_ref, dv_ref, *, tile,
):
    n = ext_k_ref.shape[0]
    tiles = n // tile
    pairs = qkv_ref.shape[2] // 128
    heads = range(2 * pairs)

    def lanes(head):
        return slice(head // 2 * 128, head // 2 * 128 + 128)

    def own_rows(head):
        return slice(head % 2 * DH, head % 2 * DH + DH)

    def rows(step):
        return pl.ds(pl.multiple_of(step * tile, tile), tile)

    @pl.loop(0, tiles)
    def _(step):
        at = rows(step)
        zeros = jnp.zeros((tile, 128), BF16)
        lane = lax.broadcasted_iota(jnp.int32, (tile, 128), 1)
        ext_k = ext_k_ref[at, :]
        for pair in range(pairs):
            cut = lanes(2 * pair)
            grad = grad_ref[at, cut]
            out = att_ref[at, cut].astype(F32) + rest_ref[at, cut].astype(F32)
            product = grad.astype(F32) * out
            query = scaled(qkv_ref[0, at, cut])
            turned_ref[pair, step] = scaled(qkv_ref[1, at, cut]).astype(F32).T.astype(BF16)
            for half in range(2):
                head = 2 * pair + half
                keys_ref[head, at, :] = half_lanes(qkv_ref[1, at, cut], half, ext_k)
                values_ref[head, at, :] = half_lanes(qkv_ref[2, at, cut], half, ext_k)
                queries_ref[head, at, :] = half_lanes(query, half, ext_ref[at, cut])
                plain_ref[head, at, :] = half_lanes(query, half, zeros)
                plain_grads_ref[head, at, :] = half_lanes(grad, half, zeros)
                inner = jnp.sum(half_lanes(product, half, 0.0), axis=1, keepdims=True)
                extra = jnp.zeros((tile, 128), F32)
                for place, term in enumerate(three_terms(-inner)):
                    extra = jnp.where((lane & (DH - 1)) == SEGMENTS + place, term, extra)
                grads_ref[head, at, :] = half_lanes(grad, half, extra.astype(BF16))

    dk_ref[...] = jnp.zeros(dk_ref.shape, F32)
    dv_ref[...] = jnp.zeros(dv_ref.shape, F32)

    @pl.loop(0, tiles)
    def _(step):
        def one_block(block, totals):
            after = []
            for pair in range(pairs):
                probs, slopes = [], []
                for head in (2 * pair, 2 * pair + 1):
                    weights = jnp.exp(
                        mm(keys_ref[head, rows(block), :], queries_ref[head, rows(step), :], NT)
                    )
                    flow = mm(values_ref[head, rows(block), :], grads_ref[head, rows(step), :], NT)
                    slope = (weights * flow).astype(BF16)
                    probs.append(weights.astype(BF16))
                    slopes.append(slope)
                    after.append(totals[head] + mm(turned_ref[pair, block, own_rows(head), :], slope))
                both = range(2 * pair, 2 * pair + 2)
                plain = jnp.concatenate([plain_ref[h, rows(step), :] for h in both], axis=0)
                grads = jnp.concatenate([plain_grads_ref[h, rows(step), :] for h in both], axis=0)
                at = lanes(2 * pair)
                dv_ref[rows(block), at] += mm(jnp.concatenate(probs, axis=1), grads)
                dk_ref[rows(block), at] += mm(jnp.concatenate(slopes, axis=1), plain)
            return tuple(after)

        zero = jnp.zeros((DH, tile), F32)
        totals = lax.fori_loop(
            span_ref[step], span_ref[tiles + step], one_block, tuple(zero for _ in heads)
        )
        for pair in range(pairs):
            both = jnp.concatenate(totals[2 * pair : 2 * pair + 2], axis=0)
            dq_ref[rows(step), lanes(2 * pair)] = both.T

    def finish(step, sums):
        cosine, sine = cos_ref[rows(step), :], sin_ref[rows(step), :]
        added = []
        for which, src in enumerate((dq_ref, dk_ref, dv_ref)):
            for pair in range(pairs):
                at = lanes(2 * pair)
                block = src[rows(step), at]
                if which < 2:
                    block = block * cosine - swap_halves(block) * sine
                low = block.astype(BF16)
                out_ref[which, rows(step), at] = low
                total = jnp.sum(low.astype(F32), axis=0, keepdims=True)
                added.append(sums[which * pairs + pair] + total)
        return tuple(added)

    zero = jnp.zeros((1, 128), F32)
    sums = lax.fori_loop(0, tiles, finish, (zero,) * (3 * pairs))
    sums = [jnp.concatenate(sums[w * pairs : (w + 1) * pairs], axis=1) for w in range(3)]
    sum_ref[...] = jnp.concatenate(sums + [jnp.zeros((5, pairs * 128), F32)], axis=0)


def attention_backward(
    spans, qkv, ext, attended, rest, grads, ext_k, cosine, sine, tile
):
    _, n, width = qkv.shape
    span = min(width, ATTENTION_LANES)
    wide = pl.BlockSpec((n, span), lambda i, *_: (0, i))
    three = pl.BlockSpec((3, n, span), lambda i, *_: (0, 0, i))
    tiles, pairs = n // tile, span // 128
    heads = pltpu.VMEM((2 * pairs, n, 128), BF16)
    return call(
        functools.partial(attention_backward_kernel, tile=tile), "attention_backward",
        (width // span,),
        [three, wide, wide, wide, wide, held((n, 128)), held((n, 128)), held((n, 128))],
        [three, pl.BlockSpec((8, span), lambda i, *_: (0, i))],
        [shaped(BF16, 3, n, width), shaped(F32, 8, width)],
        (spans, qkv, ext, attended, rest, grads, ext_k, cosine, sine), 0,
        prefetch=1,
        scratch=[heads, pltpu.VMEM((pairs, tiles, 128, tile), BF16)] + [heads] * 5
        + [pltpu.VMEM((n, span), F32)] * 3,
    )


STRIP = 32


def token_sums(width, queries):
    token = lax.broadcasted_iota(jnp.int32, (width, queries), 0) // QLEN
    return token == lax.broadcasted_iota(jnp.int32, (width, queries), 1)


def score_kernel(low_ref, high_ref, doc_ref, query_ref, pick_ref, out_ref, sum_ref):
    group = pl.program_id(0)
    docs, width = pick_ref.shape[1:]
    doc_rows = doc_ref.shape[0]
    strips = doc_rows // STRIP
    chunk = min(256, doc_rows)
    row = lax.broadcasted_iota(jnp.int32, (STRIP, width), 0)
    sum_ref[...] = jnp.zeros(sum_ref.shape, F32)

    def add_strip(sim, first, doc, pick):
        kept = jnp.where(row == pick - first, sim, 0.0)
        sum_ref[pl.ds(doc, 1)] += jnp.sum(kept.reshape(1, STRIP // 8, 8, width), axis=1)

    for start in range(0, doc_rows, chunk):
        sims = mm(doc_ref[start : start + chunk, :], query_ref[...], NT)
        for first in range(0, chunk, STRIP):
            place = group * strips + (start + first) // STRIP
            low, high = low_ref[place], high_ref[place]
            sim = sims[first : first + STRIP]
            add_strip(sim, start + first, low, pick_ref[0, pl.ds(low, 1), :])
            pick = jnp.where(high > low, pick_ref[0, pl.ds(high, 1), :], -1)
            add_strip(sim, start + first, high, pick)

    @pl.loop(0, strips)
    def _(strip):
        low, high = low_ref[group * strips + strip], high_ref[group * strips + strip]

        @pl.when(high > low + 1)
        def _():
            first = pl.multiple_of(strip * STRIP, STRIP)
            sim = mm(doc_ref[pl.ds(first, STRIP), :], query_ref[...], NT)

            @pl.loop(low + 1, high)
            def _(doc):
                add_strip(sim, first, doc, pick_ref[0, pl.ds(doc, 1), :])

    totals = jnp.sum(sum_ref[...], axis=1)
    totals = jnp.concatenate([totals, jnp.zeros((8 - docs, width), F32)], axis=0)
    spread = token_sums(width, out_ref.shape[2]).astype(F32)
    out_ref[0] = lax.dot_general(
        totals, spread, NN, precision=lax.Precision.HIGHEST, preferred_element_type=F32
    )[:docs]


def score_grad_kernel(
    low_ref, high_ref, doc_ref, query_ref, pick_ref, weight_ref, doc_out, query_out,
    sparse_ref, token_ref,
):
    group = pl.program_id(0)
    docs, width = pick_ref.shape[1:]
    doc_rows = doc_ref.shape[0]
    strips = doc_rows // STRIP
    chunk = min(256, doc_rows)
    row = lax.broadcasted_iota(jnp.int32, (STRIP, width), 0)
    spread = token_sums(width, weight_ref.shape[2]).astype(F32).astype(BF16)
    weights = jnp.concatenate(
        [weight_ref[0], jnp.zeros((16 - docs, weight_ref.shape[2]), F32)], axis=0
    )
    token_ref[...] = mm(weights.astype(BF16), spread, NT)

    def fill(held, first, doc, pick):
        return jnp.where(row == pick - first, token_ref[pl.ds(doc, 1), :], held)

    @pl.when(group == 0)
    def _():
        query_out[...] = jnp.zeros_like(query_out)

    total = None
    for start in range(0, doc_rows, chunk):
        for first in range(start, start + chunk, STRIP):
            place = group * strips + first // STRIP
            low, high = low_ref[place], high_ref[place]
            held = fill(jnp.zeros((STRIP, width), F32), first, low, pick_ref[0, pl.ds(low, 1), :])
            pick = jnp.where(high > low, pick_ref[0, pl.ds(high, 1), :], -1)
            sparse_ref[first : first + STRIP, :] = fill(held, first, high, pick).astype(BF16)
        sparse = sparse_ref[start : start + chunk, :]
        doc_out[start : start + chunk, :] = mm(sparse, query_ref[...])
        turned = doc_ref[start : start + chunk, :].astype(F32).T.astype(BF16)
        part = mm(turned, sparse)
        total = part if total is None else total + part
    query_out[...] += total

    @pl.loop(0, strips)
    def _(strip):
        low, high = low_ref[group * strips + strip], high_ref[group * strips + strip]

        @pl.when(high > low + 1)
        def _():
            first = pl.multiple_of(strip * STRIP, STRIP)
            held = lax.fori_loop(
                low + 1,
                high,
                lambda doc, held: fill(held, first, doc, pick_ref[0, pl.ds(doc, 1), :]),
                jnp.zeros((STRIP, width), F32),
            ).astype(BF16)
            doc_out[pl.ds(first, STRIP), :] += mm(held, query_ref[...])
            turned = doc_ref[pl.ds(first, STRIP), :].astype(F32).T.astype(BF16)
            query_out[...] += mm(turned, held)


def score_specs(doc_tile, query_tile, picks, queries):
    groups, docs, width = picks.shape
    doc_rows = doc_tile.shape[0] // groups
    return (
        pl.BlockSpec((doc_rows, 128), lambda i, *_: (i, 0)),
        held(query_tile.shape),
        pl.BlockSpec((1, docs, width), lambda i, *_: (i, 0, 0)),
        pl.BlockSpec((1, docs, queries), lambda i, *_: (i, 0, 0)),
    )


def score_forward(lows, highs, doc_tile, query_tile, picks):
    groups, docs, width = picks.shape
    queries = width // QLEN
    doc_spec, query_spec, pick_spec, out_spec = score_specs(doc_tile, query_tile, picks, queries)
    return call(
        score_kernel, "score_forward", (groups,),
        [doc_spec, query_spec, pick_spec], [out_spec],
        [shaped(F32, groups, docs, queries)],
        (lows, highs, doc_tile, query_tile, picks), 2 * doc_tile.shape[0] * width * 128,
        prefetch=2, scratch=[pltpu.VMEM((docs, 8, width), F32)],
    )[0]


def score_backward(lows, highs, doc_tile, query_tile, picks, weights):
    groups, docs, width = picks.shape
    doc_spec, query_spec, pick_spec, weight_spec = score_specs(
        doc_tile, query_tile, picks, weights.shape[2]
    )
    return call(
        score_grad_kernel, "score_backward", (groups,),
        [doc_spec, query_spec, pick_spec, weight_spec],
        [doc_spec, pl.BlockSpec((128, width), lambda i, *_: (0, 0))],
        [shaped(F32, *doc_tile.shape), shaped(F32, 128, width)],
        (lows, highs, doc_tile, query_tile, picks, weights), 4 * doc_tile.shape[0] * width * 128,
        prefetch=2,
        scratch=[
            pltpu.VMEM((doc_tile.shape[0] // groups, width), BF16), pltpu.VMEM((16, width), F32)
        ],
    )


def rotary_tables(position):
    half_size = DH // 2
    frequency = jnp.exp(
        jnp.arange(half_size, dtype=F32) * (-2.0 * math.log(10000.0) / DH)
    )
    angles = position.astype(F32)[:, None] * frequency[None, :]
    cosine, sine = jnp.cos(angles), jnp.sin(angles)
    return (
        jnp.concatenate([cosine] * 4, axis=1),
        jnp.concatenate([-sine, sine, -sine, sine], axis=1),
    )


def on_device(
    tokens,
    doc_lengths,
    match_picks,
    labels,
    w_qkv,
    b_qkv,
    w_out,
    b_out,
    ln1_gain,
    ln1_bias,
    w_up,
    b_up,
    w_down,
    b_down,
    ln2_gain,
    ln2_bias,
    w_proj,
    log_scale,
):
    Order.last = ()
    C = lax.axis_size("cols")
    R = lax.axis_size("rows")
    c = lax.axis_index("cols")
    r = lax.axis_index("rows")
    width = tokens.shape[1]
    D = width * C
    Q = ROW_LEN // C
    DS = (tokens.shape[0] - ROW_LEN) // C
    n = Q + DS
    tile = math.gcd(256, math.gcd(Q, DS))

    def shift_cols(value, k):
        return lax.ppermute(value, "cols", [(i, (i + k) % C) for i in range(C)])

    def swap_rows(value, bit):
        return lax.ppermute(value, "rows", [(i, i ^ bit) for i in range(R)])

    def in_order(slots):
        if len(slots) == 1:
            return slots
        if len(slots) == 2:
            return [lax.select(c == 0, slots[0], slots[1]), lax.select(c == 0, slots[1], slots[0])]
        stacked = jnp.stack(slots)
        return [
            lax.dynamic_index_in_dim(stacked, (c - j) % C, 0, keepdims=False) for j in range(C)
        ]

    parts = jnp.concatenate(
        [tokens[:ROW_LEN].reshape(C, Q, width), tokens[ROW_LEN:].reshape(C, DS, width)], axis=1
    )

    def part(k):
        return lax.dynamic_index_in_dim(parts, (c + k) % C, 0, keepdims=False)

    arrived = [shift_cols(part(k), k) for k in range(1, C)]
    x = jnp.concatenate(in_order([part(0)] + arrived), axis=1)

    def gather_slots(shard, behind):
        flat = shard.reshape(-1, shard.shape[-1])
        piece = lax.dynamic_index_in_dim(
            flat.reshape(R, flat.shape[0] // R, flat.shape[1]), r, 0, keepdims=False
        )
        if behind:
            piece, _ = lax.optimization_barrier((piece, arrived))
        others = [
            lax.all_gather(shift_cols(piece, k), "rows", axis=0, tiled=True).reshape(shard.shape)
            for k in range(1, C)
        ]
        return [shard] + others

    wqkv_slots = gather_slots(w_qkv, False)
    wout_slots = gather_slots(w_out, True)
    wup_slots = gather_slots(w_up, True)
    wdown_slots = gather_slots(w_down, True)
    own_proj, _ = lax.optimization_barrier((w_proj, arrived))
    wproj = jnp.concatenate(
        in_order([own_proj] + [shift_cols(own_proj, k) for k in range(1, C)]), axis=0
    )

    pack = [b_qkv.reshape(-1), b_up, b_out, ln1_gain, ln1_bias, b_down, ln2_gain, ln2_bias]
    ends = [0]
    for vector in pack:
        ends.append(ends[-1] + vector.shape[0])
    packed, _ = lax.optimization_barrier((jnp.concatenate(pack), arrived))
    packs = [packed] + [shift_cols(packed, k) for k in range(1, C)]
    ordered_packs = in_order(packs)

    def of_slot(which, k):
        return packs[k][ends[which] : ends[which + 1]]

    def whole(which):
        return jnp.concatenate([p[ends[which] : ends[which + 1]] for p in ordered_packs])

    bqkv_slots = [of_slot(0, k).reshape(b_qkv.shape) for k in range(C)]
    bup_slots = [of_slot(1, k)[None, :] for k in range(C)]
    bout, gain1, bias1, bdown, gain2, bias2 = [whole(which) for which in range(2, 8)]
    zero_row = jnp.zeros_like(bout)
    vectors = jnp.stack([bout, gain1, bias1, bdown, gain2, bias2, zero_row, zero_row])

    own_sizes = lax.dynamic_index_in_dim(
        lax.dynamic_index_in_dim(doc_lengths, r, 0, keepdims=False), c, 0, keepdims=False
    )
    own_ends = jnp.cumsum(own_sizes)
    places = jnp.arange(DS, dtype=jnp.int32)
    passed = places[:, None] >= own_ends[None, :]
    slot_id = jnp.sum(passed.astype(jnp.int32), axis=1)
    slot_begin = jnp.sum(jnp.where(passed, own_sizes[None, :], 0), axis=1)
    query_places = jnp.arange(Q, dtype=jnp.int32)
    position = jnp.concatenate([query_places % QLEN, places - slot_begin])
    cosine, sine = rotary_tables(position)
    segment = jnp.concatenate([(query_places // QLEN) % SEGMENTS, slot_id])
    lane = jnp.arange(128, dtype=jnp.int32)[None, :] % DH
    same = segment[:, None] == lane
    ext_k = (same | ((lane >= SEGMENTS) & (lane < SEGMENTS + 3))).astype(BF16)
    ext_q = jnp.where((lane < SEGMENTS) & ~same, -1e30, 0.0).astype(BF16)
    q_tiles, d_tiles = Q // tile, DS // tile
    steps = jnp.arange(q_tiles, dtype=jnp.int32)
    first_rows = jnp.arange(d_tiles, dtype=jnp.int32) * tile
    is_passed = first_rows[:, None] >= own_ends[None, :]
    low_rows = jnp.sum(jnp.where(is_passed, own_sizes[None, :], 0), axis=1)
    last_passed = (first_rows + tile - 1)[:, None] >= own_ends[None, :]
    high_rows = jnp.min(jnp.where(last_passed, DS, own_ends[None, :]), axis=1)
    spans = jnp.concatenate(
        [steps, q_tiles + low_rows // tile, steps + 1, q_tiles + (high_rows + tile - 1) // tile]
    ).astype(jnp.int32)

    queries_here, tile_docs, _ = match_picks.shape
    docs = own_sizes.shape[0]
    sizes = lax.dynamic_index_in_dim(doc_lengths, c, 1, keepdims=False)
    doc_ends = jnp.cumsum(sizes, axis=1)
    begins = doc_ends - sizes
    picks = jnp.transpose(match_picks, (1, 0, 2)).reshape(tile_docs, queries_here * QLEN)
    picks = begins.reshape(-1)[:, None] + picks % sizes.reshape(-1)[:, None]
    picks = picks.reshape(R, docs, queries_here * QLEN)
    strip_rows = (jnp.arange(DS // STRIP, dtype=jnp.int32) * STRIP)[None, :, None]
    lows = jnp.sum(doc_ends[:, None, :] <= strip_rows, axis=2).astype(jnp.int32).reshape(-1)
    highs = jnp.sum(begins[:, None, :] < strip_rows + STRIP, axis=2).astype(jnp.int32) - 1
    highs = highs.reshape(-1)

    qkv, attended, rests, exts = [], [], [], []
    for k in range(C):
        first = (picks, lows, highs) if k == 0 else ()
        qkv.append(project_qkv(x, wqkv_slots[k], bqkv_slots[k], cosine, sine, first))
        out, rest, ext = attention_forward(spans, qkv[k], ext_k, ext_q, tile)
        attended.append(out)
        rests.append(rest)
        exts.append(ext)
    normed_one, inverse_one, hidden_low, hidden_t = out_and_norm(x, vectors, attended, wout_slots)
    active, slopes = zip(*[up_and_gelu(hidden_low, wup_slots[k], bup_slots[k]) for k in range(C)])
    normed_two, inverse_two, output_low, unit, unit_low, unit_inverse = down_and_norm(
        normed_one, vectors, wproj, active, wdown_slots
    )

    doc_tile = lax.all_gather(unit_low[Q:], "rows", axis=0, tiled=True)
    query_tile = jnp.concatenate(
        in_order([unit_low[:Q]] + [shift_cols(unit_low[:Q], k) for k in range(1, C)]), axis=0
    )
    sims = score_forward(lows, highs, doc_tile, query_tile, picks)
    scores = sims.reshape(tile_docs, queries_here).T

    scale = jnp.exp(log_scale[0])
    z = scale * scores
    row_top = jnp.max(z, axis=1)
    row_mass = jnp.sum(jnp.exp(z - row_top[:, None]), axis=1)
    is_label = (
        jnp.arange(tile_docs, dtype=jnp.int32)[None, :] == (labels - c * tile_docs)[:, None]
    )
    chosen = jnp.sum(jnp.where(is_label, z, 0.0), axis=1)
    own_stats = jnp.stack([row_top, row_mass, chosen])
    stats = jnp.stack([own_stats] + [shift_cols(own_stats, k) for k in range(1, C)])
    top_all = jnp.max(stats[:, 0], axis=0)
    mass_all = jnp.sum(stats[:, 1] * jnp.exp(stats[:, 0] - top_all), axis=0)
    log_total = top_all + jnp.log(mass_all)
    loss = log_total - jnp.sum(stats[:, 2], axis=0)
    dz = (jnp.exp(z - log_total[:, None]) - is_label.astype(F32)) / (queries_here * R)
    scale_part = jnp.sum(dz * z)
    dscores = (scale * dz).T.reshape(R, docs, queries_here)
    doc_grad, query_grad_t = score_backward(lows, highs, doc_tile, query_tile, picks, dscores)
    query_parts = query_grad_t.T.reshape(C, Q, 128)

    def query_part(k):
        return lax.dynamic_index_in_dim(query_parts, (c + k) % C, 0, keepdims=False)

    query_grad = query_part(0)
    for k in range(1, C):
        query_grad = query_grad + shift_cols(query_part(k), k)

    def halve(total, bit, wire):
        size = total.shape[0] // 2
        pairs = total.reshape((size, 2) + total.shape[1:])
        mine = (r // bit) % 2
        send = lax.dynamic_index_in_dim(pairs, 1 - mine, 1, keepdims=False).astype(wire)
        keep = lax.dynamic_index_in_dim(pairs, mine, 1, keepdims=False)
        return keep + swap_rows(send, bit).astype(F32)

    doc_sum = doc_grad.reshape(R, DS, 128)
    bit = 1
    while bit < R:
        doc_sum = halve(doc_sum, bit, BF16)
        bit *= 2
    unit_grad = jnp.concatenate([query_grad, doc_sum[0]], axis=0)

    core = r % 2
    slots_back = range(C - 1, -1, -1)
    share = D // R
    x_bit, *z_bits = [1 << b for b in range(1, R.bit_length() - 1)]

    def side_of(bit):
        return ((r // bit) % 2).astype(jnp.int32)

    keep_places = jnp.stack([core, side_of(z_bits[0])]).astype(jnp.int32)
    send_places = jnp.stack([1 - core, 0 * core]).astype(jnp.int32)

    def halves_of(left_t):
        return left_t.reshape(R // 2, 2, share, n)

    def send_half(lefts, rights):
        return swap_rows(weight_pull(send_places, lefts, rights)[0], 1)

    def keep_half(left, right, arrived, k):
        kept = weight_pull(keep_places, [left], [right], arrived, F32 if k == 0 else BF16)[0]
        return kept if k == 0 else shift_cols(kept, C - k)

    def next_fold(states, bit, inner):
        send, keep = fold(side_of(bit), [s[0] for s in states], [s[1] for s in states], inner)
        return keep, swap_rows(send, bit)

    def close(state):
        return state[0] + state[1].astype(F32)

    def cols_state(kept):
        rest = kept[1]
        for other in kept[2:]:
            rest = rest.astype(F32) + other.astype(F32)
        return kept[0], rest

    embed_grad, resid_two_grad, branch, branch_t, head_sums = head_pull(
        unit_grad, unit, unit_inverse, wproj, normed_two, inverse_two, vectors
    )
    down_left, down_right = halves_of(branch_t), [a[None] for a in active]
    pre_grads, up_sums, down_kept = [None] * C, [None] * C, [None] * C
    down_arrived = [None] * C
    for k in slots_back:
        down_arrived[k] = send_half([down_left], [down_right[k]])
    for k in slots_back:
        pre_grads[k], up_sums[k] = up_pull(branch, wdown_slots[k], slopes[k])
        if k > 0:
            down_kept[k] = keep_half(down_left, down_right[k], down_arrived[k], k)
    up_left, up_right = halves_of(hidden_t), [g[None] for g in pre_grads]
    up_arrived, up_kept = [None] * C, [None] * C
    for k in slots_back:
        up_arrived[k] = send_half([up_left], [up_right[k]])
    down_kept[0] = keep_half(down_left, down_right[0], down_arrived[0], 0)
    for k in slots_back[:-1]:
        up_kept[k] = keep_half(up_left, up_right[k], up_arrived[k], k)
    resid_one_grad, branch_one_t, hidden_sums, *attended_grads = hidden_pull(
        resid_two_grad, normed_one, inverse_one, vectors, pre_grads, wup_slots, wout_slots
    )
    up_kept[0] = keep_half(up_left, up_right[0], up_arrived[0], 0)
    mixed_grads, mixed_sums = [None] * C, [None] * C
    late_lefts, late_state, late_arrived = [halves_of(x.T), halves_of(branch_one_t)], [None] * C, [None] * C

    def late_rights(k):
        return [mixed_grads[k], attended[k][None]]

    def pull_attention(k):
        mixed_grads[k], mixed_sums[k] = attention_backward(
            spans, qkv[k], exts[k], attended[k], rests[k], attended_grads[k], ext_k, cosine, sine,
            tile,
        )
        late_arrived[k] = send_half(late_lefts, late_rights(k))

    def keep_late(k):
        send, keep = weight_pull(
            keep_places, late_lefts, late_rights(k), late_arrived[k], inner=2 * share
        )
        late_state[k] = (keep, swap_rows(send, z_bits[0]))

    for k in slots_back[:-1]:
        pull_attention(k)
    wide_state = next_fold([cols_state(down_kept), cols_state(up_kept)], x_bit, share)
    pull_attention(0)
    for k in slots_back[:-1]:
        keep_late(k)
    sent = [
        shift_cols(token_pull((c + k) % C, resid_one_grad, mixed_grads, wqkv_slots, BF16), k)
        for k in range(1, C)
    ]
    keep_late(0)
    for k in slots_back[:-1]:
        late_state[k] = next_fold([late_state[k]], (z_bits + [x_bit])[1], 2 * share)
    own_tokens = token_pull(c, resid_one_grad, mixed_grads, wqkv_slots, F32)
    wide_state = next_fold([wide_state], z_bits[0], share)
    for bit in z_bits[2:] + [x_bit]:
        for k in slots_back[:-1]:
            late_state[k] = next_fold([late_state[k]], bit, share if bit == x_bit else 2 * share)
    for bit in z_bits[1:] + [x_bit]:
        late_state[0] = next_fold([late_state[0]], bit, share if bit == x_bit else 2 * share)
        if bit != x_bit:
            wide_state = next_fold([wide_state], bit, share)
    late_grad = close(late_state[0])
    for k in slots_back[:-1]:
        late_grad = late_grad + shift_cols(close(late_state[k]).astype(BF16), C - k).astype(F32)
    qkv_grad, out_grad = late_grad[:3], late_grad[3]
    down_grad, up_grad = close(wide_state)
    ordered = in_order([own_tokens] + [s.astype(F32) for s in sent])
    tokens_grad = jnp.concatenate([s[:Q] for s in ordered] + [s[Q:] for s in ordered], axis=0)
    proj_grad = mm(embed_grad, output_low, TN).reshape(R, -1, C, width)

    def cut(values, slot_rows):
        return values.reshape(slot_rows, R, -1)

    own_order = [(c - k) % C for k in range(C)]
    canonical = jnp.stack(
        [hidden_sums[0], hidden_sums[1], hidden_sums[2], head_sums[0], head_sums[1], head_sums[2]]
    ).reshape(6, C, R, -1)
    slots_small = []
    for k in range(C):
        rows = [mixed_sums[k][j].reshape(R, -1) for j in range(3)]
        rows.append(up_sums[k][0].reshape(R, -1))
        rows += [
            lax.dynamic_index_in_dim(canonical[j], own_order[k], 0, keepdims=False)
            for j in range(6)
        ]
        own_proj_grad = lax.dynamic_index_in_dim(proj_grad, own_order[k], 2, keepdims=False)
        rows.append(own_proj_grad.reshape(R, -1))
        rows.append(jnp.broadcast_to(scale_part, (R, 1)))
        slots_small.append(jnp.concatenate(rows, axis=1))
    small = jnp.stack(in_order(slots_small)).reshape(C * R, -1)
    small = lax.psum_scatter(small, ("cols", "rows"), scatter_dimension=0, tiled=True)[0]
    one = D // (C * R)
    up_part = bup_slots[0].shape[1] // R
    bounds = [3 * one, 3 * one + up_part]
    for _ in range(6):
        bounds.append(bounds[-1] + one)
    pieces = [small[a:b] for a, b in zip(bounds[:-1], bounds[1:])]
    bup_out, bout_out, gain1_out, bias1_out, bdown_out, gain2_out, bias2_out = pieces
    return (
        scores,
        loss,
        tokens_grad,
        qkv_grad,
        small[: bounds[0]].reshape(3, one),
        out_grad.T,
        bout_out,
        gain1_out,
        bias1_out,
        up_grad,
        bup_out,
        down_grad.T,
        bdown_out,
        gain2_out,
        bias2_out,
        small[bounds[-1] : -1].reshape(-1, width).T,
        small[-1:],
    )


def solution(mesh):
    in_specs = (
        P("rows", "cols"),
        P(),
        P("rows", "cols", None),
        P("rows"),
        P(None, None, "cols"),
        P(None, "cols"),
        P("cols", None),
        P("cols"),
        P("cols"),
        P("cols"),
        P(None, "cols"),
        P("cols"),
        P("cols", None),
        P("cols"),
        P("cols"),
        P("cols"),
        P("cols", None),
        P(),
    )
    out_specs = (
        P("rows", "cols"),
        P("rows"),
        P("rows", "cols"),
        P(None, "rows", "cols"),
        P(None, ("cols", "rows")),
        P("cols", "rows"),
        P(("cols", "rows")),
        P(("cols", "rows")),
        P(("cols", "rows")),
        P("rows", "cols"),
        P(("cols", "rows")),
        P("cols", "rows"),
        P(("cols", "rows")),
        P(("cols", "rows")),
        P(("cols", "rows")),
        P("cols", "rows"),
        P(),
    )
    return jax.shard_map(
        on_device, mesh=mesh, in_specs=in_specs, out_specs=out_specs, check_vma=False
    )
```

```python
import functools
import math

import jax
import jax.numpy as jnp
from jax import lax
from jax.experimental import pallas as pl
from jax.experimental.pallas import tpu as pltpu
from jax.sharding import PartitionSpec as P

DH = 64
QLEN = 32
ROW_LEN = 1024
F32 = jnp.float32
BF16 = jnp.bfloat16
VMEM_LIMIT = 56 * 1024 * 1024
NT = (((1,), (1,)), ((), ()))
NN = (((1,), (0,)), ((), ()))
TN = (((0,), (0,)), ((), ()))


def mm(left, right, dims=NN):
    return lax.dot_general(left, right, dims, preferred_element_type=F32)


def row_step(rows):
    return 512 if rows % 512 == 0 else 128


def parts_of(step):
    size = min(step, 256)
    return [slice(first, first + size) for first in range(0, step, size)]


def held(shape):
    return pl.BlockSpec(shape, lambda *_: (0,) * len(shape), pipeline_mode=pl.Buffered(1))


def shaped(dtype, *shape):
    return jax.ShapeDtypeStruct(shape, dtype)


class Order:
    last = ()


def call(
    body, name, grid, in_specs, out_specs, out_shape, operands, flops, scratch=(), prefetch=0, after=(),
    remote=None,
):
    count = len(operands)
    after = tuple(after) + Order.last

    def wrapped(*refs):
        body(*refs[:count], *refs[count + len(after) :])

    size = sum(math.prod(o.shape) * o.dtype.itemsize for o in list(operands) + list(out_shape))
    if flops == 0:
        size = 1024
    outs = pl.pallas_call(
        wrapped,
        grid_spec=pltpu.PrefetchScalarGridSpec(
            num_scalar_prefetch=prefetch,
            grid=grid,
            in_specs=list(in_specs) + [pl.BlockSpec(memory_space=pl.ANY)] * len(after),
            out_specs=out_specs,
            scratch_shapes=list(scratch),
        ),
        out_shape=out_shape,
        compiler_params=pltpu.CompilerParams(
            vmem_limit_bytes=VMEM_LIMIT, collective_id=remote, has_side_effects=remote is not None
        ),
        cost_estimate=pl.CostEstimate(flops=flops, bytes_accessed=size, transcendentals=0),
        name=name,
    )(*operands, *after)
    Order.last = (min(outs, key=lambda out: out.size * out.dtype.itemsize),)
    return outs


def row_spec(step, width):
    return pl.BlockSpec((step, width), lambda i, *_: (i, 0))


def column_spec(width, step):
    return pl.BlockSpec((width, step), lambda i, *_: (0, i))


MESH = pl.DeviceIdType.MESH
ANYWHERE = pl.BlockSpec(memory_space=pl.ANY)


def side_at(row, bit):
    return (row // bit) % 2


def across(row, bit):
    return row + bit * (1 - 2 * side_at(row, bit))


def flipped(row, bits):
    bit = 1
    while bit <= bits:
        if bits & bit:
            row = across(row, bit)
        bit *= 2
    return row


def greet(devices):
    barrier = pltpu.get_barrier_semaphore()
    for device in devices:
        pl.semaphore_signal(barrier, inc=1, device_id=device, device_id_type=MESH)
    pl.semaphore_wait(barrier, len(devices))


def send(source, target, sent, arrived, device):
    copy = pltpu.make_async_remote_copy(
        src_ref=source,
        dst_ref=target,
        send_sem=sent,
        recv_sem=arrived,
        device_id=device,
        device_id_type=MESH,
    )
    copy.start()
    return copy


def spread_order(count):
    pieces = sorted(range(count), key=lambda piece: (piece.bit_count(), -piece))
    order = []
    for piece in pieces:
        lowest = piece & -piece if piece else count
        bit = lowest // 2
        bits = []
        while bit:
            bits.append(bit)
            bit //= 2
        order.append((piece, bits))
    return order


def start_kernel(rows, cols_width, parts, *refs):
    (tokens, qkv, out, up, down, proj, pack), refs = refs[:7], refs[7:]
    (x, qkv_o, out_o, up_o, down_o, proj_o, pack_o), refs = refs[:7], refs[7:]
    own_sem, sent, arrived, wide_sent, wide_arrived = refs
    r, c = lax.axis_index("rows"), lax.axis_index("cols")
    partner = {"cols": 1 - c}
    bits = [1 << b for b in range(rows.bit_length() - 1)]
    greet([partner] + [{"rows": across(r, bit)} for bit in bits])
    wide = [(qkv, qkv_o), (out, out_o), (up, up_o)]
    copies, first = [], []
    for place, (source, target) in enumerate(wide):
        first.append(
            send(source.at[r], target.at[r], sent.at[place], arrived.at[place], partner)
        )
    q_rows, d_rows, first_doc = parts
    own = pl.ds(pl.multiple_of(c * cols_width, cols_width), cols_width)
    spans = [(0, q_rows, 0), (first_doc, d_rows, q_rows)]
    for place, (base, size, here) in enumerate(spans):
        theirs = pl.ds(pl.multiple_of(base + (1 - c) * size, size), size)
        mine = pl.ds(pl.multiple_of(base + c * size, size), size)
        target = x.at[pl.ds(here, size), own]
        copies.append(
            send(tokens.at[theirs], target, sent.at[3 + place], arrived.at[3 + place], partner)
        )
        pltpu.make_async_copy(tokens.at[mine], target, own_sem.at[place]).start()
    for place, (source, target) in enumerate([(proj, proj_o), (pack, pack_o), (down.at[r], down_o)]):
        copies.append(
            send(source, target, sent.at[5 + place], arrived.at[5 + place], partner)
        )
    wide_copies = {}
    for piece, over in spread_order(rows):
        row = flipped(r, piece)
        for place, (_, target) in enumerate(wide):
            if piece == 0:
                first[place].wait_recv()
            else:
                wide_copies[place, piece].wait_recv()
            for bit in over:
                wide_copies[place, piece | bit] = send(
                    target.at[row], target.at[row],
                    wide_sent.at[place, piece | bit], wide_arrived.at[place, piece | bit],
                    {"rows": across(r, bit)},
                )
    for copy in first + list(wide_copies.values()):
        copy.wait_send()
    for copy in copies:
        copy.wait()
    for place, (base, size, here) in enumerate(spans):
        mine = pl.ds(pl.multiple_of(base + c * size, size), size)
        target = x.at[pl.ds(here, size), own]
        pltpu.make_async_copy(tokens.at[mine], target, own_sem.at[place]).wait()


def start_up(rows, parts, tokens, qkv, out, up, down, proj, pack):
    width = tokens.shape[1]

    def pieces(array):
        return array.reshape(rows, -1, array.shape[-1])

    weights = [pieces(array) for array in (qkv, out, up, down)]
    qkv_p, out_p, up_p, down_p = weights
    operands = (tokens, *weights, proj, pack)
    n = parts[0] + parts[1]
    x, qkv_o, out_o, up_o, down_o, proj_o, pack_o = call(
        functools.partial(start_kernel, rows, width, parts), "start_up", (1,),
        [ANYWHERE] * 7, [ANYWHERE] * 7,
        [
            shaped(BF16, n, 2 * width), shaped(BF16, *qkv_p.shape), shaped(BF16, *out_p.shape),
            shaped(BF16, *up_p.shape), shaped(BF16, *down_p.shape[1:]), shaped(BF16, *proj.shape),
            shaped(F32, *pack.shape),
        ],
        operands, 0, remote=1,
        scratch=[
            pltpu.SemaphoreType.DMA((2,)), pltpu.SemaphoreType.DMA((8,)),
            pltpu.SemaphoreType.DMA((8,)), pltpu.SemaphoreType.DMA((3, rows)),
            pltpu.SemaphoreType.DMA((3, rows)),
        ],
    )
    return (
        x, qkv_o.reshape(qkv.shape), out_o.reshape(out.shape), up_o.reshape(up.shape), down_o,
        proj_o, pack_o,
    )


def gather_kernel(rows, own, out, own_sem, sent, arrived):
    r = lax.axis_index("rows")
    bits = [1 << b for b in range(rows.bit_length() - 1)]
    greet([{"rows": across(r, bit)} for bit in bits])
    local = pltpu.make_async_copy(own, out.at[r], own_sem)
    local.start()
    copies = {}
    for piece, over in spread_order(rows):
        row = flipped(r, piece)
        if piece:
            copies[piece].wait_recv()
        for bit in over:
            copies[piece | bit] = send(
                out.at[row] if piece else own, out.at[row],
                sent.at[piece | bit], arrived.at[piece | bit], {"rows": across(r, bit)},
            )
    for copy in copies.values():
        copy.wait_send()
    local.wait()


def gather_rows(rows, own):
    return call(
        functools.partial(gather_kernel, rows), "gather_rows", (1,), [ANYWHERE], [ANYWHERE],
        [shaped(own.dtype, rows, *own.shape)], (own,), 0, remote=2,
        scratch=[
            pltpu.SemaphoreType.DMA, pltpu.SemaphoreType.DMA((rows,)),
            pltpu.SemaphoreType.DMA((rows,)),
        ],
    )[0]


def scatter_kernel(rows, parts, out, sent, arrived, *buffers):
    r = lax.axis_index("rows")
    bits = [1 << b for b in range(rows.bit_length() - 1)]
    greet([{"rows": across(r, bit)} for bit in bits])
    outgoing, incoming = buffers[: len(bits)], buffers[len(bits) :]
    copies = {}

    def total(flips, levels):
        row = flipped(r, flips)
        value = parts[row]
        for level in range(levels):
            copies[level, flips >> (level + 1)].wait_recv()
            value = value + incoming[level][row // (2 << level)].astype(F32)
        return value

    for level, bit in enumerate(bits):
        count = rows // (2 << level)
        for turn in sorted(range(count), key=lambda f: tuple(-((f >> b) & 1) for b in range(8))):
            flips = (turn << (level + 1)) | bit
            place = flipped(r, flips) // (2 << level)
            outgoing[level][place] = total(flips, level).astype(BF16)
            copies[level, turn] = send(
                outgoing[level].at[place], incoming[level].at[place],
                sent.at[rows - 2 * count + turn], arrived.at[rows - 2 * count + turn],
                {"rows": across(r, bit)},
            )
    out[...] = total(0, len(bits))
    for copy in copies.values():
        copy.wait_send()


def scatter_rows(parts):
    rows, height, width = parts.shape
    levels = rows.bit_length() - 1
    buffers = [
        pltpu.VMEM((rows // (2 << level), height, width), BF16) for level in range(levels)
    ]
    return call(
        functools.partial(scatter_kernel, rows), "scatter_rows", (1,), [held(parts.shape)],
        [pl.BlockSpec((height, width), lambda *_: (0, 0))], [shaped(F32, height, width)],
        (parts,), 0, remote=3,
        scratch=[pltpu.SemaphoreType.DMA((rows,)), pltpu.SemaphoreType.DMA((rows,))]
        + buffers + buffers,
    )[0]


def small_kernel(rows, cols, parts, out, *refs):
    bits = [1 << b for b in range(rows.bit_length() - 1)]
    sent, arrived = refs[:2]
    core_in, cols_in, totals, row_ins = refs[2], refs[3], refs[4 : 4 + len(bits)], refs[4 + len(bits) :]
    r, c = lax.axis_index("rows"), lax.axis_index("cols")
    others = [{"cols": (c + cols - k) % cols} for k in range(1, cols)]
    greet([{"rows": across(r, bit)} for bit in bits] + others)
    core = side_at(r, 1)
    copy = send(parts.at[:, 1 - core], core_in, sent.at[0], arrived.at[0], {"rows": across(r, 1)})
    copy.wait()
    sums = parts[:, core] + core_in[...]
    cols_out = totals[0]
    cols_out[...] = sums
    copies = [
        send(cols_out.at[:, k], cols_in.at[k - 1], sent.at[k], arrived.at[k], others[k - 1])
        for k in range(1, cols)
    ]
    total = sums[:, 0]
    for k, copy in enumerate(copies):
        copy.wait()
        total = total + cols_in[k]
    for level, bit in enumerate(bits[1:]):
        held_total, arriving = totals[1 + level], row_ins[level]
        held_total[...] = total.reshape(held_total.shape)
        side = side_at(r, bit)
        copy = send(
            held_total.at[:, 1 - side], arriving, sent.at[cols + level], arrived.at[cols + level],
            {"rows": across(r, bit)},
        )
        copy.wait()
        total = held_total[:, side] + arriving[...]
    out[...] = total[0]


def small_sum(rows, cols, parts):
    length = parts.shape[2]
    width = -(-length // 1024) * 128
    parts = jnp.pad(parts, ((0, 0), (0, 0), (0, 8 * width - length)))
    parts = parts.reshape(rows // 2, 2, cols, 8, width)
    levels = rows.bit_length() - 1
    sizes = [rows >> (level + 1) for level in range(1, levels)]
    scratch = [
        pltpu.SemaphoreType.DMA((cols + levels,)), pltpu.SemaphoreType.DMA((cols + levels,)),
        pltpu.VMEM((rows // 2, cols, 8, width), F32),
        pltpu.VMEM((cols - 1, rows // 2, 8, width), F32),
        pltpu.VMEM((rows // 2, cols, 8, width), F32),
    ]
    scratch += [pltpu.VMEM((size, 2, 8, width), F32) for size in sizes]
    scratch += [pltpu.VMEM((size, 8, width), F32) for size in sizes]
    total = call(
        functools.partial(small_kernel, rows, cols), "small_sum", (1,), [held(parts.shape)],
        [pl.BlockSpec((8, width), lambda *_: (0, 0))], [shaped(F32, 8, width)], (parts,), 0,
        remote=4, scratch=scratch,
    )[0]
    return total.reshape(-1)[:length]


def swap_halves(block):
    lane = lax.broadcasted_iota(jnp.int32, block.shape, 1)
    return jnp.where((lane & 32) == 0, pltpu.roll(block, 96, 1), pltpu.roll(block, 32, 1))


def qkv_kernel(x_ref, w_ref, b_ref, cos_ref, sin_ref, out_ref):
    which = pl.program_id(0)
    bias = b_ref[pl.ds(which, 1), :]

    @pl.when(which < 2)
    def _():
        for at in parts_of(x_ref.shape[0]):
            mixed = mm(x_ref[at, :], w_ref[0]) + bias
            for first in range(0, mixed.shape[1], 128):
                block = mixed[:, first : first + 128]
                turned = block * cos_ref[at, :] + swap_halves(block) * sin_ref[at, :]
                out_ref[0, at, first : first + 128] = turned.astype(BF16)

    @pl.when(which == 2)
    def _():
        for at in parts_of(x_ref.shape[0]):
            out_ref[0, at, :] = (mm(x_ref[at, :], w_ref[0]) + bias).astype(BF16)


def project_qkv(x, weight, bias, cosine, sine, after=()):
    n, D = x.shape
    width = weight.shape[2]
    step = row_step(n)
    return call(
        qkv_kernel, "project_qkv", (3, n // step),
        [
            pl.BlockSpec((step, D), lambda j, i: (i, 0)),
            pl.BlockSpec((1, D, width), lambda j, i: (j, 0, 0)),
            held(bias.shape),
            pl.BlockSpec((step, 128), lambda j, i: (i, 0)),
            pl.BlockSpec((step, 128), lambda j, i: (i, 0)),
        ],
        [pl.BlockSpec((1, step, width), lambda j, i: (j, i, 0))],
        [shaped(BF16, 3, n, width)],
        (x, weight, bias, cosine, sine), 6 * n * D * width, after=after,
    )[0]


def normed_rows(residual):
    mean = jnp.mean(residual, axis=1, keepdims=True)
    centred = residual - mean
    inverse = lax.rsqrt(jnp.mean(centred * centred, axis=1, keepdims=True) + 1e-05)
    return centred * inverse, inverse


def norm_pull(grad_rows, normed, inverse, gain):
    spread = grad_rows * gain
    return inverse * (
        spread
        - jnp.mean(spread, axis=1, keepdims=True)
        - normed * jnp.mean(spread * normed, axis=1, keepdims=True)
    )


def column_sums(*arrays):
    rows = [jnp.sum(array, axis=0, keepdims=True) for array in arrays]
    rows.append(jnp.zeros((8 - len(rows), rows[0].shape[1]), F32))
    return jnp.concatenate(rows, axis=0)


def add_over_steps(ref, value):
    first = pl.program_id(0) == 0

    @pl.when(first)
    def _():
        ref[...] = value

    @pl.when(jnp.logical_not(first))
    def _():
        ref[...] += value


def out_norm_kernel(slots, *refs):
    x_ref, vec_ref = refs[:2]
    att_refs, w_refs = refs[2 : 2 + slots], refs[2 + slots : 2 + 2 * slots]
    normed_ref, inverse_ref, low_ref, turned_ref = refs[2 + 2 * slots :]
    for at in parts_of(x_ref.shape[0]):
        residual = x_ref[at, :].astype(F32) + vec_ref[0:1, :]
        for att_ref, w_ref in zip(att_refs, w_refs):
            residual = residual + mm(att_ref[at, :], w_ref[...])
        normed, inverse = normed_rows(residual)
        hidden = normed * vec_ref[1:2, :] + vec_ref[2:3, :]
        normed_ref[at, :] = normed
        inverse_ref[at, :] = inverse
        low_ref[at, :] = hidden.astype(BF16)
        turned_ref[:, at] = hidden.T.astype(BF16)


def out_and_norm(x, vectors, attended, weights):
    n, D = x.shape
    step = row_step(n)
    slots = len(attended)
    width = attended[0].shape[1]
    return call(
        functools.partial(out_norm_kernel, slots), "out_and_norm", (n // step,),
        [row_spec(step, D), held(vectors.shape)]
        + [row_spec(step, width)] * slots + [held((width, D))] * slots,
        [row_spec(step, D), row_spec(step, 1), row_spec(step, D), column_spec(D, step)],
        [shaped(F32, n, D), shaped(F32, n, 1), shaped(BF16, n, D), shaped(BF16, D, n)],
        (x, vectors, *attended, *weights), 2 * n * D * D,
    )


GELU_TERMS = (
    0.23532527933595032, 0.09138803439798156, 0.6495603483388861,
    -0.6354014529895687, 0.8866650885491606, -0.22753729931242958,
)


def gelu_parts(values):
    size = jnp.abs(values)
    part = pl.reciprocal(1.0 + (0.39 / math.sqrt(2.0)) * size)
    bell = jnp.exp(-0.5 * (values * values))
    series = 0.5 * GELU_TERMS[-1]
    for term in GELU_TERMS[-2::-1]:
        series = series * part + 0.5 * term
    tail = series * part * bell
    below = jnp.where(values >= 0.0, 1.0 - tail, tail)
    return values * below, below + values * bell * (1.0 / math.sqrt(2.0 * math.pi))


def up_kernel(x_ref, w_ref, b_ref, active_ref, slope_ref):
    width = w_ref.shape[1]
    chunk = min(256, width)
    for first in range(0, width, chunk):
        at = slice(first, first + chunk)
        active, slope = gelu_parts(mm(x_ref[...], w_ref[:, at]) + b_ref[:, at])
        active_ref[:, at] = active.astype(BF16)
        slope_ref[:, at] = slope


def up_and_gelu(x, weight, bias):
    n, D = x.shape
    width = weight.shape[1]
    step = row_step(n)
    return call(
        up_kernel, "up_and_gelu", (n // step,),
        [row_spec(step, D), held(weight.shape), held(bias.shape)],
        [row_spec(step, width)] * 2,
        [shaped(BF16, n, width), shaped(F32, n, width)],
        (x, weight, bias), 5 * n * D * width,
    )


def down_norm_kernel(slots, *refs):
    normed_ref, vec_ref, proj_ref = refs[:3]
    act_refs, w_refs = refs[3 : 3 + slots], refs[3 + slots : 3 + 2 * slots]
    normed_out, inverse_ref, low_ref, unit_ref, unit_low_ref, unit_inverse_ref = refs[3 + 2 * slots :]
    for at in parts_of(normed_ref.shape[0]):
        residual = normed_ref[at, :] * vec_ref[1:2, :] + vec_ref[2:3, :] + vec_ref[3:4, :]
        for act_ref, w_ref in zip(act_refs, w_refs):
            residual = residual + mm(act_ref[at, :], w_ref[...])
        normed, inverse = normed_rows(residual)
        normed_out[at, :] = normed
        inverse_ref[at, :] = inverse
        low = (normed * vec_ref[4:5, :] + vec_ref[5:6, :]).astype(BF16)
        low_ref[at, :] = low
        embedding = mm(low, proj_ref[...])
        unit_inverse = lax.rsqrt(jnp.sum(embedding * embedding, axis=1, keepdims=True) + 1e-06)
        unit = embedding * unit_inverse
        unit_ref[at, :] = unit
        unit_low_ref[at, :] = unit.astype(BF16)
        unit_inverse_ref[at, :] = unit_inverse


def down_and_norm(normed, vectors, proj, active, weights):
    n, D = normed.shape
    step = row_step(n)
    slots = len(active)
    width = active[0].shape[1]
    return call(
        functools.partial(down_norm_kernel, slots), "down_and_norm", (n // step,),
        [row_spec(step, D), held(vectors.shape), held(proj.shape)]
        + [row_spec(step, width)] * slots + [held((width, D))] * slots,
        [
            row_spec(step, D), row_spec(step, 1), row_spec(step, D),
            row_spec(step, 128), row_spec(step, 128), row_spec(step, 1),
        ],
        [
            shaped(F32, n, D), shaped(F32, n, 1), shaped(BF16, n, D),
            shaped(F32, n, 128), shaped(BF16, n, 128), shaped(F32, n, 1),
        ],
        (normed, vectors, proj, *active, *weights), 2 * n * D * width * slots,
    )


def head_pull_kernel(
    grad_ref, unit_ref, unit_inverse_ref, proj_ref, normed_ref, inverse_ref, vec_ref,
    embed_ref, residual_ref, low_ref, turned_ref, sum_ref,
):
    sums = []
    for at in parts_of(grad_ref.shape[0]):
        grad, unit = grad_ref[at, :], unit_ref[at, :]
        embed = grad - unit * jnp.sum(grad * unit, axis=1, keepdims=True)
        embed = (unit_inverse_ref[at, :] * embed).astype(BF16)
        embed_ref[at, :] = embed
        output_grad = mm(embed, proj_ref[...], NT)
        normed = normed_ref[at, :]
        residual = norm_pull(output_grad, normed, inverse_ref[at, :], vec_ref[4:5, :])
        residual_ref[at, :] = residual
        low_ref[at, :] = residual.astype(BF16)
        turned_ref[:, at] = residual.T.astype(BF16)
        sums.append(column_sums(residual, output_grad * normed, output_grad))
    add_over_steps(sum_ref, sum(sums))


def head_pull(unit_grad, unit, unit_inverse, proj, normed, inverse, vectors):
    n, D = normed.shape
    step = row_step(n)
    return call(
        head_pull_kernel, "head_pull", (n // step,),
        [
            row_spec(step, 128), row_spec(step, 128), row_spec(step, 1), held(proj.shape),
            row_spec(step, D), row_spec(step, 1), held(vectors.shape),
        ],
        [
            row_spec(step, 128), row_spec(step, D), row_spec(step, D),
            column_spec(D, step), pl.BlockSpec((8, D), lambda i: (0, 0)),
        ],
        [
            shaped(BF16, n, 128), shaped(F32, n, D), shaped(BF16, n, D),
            shaped(BF16, D, n), shaped(F32, 8, D),
        ],
        (unit_grad, unit, unit_inverse, proj, normed, inverse, vectors), 4 * n * D * 128,
    )


def up_pull_kernel(branch_ref, w_ref, slope_ref, out_ref, sum_ref):
    width = w_ref.shape[0]
    chunk = min(512, width)
    sums = []
    for first in range(0, width, chunk):
        at = slice(first, first + chunk)
        low = (mm(branch_ref[...], w_ref[at, :], NT) * slope_ref[:, at]).astype(BF16)
        out_ref[:, at] = low
        sums.append(column_sums(low.astype(F32)))
    add_over_steps(sum_ref, jnp.concatenate(sums, axis=1))


def up_pull(branch, weight, slope):
    n, D = branch.shape
    width = weight.shape[0]
    step = row_step(n)
    return call(
        up_pull_kernel, "up_pull", (n // step,),
        [row_spec(step, D), held(weight.shape), row_spec(step, width)],
        [row_spec(step, width), pl.BlockSpec((8, width), lambda i: (0, 0))],
        [shaped(BF16, n, width), shaped(F32, 8, width)],
        (branch, weight, slope), 2 * n * D * width,
    )


def hidden_pull_kernel(slots, *refs):
    residual_ref, normed_ref, inverse_ref, vec_ref = refs[:4]
    pre_refs, up_refs, out_refs = (refs[4 + j * slots : 4 + (j + 1) * slots] for j in range(3))
    rest = refs[4 + 3 * slots :]
    grad_ref, turned_ref, sum_ref = rest[:3]
    att_refs = rest[3:]
    sums = []
    for at in parts_of(residual_ref.shape[0]):
        hidden_grad = residual_ref[at, :]
        for pre_ref, up_ref in zip(pre_refs, up_refs):
            hidden_grad = hidden_grad + mm(pre_ref[at, :], up_ref[...], NT)
        normed = normed_ref[at, :]
        residual = norm_pull(hidden_grad, normed, inverse_ref[at, :], vec_ref[1:2, :])
        grad_ref[at, :] = residual
        low = residual.astype(BF16)
        turned_ref[:, at] = residual.T.astype(BF16)
        sums.append(column_sums(residual, hidden_grad * normed, hidden_grad))
        for att_ref, out_ref in zip(att_refs, out_refs):
            att_ref[at, :] = mm(low, out_ref[...], NT).astype(BF16)
    add_over_steps(sum_ref, sum(sums))


def hidden_pull(residual, normed, inverse, vectors, pre_grads, ups, outs):
    n, D = residual.shape
    step = row_step(n)
    slots = len(ups)
    wide, width = ups[0].shape[1], outs[0].shape[0]
    return call(
        functools.partial(hidden_pull_kernel, slots), "hidden_pull", (n // step,),
        [row_spec(step, D), row_spec(step, D), row_spec(step, 1), held(vectors.shape)]
        + [row_spec(step, wide)] * slots + [held((D, wide))] * slots
        + [held((width, D))] * slots,
        [row_spec(step, D), column_spec(D, step), pl.BlockSpec((8, D), lambda i: (0, 0))]
        + [row_spec(step, width)] * slots,
        [shaped(F32, n, D), shaped(BF16, D, n), shaped(F32, 8, D)]
        + [shaped(BF16, n, width)] * slots,
        (residual, normed, inverse, vectors, *pre_grads, *ups, *outs),
        0,
    )


def token_pull_kernel(slots, place_ref, *refs):
    residual_ref = refs[0]
    mixed_refs, w_refs = refs[1 : 1 + slots], refs[1 + slots : 1 + 2 * slots]
    out_ref = refs[-1]
    width = out_ref.shape[1]
    at = pl.ds(pl.multiple_of(place_ref[0] * width, width), width)
    total = residual_ref[...]
    for mixed_ref, w_ref in zip(mixed_refs, w_refs):
        for which in range(3):
            total = total + mm(mixed_ref[which], w_ref[which, at, :], NT)
    out_ref[...] = total.astype(out_ref.dtype)


def token_pull(place, residual, mixed_grads, weights, dtype):
    n, D = residual.shape
    step = row_step(n)
    slots = len(weights)
    width = weights[0].shape[2]
    return call(
        functools.partial(token_pull_kernel, slots), "token_pull", (n // step,),
        [pl.BlockSpec((step, width), lambda i, p: (i, p[0]))]
        + [pl.BlockSpec((3, step, width), lambda i, p: (0, i, 0))] * slots
        + [held((3, D, width))] * slots,
        [row_spec(step, width)],
        [shaped(dtype, n, width)],
        (place.reshape(1), residual, *mixed_grads, *weights), 6 * n * D * width, prefetch=1,
    )[0]


def put_halves(total, inner, side, refs):
    pairs = total.reshape(-1, 2, inner, total.shape[1])
    keep = jnp.where(side == 0, pairs[:, 0], pairs[:, 1]).reshape(-1, total.shape[1])
    send = jnp.where(side == 0, pairs[:, 1], pairs[:, 0]).reshape(-1, total.shape[1])
    refs[0][0] = send.astype(BF16)
    refs[1][0] = keep


def grouped_index(starts, place, count):
    def index(j, i, *_):
        inside = (j >= starts[place]) & (j < starts[place + 1])
        row = jnp.clip(j - starts[place], 0, starts[place + 1] - starts[place] - 1)
        rest = jnp.where(j < starts[place], 0, count - 1)
        return row, 0, jnp.where(inside, i, rest)

    return index


def for_group(starts, body):
    if len(starts) == 2:
        body(0)
        return
    for place in range(len(starts) - 1):

        @pl.when((pl.program_id(0) >= starts[place]) & (pl.program_id(0) < starts[place + 1]))
        def _(place=place):
            body(place)


def weight_pull_kernel(starts, added, inner, place_ref, *refs):
    groups = len(starts) - 1
    lefts, rights, refs = refs[:groups], refs[groups : 2 * groups], refs[2 * groups :]

    def one_group(place):
        left = lefts[place]
        total = mm(left[:, 0].reshape(-1, left.shape[-1]), rights[place][0])
        outs = refs
        if added:
            total = total + refs[0][0].astype(F32)
            outs = refs[1:]
        if inner:
            put_halves(total, inner, place_ref[1], outs)
        else:
            outs[0][0] = total.astype(outs[0].dtype)

    for_group(starts, one_group)


def weight_pull(places, lefts, rights, arrived=None, dtype=BF16, inner=0):
    pairs, _, share, n = lefts[0].shape
    m = rights[0].shape[2]
    rows = pairs * share
    chunk = min(512, m)
    starts = [0]
    for right in rights:
        starts.append(starts[-1] + right.shape[0])

    def spec(size):
        return pl.BlockSpec((1, size, chunk), lambda j, i, p: (j, 0, i))

    half = rows // 2
    outs = [(BF16, half), (F32, half)] if inner else [(dtype, rows)]
    return call(
        functools.partial(weight_pull_kernel, starts, arrived is not None, inner), "weight_pull",
        (starts[-1], m // chunk),
        [pl.BlockSpec((pairs, 1, share, n), lambda j, i, p: (0, p[0], 0, 0)) for _ in lefts]
        + [
            pl.BlockSpec((1, n, chunk), grouped_index(starts, place, m // chunk))
            for place in range(len(rights))
        ] + ([] if arrived is None else [spec(rows)]),
        [spec(size) for _, size in outs],
        [shaped(kind, starts[-1], size, m) for kind, size in outs],
        (places, *lefts, *rights) + (() if arrived is None else (arrived,)),
        0, prefetch=1,
    )


def pass_on_kernel(in_ref, out_ref):
    out_ref[...] = in_ref[...]


def pass_on(array):
    spec = held(array.shape)
    return call(
        pass_on_kernel, "pass_on", (1,), [spec], [pl.BlockSpec(array.shape, lambda *_: (0,) * array.ndim)],
        [shaped(array.dtype, *array.shape)], (array,), 0,
    )[0]


def fold_kernel(starts, inner, place_ref, *refs):
    groups = len(starts) - 1

    def one_group(place):
        total = refs[place][0] + refs[groups + place][0].astype(F32)
        put_halves(total, inner, place_ref[0], refs[2 * groups :])

    for_group(starts, one_group)


def fold(side, owns, arrived, inner):
    _, rows, m = owns[0].shape
    chunk = min(1024, m)
    starts = [0]
    for own in owns:
        starts.append(starts[-1] + own.shape[0])

    def spec(size):
        return pl.BlockSpec((1, size, chunk), lambda j, i, p: (j, 0, i))

    half = rows // 2
    specs = [
        pl.BlockSpec((1, rows, chunk), grouped_index(starts, place, m // chunk))
        for place in range(len(owns))
    ]
    return call(
        functools.partial(fold_kernel, starts, inner), "fold", (starts[-1], m // chunk),
        specs + specs, [spec(half), spec(half)],
        [shaped(BF16, starts[-1], half, m), shaped(F32, starts[-1], half, m)],
        (side.reshape(1), *owns, *arrived), 0, prefetch=1,
    )


SEGMENTS = 8
ATTENTION_LANES = 128


def half_lanes(block, head, other):
    lane = lax.broadcasted_iota(jnp.int32, block.shape, 1)
    return jnp.where((lane >= DH) == (head == 1), block, other)


def scaled(block):
    return (block.astype(F32) * DH**-0.5).astype(BF16)


def three_terms(value):
    high = value.astype(BF16).astype(F32)
    middle = (value - high).astype(BF16).astype(F32)
    return high, middle, value - high - middle


def for_spans(span_ref, tiles, body):
    @pl.loop(0, tiles)
    def _(step):
        low, high = span_ref[step], span_ref[tiles + step]
        for count in range(1, tiles + 1):

            @pl.when(high - low == count)
            def _(count=count):
                body(step, low, count)


def attention_forward_kernel(
    span_ref, qkv_ref, ext_k_ref, ext_q_ref, out_ref, rest_ref, ext_ref,
    keys_ref, queries_ref, turned_ref, values_ref, *, tile,
):
    n = ext_k_ref.shape[0]
    tiles = n // tile
    pairs = qkv_ref.shape[2] // 128
    heads = range(2 * pairs)

    def lanes(head):
        return slice(head // 2 * 128, head // 2 * 128 + 128)

    def own_rows(head):
        return slice(head % 2 * DH, head % 2 * DH + DH)

    for head in heads:
        keys_ref[head] = half_lanes(qkv_ref[1, :, lanes(head)], head % 2, ext_k_ref[...])
        queries_ref[head] = half_lanes(
            scaled(qkv_ref[0, :, lanes(head)]), head % 2, ext_q_ref[...]
        )
    for pair in range(pairs):
        for step in range(tiles):
            at = slice(step * tile, (step + 1) * tile)
            values_ref[pair, :, at] = qkv_ref[2, at, lanes(2 * pair)].astype(F32).T.astype(BF16)
            for head in (2 * pair, 2 * pair + 1):
                turned_ref[head, step] = queries_ref[head, at, :].astype(F32).T.astype(BF16)

    def attend(step, low, count):
        rows = pl.ds(pl.multiple_of(step * tile, tile), tile)
        window = pl.ds(pl.multiple_of(low * tile, tile), count * tile)
        for pair in range(pairs):
            outs, extras = [], []
            for head in (2 * pair, 2 * pair + 1):
                logits = mm(keys_ref[head, window, :], turned_ref[head, step])
                top = jnp.max(logits, axis=0, keepdims=True)
                weights = jnp.exp(logits - top)
                mass = jnp.sum(weights, axis=0, keepdims=True)
                probs = (weights * (1.0 / mass)).astype(BF16)
                outs.append(mm(values_ref[pair, own_rows(head), window], probs))
                terms = three_terms(-(top + jnp.log(mass)))
                extras.append(
                    [jnp.zeros((8, tile), F32), *terms, jnp.zeros((DH - 11, tile), F32)]
                )
            at = lanes(2 * pair)
            out = jnp.concatenate(outs, axis=0).T
            out_ref[rows, at] = out.astype(BF16)
            rest_ref[rows, at] = (out - out.astype(BF16).astype(F32)).astype(BF16)
            extra = jnp.concatenate(extras[1] + extras[0], axis=0).T
            ext_ref[rows, at] = (extra + ext_q_ref[rows, :].astype(F32)).astype(BF16)

    for_spans(span_ref, tiles, attend)


def attention_forward(spans, qkv, ext_k, ext_q, tile):
    _, n, width = qkv.shape
    span = min(width, ATTENTION_LANES)
    wide = pl.BlockSpec((n, span), lambda i, *_: (0, i))
    tiles, pairs = n // tile, span // 128
    return call(
        functools.partial(attention_forward_kernel, tile=tile), "attention_forward",
        (width // span,),
        [pl.BlockSpec((3, n, span), lambda i, *_: (0, 0, i)), held((n, 128)), held((n, 128))],
        [wide, wide, wide],
        [shaped(BF16, n, width)] * 3,
        (spans, qkv, ext_k, ext_q), 0, prefetch=1,
        scratch=[
            pltpu.VMEM((2 * pairs, n, 128), BF16), pltpu.VMEM((2 * pairs, n, 128), BF16),
            pltpu.VMEM((2 * pairs, tiles, 128, tile), BF16), pltpu.VMEM((pairs, 128, n), BF16),
        ],
    )


def attention_backward_kernel(
    span_ref, qkv_ref, ext_ref, att_ref, rest_ref, grad_ref, ext_k_ref, cos_ref, sin_ref,
    out_ref, sum_ref,
    keys_ref, turned_ref, values_ref, queries_ref, plain_ref, grads_ref, plain_grads_ref,
    dq_ref, dk_ref, dv_ref, *, tile,
):
    n = ext_k_ref.shape[0]
    tiles = n // tile
    pairs = qkv_ref.shape[2] // 128
    heads = range(2 * pairs)

    def lanes(head):
        return slice(head // 2 * 128, head // 2 * 128 + 128)

    def own_rows(head):
        return slice(head % 2 * DH, head % 2 * DH + DH)

    def rows(step):
        return pl.ds(pl.multiple_of(step * tile, tile), tile)

    @pl.loop(0, tiles)
    def _(step):
        at = rows(step)
        zeros = jnp.zeros((tile, 128), BF16)
        lane = lax.broadcasted_iota(jnp.int32, (tile, 128), 1)
        ext_k = ext_k_ref[at, :]
        for pair in range(pairs):
            cut = lanes(2 * pair)
            grad = grad_ref[at, cut]
            out = att_ref[at, cut].astype(F32) + rest_ref[at, cut].astype(F32)
            product = grad.astype(F32) * out
            query = scaled(qkv_ref[0, at, cut])
            turned_ref[pair, :, at] = scaled(qkv_ref[1, at, cut]).astype(F32).T.astype(BF16)
            for half in range(2):
                head = 2 * pair + half
                keys_ref[head, at, :] = half_lanes(qkv_ref[1, at, cut], half, ext_k)
                values_ref[head, at, :] = half_lanes(qkv_ref[2, at, cut], half, ext_k)
                whole = half_lanes(query, half, ext_ref[at, cut])
                queries_ref[head, step] = whole.astype(F32).T.astype(BF16)
                plain_ref[head, at, :] = half_lanes(query, half, zeros)
                plain_grads_ref[head, at, :] = half_lanes(grad, half, zeros)
                inner = jnp.sum(half_lanes(product, half, 0.0), axis=1, keepdims=True)
                extra = jnp.zeros((tile, 128), F32)
                for place, term in enumerate(three_terms(-inner)):
                    extra = jnp.where((lane & (DH - 1)) == SEGMENTS + place, term, extra)
                whole = half_lanes(grad.astype(F32), half, extra)
                grads_ref[head, step] = whole.T.astype(BF16)

    dk_ref[...] = jnp.zeros(dk_ref.shape, F32)
    dv_ref[...] = jnp.zeros(dv_ref.shape, F32)

    def pull(step, low, count):
        at = rows(step)
        window = pl.ds(pl.multiple_of(low * tile, tile), count * tile)
        for pair in range(pairs):
            probs, slopes, dq = [], [], []
            both = range(2 * pair, 2 * pair + 2)
            for head in both:
                weights = jnp.exp(mm(keys_ref[head, window, :], queries_ref[head, step]))
                flow = mm(values_ref[head, window, :], grads_ref[head, step])
                slope = (weights * flow).astype(BF16)
                probs.append(weights.astype(BF16))
                slopes.append(slope)
                dq.append(mm(turned_ref[pair, own_rows(head), window], slope))
            plain = jnp.concatenate([plain_ref[h, at, :] for h in both], axis=0)
            grads = jnp.concatenate([plain_grads_ref[h, at, :] for h in both], axis=0)
            cut = lanes(2 * pair)
            dv_ref[window, cut] += mm(jnp.concatenate(probs, axis=1), grads)
            dk_ref[window, cut] += mm(jnp.concatenate(slopes, axis=1), plain)
            dq_ref[at, cut] = jnp.concatenate(dq, axis=0).T

    for_spans(span_ref, tiles, pull)

    def finish(step, sums):
        cosine, sine = cos_ref[rows(step), :], sin_ref[rows(step), :]
        added = []
        for which, src in enumerate((dq_ref, dk_ref, dv_ref)):
            for pair in range(pairs):
                at = lanes(2 * pair)
                block = src[rows(step), at]
                if which < 2:
                    block = block * cosine - swap_halves(block) * sine
                low = block.astype(BF16)
                out_ref[which, rows(step), at] = low
                total = jnp.sum(low.astype(F32), axis=0, keepdims=True)
                added.append(sums[which * pairs + pair] + total)
        return tuple(added)

    zero = jnp.zeros((1, 128), F32)
    sums = lax.fori_loop(0, tiles, finish, (zero,) * (3 * pairs))
    sums = [jnp.concatenate(sums[w * pairs : (w + 1) * pairs], axis=1) for w in range(3)]
    sum_ref[...] = jnp.concatenate(sums + [jnp.zeros((5, pairs * 128), F32)], axis=0)


def attention_backward(
    spans, qkv, ext, attended, rest, grads, ext_k, cosine, sine, tile
):
    _, n, width = qkv.shape
    span = min(width, ATTENTION_LANES)
    wide = pl.BlockSpec((n, span), lambda i, *_: (0, i))
    three = pl.BlockSpec((3, n, span), lambda i, *_: (0, 0, i))
    tiles, pairs = n // tile, span // 128
    heads = pltpu.VMEM((2 * pairs, n, 128), BF16)
    turned = pltpu.VMEM((2 * pairs, tiles, 128, tile), BF16)
    return call(
        functools.partial(attention_backward_kernel, tile=tile), "attention_backward",
        (width // span,),
        [three, wide, wide, wide, wide, held((n, 128)), held((n, 128)), held((n, 128))],
        [three, pl.BlockSpec((8, span), lambda i, *_: (0, i))],
        [shaped(BF16, 3, n, width), shaped(F32, 8, width)],
        (spans, qkv, ext, attended, rest, grads, ext_k, cosine, sine), 0,
        prefetch=1,
        scratch=[
            heads, pltpu.VMEM((pairs, 128, n), BF16), heads, turned, heads, turned, heads,
        ] + [pltpu.VMEM((n, span), F32)] * 3,
    )


STRIP = 32


def token_sums(width, queries):
    token = lax.broadcasted_iota(jnp.int32, (width, queries), 0) // QLEN
    return token == lax.broadcasted_iota(jnp.int32, (width, queries), 1)


def score_kernel(low_ref, high_ref, doc_ref, query_ref, pick_ref, out_ref, sum_ref):
    group = pl.program_id(0)
    docs, width = pick_ref.shape[1:]
    doc_rows = doc_ref.shape[0]
    strips = doc_rows // STRIP
    chunk = min(256, doc_rows)
    row = lax.broadcasted_iota(jnp.int32, (STRIP, width), 0)
    sum_ref[...] = jnp.zeros(sum_ref.shape, F32)

    def add_strip(sim, first, doc, pick):
        kept = jnp.where(row == pick - first, sim, 0.0)
        sum_ref[pl.ds(doc, 1)] += jnp.sum(kept.reshape(1, STRIP // 8, 8, width), axis=1)

    for start in range(0, doc_rows, chunk):
        sims = mm(doc_ref[start : start + chunk, :], query_ref[...], NT)
        for first in range(0, chunk, STRIP):
            place = group * strips + (start + first) // STRIP
            low, high = low_ref[place], high_ref[place]
            sim = sims[first : first + STRIP]
            add_strip(sim, start + first, low, pick_ref[0, pl.ds(low, 1), :])
            pick = jnp.where(high > low, pick_ref[0, pl.ds(high, 1), :], -1)
            add_strip(sim, start + first, high, pick)

    @pl.loop(0, strips)
    def _(strip):
        low, high = low_ref[group * strips + strip], high_ref[group * strips + strip]

        @pl.when(high > low + 1)
        def _():
            first = pl.multiple_of(strip * STRIP, STRIP)
            sim = mm(doc_ref[pl.ds(first, STRIP), :], query_ref[...], NT)

            @pl.loop(low + 1, high)
            def _(doc):
                add_strip(sim, first, doc, pick_ref[0, pl.ds(doc, 1), :])

    totals = jnp.sum(sum_ref[...], axis=1)
    totals = jnp.concatenate([totals, jnp.zeros((8 - docs, width), F32)], axis=0)
    spread = token_sums(width, out_ref.shape[2]).astype(F32)
    out_ref[0] = lax.dot_general(
        totals, spread, NN, precision=lax.Precision.HIGHEST, preferred_element_type=F32
    )[:docs]


def score_grad_kernel(
    low_ref, high_ref, doc_ref, query_ref, pick_ref, weight_ref, doc_out, query_out,
    sparse_ref, token_ref,
):
    group = pl.program_id(0)
    docs, width = pick_ref.shape[1:]
    doc_rows = doc_ref.shape[0]
    strips = doc_rows // STRIP
    chunk = min(256, doc_rows)
    row = lax.broadcasted_iota(jnp.int32, (STRIP, width), 0)
    spread = token_sums(width, weight_ref.shape[2]).astype(F32).astype(BF16)
    weights = jnp.concatenate(
        [weight_ref[0], jnp.zeros((16 - docs, weight_ref.shape[2]), F32)], axis=0
    )
    token_ref[...] = mm(weights.astype(BF16), spread, NT)

    def fill(held, first, doc, pick):
        return jnp.where(row == pick - first, token_ref[pl.ds(doc, 1), :], held)

    @pl.when(group == 0)
    def _():
        query_out[...] = jnp.zeros_like(query_out)

    total = None
    for start in range(0, doc_rows, chunk):
        for first in range(start, start + chunk, STRIP):
            place = group * strips + first // STRIP
            low, high = low_ref[place], high_ref[place]
            held = fill(jnp.zeros((STRIP, width), F32), first, low, pick_ref[0, pl.ds(low, 1), :])
            pick = jnp.where(high > low, pick_ref[0, pl.ds(high, 1), :], -1)
            sparse_ref[first : first + STRIP, :] = fill(held, first, high, pick).astype(BF16)
        sparse = sparse_ref[start : start + chunk, :]
        doc_out[start : start + chunk, :] = mm(sparse, query_ref[...])
        turned = doc_ref[start : start + chunk, :].astype(F32).T.astype(BF16)
        part = mm(turned, sparse)
        total = part if total is None else total + part
    query_out[...] += total

    @pl.loop(0, strips)
    def _(strip):
        low, high = low_ref[group * strips + strip], high_ref[group * strips + strip]

        @pl.when(high > low + 1)
        def _():
            first = pl.multiple_of(strip * STRIP, STRIP)
            held = lax.fori_loop(
                low + 1,
                high,
                lambda doc, held: fill(held, first, doc, pick_ref[0, pl.ds(doc, 1), :]),
                jnp.zeros((STRIP, width), F32),
            ).astype(BF16)
            doc_out[pl.ds(first, STRIP), :] += mm(held, query_ref[...])
            turned = doc_ref[pl.ds(first, STRIP), :].astype(F32).T.astype(BF16)
            query_out[...] += mm(turned, held)


def score_specs(doc_tile, query_tile, picks, queries):
    groups, docs, width = picks.shape
    doc_rows = doc_tile.shape[0] // groups
    return (
        pl.BlockSpec((doc_rows, 128), lambda i, *_: (i, 0)),
        held(query_tile.shape),
        pl.BlockSpec((1, docs, width), lambda i, *_: (i, 0, 0)),
        pl.BlockSpec((1, docs, queries), lambda i, *_: (i, 0, 0)),
    )


def score_forward(lows, highs, doc_tile, query_tile, picks):
    groups, docs, width = picks.shape
    queries = width // QLEN
    doc_spec, query_spec, pick_spec, out_spec = score_specs(doc_tile, query_tile, picks, queries)
    return call(
        score_kernel, "score_forward", (groups,),
        [doc_spec, query_spec, pick_spec], [out_spec],
        [shaped(F32, groups, docs, queries)],
        (lows, highs, doc_tile, query_tile, picks), 2 * doc_tile.shape[0] * width * 128,
        prefetch=2, scratch=[pltpu.VMEM((docs, 8, width), F32)],
    )[0]


def score_backward(lows, highs, doc_tile, query_tile, picks, weights):
    groups, docs, width = picks.shape
    doc_spec, query_spec, pick_spec, weight_spec = score_specs(
        doc_tile, query_tile, picks, weights.shape[2]
    )
    return call(
        score_grad_kernel, "score_backward", (groups,),
        [doc_spec, query_spec, pick_spec, weight_spec],
        [doc_spec, pl.BlockSpec((128, width), lambda i, *_: (0, 0))],
        [shaped(F32, *doc_tile.shape), shaped(F32, 128, width)],
        (lows, highs, doc_tile, query_tile, picks, weights), 4 * doc_tile.shape[0] * width * 128,
        prefetch=2,
        scratch=[
            pltpu.VMEM((doc_tile.shape[0] // groups, width), BF16), pltpu.VMEM((16, width), F32)
        ],
    )


def rotary_tables(position):
    half_size = DH // 2
    frequency = jnp.exp(
        jnp.arange(half_size, dtype=F32) * (-2.0 * math.log(10000.0) / DH)
    )
    angles = position.astype(F32)[:, None] * frequency[None, :]
    cosine, sine = jnp.cos(angles), jnp.sin(angles)
    return (
        jnp.concatenate([cosine] * 4, axis=1),
        jnp.concatenate([-sine, sine, -sine, sine], axis=1),
    )


def on_device(
    tokens,
    doc_lengths,
    match_picks,
    labels,
    w_qkv,
    b_qkv,
    w_out,
    b_out,
    ln1_gain,
    ln1_bias,
    w_up,
    b_up,
    w_down,
    b_down,
    ln2_gain,
    ln2_bias,
    w_proj,
    log_scale,
):
    Order.last = ()
    C = lax.axis_size("cols")
    R = lax.axis_size("rows")
    c = lax.axis_index("cols")
    r = lax.axis_index("rows")
    width = tokens.shape[1]
    D = width * C
    Q = ROW_LEN // C
    DS = (tokens.shape[0] - ROW_LEN) // C
    n = Q + DS
    tile = math.gcd(256, math.gcd(Q, DS))

    def shift_cols(value, k):
        return lax.ppermute(value, "cols", [(i, (i + k) % C) for i in range(C)])

    def swap_rows(value, bit):
        return lax.ppermute(value, "rows", [(i, i ^ bit) for i in range(R)])

    def in_order(slots):
        if len(slots) == 1:
            return slots
        if len(slots) == 2:
            return [lax.select(c == 0, slots[0], slots[1]), lax.select(c == 0, slots[1], slots[0])]
        stacked = jnp.stack(slots)
        return [
            lax.dynamic_index_in_dim(stacked, (c - j) % C, 0, keepdims=False) for j in range(C)
        ]

    pack = [b_qkv.reshape(-1), b_up, b_out, ln1_gain, ln1_bias, b_down, ln2_gain, ln2_bias]
    ends = [0]
    for vector in pack:
        ends.append(ends[-1] + vector.shape[0])
    packed = jnp.concatenate(pack)

    def gather_pieces(pieces):
        return [lax.all_gather(piece, "rows", axis=0, tiled=True) for piece in pieces]

    if C == 2:
        x, *others, down_piece, proj_other, pack_other = start_up(
            R, (Q, DS, ROW_LEN), tokens, w_qkv, w_out, w_up, w_down, w_proj,
            packed.reshape(8, -1),
        )
        wqkv_slots, wout_slots, wup_slots = (
            [own, other] for own, other in zip((w_qkv, w_out, w_up), others)
        )
        wdown_slots = [w_down] + gather_pieces([down_piece])
        wproj = jnp.concatenate(in_order([w_proj, proj_other]), axis=0)
        packs = [packed, pack_other.reshape(-1)]
    else:
        parts = jnp.concatenate(
            [tokens[:ROW_LEN].reshape(C, Q, width), tokens[ROW_LEN:].reshape(C, DS, width)], axis=1
        )

        def part(k):
            return lax.dynamic_index_in_dim(parts, (c + k) % C, 0, keepdims=False)

        x = jnp.concatenate(
            in_order([part(0)] + [shift_cols(part(k), k) for k in range(1, C)]), axis=1
        )

        def gather_slots(shard):
            flat = shard.reshape(-1, shard.shape[-1])
            piece = lax.dynamic_index_in_dim(
                flat.reshape(R, flat.shape[0] // R, flat.shape[1]), r, 0, keepdims=False
            )
            others = gather_pieces([shift_cols(piece, k) for k in range(1, C)])
            return [shard] + [other.reshape(shard.shape) for other in others]

        wqkv_slots, wout_slots, wup_slots, wdown_slots = (
            gather_slots(shard) for shard in (w_qkv, w_out, w_up, w_down)
        )
        wproj = jnp.concatenate(
            in_order([w_proj] + [shift_cols(w_proj, k) for k in range(1, C)]), axis=0
        )
        packs = [packed] + [shift_cols(packed, k) for k in range(1, C)]

    ordered_packs = in_order(packs)

    def of_slot(which, k):
        return packs[k][ends[which] : ends[which + 1]]

    def whole(which):
        return jnp.concatenate([p[ends[which] : ends[which + 1]] for p in ordered_packs])

    bqkv_slots = [of_slot(0, k).reshape(b_qkv.shape) for k in range(C)]
    bup_slots = [of_slot(1, k)[None, :] for k in range(C)]
    bout, gain1, bias1, bdown, gain2, bias2 = [whole(which) for which in range(2, 8)]
    zero_row = jnp.zeros_like(bout)
    vectors = jnp.stack([bout, gain1, bias1, bdown, gain2, bias2, zero_row, zero_row])

    own_sizes = lax.dynamic_index_in_dim(
        lax.dynamic_index_in_dim(doc_lengths, r, 0, keepdims=False), c, 0, keepdims=False
    )
    own_ends = jnp.cumsum(own_sizes)
    places = jnp.arange(DS, dtype=jnp.int32)
    passed = places[:, None] >= own_ends[None, :]
    slot_id = jnp.sum(passed.astype(jnp.int32), axis=1)
    slot_begin = jnp.sum(jnp.where(passed, own_sizes[None, :], 0), axis=1)
    query_places = jnp.arange(Q, dtype=jnp.int32)
    position = jnp.concatenate([query_places % QLEN, places - slot_begin])
    cosine, sine = rotary_tables(position)
    segment = jnp.concatenate([(query_places // QLEN) % SEGMENTS, slot_id])
    lane = jnp.arange(128, dtype=jnp.int32)[None, :] % DH
    same = segment[:, None] == lane
    ext_k = (same | ((lane >= SEGMENTS) & (lane < SEGMENTS + 3))).astype(BF16)
    ext_q = jnp.where((lane < SEGMENTS) & ~same, -1e30, 0.0).astype(BF16)
    q_tiles, d_tiles = Q // tile, DS // tile
    steps = jnp.arange(q_tiles, dtype=jnp.int32)
    first_rows = jnp.arange(d_tiles, dtype=jnp.int32) * tile
    is_passed = first_rows[:, None] >= own_ends[None, :]
    low_rows = jnp.sum(jnp.where(is_passed, own_sizes[None, :], 0), axis=1)
    last_passed = (first_rows + tile - 1)[:, None] >= own_ends[None, :]
    high_rows = jnp.min(jnp.where(last_passed, DS, own_ends[None, :]), axis=1)
    spans = jnp.concatenate(
        [steps, q_tiles + low_rows // tile, steps + 1, q_tiles + (high_rows + tile - 1) // tile]
    ).astype(jnp.int32)

    queries_here, tile_docs, _ = match_picks.shape
    docs = own_sizes.shape[0]
    sizes = lax.dynamic_index_in_dim(doc_lengths, c, 1, keepdims=False)
    doc_ends = jnp.cumsum(sizes, axis=1)
    begins = doc_ends - sizes
    picks = jnp.transpose(match_picks, (1, 0, 2)).reshape(tile_docs, queries_here * QLEN)
    picks = begins.reshape(-1)[:, None] + picks % sizes.reshape(-1)[:, None]
    picks = picks.reshape(R, docs, queries_here * QLEN)
    strip_rows = (jnp.arange(DS // STRIP, dtype=jnp.int32) * STRIP)[None, :, None]
    lows = jnp.sum(doc_ends[:, None, :] <= strip_rows, axis=2).astype(jnp.int32).reshape(-1)
    highs = jnp.sum(begins[:, None, :] < strip_rows + STRIP, axis=2).astype(jnp.int32) - 1
    highs = highs.reshape(-1)

    qkv, attended, rests, exts = [], [], [], []
    for k in range(C):
        first = (picks, lows, highs) if k == 0 else ()
        qkv.append(project_qkv(x, wqkv_slots[k], bqkv_slots[k], cosine, sine, first))
        out, rest, ext = attention_forward(spans, qkv[k], ext_k, ext_q, tile)
        attended.append(out)
        rests.append(rest)
        exts.append(ext)
    normed_one, inverse_one, hidden_low, hidden_t = out_and_norm(x, vectors, attended, wout_slots)
    active, slopes = zip(*[up_and_gelu(hidden_low, wup_slots[k], bup_slots[k]) for k in range(C)])
    normed_two, inverse_two, output_low, unit, unit_low, unit_inverse = down_and_norm(
        normed_one, vectors, wproj, active, wdown_slots
    )

    doc_tile = gather_rows(R, unit_low[Q:]).reshape(R * DS, 128)
    query_tile = jnp.concatenate(
        in_order([unit_low[:Q]] + [shift_cols(unit_low[:Q], k) for k in range(1, C)]), axis=0
    )
    sims = score_forward(lows, highs, doc_tile, query_tile, picks)
    scores = sims.reshape(tile_docs, queries_here).T

    scale = jnp.exp(log_scale[0])
    z = scale * scores
    row_top = jnp.max(z, axis=1)
    row_mass = jnp.sum(jnp.exp(z - row_top[:, None]), axis=1)
    is_label = (
        jnp.arange(tile_docs, dtype=jnp.int32)[None, :] == (labels - c * tile_docs)[:, None]
    )
    chosen = jnp.sum(jnp.where(is_label, z, 0.0), axis=1)
    own_stats = jnp.stack([row_top, row_mass, chosen])
    stats = jnp.stack([own_stats] + [shift_cols(own_stats, k) for k in range(1, C)])
    top_all = jnp.max(stats[:, 0], axis=0)
    mass_all = jnp.sum(stats[:, 1] * jnp.exp(stats[:, 0] - top_all), axis=0)
    log_total = top_all + jnp.log(mass_all)
    loss = log_total - jnp.sum(stats[:, 2], axis=0)
    dz = (jnp.exp(z - log_total[:, None]) - is_label.astype(F32)) / (queries_here * R)
    scale_part = jnp.sum(dz * z)
    dscores = (scale * dz).T.reshape(R, docs, queries_here)
    doc_grad, query_grad_t = score_backward(lows, highs, doc_tile, query_tile, picks, dscores)
    query_parts = query_grad_t.T.reshape(C, Q, 128)

    def query_part(k):
        return lax.dynamic_index_in_dim(query_parts, (c + k) % C, 0, keepdims=False)

    query_grad = query_part(0)
    for k in range(1, C):
        query_grad = query_grad + shift_cols(query_part(k), k)

    doc_sum = scatter_rows(doc_grad.reshape(R, DS, 128))
    unit_grad = jnp.concatenate([query_grad, doc_sum], axis=0)

    core = r % 2
    slots_back = range(C - 1, -1, -1)
    share = D // R
    x_bit, *z_bits = [1 << b for b in range(1, R.bit_length() - 1)]

    def side_of(bit):
        return ((r // bit) % 2).astype(jnp.int32)

    keep_places = jnp.stack([core, side_of(z_bits[0])]).astype(jnp.int32)
    send_places = jnp.stack([1 - core, 0 * core]).astype(jnp.int32)

    def halves_of(left_t):
        return left_t.reshape(R // 2, 2, share, n)

    def send_half(lefts, rights):
        return swap_rows(weight_pull(send_places, lefts, rights)[0], 1)

    def rows_of(left, side):
        return lax.dynamic_index_in_dim(left, side, 1, keepdims=False).reshape(-1, n)

    def send_plain(left, right):
        part = mm(rows_of(left, 1 - core), right).astype(BF16)
        Order.last += (part,)
        return swap_rows(part, 1)

    def keep_plain(left, right, arrived, k):
        kept = mm(rows_of(left, core), right) + arrived.astype(F32)
        if k > 0:
            kept = kept.astype(BF16)
        Order.last += (kept,)
        return kept[None] if k == 0 else shift_cols(kept, C - k)[None]

    def next_fold(states, bit, inner):
        send, keep = fold(side_of(bit), [s[0] for s in states], [s[1] for s in states], inner)
        return keep, swap_rows(send, bit)

    def close(state):
        return state[0] + state[1].astype(F32)

    def cols_state(kept):
        rest = kept[1]
        for other in kept[2:]:
            rest = rest.astype(F32) + other.astype(F32)
        return kept[0], rest

    embed_grad, resid_two_grad, branch, branch_t, head_sums = head_pull(
        unit_grad, unit, unit_inverse, wproj, normed_two, inverse_two, vectors
    )
    down_left, down_right = halves_of(branch_t), active
    pre_grads, up_sums, down_kept = [None] * C, [None] * C, [None] * C
    down_arrived = [None] * C
    for k in slots_back:
        down_arrived[k] = send_plain(down_left, down_right[k])
    for k in slots_back:
        pre_grads[k], up_sums[k] = up_pull(branch, wdown_slots[k], slopes[k])
        if k > 0:
            down_kept[k] = keep_plain(down_left, down_right[k], down_arrived[k], k)
    up_left, up_right = halves_of(hidden_t), pre_grads
    up_arrived, up_kept = [None] * C, [None] * C
    for k in slots_back:
        up_arrived[k] = send_plain(up_left, up_right[k])
    down_kept[0] = keep_plain(down_left, down_right[0], down_arrived[0], 0)
    for k in slots_back[:-1]:
        up_kept[k] = keep_plain(up_left, up_right[k], up_arrived[k], k)
    resid_one_grad, branch_one_t, hidden_sums, *attended_grads = hidden_pull(
        resid_two_grad, normed_one, inverse_one, vectors, pre_grads, wup_slots, wout_slots
    )
    up_kept[0] = keep_plain(up_left, up_right[0], up_arrived[0], 0)
    mixed_grads, mixed_sums = [None] * C, [None] * C
    late_lefts, late_state, late_arrived = [halves_of(x.T), halves_of(branch_one_t)], [None] * C, [None] * C

    def late_rights(k):
        return [mixed_grads[k], attended[k][None]]

    def gather_small():
        proj_grad = mm(embed_grad, output_low, TN).reshape(R, -1, C, width)
        def cut(values, slot_rows):
            return values.reshape(slot_rows, R, -1)

        own_order = [(c - k) % C for k in range(C)]
        canonical = jnp.stack(
            [hidden_sums[0], hidden_sums[1], hidden_sums[2], head_sums[0], head_sums[1], head_sums[2]]
        ).reshape(6, C, R, -1)
        slots_small = []
        for k in range(C):
            rows = [mixed_sums[k][j].reshape(R, -1) for j in range(3)]
            rows.append(up_sums[k][0].reshape(R, -1))
            rows += [
                lax.dynamic_index_in_dim(canonical[j], own_order[k], 0, keepdims=False)
                for j in range(6)
            ]
            own_proj_grad = lax.dynamic_index_in_dim(proj_grad, own_order[k], 2, keepdims=False)
            rows.append(own_proj_grad.reshape(R, -1))
            rows.append(jnp.broadcast_to(scale_part, (R, 1)))
            slots_small.append(jnp.concatenate(rows, axis=1))
        return jnp.stack(slots_small, axis=1)

    def pull_attention(k):
        mixed_grads[k], mixed_sums[k] = attention_backward(
            spans, qkv[k], exts[k], attended[k], rests[k], attended_grads[k], ext_k, cosine, sine,
            tile,
        )
        late_arrived[k] = send_half(late_lefts, late_rights(k))

    def keep_late(k):
        send, keep = weight_pull(
            keep_places, late_lefts, late_rights(k), late_arrived[k], inner=2 * share
        )
        late_state[k] = (keep, swap_rows(send, z_bits[0]))

    for k in slots_back[:-1]:
        pull_attention(k)
    wide_state = next_fold([cols_state(down_kept), cols_state(up_kept)], x_bit, share)
    pull_attention(0)
    for k in slots_back[:-1]:
        keep_late(k)
    wide_state = next_fold([wide_state], z_bits[0], share)
    sent = [
        shift_cols(token_pull((c + k) % C, resid_one_grad, mixed_grads, wqkv_slots, BF16), k)
        for k in range(1, C)
    ]
    keep_late(0)
    for k in slots_back[:-1]:
        late_state[k] = next_fold([late_state[k]], (z_bits + [x_bit])[1], 2 * share)
    own_tokens = token_pull(c, resid_one_grad, mixed_grads, wqkv_slots, F32)
    small = small_sum(R, C, gather_small())
    for bit in z_bits[2:] + [x_bit]:
        for k in slots_back[:-1]:
            late_state[k] = next_fold([late_state[k]], bit, share if bit == x_bit else 2 * share)
    for bit in z_bits[1:] + [x_bit]:
        late_state[0] = next_fold([late_state[0]], bit, share if bit == x_bit else 2 * share)
        if bit != x_bit:
            wide_state = next_fold([wide_state], bit, share)
    late_grad = close(late_state[0])
    for k in slots_back[:-1]:
        late_grad = late_grad + shift_cols(close(late_state[k]).astype(BF16), C - k).astype(F32)
    qkv_grad, out_grad = late_grad[:3], late_grad[3]
    down_grad, up_grad = close(wide_state)
    ordered = in_order([own_tokens] + [s.astype(F32) for s in sent])
    tokens_grad = jnp.concatenate([s[:Q] for s in ordered] + [s[Q:] for s in ordered], axis=0)
    one = D // (C * R)
    up_part = bup_slots[0].shape[1] // R
    bounds = [3 * one, 3 * one + up_part]
    for _ in range(6):
        bounds.append(bounds[-1] + one)
    pieces = [small[a:b] for a, b in zip(bounds[:-1], bounds[1:])]
    bup_out, bout_out, gain1_out, bias1_out, bdown_out, gain2_out, bias2_out = pieces
    return (
        scores,
        loss,
        tokens_grad,
        qkv_grad,
        small[: bounds[0]].reshape(3, one),
        out_grad.T,
        bout_out,
        gain1_out,
        bias1_out,
        up_grad,
        bup_out,
        down_grad.T,
        bdown_out,
        gain2_out,
        bias2_out,
        small[bounds[-1] : -1].reshape(-1, width).T,
        small[-1:],
    )


def solution(mesh):
    in_specs = (
        P("rows", "cols"),
        P(),
        P("rows", "cols", None),
        P("rows"),
        P(None, None, "cols"),
        P(None, "cols"),
        P("cols", None),
        P("cols"),
        P("cols"),
        P("cols"),
        P(None, "cols"),
        P("cols"),
        P("cols", None),
        P("cols"),
        P("cols"),
        P("cols"),
        P("cols", None),
        P(),
    )
    out_specs = (
        P("rows", "cols"),
        P("rows"),
        P("rows", "cols"),
        P(None, "rows", "cols"),
        P(None, ("cols", "rows")),
        P("cols", "rows"),
        P(("cols", "rows")),
        P(("cols", "rows")),
        P(("cols", "rows")),
        P("rows", "cols"),
        P(("cols", "rows")),
        P("cols", "rows"),
        P(("cols", "rows")),
        P(("cols", "rows")),
        P(("cols", "rows")),
        P("cols", "rows"),
        P(),
    )
    return jax.shard_map(
        on_device, mesh=mesh, in_specs=in_specs, out_specs=out_specs, check_vma=False
    )
```

```python
import functools
import math

import jax
import jax.numpy as jnp
from jax import lax
from jax.experimental import pallas as pl
from jax.experimental.pallas import tpu as pltpu
from jax.sharding import PartitionSpec as P

DH = 64
QLEN = 32
ROW_LEN = 1024
F32 = jnp.float32
BF16 = jnp.bfloat16
VMEM_LIMIT = 56 * 1024 * 1024
NT = (((1,), (1,)), ((), ()))
NN = (((1,), (0,)), ((), ()))
TN = (((0,), (0,)), ((), ()))


def mm(left, right, dims=NN):
    return lax.dot_general(left, right, dims, preferred_element_type=F32)


def row_step(rows):
    return 512 if rows % 512 == 0 else 128


def parts_of(step):
    size = min(step, 256)
    return [slice(first, first + size) for first in range(0, step, size)]


def held(shape):
    return pl.BlockSpec(shape, lambda *_: (0,) * len(shape), pipeline_mode=pl.Buffered(1))


def shaped(dtype, *shape):
    return jax.ShapeDtypeStruct(shape, dtype)


class Order:
    last = ()


def call(
    body, name, grid, in_specs, out_specs, out_shape, operands, flops, scratch=(), prefetch=0, after=(),
    remote=None,
):
    count = len(operands)
    after = tuple(after) + Order.last

    def wrapped(*refs):
        body(*refs[:count], *refs[count + len(after) :])

    size = sum(math.prod(o.shape) * o.dtype.itemsize for o in list(operands) + list(out_shape))
    if flops == 0:
        size = 1024
    outs = pl.pallas_call(
        wrapped,
        grid_spec=pltpu.PrefetchScalarGridSpec(
            num_scalar_prefetch=prefetch,
            grid=grid,
            in_specs=list(in_specs) + [pl.BlockSpec(memory_space=pl.ANY)] * len(after),
            out_specs=out_specs,
            scratch_shapes=list(scratch),
        ),
        out_shape=out_shape,
        compiler_params=pltpu.CompilerParams(
            vmem_limit_bytes=VMEM_LIMIT, collective_id=remote, has_side_effects=remote is not None
        ),
        cost_estimate=pl.CostEstimate(flops=flops, bytes_accessed=size, transcendentals=0),
        name=name,
    )(*operands, *after)
    Order.last = (min(outs, key=lambda out: out.size * out.dtype.itemsize),)
    return outs


def row_spec(step, width):
    return pl.BlockSpec((step, width), lambda i, *_: (i, 0))


def by_core(block, paired):
    if not paired:
        return block
    firsts, seconds = [], []
    for at in range(0, block.shape[1], 256):
        one, two = block[:, at : at + 128], block[:, at + 128 : at + 256]
        low = lax.broadcasted_iota(jnp.int32, one.shape, 1) < 64
        firsts.append(jnp.where(low, one, pltpu.roll(two, 64, 1)))
        seconds.append(jnp.where(low, pltpu.roll(one, 64, 1), two))
    return jnp.concatenate(firsts + seconds, axis=1)


MESH = pl.DeviceIdType.MESH
ANYWHERE = pl.BlockSpec(memory_space=pl.ANY)


def side_at(row, bit):
    return (row // bit) % 2


def across(row, bit):
    return row + bit * (1 - 2 * side_at(row, bit))


def flipped(row, bits):
    bit = 1
    while bit <= bits:
        if bits & bit:
            row = across(row, bit)
        bit *= 2
    return row


def greet(devices):
    barrier = pltpu.get_barrier_semaphore()
    for device in devices:
        pl.semaphore_signal(barrier, inc=1, device_id=device, device_id_type=MESH)
    pl.semaphore_wait(barrier, len(devices))


def send(source, target, sent, arrived, device):
    copy = pltpu.make_async_remote_copy(
        src_ref=source,
        dst_ref=target,
        send_sem=sent,
        recv_sem=arrived,
        device_id=device,
        device_id_type=MESH,
    )
    copy.start()
    return copy


def spread_order(count):
    pieces = sorted(range(count), key=lambda piece: (piece.bit_count(), -piece))
    order = []
    for piece in pieces:
        lowest = piece & -piece if piece else count
        bit = lowest // 2
        bits = []
        while bit:
            bits.append(bit)
            bit //= 2
        order.append((piece, bits))
    return order


def start_kernel(rows, cols_width, parts, *refs):
    (tokens, qkv, out, up, down, proj, pack), refs = refs[:7], refs[7:]
    (x, qkv_o, out_o, up_o, down_o, proj_o, pack_o), refs = refs[:7], refs[7:]
    own_sem, sent, arrived, wide_sent, wide_arrived = refs
    r, c = lax.axis_index("rows"), lax.axis_index("cols")
    partner = {"cols": 1 - c}
    bits = [1 << b for b in range(rows.bit_length() - 1)]
    greet([partner] + [{"rows": across(r, bit)} for bit in bits])
    wide = [(qkv, qkv_o)]
    copies, first = [], []
    for place, (source, target) in enumerate(wide):
        first.append(
            send(source.at[r], target.at[r], sent.at[place], arrived.at[place], partner)
        )
    q_rows, d_rows, first_doc = parts
    own = pl.ds(pl.multiple_of(c * cols_width, cols_width), cols_width)
    spans = [(0, q_rows, 0), (first_doc, d_rows, q_rows)]
    for place, (base, size, here) in enumerate(spans):
        theirs = pl.ds(pl.multiple_of(base + (1 - c) * size, size), size)
        mine = pl.ds(pl.multiple_of(base + c * size, size), size)
        target = x.at[pl.ds(here, size), own]
        copies.append(
            send(tokens.at[theirs], target, sent.at[3 + place], arrived.at[3 + place], partner)
        )
        pltpu.make_async_copy(tokens.at[mine], target, own_sem.at[place]).start()
    narrow = [(proj, proj_o), (pack, pack_o), (out.at[r], out_o), (up.at[r], up_o), (down.at[r], down_o)]
    for place, (source, target) in enumerate(narrow):
        copies.append(
            send(source, target, sent.at[5 + place], arrived.at[5 + place], partner)
        )
    wide_copies = {}
    for piece, over in spread_order(rows):
        row = flipped(r, piece)
        for place, (_, target) in enumerate(wide):
            if piece == 0:
                first[place].wait_recv()
            else:
                wide_copies[place, piece].wait_recv()
            for bit in over:
                wide_copies[place, piece | bit] = send(
                    target.at[row], target.at[row],
                    wide_sent.at[place, piece | bit], wide_arrived.at[place, piece | bit],
                    {"rows": across(r, bit)},
                )
    for copy in first + list(wide_copies.values()):
        copy.wait_send()
    for copy in copies:
        copy.wait()
    for place, (base, size, here) in enumerate(spans):
        mine = pl.ds(pl.multiple_of(base + c * size, size), size)
        target = x.at[pl.ds(here, size), own]
        pltpu.make_async_copy(tokens.at[mine], target, own_sem.at[place]).wait()


def start_up(rows, parts, tokens, qkv, out, up, down, proj, pack):
    width = tokens.shape[1]

    def pieces(array):
        return array.reshape(rows, -1, array.shape[-1])

    weights = [pieces(array) for array in (qkv, out, up, down)]
    qkv_p, out_p, up_p, down_p = weights
    operands = (tokens, *weights, proj, pack)
    n = parts[0] + parts[1]
    x, qkv_o, out_o, up_o, down_o, proj_o, pack_o = call(
        functools.partial(start_kernel, rows, width, parts), "start_up", (1,),
        [ANYWHERE] * 7, [ANYWHERE] * 7,
        [
            shaped(BF16, n, 2 * width), shaped(BF16, *qkv_p.shape), shaped(BF16, *out_p.shape[1:]),
            shaped(BF16, *up_p.shape[1:]), shaped(BF16, *down_p.shape[1:]),
            shaped(BF16, *proj.shape), shaped(F32, *pack.shape),
        ],
        operands, 0, remote=1,
        scratch=[
            pltpu.SemaphoreType.DMA((2,)), pltpu.SemaphoreType.DMA((10,)),
            pltpu.SemaphoreType.DMA((10,)), pltpu.SemaphoreType.DMA((1, rows)),
            pltpu.SemaphoreType.DMA((1, rows)),
        ],
    )
    return x, qkv_o.reshape(qkv.shape), out_o, up_o, down_o, proj_o, pack_o


def gather_kernel(rows, own, out, own_sem, sent, arrived):
    r = lax.axis_index("rows")
    bits = [1 << b for b in range(rows.bit_length() - 1)]
    greet([{"rows": across(r, bit)} for bit in bits])
    local = pltpu.make_async_copy(own, out.at[r], own_sem)
    local.start()
    copies = {}
    for piece, over in spread_order(rows):
        row = flipped(r, piece)
        if piece:
            copies[piece].wait_recv()
        for bit in over:
            copies[piece | bit] = send(
                out.at[row] if piece else own, out.at[row],
                sent.at[piece | bit], arrived.at[piece | bit], {"rows": across(r, bit)},
            )
    for copy in copies.values():
        copy.wait_send()
    local.wait()


def gather_rows(rows, own):
    return call(
        functools.partial(gather_kernel, rows), "gather_rows", (1,), [ANYWHERE], [ANYWHERE],
        [shaped(own.dtype, rows, *own.shape)], (own,), 0, remote=2,
        scratch=[
            pltpu.SemaphoreType.DMA, pltpu.SemaphoreType.DMA((rows,)),
            pltpu.SemaphoreType.DMA((rows,)),
        ],
    )[0]


def scatter_kernel(rows, parts, out, sent, arrived, *buffers):
    r = lax.axis_index("rows")
    bits = [1 << b for b in range(rows.bit_length() - 1)]
    greet([{"rows": across(r, bit)} for bit in bits])
    outgoing, incoming = buffers[: len(bits)], buffers[len(bits) :]
    copies = {}

    def total(flips, levels):
        row = flipped(r, flips)
        value = parts[row]
        for level in range(levels):
            copies[level, flips >> (level + 1)].wait_recv()
            value = value + incoming[level][row // (2 << level)].astype(F32)
        return value

    for level, bit in enumerate(bits):
        count = rows // (2 << level)
        for turn in sorted(range(count), key=lambda f: tuple(-((f >> b) & 1) for b in range(8))):
            flips = (turn << (level + 1)) | bit
            place = flipped(r, flips) // (2 << level)
            outgoing[level][place] = total(flips, level).astype(BF16)
            copies[level, turn] = send(
                outgoing[level].at[place], incoming[level].at[place],
                sent.at[rows - 2 * count + turn], arrived.at[rows - 2 * count + turn],
                {"rows": across(r, bit)},
            )
    out[...] = total(0, len(bits))
    for copy in copies.values():
        copy.wait_send()


def scatter_rows(parts):
    rows, height, width = parts.shape
    levels = rows.bit_length() - 1
    buffers = [
        pltpu.VMEM((rows // (2 << level), height, width), BF16) for level in range(levels)
    ]
    return call(
        functools.partial(scatter_kernel, rows), "scatter_rows", (1,), [held(parts.shape)],
        [pl.BlockSpec((height, width), lambda *_: (0, 0))], [shaped(F32, height, width)],
        (parts,), 0, remote=3,
        scratch=[pltpu.SemaphoreType.DMA((rows,)), pltpu.SemaphoreType.DMA((rows,))]
        + buffers + buffers,
    )[0]


def small_kernel(rows, cols, parts, out, *refs):
    bits = [1 << b for b in range(rows.bit_length() - 1)]
    sent, arrived = refs[:2]
    core_in, cols_in, totals, row_ins = refs[2], refs[3], refs[4 : 4 + len(bits)], refs[4 + len(bits) :]
    r, c = lax.axis_index("rows"), lax.axis_index("cols")
    others = [{"cols": (c + cols - k) % cols} for k in range(1, cols)]
    greet([{"rows": across(r, bit)} for bit in bits] + others)
    core = side_at(r, 1)
    copy = send(parts.at[:, 1 - core], core_in, sent.at[0], arrived.at[0], {"rows": across(r, 1)})
    copy.wait()
    sums = parts[:, core] + core_in[...]
    cols_out = totals[0]
    cols_out[...] = sums
    copies = [
        send(cols_out.at[:, k], cols_in.at[k - 1], sent.at[k], arrived.at[k], others[k - 1])
        for k in range(1, cols)
    ]
    total = sums[:, 0]
    for k, copy in enumerate(copies):
        copy.wait()
        total = total + cols_in[k]
    for level, bit in enumerate(bits[1:]):
        held_total, arriving = totals[1 + level], row_ins[level]
        held_total[...] = total.reshape(held_total.shape)
        side = side_at(r, bit)
        copy = send(
            held_total.at[:, 1 - side], arriving, sent.at[cols + level], arrived.at[cols + level],
            {"rows": across(r, bit)},
        )
        copy.wait()
        total = held_total[:, side] + arriving[...]
    out[...] = total[0]


def small_sum(rows, cols, parts):
    length = parts.shape[2]
    width = -(-length // 1024) * 128
    parts = jnp.pad(parts, ((0, 0), (0, 0), (0, 8 * width - length)))
    parts = parts.reshape(rows // 2, 2, cols, 8, width)
    levels = rows.bit_length() - 1
    sizes = [rows >> (level + 1) for level in range(1, levels)]
    scratch = [
        pltpu.SemaphoreType.DMA((cols + levels,)), pltpu.SemaphoreType.DMA((cols + levels,)),
        pltpu.VMEM((rows // 2, cols, 8, width), F32),
        pltpu.VMEM((cols - 1, rows // 2, 8, width), F32),
        pltpu.VMEM((rows // 2, cols, 8, width), F32),
    ]
    scratch += [pltpu.VMEM((size, 2, 8, width), F32) for size in sizes]
    scratch += [pltpu.VMEM((size, 8, width), F32) for size in sizes]
    total = call(
        functools.partial(small_kernel, rows, cols), "small_sum", (1,), [held(parts.shape)],
        [pl.BlockSpec((8, width), lambda *_: (0, 0))], [shaped(F32, 8, width)], (parts,), 0,
        remote=4, scratch=scratch,
    )[0]
    return total.reshape(-1)[:length]


def swap_halves(block):
    lane = lax.broadcasted_iota(jnp.int32, block.shape, 1)
    return jnp.where((lane & 32) == 0, pltpu.roll(block, 96, 1), pltpu.roll(block, 32, 1))


def qkv_kernel(x_ref, w_ref, b_ref, cos_ref, sin_ref, out_ref):
    which = pl.program_id(0)
    bias = b_ref[pl.ds(which, 1), :]

    @pl.when(which < 2)
    def _():
        for at in parts_of(x_ref.shape[0]):
            mixed = mm(x_ref[at, :], w_ref[0]) + bias
            for first in range(0, mixed.shape[1], 128):
                block = mixed[:, first : first + 128]
                turned = block * cos_ref[at, :] + swap_halves(block) * sin_ref[at, :]
                out_ref[0, at, first : first + 128] = turned.astype(BF16)

    @pl.when(which == 2)
    def _():
        for at in parts_of(x_ref.shape[0]):
            out_ref[0, at, :] = (mm(x_ref[at, :], w_ref[0]) + bias).astype(BF16)


def project_qkv(x, weight, bias, cosine, sine, after=()):
    n, D = x.shape
    width = weight.shape[2]
    step = row_step(n)
    return call(
        qkv_kernel, "project_qkv", (3, n // step),
        [
            pl.BlockSpec((step, D), lambda j, i: (i, 0)),
            pl.BlockSpec((1, D, width), lambda j, i: (j, 0, 0)),
            held(bias.shape),
            pl.BlockSpec((step, 128), lambda j, i: (i, 0)),
            pl.BlockSpec((step, 128), lambda j, i: (i, 0)),
        ],
        [pl.BlockSpec((1, step, width), lambda j, i: (j, i, 0))],
        [shaped(BF16, 3, n, width)],
        (x, weight, bias, cosine, sine), 6 * n * D * width, after=after,
    )[0]


def normed_rows(residual):
    mean = jnp.mean(residual, axis=1, keepdims=True)
    centred = residual - mean
    inverse = lax.rsqrt(jnp.mean(centred * centred, axis=1, keepdims=True) + 1e-05)
    return centred * inverse, inverse


def norm_pull(grad_rows, normed, inverse, gain):
    spread = grad_rows * gain
    return inverse * (
        spread
        - jnp.mean(spread, axis=1, keepdims=True)
        - normed * jnp.mean(spread * normed, axis=1, keepdims=True)
    )


def column_sums(*arrays):
    rows = [jnp.sum(array, axis=0, keepdims=True) for array in arrays]
    rows.append(jnp.zeros((8 - len(rows), rows[0].shape[1]), F32))
    return jnp.concatenate(rows, axis=0)


def add_over_steps(ref, value):
    first = pl.program_id(0) == 0

    @pl.when(first)
    def _():
        ref[...] = value

    @pl.when(jnp.logical_not(first))
    def _():
        ref[...] += value


def out_norm_kernel(slots, paired, *refs):
    x_ref, vec_ref = refs[:2]
    att_refs, w_refs = refs[2 : 2 + slots], refs[2 + slots : 2 + 2 * slots]
    normed_ref, inverse_ref, low_ref, turned_ref = refs[2 + 2 * slots :]
    for at in parts_of(x_ref.shape[0]):
        residual = x_ref[at, :].astype(F32) + vec_ref[0:1, :]
        for att_ref, w_ref in zip(att_refs, w_refs):
            residual = residual + mm(att_ref[at, :], w_ref[...])
        normed, inverse = normed_rows(residual)
        hidden = normed * vec_ref[1:2, :] + vec_ref[2:3, :]
        normed_ref[at, :] = normed
        inverse_ref[at, :] = inverse
        low_ref[at, :] = hidden.astype(BF16)
        turned_ref[at, :] = by_core(hidden, paired).astype(BF16)


def out_and_norm(x, vectors, attended, weights, paired):
    n, D = x.shape
    step = row_step(n)
    slots = len(attended)
    width = attended[0].shape[1]
    return call(
        functools.partial(out_norm_kernel, slots, paired), "out_and_norm", (n // step,),
        [row_spec(step, D), held(vectors.shape)]
        + [row_spec(step, width)] * slots + [held((width, D))] * slots,
        [row_spec(step, D), row_spec(step, 1), row_spec(step, D), row_spec(step, D)],
        [shaped(F32, n, D), shaped(F32, n, 1), shaped(BF16, n, D), shaped(BF16, n, D)],
        (x, vectors, *attended, *weights), 2 * n * D * D,
    )


GELU_TERMS = (
    0.23532527933595032, 0.09138803439798156, 0.6495603483388861,
    -0.6354014529895687, 0.8866650885491606, -0.22753729931242958,
)


def gelu_parts(values):
    size = jnp.abs(values)
    part = pl.reciprocal(1.0 + (0.39 / math.sqrt(2.0)) * size)
    bell = jnp.exp(-0.5 * (values * values))
    series = 0.5 * GELU_TERMS[-1]
    for term in GELU_TERMS[-2::-1]:
        series = series * part + 0.5 * term
    tail = series * part * bell
    below = jnp.where(values >= 0.0, 1.0 - tail, tail)
    return values * below, below + values * bell * (1.0 / math.sqrt(2.0 * math.pi))


def up_kernel(x_ref, w_ref, b_ref, active_ref, slope_ref):
    width = w_ref.shape[1]
    chunk = min(256, width)
    for first in range(0, width, chunk):
        at = slice(first, first + chunk)
        active, slope = gelu_parts(mm(x_ref[...], w_ref[:, at]) + b_ref[:, at])
        active_ref[:, at] = active.astype(BF16)
        slope_ref[:, at] = slope


def up_and_gelu(x, weight, bias):
    n, D = x.shape
    width = weight.shape[1]
    step = row_step(n)
    return call(
        up_kernel, "up_and_gelu", (n // step,),
        [row_spec(step, D), held(weight.shape), held(bias.shape)],
        [row_spec(step, width)] * 2,
        [shaped(BF16, n, width), shaped(F32, n, width)],
        (x, weight, bias), 5 * n * D * width,
    )


def down_norm_kernel(slots, *refs):
    normed_ref, vec_ref, proj_ref = refs[:3]
    act_refs, w_refs = refs[3 : 3 + slots], refs[3 + slots : 3 + 2 * slots]
    normed_out, inverse_ref, low_ref, unit_ref, unit_low_ref, unit_inverse_ref = refs[3 + 2 * slots :]
    for at in parts_of(normed_ref.shape[0]):
        residual = normed_ref[at, :] * vec_ref[1:2, :] + vec_ref[2:3, :] + vec_ref[3:4, :]
        for act_ref, w_ref in zip(act_refs, w_refs):
            residual = residual + mm(act_ref[at, :], w_ref[...])
        normed, inverse = normed_rows(residual)
        normed_out[at, :] = normed
        inverse_ref[at, :] = inverse
        low = (normed * vec_ref[4:5, :] + vec_ref[5:6, :]).astype(BF16)
        low_ref[at, :] = low
        embedding = mm(low, proj_ref[...])
        unit_inverse = lax.rsqrt(jnp.sum(embedding * embedding, axis=1, keepdims=True) + 1e-06)
        unit = embedding * unit_inverse
        unit_ref[at, :] = unit
        unit_low_ref[at, :] = unit.astype(BF16)
        unit_inverse_ref[at, :] = unit_inverse


def down_and_norm(normed, vectors, proj, active, weights):
    n, D = normed.shape
    step = row_step(n)
    slots = len(active)
    width = active[0].shape[1]
    return call(
        functools.partial(down_norm_kernel, slots), "down_and_norm", (n // step,),
        [row_spec(step, D), held(vectors.shape), held(proj.shape)]
        + [row_spec(step, width)] * slots + [held((width, D))] * slots,
        [
            row_spec(step, D), row_spec(step, 1), row_spec(step, D),
            row_spec(step, 128), row_spec(step, 128), row_spec(step, 1),
        ],
        [
            shaped(F32, n, D), shaped(F32, n, 1), shaped(BF16, n, D),
            shaped(F32, n, 128), shaped(BF16, n, 128), shaped(F32, n, 1),
        ],
        (normed, vectors, proj, *active, *weights), 2 * n * D * width * slots,
    )


def head_pull_kernel(
    paired, grad_ref, unit_ref, unit_inverse_ref, proj_ref, normed_ref, inverse_ref, vec_ref,
    embed_ref, residual_ref, low_ref, turned_ref, sum_ref,
):
    sums = []
    for at in parts_of(grad_ref.shape[0]):
        grad, unit = grad_ref[at, :], unit_ref[at, :]
        embed = grad - unit * jnp.sum(grad * unit, axis=1, keepdims=True)
        embed = (unit_inverse_ref[at, :] * embed).astype(BF16)
        embed_ref[at, :] = embed
        output_grad = mm(embed, proj_ref[...], NT)
        normed = normed_ref[at, :]
        residual = norm_pull(output_grad, normed, inverse_ref[at, :], vec_ref[4:5, :])
        residual_ref[at, :] = residual
        low_ref[at, :] = residual.astype(BF16)
        turned_ref[at, :] = by_core(residual, paired).astype(BF16)
        sums.append(column_sums(residual, output_grad * normed, output_grad))
    add_over_steps(sum_ref, sum(sums))


def head_pull(unit_grad, unit, unit_inverse, proj, normed, inverse, vectors, paired):
    n, D = normed.shape
    step = row_step(n)
    return call(
        functools.partial(head_pull_kernel, paired), "head_pull", (n // step,),
        [
            row_spec(step, 128), row_spec(step, 128), row_spec(step, 1), held(proj.shape),
            row_spec(step, D), row_spec(step, 1), held(vectors.shape),
        ],
        [
            row_spec(step, 128), row_spec(step, D), row_spec(step, D),
            row_spec(step, D), pl.BlockSpec((8, D), lambda i: (0, 0)),
        ],
        [
            shaped(BF16, n, 128), shaped(F32, n, D), shaped(BF16, n, D),
            shaped(BF16, n, D), shaped(F32, 8, D),
        ],
        (unit_grad, unit, unit_inverse, proj, normed, inverse, vectors), 4 * n * D * 128,
    )


def up_pull_kernel(branch_ref, w_ref, slope_ref, out_ref, sum_ref):
    width = w_ref.shape[0]
    chunk = min(512, width)
    sums = []
    for first in range(0, width, chunk):
        at = slice(first, first + chunk)
        low = (mm(branch_ref[...], w_ref[at, :], NT) * slope_ref[:, at]).astype(BF16)
        out_ref[:, at] = low
        sums.append(column_sums(low.astype(F32)))
    add_over_steps(sum_ref, jnp.concatenate(sums, axis=1))


def up_pull(branch, weight, slope):
    n, D = branch.shape
    width = weight.shape[0]
    step = row_step(n)
    return call(
        up_pull_kernel, "up_pull", (n // step,),
        [row_spec(step, D), held(weight.shape), row_spec(step, width)],
        [row_spec(step, width), pl.BlockSpec((8, width), lambda i: (0, 0))],
        [shaped(BF16, n, width), shaped(F32, 8, width)],
        (branch, weight, slope), 2 * n * D * width,
    )


def hidden_pull_kernel(slots, paired, *refs):
    residual_ref, normed_ref, inverse_ref, vec_ref = refs[:4]
    pre_refs, up_refs, out_refs = (refs[4 + j * slots : 4 + (j + 1) * slots] for j in range(3))
    rest = refs[4 + 3 * slots :]
    grad_ref, turned_ref, sum_ref = rest[:3]
    att_refs = rest[3:]
    sums = []
    for at in parts_of(residual_ref.shape[0]):
        hidden_grad = residual_ref[at, :]
        for pre_ref, up_ref in zip(pre_refs, up_refs):
            hidden_grad = hidden_grad + mm(pre_ref[at, :], up_ref[...], NT)
        normed = normed_ref[at, :]
        residual = norm_pull(hidden_grad, normed, inverse_ref[at, :], vec_ref[1:2, :])
        grad_ref[at, :] = residual
        low = residual.astype(BF16)
        turned_ref[at, :] = by_core(residual, paired).astype(BF16)
        sums.append(column_sums(residual, hidden_grad * normed, hidden_grad))
        for att_ref, out_ref in zip(att_refs, out_refs):
            att_ref[at, :] = mm(low, out_ref[...], NT).astype(BF16)
    add_over_steps(sum_ref, sum(sums))


def hidden_pull(residual, normed, inverse, vectors, pre_grads, ups, outs, paired):
    n, D = residual.shape
    step = row_step(n)
    slots = len(ups)
    wide, width = ups[0].shape[1], outs[0].shape[0]
    return call(
        functools.partial(hidden_pull_kernel, slots, paired), "hidden_pull", (n // step,),
        [row_spec(step, D), row_spec(step, D), row_spec(step, 1), held(vectors.shape)]
        + [row_spec(step, wide)] * slots + [held((D, wide))] * slots
        + [held((width, D))] * slots,
        [row_spec(step, D), row_spec(step, D), pl.BlockSpec((8, D), lambda i: (0, 0))]
        + [row_spec(step, width)] * slots,
        [shaped(F32, n, D), shaped(BF16, n, D), shaped(F32, 8, D)]
        + [shaped(BF16, n, width)] * slots,
        (residual, normed, inverse, vectors, *pre_grads, *ups, *outs),
        0,
    )


def token_pull_kernel(slots, span, place_ref, *refs):
    residual_ref = refs[0]
    mixed_refs, w_refs = refs[1 : 1 + slots], refs[1 + slots : 1 + 2 * slots]
    out_ref = refs[-1]
    width = out_ref.shape[1]
    at = pl.ds(pl.multiple_of(place_ref[0] * width, width), width)
    total = residual_ref[...]
    for mixed_ref, w_ref in zip(mixed_refs, w_refs):
        for first in range(0, width, span):
            for which in range(3):
                start = 4 * first + which * span
                mixed = mixed_ref[:, start : start + span]
                total = total + mm(mixed, w_ref[which, at, first : first + span], NT)
    out_ref[...] = total.astype(out_ref.dtype)


def token_pull(place, residual, mixed_grads, weights, dtype):
    n, D = residual.shape
    step = row_step(n)
    slots = len(weights)
    width = weights[0].shape[2]
    return call(
        functools.partial(token_pull_kernel, slots, min(width, ATTENTION_LANES)), "token_pull", (n // step,),
        [pl.BlockSpec((step, width), lambda i, p: (i, p[0]))]
        + [row_spec(step, 4 * width)] * slots
        + [held((3, D, width))] * slots,
        [row_spec(step, width)],
        [shaped(dtype, n, width)],
        (place.reshape(1), residual, *mixed_grads, *weights), 6 * n * D * width, prefetch=1,
    )[0]


def put_halves(total, inner, side, refs):
    pairs = total.reshape(-1, 2, inner, total.shape[1])
    keep = jnp.where(side == 0, pairs[:, 0], pairs[:, 1]).reshape(-1, total.shape[1])
    send = jnp.where(side == 0, pairs[:, 1], pairs[:, 0]).reshape(-1, total.shape[1])
    refs[0][0] = send.astype(BF16)
    refs[1][0] = keep


def grouped_index(starts, place, count):
    def index(j, i, *_):
        inside = (j >= starts[place]) & (j < starts[place + 1])
        row = jnp.clip(j - starts[place], 0, starts[place + 1] - starts[place] - 1)
        rest = jnp.where(j < starts[place], 0, count - 1)
        return row, 0, jnp.where(inside, i, rest)

    return index


def for_group(starts, body):
    if len(starts) == 2:
        body(0)
        return
    for place in range(len(starts) - 1):

        @pl.when((pl.program_id(0) >= starts[place]) & (pl.program_id(0) < starts[place + 1]))
        def _(place=place):
            body(place)


def fold_kernel(starts, inner, place_ref, *refs):
    groups = len(starts) - 1

    def one_group(place):
        total = refs[place][0] + refs[groups + place][0].astype(F32)
        put_halves(total, inner, place_ref[0], refs[2 * groups :])

    for_group(starts, one_group)


def fold(side, owns, arrived, inner):
    _, rows, m = owns[0].shape
    chunk = min(1024, m)
    starts = [0]
    for own in owns:
        starts.append(starts[-1] + own.shape[0])

    def spec(size):
        return pl.BlockSpec((1, size, chunk), lambda j, i, p: (j, 0, i))

    half = rows // 2
    specs = [
        pl.BlockSpec((1, rows, chunk), grouped_index(starts, place, m // chunk))
        for place in range(len(owns))
    ]
    return call(
        functools.partial(fold_kernel, starts, inner), "fold", (starts[-1], m // chunk),
        specs + specs, [spec(half), spec(half)],
        [shaped(BF16, starts[-1], half, m), shaped(F32, starts[-1], half, m)],
        (side.reshape(1), *owns, *arrived), 0, prefetch=1,
    )


SEGMENTS = 8
ATTENTION_LANES = 256


def half_lanes(block, head, other):
    lane = lax.broadcasted_iota(jnp.int32, block.shape, 1)
    return jnp.where((lane >= DH) == (head == 1), block, other)


def scaled(block):
    return (block.astype(F32) * DH**-0.5).astype(BF16)


def three_terms(value):
    high = value.astype(BF16).astype(F32)
    middle = (value - high).astype(BF16).astype(F32)
    return high, middle, value - high - middle


def for_spans(span_ref, tiles, body):
    @pl.loop(0, tiles)
    def _(step):
        low, high = span_ref[step], span_ref[tiles + step]
        for count in range(1, tiles + 1):

            @pl.when(high - low == count)
            def _(count=count):
                body(step, low, count)


def attention_forward_kernel(
    span_ref, qkv_ref, ext_k_ref, ext_q_ref, out_ref, rest_ref, ext_ref,
    keys_ref, queries_ref, *, tile,
):
    n = ext_k_ref.shape[0]
    tiles = n // tile
    pairs = qkv_ref.shape[2] // 128

    def lanes(pair):
        return slice(pair * 128, pair * 128 + 128)

    for pair in range(pairs):
        query = scaled(qkv_ref[0, :, lanes(pair)])
        for half in range(2):
            keys_ref[2 * pair + half] = half_lanes(qkv_ref[1, :, lanes(pair)], half, ext_k_ref[...])
            queries_ref[2 * pair + half] = half_lanes(query, half, ext_q_ref[...])

    def attend(step, low, count):
        rows = pl.ds(pl.multiple_of(step * tile, tile), tile)
        window = pl.ds(pl.multiple_of(low * tile, tile), count * tile)
        lane = lax.broadcasted_iota(jnp.int32, (tile, 128), 1)
        for pair in range(pairs):
            at = lanes(pair)
            outs, extra = [], ext_q_ref[rows, :].astype(F32)
            for half in range(2):
                head = 2 * pair + half
                logits = mm(queries_ref[head, rows, :], keys_ref[head, window, :], NT)
                top = jnp.max(logits, axis=1, keepdims=True)
                weights = jnp.exp(logits - top)
                mass = jnp.sum(weights, axis=1, keepdims=True)
                probs = (weights * (1.0 / mass)).astype(BF16)
                outs.append(mm(probs, qkv_ref[2, window, at]))
                first = SEGMENTS + DH * (1 - half)
                for place, term in enumerate(three_terms(-(top + jnp.log(mass)))):
                    extra = jnp.where(lane == first + place, term, extra)
            out = jnp.where(lane < DH, outs[0], outs[1])
            out_ref[rows, at] = out.astype(BF16)
            rest_ref[rows, at] = (out - out.astype(BF16).astype(F32)).astype(BF16)
            ext_ref[rows, at] = extra.astype(BF16)

    for_spans(span_ref, tiles, attend)


def attention_forward(spans, qkv, ext_k, ext_q, tile):
    _, n, width = qkv.shape
    span = min(width, ATTENTION_LANES)
    wide = pl.BlockSpec((n, span), lambda i, *_: (0, i))
    heads = pltpu.VMEM((span // DH, n, 128), BF16)
    return call(
        functools.partial(attention_forward_kernel, tile=tile), "attention_forward",
        (width // span,),
        [pl.BlockSpec((3, n, span), lambda i, *_: (0, 0, i)), held((n, 128)), held((n, 128))],
        [wide, wide, wide],
        [shaped(BF16, n, width)] * 3,
        (spans, qkv, ext_k, ext_q), 0, prefetch=1, scratch=[heads, heads],
    )


def attention_backward_kernel(
    span_ref, qkv_ref, ext_ref, att_ref, rest_ref, grad_ref, ext_k_ref, cos_ref, sin_ref,
    out_ref, sum_ref,
    keys_ref, turned_ref, values_ref, queries_ref, plain_ref, grads_ref, plain_grads_ref,
    dq_ref, dk_ref, dv_ref, *, tile,
):
    n = ext_k_ref.shape[0]
    tiles = n // tile
    pairs = qkv_ref.shape[2] // 128
    heads = range(2 * pairs)

    def lanes(head):
        return slice(head // 2 * 128, head // 2 * 128 + 128)

    def own_rows(head):
        return slice(head % 2 * DH, head % 2 * DH + DH)

    def rows(step):
        return pl.ds(pl.multiple_of(step * tile, tile), tile)

    @pl.loop(0, tiles)
    def _(step):
        at = rows(step)
        zeros = jnp.zeros((tile, 128), BF16)
        lane = lax.broadcasted_iota(jnp.int32, (tile, 128), 1)
        ext_k = ext_k_ref[at, :]
        for pair in range(pairs):
            cut = lanes(2 * pair)
            grad = grad_ref[at, cut]
            out = att_ref[at, cut].astype(F32) + rest_ref[at, cut].astype(F32)
            product = grad.astype(F32) * out
            query = scaled(qkv_ref[0, at, cut])
            turned_ref[pair, :, at] = scaled(qkv_ref[1, at, cut]).astype(F32).T.astype(BF16)
            for half in range(2):
                head = 2 * pair + half
                keys_ref[head, at, :] = half_lanes(qkv_ref[1, at, cut], half, ext_k)
                values_ref[head, at, :] = half_lanes(qkv_ref[2, at, cut], half, ext_k)
                queries_ref[head, at, :] = half_lanes(query, half, ext_ref[at, cut])
                plain_ref[head, at, :] = half_lanes(query, half, zeros)
                plain_grads_ref[head, at, :] = half_lanes(grad, half, zeros)
                inner = jnp.sum(half_lanes(product, half, 0.0), axis=1, keepdims=True)
                extra = jnp.zeros((tile, 128), F32)
                for place, term in enumerate(three_terms(-inner)):
                    extra = jnp.where((lane & (DH - 1)) == SEGMENTS + place, term, extra)
                grads_ref[head, at, :] = half_lanes(grad, half, extra.astype(BF16))

    dk_ref[...] = jnp.zeros(dk_ref.shape, F32)
    dv_ref[...] = jnp.zeros(dv_ref.shape, F32)

    def pull(step, low, count):
        at = rows(step)
        window = pl.ds(pl.multiple_of(low * tile, tile), count * tile)
        for pair in range(pairs):
            probs, slopes, dq = [], [], []
            both = range(2 * pair, 2 * pair + 2)
            for head in both:
                weights = jnp.exp(mm(keys_ref[head, window, :], queries_ref[head, at, :], NT))
                flow = mm(values_ref[head, window, :], grads_ref[head, at, :], NT)
                slope = (weights * flow).astype(BF16)
                probs.append(weights.astype(BF16))
                slopes.append(slope)
                dq.append(mm(turned_ref[pair, own_rows(head), window], slope))
            plain = jnp.concatenate([plain_ref[h, at, :] for h in both], axis=0)
            grads = jnp.concatenate([plain_grads_ref[h, at, :] for h in both], axis=0)
            cut = lanes(2 * pair)
            dv_ref[window, cut] += mm(jnp.concatenate(probs, axis=1), grads)
            dk_ref[window, cut] += mm(jnp.concatenate(slopes, axis=1), plain)
            dq_ref[at, cut] = jnp.concatenate(dq, axis=0).T

    for_spans(span_ref, tiles, pull)

    def finish(step, sums):
        cosine, sine = cos_ref[rows(step), :], sin_ref[rows(step), :]
        added = []
        out_ref[rows(step), 3 * pairs * 128 :] = att_ref[rows(step), :]
        for which, src in enumerate((dq_ref, dk_ref, dv_ref)):
            for pair in range(pairs):
                at = lanes(2 * pair)
                block = src[rows(step), at]
                if which < 2:
                    block = block * cosine - swap_halves(block) * sine
                low = block.astype(BF16)
                first = (which * pairs + pair) * 128
                out_ref[rows(step), first : first + 128] = low
                total = jnp.sum(low.astype(F32), axis=0, keepdims=True)
                added.append(sums[which * pairs + pair] + total)
        return tuple(added)

    zero = jnp.zeros((1, 128), F32)
    sums = lax.fori_loop(0, tiles, finish, (zero,) * (3 * pairs))
    sums = [jnp.concatenate(sums[w * pairs : (w + 1) * pairs], axis=1) for w in range(3)]
    sum_ref[...] = jnp.concatenate(sums + [jnp.zeros((5, pairs * 128), F32)], axis=0)


def attention_backward(
    spans, qkv, ext, attended, rest, grads, ext_k, cosine, sine, tile
):
    _, n, width = qkv.shape
    span = min(width, ATTENTION_LANES)
    wide = pl.BlockSpec((n, span), lambda i, *_: (0, i))
    three = pl.BlockSpec((3, n, span), lambda i, *_: (0, 0, i))
    pairs = span // 128
    heads = pltpu.VMEM((2 * pairs, n, 128), BF16)
    return call(
        functools.partial(attention_backward_kernel, tile=tile), "attention_backward",
        (width // span,),
        [three, wide, wide, wide, wide, held((n, 128)), held((n, 128)), held((n, 128))],
        [
            pl.BlockSpec((n, 4 * span), lambda i, *_: (0, i)),
            pl.BlockSpec((8, span), lambda i, *_: (0, i)),
        ],
        [shaped(BF16, n, 4 * width), shaped(F32, 8, width)],
        (spans, qkv, ext, attended, rest, grads, ext_k, cosine, sine), 0,
        prefetch=1,
        scratch=[
            heads, pltpu.VMEM((pairs, 128, n), BF16), heads, heads, heads, heads, heads,
        ] + [pltpu.VMEM((n, span), F32)] * 3,
    )


STRIP = 32


def token_sums(width, queries):
    token = lax.broadcasted_iota(jnp.int32, (width, queries), 0) // QLEN
    return token == lax.broadcasted_iota(jnp.int32, (width, queries), 1)


def score_kernel(low_ref, high_ref, doc_ref, query_ref, pick_ref, out_ref, sum_ref, total_ref):
    group = pl.program_id(0)
    docs, width = pick_ref.shape[1:]
    doc_rows = doc_ref.shape[0]
    strips = doc_rows // STRIP
    chunk = min(256, doc_rows)
    row = lax.broadcasted_iota(jnp.int32, (STRIP, width), 0)
    sum_ref[...] = jnp.zeros(sum_ref.shape, F32)

    def add_strip(sim, first, doc, pick):
        kept = jnp.where(row == pick - first, sim, 0.0)
        sum_ref[pl.ds(doc, 1)] += jnp.sum(kept.reshape(1, STRIP // 8, 8, width), axis=1)

    for start in range(0, doc_rows, chunk):
        sims = mm(doc_ref[start : start + chunk, :], query_ref[...], NT)
        for first in range(0, chunk, STRIP):
            place = group * strips + (start + first) // STRIP
            low, high = low_ref[place], high_ref[place]
            sim = sims[first : first + STRIP]
            add_strip(sim, start + first, low, pick_ref[0, pl.ds(low, 1), :])
            pick = jnp.where(high > low, pick_ref[0, pl.ds(high, 1), :], -1)
            add_strip(sim, start + first, high, pick)

    @pl.loop(0, strips)
    def _(strip):
        low, high = low_ref[group * strips + strip], high_ref[group * strips + strip]

        @pl.when(high > low + 1)
        def _():
            first = pl.multiple_of(strip * STRIP, STRIP)
            sim = mm(doc_ref[pl.ds(first, STRIP), :], query_ref[...], NT)

            @pl.loop(low + 1, high)
            def _(doc):
                add_strip(sim, first, doc, pick_ref[0, pl.ds(doc, 1), :])

    total_ref[group] = jnp.sum(sum_ref[...], axis=1)

    @pl.when(group == pl.num_programs(0) - 1)
    def _():
        spread = token_sums(width, out_ref.shape[1]).astype(F32).astype(BF16)
        total = jnp.concatenate([total_ref[g] for g in range(total_ref.shape[0])], axis=0)
        out_ref[...] = sum(mm(term.astype(BF16), spread) for term in three_terms(total))


def score_grad_kernel(
    low_ref, high_ref, doc_ref, query_ref, pick_ref, weight_ref, doc_out, query_out,
    sparse_ref, token_ref,
):
    group = pl.program_id(0)
    docs, width = pick_ref.shape[1:]
    doc_rows = doc_ref.shape[0]
    strips = doc_rows // STRIP
    chunk = min(256, doc_rows)
    row = lax.broadcasted_iota(jnp.int32, (STRIP, width), 0)

    def fill(held, first, doc, pick):
        return jnp.where(row == pick - first, token_ref[group, pl.ds(doc, 1), :], held)

    @pl.when(group == 0)
    def _():
        query_out[...] = jnp.zeros_like(query_out)
        spread = token_sums(width, weight_ref.shape[1]).astype(F32).astype(BF16)
        weights = mm(weight_ref[...].astype(BF16), spread, NT)
        for g in range(token_ref.shape[0]):
            token_ref[g] = weights[g * docs : (g + 1) * docs]

    total = None
    for start in range(0, doc_rows, chunk):
        for first in range(start, start + chunk, STRIP):
            place = group * strips + first // STRIP
            low, high = low_ref[place], high_ref[place]
            held = fill(jnp.zeros((STRIP, width), F32), first, low, pick_ref[0, pl.ds(low, 1), :])
            pick = jnp.where(high > low, pick_ref[0, pl.ds(high, 1), :], -1)
            sparse_ref[first : first + STRIP, :] = fill(held, first, high, pick).astype(BF16)
        sparse = sparse_ref[start : start + chunk, :]
        doc_out[start : start + chunk, :] = mm(sparse, query_ref[...])
        turned = doc_ref[start : start + chunk, :].astype(F32).T.astype(BF16)
        part = mm(turned, sparse)
        total = part if total is None else total + part
    query_out[...] += total

    @pl.loop(0, strips)
    def _(strip):
        low, high = low_ref[group * strips + strip], high_ref[group * strips + strip]

        @pl.when(high > low + 1)
        def _():
            first = pl.multiple_of(strip * STRIP, STRIP)
            held = lax.fori_loop(
                low + 1,
                high,
                lambda doc, held: fill(held, first, doc, pick_ref[0, pl.ds(doc, 1), :]),
                jnp.zeros((STRIP, width), F32),
            ).astype(BF16)
            doc_out[pl.ds(first, STRIP), :] += mm(held, query_ref[...])
            turned = doc_ref[pl.ds(first, STRIP), :].astype(F32).T.astype(BF16)
            query_out[...] += mm(turned, held)


def score_specs(doc_tile, query_tile, picks):
    groups, docs, width = picks.shape
    doc_rows = doc_tile.shape[0] // groups
    return (
        pl.BlockSpec((doc_rows, 128), lambda i, *_: (i, 0)),
        held(query_tile.shape),
        pl.BlockSpec((1, docs, width), lambda i, *_: (i, 0, 0)),
    )


def score_forward(lows, highs, doc_tile, query_tile, picks):
    groups, docs, width = picks.shape
    queries = width // QLEN
    doc_spec, query_spec, pick_spec = score_specs(doc_tile, query_tile, picks)
    return call(
        score_kernel, "score_forward", (groups,),
        [doc_spec, query_spec, pick_spec],
        [pl.BlockSpec((groups * docs, queries), lambda i, *_: (0, 0))],
        [shaped(F32, groups * docs, queries)],
        (lows, highs, doc_tile, query_tile, picks), 2 * doc_tile.shape[0] * width * 128,
        prefetch=2,
        scratch=[pltpu.VMEM((docs, 8, width), F32), pltpu.VMEM((groups, docs, width), F32)],
    )[0]


def score_backward(lows, highs, doc_tile, query_tile, picks, weights):
    groups, docs, width = picks.shape
    doc_spec, query_spec, pick_spec = score_specs(doc_tile, query_tile, picks)
    return call(
        score_grad_kernel, "score_backward", (groups,),
        [doc_spec, query_spec, pick_spec, held(weights.shape)],
        [doc_spec, pl.BlockSpec((128, width), lambda i, *_: (0, 0))],
        [shaped(F32, *doc_tile.shape), shaped(F32, 128, width)],
        (lows, highs, doc_tile, query_tile, picks, weights), 4 * doc_tile.shape[0] * width * 128,
        prefetch=2,
        scratch=[
            pltpu.VMEM((doc_tile.shape[0] // groups, width), BF16),
            pltpu.VMEM((groups, docs, width), F32),
        ],
    )


def rotary_tables(position):
    half_size = DH // 2
    frequency = jnp.exp(
        jnp.arange(half_size, dtype=F32) * (-2.0 * math.log(10000.0) / DH)
    )
    angles = position.astype(F32)[:, None] * frequency[None, :]
    cosine, sine = jnp.cos(angles), jnp.sin(angles)
    return (
        jnp.concatenate([cosine] * 4, axis=1),
        jnp.concatenate([-sine, sine, -sine, sine], axis=1),
    )


def on_device(
    tokens,
    doc_lengths,
    match_picks,
    labels,
    w_qkv,
    b_qkv,
    w_out,
    b_out,
    ln1_gain,
    ln1_bias,
    w_up,
    b_up,
    w_down,
    b_down,
    ln2_gain,
    ln2_bias,
    w_proj,
    log_scale,
):
    Order.last = ()
    C = lax.axis_size("cols")
    R = lax.axis_size("rows")
    c = lax.axis_index("cols")
    r = lax.axis_index("rows")
    width = tokens.shape[1]
    D = width * C
    Q = ROW_LEN // C
    DS = (tokens.shape[0] - ROW_LEN) // C
    n = Q + DS
    tile = math.gcd(256, math.gcd(Q, DS))

    def shift_cols(value, k):
        return lax.ppermute(value, "cols", [(i, (i + k) % C) for i in range(C)])

    def swap_rows(value, bit):
        return lax.ppermute(value, "rows", [(i, i ^ bit) for i in range(R)])

    def in_order(slots):
        if len(slots) == 1:
            return slots
        if len(slots) == 2:
            return [lax.select(c == 0, slots[0], slots[1]), lax.select(c == 0, slots[1], slots[0])]
        stacked = jnp.stack(slots)
        return [
            lax.dynamic_index_in_dim(stacked, (c - j) % C, 0, keepdims=False) for j in range(C)
        ]

    pack = [b_qkv.reshape(-1), b_up, b_out, ln1_gain, ln1_bias, b_down, ln2_gain, ln2_bias]
    ends = [0]
    for vector in pack:
        ends.append(ends[-1] + vector.shape[0])
    packed = jnp.concatenate(pack)

    def gather_pieces(pieces):
        return [lax.all_gather(piece, "rows", axis=0, tiled=True) for piece in pieces]

    if C == 2:
        x, qkv_other, *pieces, proj_other, pack_other = start_up(
            R, (Q, DS, ROW_LEN), tokens, w_qkv, w_out, w_up, w_down, w_proj,
            packed.reshape(8, -1),
        )
        wqkv_slots = [w_qkv, qkv_other]
        wout_slots, wup_slots, wdown_slots = (
            [own, other] for own, other in zip((w_out, w_up, w_down), gather_pieces(pieces))
        )
        wproj = jnp.concatenate(in_order([w_proj, proj_other]), axis=0)
        packs = [packed, pack_other.reshape(-1)]
    else:
        parts = jnp.concatenate(
            [tokens[:ROW_LEN].reshape(C, Q, width), tokens[ROW_LEN:].reshape(C, DS, width)], axis=1
        )

        def part(k):
            return lax.dynamic_index_in_dim(parts, (c + k) % C, 0, keepdims=False)

        x = jnp.concatenate(
            in_order([part(0)] + [shift_cols(part(k), k) for k in range(1, C)]), axis=1
        )

        def gather_slots(shard):
            flat = shard.reshape(-1, shard.shape[-1])
            piece = lax.dynamic_index_in_dim(
                flat.reshape(R, flat.shape[0] // R, flat.shape[1]), r, 0, keepdims=False
            )
            others = gather_pieces([shift_cols(piece, k) for k in range(1, C)])
            return [shard] + [other.reshape(shard.shape) for other in others]

        wqkv_slots, wout_slots, wup_slots, wdown_slots = (
            gather_slots(shard) for shard in (w_qkv, w_out, w_up, w_down)
        )
        wproj = jnp.concatenate(
            in_order([w_proj] + [shift_cols(w_proj, k) for k in range(1, C)]), axis=0
        )
        packs = [packed] + [shift_cols(packed, k) for k in range(1, C)]

    ordered_packs = in_order(packs)

    def of_slot(which, k):
        return packs[k][ends[which] : ends[which + 1]]

    def whole(which):
        return jnp.concatenate([p[ends[which] : ends[which + 1]] for p in ordered_packs])

    bqkv_slots = [of_slot(0, k).reshape(b_qkv.shape) for k in range(C)]
    bup_slots = [of_slot(1, k)[None, :] for k in range(C)]
    bout, gain1, bias1, bdown, gain2, bias2 = [whole(which) for which in range(2, 8)]
    zero_row = jnp.zeros_like(bout)
    vectors = jnp.stack([bout, gain1, bias1, bdown, gain2, bias2, zero_row, zero_row])

    own_sizes = lax.dynamic_index_in_dim(
        lax.dynamic_index_in_dim(doc_lengths, r, 0, keepdims=False), c, 0, keepdims=False
    )
    own_ends = jnp.cumsum(own_sizes)
    places = jnp.arange(DS, dtype=jnp.int32)
    passed = places[:, None] >= own_ends[None, :]
    slot_id = jnp.sum(passed.astype(jnp.int32), axis=1)
    slot_begin = jnp.sum(jnp.where(passed, own_sizes[None, :], 0), axis=1)
    query_places = jnp.arange(Q, dtype=jnp.int32)
    position = jnp.concatenate([query_places % QLEN, places - slot_begin])
    cosine, sine = rotary_tables(position)
    share = D // R
    paired = share == 64
    segment = jnp.concatenate([(query_places // QLEN) % SEGMENTS, slot_id])
    lane = jnp.arange(128, dtype=jnp.int32)[None, :] % DH
    same = segment[:, None] == lane
    ext_k = (same | ((lane >= SEGMENTS) & (lane < SEGMENTS + 3))).astype(BF16)
    ext_q = jnp.where((lane < SEGMENTS) & ~same, -1e30, 0.0).astype(BF16)
    q_tiles, d_tiles = Q // tile, DS // tile
    steps = jnp.arange(q_tiles, dtype=jnp.int32)
    first_rows = jnp.arange(d_tiles, dtype=jnp.int32) * tile
    is_passed = first_rows[:, None] >= own_ends[None, :]
    low_rows = jnp.sum(jnp.where(is_passed, own_sizes[None, :], 0), axis=1)
    last_passed = (first_rows + tile - 1)[:, None] >= own_ends[None, :]
    high_rows = jnp.min(jnp.where(last_passed, DS, own_ends[None, :]), axis=1)
    spans = jnp.concatenate(
        [steps, q_tiles + low_rows // tile, steps + 1, q_tiles + (high_rows + tile - 1) // tile]
    ).astype(jnp.int32)

    queries_here, tile_docs, _ = match_picks.shape
    docs = own_sizes.shape[0]
    sizes = lax.dynamic_index_in_dim(doc_lengths, c, 1, keepdims=False)
    doc_ends = jnp.cumsum(sizes, axis=1)
    begins = doc_ends - sizes
    picks = jnp.transpose(match_picks, (1, 0, 2)).reshape(tile_docs, queries_here * QLEN)
    picks = begins.reshape(-1)[:, None] + picks % sizes.reshape(-1)[:, None]
    picks = picks.reshape(R, docs, queries_here * QLEN)
    strip_rows = (jnp.arange(DS // STRIP, dtype=jnp.int32) * STRIP)[None, :, None]
    lows = jnp.sum(doc_ends[:, None, :] <= strip_rows, axis=2).astype(jnp.int32).reshape(-1)
    highs = jnp.sum(begins[:, None, :] < strip_rows + STRIP, axis=2).astype(jnp.int32) - 1
    highs = highs.reshape(-1)

    qkv, attended, rests, exts = [], [], [], []
    for k in range(C):
        first = (picks, lows, highs) if k == 0 else ()
        qkv.append(project_qkv(x, wqkv_slots[k], bqkv_slots[k], cosine, sine, first))
        out, rest, ext = attention_forward(spans, qkv[k], ext_k, ext_q, tile)
        attended.append(out)
        rests.append(rest)
        exts.append(ext)
    normed_one, inverse_one, hidden_low, hidden_left = out_and_norm(
        x, vectors, attended, wout_slots, paired
    )
    active, slopes = zip(*[up_and_gelu(hidden_low, wup_slots[k], bup_slots[k]) for k in range(C)])
    normed_two, inverse_two, output_low, unit, unit_low, unit_inverse = down_and_norm(
        normed_one, vectors, wproj, active, wdown_slots
    )

    doc_tile = gather_rows(R, unit_low[Q:]).reshape(R * DS, 128)
    query_tile = jnp.concatenate(
        in_order([unit_low[:Q]] + [shift_cols(unit_low[:Q], k) for k in range(1, C)]), axis=0
    )
    sims = score_forward(lows, highs, doc_tile, query_tile, picks)
    scores = sims.T

    scale = jnp.exp(log_scale[0])
    z = scale * scores
    row_top = jnp.max(z, axis=1)
    row_mass = jnp.sum(jnp.exp(z - row_top[:, None]), axis=1)
    is_label = (
        jnp.arange(tile_docs, dtype=jnp.int32)[None, :] == (labels - c * tile_docs)[:, None]
    )
    chosen = jnp.sum(jnp.where(is_label, z, 0.0), axis=1)
    own_stats = jnp.stack([row_top, row_mass, chosen])
    stats = jnp.stack([own_stats] + [shift_cols(own_stats, k) for k in range(1, C)])
    top_all = jnp.max(stats[:, 0], axis=0)
    mass_all = jnp.sum(stats[:, 1] * jnp.exp(stats[:, 0] - top_all), axis=0)
    log_total = top_all + jnp.log(mass_all)
    loss = log_total - jnp.sum(stats[:, 2], axis=0)
    dz = (jnp.exp(z - log_total[:, None]) - is_label.astype(F32)) / (queries_here * R)
    scale_part = jnp.sum(dz * z)
    dscores = (scale * dz).T
    doc_grad, query_grad_t = score_backward(lows, highs, doc_tile, query_tile, picks, dscores)
    query_parts = query_grad_t.T.reshape(C, Q, 128)

    def query_part(k):
        return lax.dynamic_index_in_dim(query_parts, (c + k) % C, 0, keepdims=False)

    query_grad = query_part(0)
    for k in range(1, C):
        query_grad = query_grad + shift_cols(query_part(k), k)

    doc_sum = scatter_rows(doc_grad.reshape(R, DS, 128))
    unit_grad = jnp.concatenate([query_grad, doc_sum], axis=0)

    core = r % 2
    slots_back = range(C - 1, -1, -1)
    x_bit, *z_bits = [1 << b for b in range(1, R.bit_length() - 1)]
    half = D // 2

    def side_of(bit):
        return ((r // bit) % 2).astype(jnp.int32)

    def core_order(left):
        if paired:
            return left
        return left.reshape(n, R // 2, 2, share).transpose(0, 2, 1, 3).reshape(n, D)

    def columns_of(left, side):
        return lax.dynamic_slice_in_dim(left, side * half, half, 1)

    def send_plain(left, right):
        part = mm(columns_of(left, 1 - core), right, TN).astype(BF16)
        Order.last += (part,)
        return swap_rows(part, 1)

    def keep_plain(left, right, arrived, k):
        kept = mm(columns_of(left, core), right, TN) + arrived.astype(F32)
        if k > 0:
            kept = kept.astype(BF16)
        Order.last += (kept,)
        return kept[None] if k == 0 else shift_cols(kept, C - k)[None]

    def next_fold(states, bit, inner):
        send, keep = fold(side_of(bit), [s[0] for s in states], [s[1] for s in states], inner)
        return keep, swap_rows(send, bit)

    def close(state):
        return state[0] + state[1].astype(F32)

    def cols_state(kept):
        rest = kept[1]
        for other in kept[2:]:
            rest = rest.astype(F32) + other.astype(F32)
        return kept[0], rest

    embed_grad, resid_two_grad, branch, branch_left, head_sums = head_pull(
        unit_grad, unit, unit_inverse, wproj, normed_two, inverse_two, vectors, paired
    )
    down_left, down_right = core_order(branch_left), active
    pre_grads, up_sums, down_kept = [None] * C, [None] * C, [None] * C
    down_arrived = [None] * C
    for k in slots_back:
        down_arrived[k] = send_plain(down_left, down_right[k])
    for k in slots_back:
        pre_grads[k], up_sums[k] = up_pull(branch, wdown_slots[k], slopes[k])
        if k > 0:
            down_kept[k] = keep_plain(down_left, down_right[k], down_arrived[k], k)
    up_left, up_right = core_order(hidden_left), pre_grads
    up_arrived, up_kept = [None] * C, [None] * C
    for k in slots_back:
        up_arrived[k] = send_plain(up_left, up_right[k])
    down_kept[0] = keep_plain(down_left, down_right[0], down_arrived[0], 0)
    for k in slots_back[:-1]:
        up_kept[k] = keep_plain(up_left, up_right[k], up_arrived[k], k)
    resid_one_grad, branch_one_left, hidden_sums, *attended_grads = hidden_pull(
        resid_two_grad, normed_one, inverse_one, vectors, pre_grads, wup_slots, wout_slots, paired
    )
    up_kept[0] = keep_plain(up_left, up_right[0], up_arrived[0], 0)
    mixed_grads, mixed_sums = [None] * C, [None] * C
    x_left = x.reshape(n, R // 2, 2, share).transpose(0, 2, 1, 3).reshape(n, D)
    late_lefts = [x_left, core_order(branch_one_left)]
    span = min(width, ATTENTION_LANES)
    late_state, late_arrived = [None] * C, [None] * C

    def gather_small():
        proj_grad = mm(embed_grad, output_low, TN).reshape(R, -1, C, width)
        def cut(values, slot_rows):
            return values.reshape(slot_rows, R, -1)

        own_order = [(c - k) % C for k in range(C)]
        canonical = jnp.stack(
            [hidden_sums[0], hidden_sums[1], hidden_sums[2], head_sums[0], head_sums[1], head_sums[2]]
        ).reshape(6, C, R, -1)
        slots_small = []
        for k in range(C):
            rows = [mixed_sums[k][j].reshape(R, -1) for j in range(3)]
            rows.append(up_sums[k][0].reshape(R, -1))
            rows += [
                lax.dynamic_index_in_dim(canonical[j], own_order[k], 0, keepdims=False)
                for j in range(6)
            ]
            own_proj_grad = lax.dynamic_index_in_dim(proj_grad, own_order[k], 2, keepdims=False)
            rows.append(own_proj_grad.reshape(R, -1))
            rows.append(jnp.broadcast_to(scale_part, (R, 1)))
            slots_small.append(jnp.concatenate(rows, axis=1))
        return jnp.stack(slots_small, axis=1)

    def pull_attention(k):
        mixed_grads[k], mixed_sums[k] = attention_backward(
            spans, qkv[k], exts[k], attended[k], rests[k], attended_grads[k], ext_k, cosine, sine,
            tile,
        )

    def late_product(columns, k):
        right = mixed_grads[k]
        parts = []
        for first in range(0, width, span):
            at = 4 * first
            parts.append(mm(columns[0], right[:, at : at + 3 * span], TN))
            parts.append(mm(columns[1], right[:, at + 3 * span : at + 4 * span], TN))
        return jnp.concatenate(parts, axis=1)

    def send_late(k):
        part = late_product([columns_of(left, 1 - core) for left in late_lefts], k).astype(BF16)
        Order.last += (part,)
        late_arrived[k] = swap_rows(part, 1)

    def keep_late(k):
        total = late_product([columns_of(left, core) for left in late_lefts], k)
        total = (total + late_arrived[k].astype(F32)).reshape(-1, 2, 2 * share, 4 * width)
        side = side_of(z_bits[0])
        part = lax.dynamic_index_in_dim(total, 1 - side, 1, keepdims=False).astype(BF16)
        kept = lax.dynamic_index_in_dim(total, side, 1, keepdims=False)
        part, kept = (v.reshape(1, half // 2, 4 * width) for v in (part, kept))
        Order.last += (part, kept)
        late_state[k] = (kept, swap_rows(part, z_bits[0]))

    for k in slots_back[:-1]:
        pull_attention(k)
        send_late(k)
    wide_state = next_fold([cols_state(down_kept), cols_state(up_kept)], x_bit, share)
    pull_attention(0)
    wide_state = next_fold([wide_state], z_bits[0], share)
    send_late(0)
    for k in slots_back[:-1]:
        keep_late(k)
    sent = [
        shift_cols(token_pull((c + k) % C, resid_one_grad, mixed_grads, wqkv_slots, BF16), k)
        for k in range(1, C)
    ]
    keep_late(0)
    late_bits = z_bits[1:] + [x_bit]

    def fold_late(k, bit):
        late_state[k] = next_fold([late_state[k]], bit, share if bit == x_bit else 2 * share)

    for k in slots_back[:-1]:
        fold_late(k, late_bits[0])
    own_tokens = token_pull(c, resid_one_grad, mixed_grads, wqkv_slots, F32)
    for place, bit in enumerate(late_bits):
        fold_late(0, bit)
        if place < len(z_bits) - 1:
            wide_state = next_fold([wide_state], z_bits[place + 1], share)
        for k in slots_back[:-1]:
            if place + 1 < len(late_bits):
                fold_late(k, late_bits[place + 1])
    small = small_sum(R, C, gather_small())
    late_grad = close(late_state[0])
    for k in slots_back[:-1]:
        late_grad = late_grad + shift_cols(close(late_state[k]).astype(BF16), C - k).astype(F32)
    late_grad = late_grad[0].reshape(share, width // span, 4, span).transpose(2, 0, 1, 3)
    late_grad = late_grad.reshape(4, share, width)
    qkv_grad, out_grad = late_grad[:3], late_grad[3]
    down_grad, up_grad = close(wide_state)
    ordered = in_order([own_tokens] + [s.astype(F32) for s in sent])
    tokens_grad = jnp.concatenate([s[:Q] for s in ordered] + [s[Q:] for s in ordered], axis=0)
    one = D // (C * R)
    up_part = bup_slots[0].shape[1] // R
    bounds = [3 * one, 3 * one + up_part]
    for _ in range(6):
        bounds.append(bounds[-1] + one)
    pieces = [small[a:b] for a, b in zip(bounds[:-1], bounds[1:])]
    bup_out, bout_out, gain1_out, bias1_out, bdown_out, gain2_out, bias2_out = pieces
    return (
        scores,
        loss,
        tokens_grad,
        qkv_grad,
        small[: bounds[0]].reshape(3, one),
        out_grad.T,
        bout_out,
        gain1_out,
        bias1_out,
        up_grad,
        bup_out,
        down_grad.T,
        bdown_out,
        gain2_out,
        bias2_out,
        small[bounds[-1] : -1].reshape(-1, width).T,
        small[-1:],
    )


def solution(mesh):
    in_specs = (
        P("rows", "cols"),
        P(),
        P("rows", "cols", None),
        P("rows"),
        P(None, None, "cols"),
        P(None, "cols"),
        P("cols", None),
        P("cols"),
        P("cols"),
        P("cols"),
        P(None, "cols"),
        P("cols"),
        P("cols", None),
        P("cols"),
        P("cols"),
        P("cols"),
        P("cols", None),
        P(),
    )
    out_specs = (
        P("rows", "cols"),
        P("rows"),
        P("rows", "cols"),
        P(None, "rows", "cols"),
        P(None, ("cols", "rows")),
        P("cols", "rows"),
        P(("cols", "rows")),
        P(("cols", "rows")),
        P(("cols", "rows")),
        P("rows", "cols"),
        P(("cols", "rows")),
        P("cols", "rows"),
        P(("cols", "rows")),
        P(("cols", "rows")),
        P(("cols", "rows")),
        P("cols", "rows"),
        P(),
    )
    return jax.shard_map(
        on_device, mesh=mesh, in_specs=in_specs, out_specs=out_specs, check_vma=False
    )
```

```python
import functools
import math

import jax
import jax.numpy as jnp
from jax import lax
from jax.experimental import pallas as pl
from jax.experimental.pallas import tpu as pltpu
from jax.sharding import PartitionSpec as P

DH = 64
QLEN = 32
ROW_LEN = 1024
F32 = jnp.float32
BF16 = jnp.bfloat16
VMEM_LIMIT = 56 * 1024 * 1024
NT = (((1,), (1,)), ((), ()))
NN = (((1,), (0,)), ((), ()))
TN = (((0,), (0,)), ((), ()))


def mm(left, right, dims=NN):
    return lax.dot_general(left, right, dims, preferred_element_type=F32)


def row_step(rows):
    return 256 if rows % 256 == 0 else 128


def parts_of(step):
    size = min(step, 256)
    return [slice(first, first + size) for first in range(0, step, size)]


def held(shape):
    return pl.BlockSpec(shape, lambda *_: (0,) * len(shape), pipeline_mode=pl.Buffered(1))


def shaped(dtype, *shape):
    return jax.ShapeDtypeStruct(shape, dtype)


class Order:
    last = ()


def call(
    body, name, grid, in_specs, out_specs, out_shape, operands, flops, scratch=(), prefetch=0, after=(),
    remote=None,
):
    count = len(operands)
    after = tuple(after) + Order.last

    def wrapped(*refs):
        body(*refs[:count], *refs[count + len(after) :])

    size = sum(math.prod(o.shape) * o.dtype.itemsize for o in list(operands) + list(out_shape))
    if flops == 0:
        size = 1024
    outs = pl.pallas_call(
        wrapped,
        grid_spec=pltpu.PrefetchScalarGridSpec(
            num_scalar_prefetch=prefetch,
            grid=grid,
            in_specs=list(in_specs) + [pl.BlockSpec(memory_space=pl.ANY)] * len(after),
            out_specs=out_specs,
            scratch_shapes=list(scratch),
        ),
        out_shape=out_shape,
        compiler_params=pltpu.CompilerParams(
            vmem_limit_bytes=VMEM_LIMIT, collective_id=remote, has_side_effects=remote is not None
        ),
        cost_estimate=pl.CostEstimate(flops=flops, bytes_accessed=size, transcendentals=0),
        name=name,
    )(*operands, *after)
    Order.last = (min(outs, key=lambda out: out.size * out.dtype.itemsize),)
    return outs


def row_spec(step, width):
    return pl.BlockSpec((step, width), lambda i, *_: (i, 0))


def column_spec(width, step):
    return pl.BlockSpec((width, step), lambda i, *_: (0, i))


MESH = pl.DeviceIdType.MESH
ANYWHERE = pl.BlockSpec(memory_space=pl.ANY)


def side_at(row, bit):
    return (row // bit) % 2


def across(row, bit):
    return row + bit * (1 - 2 * side_at(row, bit))


def flipped(row, bits):
    bit = 1
    while bit <= bits:
        if bits & bit:
            row = across(row, bit)
        bit *= 2
    return row


def greet(devices):
    barrier = pltpu.get_barrier_semaphore()
    for device in devices:
        pl.semaphore_signal(barrier, inc=1, device_id=device, device_id_type=MESH)
    pl.semaphore_wait(barrier, len(devices))


def send(source, target, sent, arrived, device):
    copy = pltpu.make_async_remote_copy(
        src_ref=source,
        dst_ref=target,
        send_sem=sent,
        recv_sem=arrived,
        device_id=device,
        device_id_type=MESH,
    )
    copy.start()
    return copy


def spread_order(count):
    pieces = sorted(range(count), key=lambda piece: (piece.bit_count(), -piece))
    order = []
    for piece in pieces:
        lowest = piece & -piece if piece else count
        bit = lowest // 2
        bits = []
        while bit:
            bits.append(bit)
            bit //= 2
        order.append((piece, bits))
    return order


def start_kernel(rows, cols_width, parts, *refs):
    (tokens, qkv, proj, pack), refs = refs[:4], refs[4:]
    (x, qkv_o, proj_o, pack_o), refs = refs[:4], refs[4:]
    own_sem, sent, arrived, wide_sent, wide_arrived = refs
    r, c = lax.axis_index("rows"), lax.axis_index("cols")
    partner = {"cols": 1 - c}
    bits = [1 << b for b in range(rows.bit_length() - 1)]
    greet([partner] + [{"rows": across(r, bit)} for bit in bits])
    wide = [(qkv, qkv_o)]
    copies, first = [], []
    for place, (source, target) in enumerate(wide):
        first.append(
            send(source.at[r], target.at[r], sent.at[place], arrived.at[place], partner)
        )
    q_rows, d_rows, first_doc = parts
    own = pl.ds(pl.multiple_of(c * cols_width, cols_width), cols_width)
    spans = [(0, q_rows, 0), (first_doc, d_rows, q_rows)]
    for place, (base, size, here) in enumerate(spans):
        theirs = pl.ds(pl.multiple_of(base + (1 - c) * size, size), size)
        mine = pl.ds(pl.multiple_of(base + c * size, size), size)
        target = x.at[pl.ds(here, size), own]
        copies.append(
            send(tokens.at[theirs], target, sent.at[3 + place], arrived.at[3 + place], partner)
        )
        pltpu.make_async_copy(tokens.at[mine], target, own_sem.at[place]).start()
    for place, (source, target) in enumerate([(proj, proj_o), (pack, pack_o)]):
        copies.append(
            send(source, target, sent.at[5 + place], arrived.at[5 + place], partner)
        )
    wide_copies = {}
    for piece, over in spread_order(rows):
        row = flipped(r, piece)
        for place, (_, target) in enumerate(wide):
            if piece == 0:
                first[place].wait_recv()
            else:
                wide_copies[place, piece].wait_recv()
            for bit in over:
                wide_copies[place, piece | bit] = send(
                    target.at[row], target.at[row],
                    wide_sent.at[place, piece | bit], wide_arrived.at[place, piece | bit],
                    {"rows": across(r, bit)},
                )
    for copy in first + list(wide_copies.values()):
        copy.wait_send()
    for copy in copies:
        copy.wait()
    for place, (base, size, here) in enumerate(spans):
        mine = pl.ds(pl.multiple_of(base + c * size, size), size)
        target = x.at[pl.ds(here, size), own]
        pltpu.make_async_copy(tokens.at[mine], target, own_sem.at[place]).wait()


def start_up(rows, parts, tokens, qkv, proj, pack):
    width = tokens.shape[1]
    pieces = qkv.reshape(rows, -1, width)
    x, qkv_o, proj_o, pack_o = call(
        functools.partial(start_kernel, rows, width, parts), "start_up", (1,),
        [ANYWHERE] * 4, [ANYWHERE] * 4,
        [
            shaped(BF16, parts[0] + parts[1], 2 * width), shaped(BF16, *pieces.shape),
            shaped(BF16, *proj.shape), shaped(F32, *pack.shape),
        ],
        (tokens, pieces, proj, pack), 0, remote=1,
        scratch=[
            pltpu.SemaphoreType.DMA((2,)), pltpu.SemaphoreType.DMA((7,)),
            pltpu.SemaphoreType.DMA((7,)), pltpu.SemaphoreType.DMA((1, rows)),
            pltpu.SemaphoreType.DMA((1, rows)),
        ],
    )
    return x, qkv_o.reshape(qkv.shape), proj_o, pack_o


def gather_kernel(rows, own, out, own_sem, sent, arrived):
    r = lax.axis_index("rows")
    bits = [1 << b for b in range(rows.bit_length() - 1)]
    greet([{"rows": across(r, bit)} for bit in bits])
    local = pltpu.make_async_copy(own, out.at[r], own_sem)
    local.start()
    copies = {}
    size = own.shape[0] // PARTS
    for piece, over in spread_order(rows):
        row = flipped(r, piece)
        for part in range(PARTS):
            at = pl.ds(part * size, size)
            if piece:
                copies[piece, part].wait_recv()
            for bit in over:
                copies[piece | bit, part] = send(
                    out.at[row, at] if piece else own.at[at], out.at[row, at],
                    sent.at[piece | bit, part], arrived.at[piece | bit, part],
                    {"rows": across(r, bit)},
                )
    for copy in copies.values():
        copy.wait_send()
    local.wait()


PARTS = 2


def gather_rows(rows, own):
    return call(
        functools.partial(gather_kernel, rows), "gather_rows", (1,), [ANYWHERE], [ANYWHERE],
        [shaped(own.dtype, rows, *own.shape)], (own,), 0, remote=2,
        scratch=[
            pltpu.SemaphoreType.DMA, pltpu.SemaphoreType.DMA((rows, PARTS)),
            pltpu.SemaphoreType.DMA((rows, PARTS)),
        ],
    )[0]


def scatter_kernel(rows, parts, out, sent, arrived, *buffers):
    r = lax.axis_index("rows")
    bits = [1 << b for b in range(rows.bit_length() - 1)]
    greet([{"rows": across(r, bit)} for bit in bits])
    outgoing, incoming = buffers[: len(bits)], buffers[len(bits) :]
    size = parts.shape[1] // PARTS
    copies = {}

    def total(flips, levels, part):
        row, at = flipped(r, flips), pl.ds(part * size, size)
        value = parts[row, at]
        for level in range(levels):
            copies[level, flips >> (level + 1), part].wait_recv()
            value = value + incoming[level][row // (2 << level), at].astype(F32)
        return value

    for level, bit in enumerate(bits):
        count = rows // (2 << level)
        for turn in sorted(range(count), key=lambda f: tuple(-((f >> b) & 1) for b in range(8))):
            flips = (turn << (level + 1)) | bit
            place = flipped(r, flips) // (2 << level)
            for part in range(PARTS):
                at = pl.ds(part * size, size)
                outgoing[level][place, at] = total(flips, level, part).astype(BF16)
                name = rows - 2 * count + turn
                copies[level, turn, part] = send(
                    outgoing[level].at[place, at], incoming[level].at[place, at],
                    sent.at[name, part], arrived.at[name, part], {"rows": across(r, bit)},
                )
    for part in range(PARTS):
        out[part * size : (part + 1) * size, :] = total(0, len(bits), part)
    for copy in copies.values():
        copy.wait_send()


def scatter_rows(parts):
    rows, height, width = parts.shape
    levels = rows.bit_length() - 1
    buffers = [
        pltpu.VMEM((rows // (2 << level), height, width), BF16) for level in range(levels)
    ]
    return call(
        functools.partial(scatter_kernel, rows), "scatter_rows", (1,), [held(parts.shape)],
        [pl.BlockSpec((height, width), lambda *_: (0, 0))], [shaped(F32, height, width)],
        (parts,), 0, remote=3,
        scratch=[
            pltpu.SemaphoreType.DMA((rows, PARTS)), pltpu.SemaphoreType.DMA((rows, PARTS)),
        ] + buffers + buffers,
    )[0]


def late_kernel(rows, cols, *refs):
    tokens_t, branch_t = refs[:2]
    rights, attended, refs = refs[2 : 2 + cols], refs[2 + cols : 2 + 2 * cols], refs[2 + 2 * cols :]
    (du_own, du_in, out, du_out), refs = refs[:4], refs[4:]
    (core_out, core_in, x_out, x_in, kept, cols_out, cols_in), refs = refs[:7], refs[7:]
    r, c = lax.axis_index("rows"), lax.axis_index("cols")
    x_bit, *z_bits = [1 << b for b in range(1, rows.bit_length() - 1)]
    levels = len(z_bits)
    z_out, z_in, z_kept = refs[:levels], refs[levels : 2 * levels], refs[2 * levels : 3 * levels]
    refs = refs[3 * levels :]
    du_z_out, du_z_in, du_kept = refs[:levels], refs[levels : 2 * levels], refs[2 * levels : 3 * levels]
    (core_sem, x_sem, cols_sem, z_sem, du_sem) = refs[3 * levels :]
    share = out.shape[1]
    others = [{"cols": (c + cols - k) % cols} for k in range(1, cols)]
    core, x_side = side_at(r, 1), side_at(r, x_bit)
    greet([{"rows": across(r, bit)} for bit in [1, x_bit] + z_bits] + others)
    chunks = range(4)
    slots = range(cols - 1, -1, -1)
    copies = {}

    def halves(total, side):
        pairs = total.reshape(-1, 2, share, total.shape[1])
        near = jnp.where(side == 0, pairs[:, 0], pairs[:, 1]).reshape(-1, total.shape[1])
        far = jnp.where(side == 0, pairs[:, 1], pairs[:, 0]).reshape(-1, total.shape[1])
        return near, far

    def product(side, slot, chunk):
        left = (tokens_t if chunk < 3 else branch_t)[:, side]
        right = rights[slot][chunk] if chunk < 3 else attended[slot][...]
        return mm(left.reshape(-1, left.shape[-1]), right)

    def begin(chunk):
        for slot in slots:
            core_out[slot, chunk] = product(1 - core, slot, chunk).astype(BF16)
            copies["core", slot, chunk] = send(
                core_out.at[slot, chunk], core_in.at[slot, chunk],
                core_sem.at[0, slot, chunk], core_sem.at[1, slot, chunk],
                {"rows": across(r, 1)},
            )

    def after_core(chunk):
        for slot in slots:
            total = product(core, slot, chunk)
            copies["core", slot, chunk].wait_recv()
            near, far = halves(total + core_in[slot, chunk].astype(F32), x_side)
            x_out[slot, chunk] = far.astype(BF16)
            kept[slot, chunk] = near
            copies["x", slot, chunk] = send(
                x_out.at[slot, chunk], x_in.at[slot, chunk], x_sem.at[0, slot, chunk],
                x_sem.at[1, slot, chunk], {"rows": across(r, x_bit)},
            )

    def after_x(chunk):
        for slot in slots:
            copies["x", slot, chunk].wait_recv()
            total = kept[slot, chunk] + x_in[slot, chunk].astype(F32)
            if slot == 0:
                kept[0, chunk] = total
            else:
                cols_out[slot - 1, chunk] = total.astype(BF16)
                copies["cols", slot, chunk] = send(
                    cols_out.at[slot - 1, chunk], cols_in.at[slot - 1, chunk],
                    cols_sem.at[0, slot - 1, chunk], cols_sem.at[1, slot - 1, chunk],
                    others[slot - 1],
                )

    def after_cols(chunk):
        total = kept[0, chunk]
        for slot in slots[:-1]:
            copies["cols", slot, chunk].wait_recv()
            total = total + cols_in[slot - 1, chunk].astype(F32)
        pass_z(chunk, 0, total)

    def pass_z(chunk, level, total):
        if level == levels:
            out[chunk] = total
            return
        bit = z_bits[level]
        near, far = halves(total, side_at(r, bit))
        z_out[level][chunk] = far.astype(BF16)
        z_kept[level][chunk] = near
        copies["z", level, chunk] = send(
            z_out[level].at[chunk], z_in[level].at[chunk], z_sem.at[0, level, chunk],
            z_sem.at[1, level, chunk], {"rows": across(r, bit)},
        )

    def after_z(chunk, level):
        copies["z", level, chunk].wait_recv()
        pass_z(chunk, level + 1, z_kept[level][chunk] + z_in[level][chunk].astype(F32))

    def pass_du(place, level, total):
        if level == levels:
            du_out[place] = total
            return
        bit = z_bits[level]
        near, far = halves(total, side_at(r, bit))
        du_z_out[level][place] = far.astype(BF16)
        du_kept[level][place] = near
        copies["du", level, place] = send(
            du_z_out[level].at[place], du_z_in[level].at[place], du_sem.at[0, level, place],
            du_sem.at[1, level, place], {"rows": across(r, bit)},
        )

    def after_du(place, level):
        copies["du", level, place].wait_recv()
        pass_du(place, level + 1, du_kept[level][place] + du_z_in[level][place].astype(F32))

    for place in range(2):
        pass_du(place, 0, du_own[place] + du_in[place].astype(F32))
    stages = [(0, begin), (1, after_core), (3, after_x), (4, after_cols)]
    stages += [(5 + level, functools.partial(after_z, level=level)) for level in range(levels)]
    for turn in range(len(chunks) + stages[-1][0]):
        for delay, stage in stages[::-1]:
            if 0 <= turn - delay < len(chunks):
                stage(turn - delay)
        if 3 <= turn < 3 + levels:
            for place in range(2):
                after_du(place, turn - 3)
    for copy in copies.values():
        copy.wait_send()


def late_sums(rows, cols, tokens_t, branch_t, rights, attended, du_own, du_in):
    share, n = tokens_t.shape[2:]
    width = attended[0].shape[1]
    wide = du_own.shape[2]
    half, quarter = rows // 2 * share, rows // 4 * share
    levels = rows.bit_length() - 3
    heights = [quarter >> (level + 1) for level in range(levels)]

    def vmem(dtype, *shape):
        return pltpu.VMEM(shape, dtype)

    def pair_of(*shape):
        return pltpu.SemaphoreType.DMA((2,) + shape)

    operands = (tokens_t, branch_t, *rights, *attended, du_own, du_in)
    scratch = [
        vmem(BF16, cols, 4, half, width), vmem(BF16, cols, 4, half, width),
        vmem(BF16, cols, 4, quarter, width), vmem(BF16, cols, 4, quarter, width),
        vmem(F32, cols, 4, quarter, width),
        vmem(BF16, cols - 1, 4, quarter, width), vmem(BF16, cols - 1, 4, quarter, width),
    ]
    for count, size in ((4, width), (2, wide)):
        for dtype in (BF16, BF16, F32):
            scratch += [vmem(dtype, count, height, size) for height in heights]
    scratch += [
        pair_of(cols, 4), pair_of(cols, 4), pair_of(cols - 1, 4), pair_of(levels, 4),
        pair_of(levels, 2),
    ]
    return call(
        functools.partial(late_kernel, rows, cols), "late_sums", (1,),
        [held(o.shape) for o in operands],
        [
            pl.BlockSpec((4, share, width), lambda *_: (0, 0, 0)),
            pl.BlockSpec((2, share, wide), lambda *_: (0, 0, 0)),
        ],
        [shaped(F32, 4, share, width), shaped(F32, 2, share, wide)],
        operands, 100_000_000_000, remote=5, scratch=scratch,
    )


def small_kernel(rows, cols, parts, out, *refs):
    bits = [1 << b for b in range(rows.bit_length() - 1)]
    sent, arrived = refs[:2]
    core_in, cols_in, totals, row_ins = refs[2], refs[3], refs[4 : 4 + len(bits)], refs[4 + len(bits) :]
    r, c = lax.axis_index("rows"), lax.axis_index("cols")
    others = [{"cols": (c + cols - k) % cols} for k in range(1, cols)]
    greet([{"rows": across(r, bit)} for bit in bits] + others)
    core = side_at(r, 1)
    copy = send(parts.at[:, 1 - core], core_in, sent.at[0], arrived.at[0], {"rows": across(r, 1)})
    copy.wait()
    sums = parts[:, core] + core_in[...]
    cols_out = totals[0]
    cols_out[...] = sums
    copies = [
        send(cols_out.at[:, k], cols_in.at[k - 1], sent.at[k], arrived.at[k], others[k - 1])
        for k in range(1, cols)
    ]
    total = sums[:, 0]
    for k, copy in enumerate(copies):
        copy.wait()
        total = total + cols_in[k]
    for level, bit in enumerate(bits[1:]):
        held_total, arriving = totals[1 + level], row_ins[level]
        held_total[...] = total.reshape(held_total.shape)
        side = side_at(r, bit)
        copy = send(
            held_total.at[:, 1 - side], arriving, sent.at[cols + level], arrived.at[cols + level],
            {"rows": across(r, bit)},
        )
        copy.wait()
        total = held_total[:, side] + arriving[...]
    out[...] = total[0]


def small_sum(rows, cols, parts):
    length = parts.shape[2]
    width = -(-length // 1024) * 128
    parts = jnp.pad(parts, ((0, 0), (0, 0), (0, 8 * width - length)))
    parts = parts.reshape(rows // 2, 2, cols, 8, width)
    levels = rows.bit_length() - 1
    sizes = [rows >> (level + 1) for level in range(1, levels)]
    scratch = [
        pltpu.SemaphoreType.DMA((cols + levels,)), pltpu.SemaphoreType.DMA((cols + levels,)),
        pltpu.VMEM((rows // 2, cols, 8, width), F32),
        pltpu.VMEM((cols - 1, rows // 2, 8, width), F32),
        pltpu.VMEM((rows // 2, cols, 8, width), F32),
    ]
    scratch += [pltpu.VMEM((size, 2, 8, width), F32) for size in sizes]
    scratch += [pltpu.VMEM((size, 8, width), F32) for size in sizes]
    total = call(
        functools.partial(small_kernel, rows, cols), "small_sum", (1,), [held(parts.shape)],
        [pl.BlockSpec((8, width), lambda *_: (0, 0))], [shaped(F32, 8, width)], (parts,), 0,
        remote=4, scratch=scratch,
    )[0]
    return total.reshape(-1)[:length]


def swap_halves(block):
    lane = lax.broadcasted_iota(jnp.int32, block.shape, 1)
    return jnp.where((lane & 32) == 0, pltpu.roll(block, 96, 1), pltpu.roll(block, 32, 1))


def qkv_kernel(x_ref, w_ref, b_ref, cos_ref, sin_ref, out_ref):
    which = pl.program_id(0)
    bias = b_ref[pl.ds(which, 1), :]

    @pl.when(which < 2)
    def _():
        for at in parts_of(x_ref.shape[0]):
            mixed = mm(x_ref[at, :], w_ref[0]) + bias
            for first in range(0, mixed.shape[1], 128):
                block = mixed[:, first : first + 128]
                turned = block * cos_ref[at, :] + swap_halves(block) * sin_ref[at, :]
                out_ref[0, at, first : first + 128] = turned.astype(BF16)

    @pl.when(which == 2)
    def _():
        for at in parts_of(x_ref.shape[0]):
            out_ref[0, at, :] = (mm(x_ref[at, :], w_ref[0]) + bias).astype(BF16)


def project_qkv(x, weight, bias, cosine, sine, after=()):
    n, D = x.shape
    width = weight.shape[2]
    step = row_step(n)
    return call(
        qkv_kernel, "project_qkv", (3, n // step),
        [
            pl.BlockSpec((step, D), lambda j, i: (i, 0)),
            pl.BlockSpec((1, D, width), lambda j, i: (j, 0, 0)),
            held(bias.shape),
            pl.BlockSpec((step, 128), lambda j, i: (i, 0)),
            pl.BlockSpec((step, 128), lambda j, i: (i, 0)),
        ],
        [pl.BlockSpec((1, step, width), lambda j, i: (j, i, 0))],
        [shaped(BF16, 3, n, width)],
        (x, weight, bias, cosine, sine), 6 * n * D * width, after=after,
    )[0]


def normed_rows(residual):
    mean = jnp.mean(residual, axis=1, keepdims=True)
    centred = residual - mean
    inverse = lax.rsqrt(jnp.mean(centred * centred, axis=1, keepdims=True) + 1e-05)
    return centred * inverse, inverse


def norm_pull(grad_rows, normed, inverse, gain):
    spread = grad_rows * gain
    return inverse * (
        spread
        - jnp.mean(spread, axis=1, keepdims=True)
        - normed * jnp.mean(spread * normed, axis=1, keepdims=True)
    )


def column_sums(*arrays):
    rows = [jnp.sum(array, axis=0, keepdims=True) for array in arrays]
    rows.append(jnp.zeros((8 - len(rows), rows[0].shape[1]), F32))
    return jnp.concatenate(rows, axis=0)


def add_over_steps(ref, value):
    first = pl.program_id(0) == 0

    @pl.when(first)
    def _():
        ref[...] = value

    @pl.when(jnp.logical_not(first))
    def _():
        ref[...] += value


def out_norm_kernel(slots, *refs):
    x_ref, vec_ref = refs[:2]
    att_refs, w_refs = refs[2 : 2 + slots], refs[2 + slots : 2 + 2 * slots]
    normed_ref, inverse_ref, low_ref, turned_ref = refs[2 + 2 * slots :]
    for at in parts_of(x_ref.shape[0]):
        residual = x_ref[at, :].astype(F32) + vec_ref[0:1, :]
        for att_ref, w_ref in zip(att_refs, w_refs):
            residual = residual + mm(att_ref[at, :], w_ref[...])
        normed, inverse = normed_rows(residual)
        hidden = normed * vec_ref[1:2, :] + vec_ref[2:3, :]
        normed_ref[at, :] = normed
        inverse_ref[at, :] = inverse
        low_ref[at, :] = hidden.astype(BF16)
        turned_ref[:, at] = hidden.T.astype(BF16)


def out_and_norm(x, vectors, attended, weights):
    n, D = x.shape
    step = row_step(n)
    slots = len(attended)
    width = attended[0].shape[1]
    return call(
        functools.partial(out_norm_kernel, slots), "out_and_norm", (n // step,),
        [row_spec(step, D), held(vectors.shape)]
        + [row_spec(step, width)] * slots + [held((width, D))] * slots,
        [row_spec(step, D), row_spec(step, 1), row_spec(step, D), column_spec(D, step)],
        [shaped(F32, n, D), shaped(F32, n, 1), shaped(BF16, n, D), shaped(BF16, D, n)],
        (x, vectors, *attended, *weights), 2 * n * D * D,
    )


GELU_TERMS = (
    0.23532527933595032, 0.09138803439798156, 0.6495603483388861,
    -0.6354014529895687, 0.8866650885491606, -0.22753729931242958,
)


def gelu_parts(values):
    size = jnp.abs(values)
    part = pl.reciprocal(1.0 + (0.39 / math.sqrt(2.0)) * size)
    bell = jnp.exp(-0.5 * (values * values))
    series = 0.5 * GELU_TERMS[-1]
    for term in GELU_TERMS[-2::-1]:
        series = series * part + 0.5 * term
    tail = series * part * bell
    below = jnp.where(values >= 0.0, 1.0 - tail, tail)
    return values * below, below + values * bell * (1.0 / math.sqrt(2.0 * math.pi))


def up_kernel(x_ref, w_ref, b_ref, active_ref, slope_ref):
    width = w_ref.shape[1]
    chunk = min(256, width)
    for first in range(0, width, chunk):
        at = slice(first, first + chunk)
        active, slope = gelu_parts(mm(x_ref[...], w_ref[:, at]) + b_ref[:, at])
        active_ref[:, at] = active.astype(BF16)
        slope_ref[:, at] = slope


def up_and_gelu(x, weight, bias):
    n, D = x.shape
    width = weight.shape[1]
    step = row_step(n)
    return call(
        up_kernel, "up_and_gelu", (n // step,),
        [row_spec(step, D), held(weight.shape), held(bias.shape)],
        [row_spec(step, width)] * 2,
        [shaped(BF16, n, width), shaped(F32, n, width)],
        (x, weight, bias), 5 * n * D * width,
    )


def down_norm_kernel(slots, *refs):
    normed_ref, vec_ref, proj_ref = refs[:3]
    act_refs, w_refs = refs[3 : 3 + slots], refs[3 + slots : 3 + 2 * slots]
    normed_out, inverse_ref, low_ref, unit_ref, unit_low_ref, unit_inverse_ref = refs[3 + 2 * slots :]
    for at in parts_of(normed_ref.shape[0]):
        residual = normed_ref[at, :] * vec_ref[1:2, :] + vec_ref[2:3, :] + vec_ref[3:4, :]
        for act_ref, w_ref in zip(act_refs, w_refs):
            residual = residual + mm(act_ref[at, :], w_ref[...])
        normed, inverse = normed_rows(residual)
        normed_out[at, :] = normed
        inverse_ref[at, :] = inverse
        low = (normed * vec_ref[4:5, :] + vec_ref[5:6, :]).astype(BF16)
        low_ref[at, :] = low
        embedding = mm(low, proj_ref[...])
        unit_inverse = lax.rsqrt(jnp.sum(embedding * embedding, axis=1, keepdims=True) + 1e-06)
        unit = embedding * unit_inverse
        unit_ref[at, :] = unit
        unit_low_ref[at, :] = unit.astype(BF16)
        unit_inverse_ref[at, :] = unit_inverse


def down_and_norm(normed, vectors, proj, active, weights):
    n, D = normed.shape
    step = row_step(n)
    slots = len(active)
    width = active[0].shape[1]
    return call(
        functools.partial(down_norm_kernel, slots), "down_and_norm", (n // step,),
        [row_spec(step, D), held(vectors.shape), held(proj.shape)]
        + [row_spec(step, width)] * slots + [held((width, D))] * slots,
        [
            row_spec(step, D), row_spec(step, 1), row_spec(step, D),
            row_spec(step, 128), row_spec(step, 128), row_spec(step, 1),
        ],
        [
            shaped(F32, n, D), shaped(F32, n, 1), shaped(BF16, n, D),
            shaped(F32, n, 128), shaped(BF16, n, 128), shaped(F32, n, 1),
        ],
        (normed, vectors, proj, *active, *weights), 2 * n * D * width * slots,
    )


def head_pull_kernel(
    grad_ref, unit_ref, unit_inverse_ref, proj_ref, normed_ref, inverse_ref, vec_ref,
    embed_ref, residual_ref, low_ref, turned_ref, sum_ref,
):
    sums = []
    for at in parts_of(grad_ref.shape[0]):
        grad, unit = grad_ref[at, :], unit_ref[at, :]
        embed = grad - unit * jnp.sum(grad * unit, axis=1, keepdims=True)
        embed = (unit_inverse_ref[at, :] * embed).astype(BF16)
        embed_ref[at, :] = embed
        output_grad = mm(embed, proj_ref[...], NT)
        normed = normed_ref[at, :]
        residual = norm_pull(output_grad, normed, inverse_ref[at, :], vec_ref[4:5, :])
        residual_ref[at, :] = residual
        low_ref[at, :] = residual.astype(BF16)
        turned_ref[:, at] = residual.T.astype(BF16)
        sums.append(column_sums(residual, output_grad * normed, output_grad))
    add_over_steps(sum_ref, sum(sums))


def head_pull(unit_grad, unit, unit_inverse, proj, normed, inverse, vectors):
    n, D = normed.shape
    step = row_step(n)
    return call(
        head_pull_kernel, "head_pull", (n // step,),
        [
            row_spec(step, 128), row_spec(step, 128), row_spec(step, 1), held(proj.shape),
            row_spec(step, D), row_spec(step, 1), held(vectors.shape),
        ],
        [
            row_spec(step, 128), row_spec(step, D), row_spec(step, D),
            column_spec(D, step), pl.BlockSpec((8, D), lambda i: (0, 0)),
        ],
        [
            shaped(BF16, n, 128), shaped(F32, n, D), shaped(BF16, n, D),
            shaped(BF16, D, n), shaped(F32, 8, D),
        ],
        (unit_grad, unit, unit_inverse, proj, normed, inverse, vectors), 4 * n * D * 128,
    )


def up_pull_kernel(branch_ref, w_ref, slope_ref, out_ref, sum_ref):
    width = w_ref.shape[0]
    chunk = min(512, width)
    sums = []
    for first in range(0, width, chunk):
        at = slice(first, first + chunk)
        low = (mm(branch_ref[...], w_ref[at, :], NT) * slope_ref[:, at]).astype(BF16)
        out_ref[:, at] = low
        sums.append(column_sums(low.astype(F32)))
    add_over_steps(sum_ref, jnp.concatenate(sums, axis=1))


def up_pull(branch, weight, slope):
    n, D = branch.shape
    width = weight.shape[0]
    step = row_step(n)
    return call(
        up_pull_kernel, "up_pull", (n // step,),
        [row_spec(step, D), held(weight.shape), row_spec(step, width)],
        [row_spec(step, width), pl.BlockSpec((8, width), lambda i: (0, 0))],
        [shaped(BF16, n, width), shaped(F32, 8, width)],
        (branch, weight, slope), 2 * n * D * width,
    )


def hidden_pull_kernel(slots, *refs):
    residual_ref, normed_ref, inverse_ref, vec_ref = refs[:4]
    pre_refs, up_refs, out_refs = (refs[4 + j * slots : 4 + (j + 1) * slots] for j in range(3))
    rest = refs[4 + 3 * slots :]
    grad_ref, turned_ref, sum_ref = rest[:3]
    att_refs = rest[3:]
    sums = []
    for at in parts_of(residual_ref.shape[0]):
        hidden_grad = residual_ref[at, :]
        for pre_ref, up_ref in zip(pre_refs, up_refs):
            hidden_grad = hidden_grad + mm(pre_ref[at, :], up_ref[...], NT)
        normed = normed_ref[at, :]
        residual = norm_pull(hidden_grad, normed, inverse_ref[at, :], vec_ref[1:2, :])
        grad_ref[at, :] = residual
        low = residual.astype(BF16)
        turned_ref[:, at] = residual.T.astype(BF16)
        sums.append(column_sums(residual, hidden_grad * normed, hidden_grad))
        for att_ref, out_ref in zip(att_refs, out_refs):
            att_ref[at, :] = mm(low, out_ref[...], NT).astype(BF16)
    add_over_steps(sum_ref, sum(sums))


def hidden_pull(residual, normed, inverse, vectors, pre_grads, ups, outs):
    n, D = residual.shape
    step = row_step(n)
    slots = len(ups)
    wide, width = ups[0].shape[1], outs[0].shape[0]
    return call(
        functools.partial(hidden_pull_kernel, slots), "hidden_pull", (n // step,),
        [row_spec(step, D), row_spec(step, D), row_spec(step, 1), held(vectors.shape)]
        + [row_spec(step, wide)] * slots + [held((D, wide))] * slots
        + [held((width, D))] * slots,
        [row_spec(step, D), column_spec(D, step), pl.BlockSpec((8, D), lambda i: (0, 0))]
        + [row_spec(step, width)] * slots,
        [shaped(F32, n, D), shaped(BF16, D, n), shaped(F32, 8, D)]
        + [shaped(BF16, n, width)] * slots,
        (residual, normed, inverse, vectors, *pre_grads, *ups, *outs),
        0,
    )


def token_pull_kernel(slots, place_ref, *refs):
    residual_ref = refs[0]
    mixed_refs, w_refs = refs[1 : 1 + slots], refs[1 + slots : 1 + 2 * slots]
    out_ref = refs[-1]
    width = out_ref.shape[1]
    at = pl.ds(pl.multiple_of(place_ref[0] * width, width), width)
    total = residual_ref[...]
    for mixed_ref, w_ref in zip(mixed_refs, w_refs):
        for which in range(3):
            total = total + mm(mixed_ref[which], w_ref[which, at, :], NT)
    out_ref[...] = total.astype(out_ref.dtype)


def token_pull(place, residual, mixed_grads, weights, dtype):
    n, D = residual.shape
    step = row_step(n)
    slots = len(weights)
    width = weights[0].shape[2]
    return call(
        functools.partial(token_pull_kernel, slots), "token_pull", (n // step,),
        [pl.BlockSpec((step, width), lambda i, p: (i, p[0]))]
        + [pl.BlockSpec((3, step, width), lambda i, p: (0, i, 0))] * slots
        + [held((3, D, width))] * slots,
        [row_spec(step, width)],
        [shaped(dtype, n, width)],
        (place.reshape(1), residual, *mixed_grads, *weights), 0, prefetch=1,
    )[0]


def put_halves(total, inner, side, refs):
    pairs = total.reshape(-1, 2, inner, total.shape[1])
    keep = jnp.where(side == 0, pairs[:, 0], pairs[:, 1]).reshape(-1, total.shape[1])
    send = jnp.where(side == 0, pairs[:, 1], pairs[:, 0]).reshape(-1, total.shape[1])
    refs[0][0] = send.astype(BF16)
    refs[1][0] = keep


def grouped_index(starts, place, count):
    def index(j, i, *_):
        inside = (j >= starts[place]) & (j < starts[place + 1])
        row = jnp.clip(j - starts[place], 0, starts[place + 1] - starts[place] - 1)
        rest = jnp.where(j < starts[place], 0, count - 1)
        return row, 0, jnp.where(inside, i, rest)

    return index


def for_group(starts, body):
    if len(starts) == 2:
        body(0)
        return
    for place in range(len(starts) - 1):

        @pl.when((pl.program_id(0) >= starts[place]) & (pl.program_id(0) < starts[place + 1]))
        def _(place=place):
            body(place)


def assemble_kernel(place_ref, *refs):
    out_ref = refs[-1]
    slot = place_ref[1 + pl.program_id(0)]
    for k, ref in enumerate(refs[:-1]):

        @pl.when(slot == k)
        def _(ref=ref):
            out_ref[...] = ref[...].astype(F32)


def assemble(c, q_rows, slots):
    n, width = slots[0].shape
    count = len(slots)
    step = math.gcd(256, q_rows)
    q_steps, d_steps = q_rows // step, (n - q_rows) // step
    turns, owners = [], []
    for base, steps in ((0, q_steps), (q_steps, d_steps)):
        for owner in range(count):
            turns += [base + turn for turn in range(steps)]
            owners += [owner] * steps
    places = jnp.concatenate([c.reshape(1), (c - jnp.array(owners)) % count]).astype(jnp.int32)

    def turn_of(j, p):
        turn = jnp.where(j < count * q_steps, j % q_steps, q_steps + (j - count * q_steps) % d_steps)
        return turn, 0

    return call(
        assemble_kernel, "assemble", (len(turns),),
        [pl.BlockSpec((step, width), turn_of)] * count,
        [pl.BlockSpec((step, width), lambda j, p: (j, 0))],
        [shaped(F32, n * count, width)], (places, *slots), 0, prefetch=1,
    )[0]


def pass_on_kernel(in_ref, out_ref):
    out_ref[...] = in_ref[...]


def pass_on(array):
    spec = held(array.shape)
    return call(
        pass_on_kernel, "pass_on", (1,), [spec], [pl.BlockSpec(array.shape, lambda *_: (0,) * array.ndim)],
        [shaped(array.dtype, *array.shape)], (array,), 0,
    )[0]


def fold_kernel(starts, inner, place_ref, *refs):
    groups = len(starts) - 1

    def one_group(place):
        total = refs[place][0] + refs[groups + place][0].astype(F32)
        put_halves(total, inner, place_ref[0], refs[2 * groups :])

    for_group(starts, one_group)


def fold(side, owns, arrived, inner):
    _, rows, m = owns[0].shape
    chunk = min(1024, m)
    starts = [0]
    for own in owns:
        starts.append(starts[-1] + own.shape[0])

    def spec(size):
        return pl.BlockSpec((1, size, chunk), lambda j, i, p: (j, 0, i))

    half = rows // 2
    specs = [
        pl.BlockSpec((1, rows, chunk), grouped_index(starts, place, m // chunk))
        for place in range(len(owns))
    ]
    return call(
        functools.partial(fold_kernel, starts, inner), "fold", (starts[-1], m // chunk),
        specs + specs, [spec(half), spec(half)],
        [shaped(BF16, starts[-1], half, m), shaped(F32, starts[-1], half, m)],
        (side.reshape(1), *owns, *arrived), 0, prefetch=1,
    )


SEGMENTS = 8
ATTENTION_LANES = 128


def half_lanes(block, head, other):
    lane = lax.broadcasted_iota(jnp.int32, block.shape, 1)
    return jnp.where((lane >= DH) == (head == 1), block, other)


def scaled(block):
    return (block.astype(F32) * DH**-0.5).astype(BF16)


def three_terms(value):
    high = value.astype(BF16).astype(F32)
    middle = (value - high).astype(BF16).astype(F32)
    return high, middle, value - high - middle


def for_spans(span_ref, tiles, body):
    @pl.loop(0, tiles)
    def _(step):
        low, high = span_ref[step], span_ref[tiles + step]
        for count in range(1, tiles + 1):

            @pl.when(high - low == count)
            def _(count=count):
                body(step, low, count)


def attention_forward_kernel(
    span_ref, qkv_ref, ext_k_ref, ext_q_ref, out_ref, rest_ref, ext_ref,
    keys_ref, queries_ref, *, tile,
):
    n = ext_k_ref.shape[0]
    tiles = n // tile
    pairs = qkv_ref.shape[2] // 128

    def lanes(pair):
        return slice(pair * 128, pair * 128 + 128)

    for pair in range(pairs):
        query = scaled(qkv_ref[0, :, lanes(pair)])
        for half in range(2):
            keys_ref[2 * pair + half] = half_lanes(qkv_ref[1, :, lanes(pair)], half, ext_k_ref[...])
            queries_ref[2 * pair + half] = half_lanes(query, half, ext_q_ref[...])

    def attend(step, low, count):
        rows = pl.ds(pl.multiple_of(step * tile, tile), tile)
        window = pl.ds(pl.multiple_of(low * tile, tile), count * tile)
        lane = lax.broadcasted_iota(jnp.int32, (tile, 128), 1)
        for pair in range(pairs):
            at = lanes(pair)
            outs, extra = [], ext_q_ref[rows, :].astype(F32)
            for half in range(2):
                head = 2 * pair + half
                logits = mm(queries_ref[head, rows, :], keys_ref[head, window, :], NT)
                top = jnp.max(logits, axis=1, keepdims=True)
                weights = jnp.exp(logits - top)
                mass = jnp.sum(weights, axis=1, keepdims=True)
                probs = (weights * (1.0 / mass)).astype(BF16)
                outs.append(mm(probs, qkv_ref[2, window, at]))
                first = SEGMENTS + DH * (1 - half)
                for place, term in enumerate(three_terms(-(top + jnp.log(mass)))):
                    extra = jnp.where(lane == first + place, term, extra)
            out = jnp.where(lane < DH, outs[0], outs[1])
            out_ref[rows, at] = out.astype(BF16)
            rest_ref[rows, at] = (out - out.astype(BF16).astype(F32)).astype(BF16)
            ext_ref[rows, at] = extra.astype(BF16)

    for_spans(span_ref, tiles, attend)


def attention_forward(spans, qkv, ext_k, ext_q, tile):
    _, n, width = qkv.shape
    span = min(width, ATTENTION_LANES)
    wide = pl.BlockSpec((n, span), lambda i, *_: (0, i))
    heads = pltpu.VMEM((span // DH, n, 128), BF16)
    return call(
        functools.partial(attention_forward_kernel, tile=tile), "attention_forward",
        (width // span,),
        [pl.BlockSpec((3, n, span), lambda i, *_: (0, 0, i)), held((n, 128)), held((n, 128))],
        [wide, wide, wide],
        [shaped(BF16, n, width)] * 3,
        (spans, qkv, ext_k, ext_q), 0, prefetch=1, scratch=[heads, heads],
    )


def attention_backward_kernel(
    span_ref, qkv_ref, ext_ref, att_ref, rest_ref, grad_ref, ext_k_ref, cos_ref, sin_ref,
    out_ref, sum_ref,
    keys_ref, turned_ref, values_ref, queries_ref, plain_ref, grads_ref, plain_grads_ref,
    dq_ref, dk_ref, dv_ref, *, tile,
):
    n = ext_k_ref.shape[0]
    tiles = n // tile
    pairs = qkv_ref.shape[2] // 128
    heads = range(2 * pairs)

    def lanes(head):
        return slice(head // 2 * 128, head // 2 * 128 + 128)

    def own_rows(head):
        return slice(head % 2 * DH, head % 2 * DH + DH)

    def rows(step):
        return pl.ds(pl.multiple_of(step * tile, tile), tile)

    @pl.loop(0, tiles)
    def _(step):
        at = rows(step)
        zeros = jnp.zeros((tile, 128), BF16)
        lane = lax.broadcasted_iota(jnp.int32, (tile, 128), 1)
        ext_k = ext_k_ref[at, :]
        for pair in range(pairs):
            cut = lanes(2 * pair)
            grad = grad_ref[at, cut]
            out = att_ref[at, cut].astype(F32) + rest_ref[at, cut].astype(F32)
            product = grad.astype(F32) * out
            query = scaled(qkv_ref[0, at, cut])
            turned_ref[pair, :, at] = scaled(qkv_ref[1, at, cut]).astype(F32).T.astype(BF16)
            for half in range(2):
                head = 2 * pair + half
                keys_ref[head, at, :] = half_lanes(qkv_ref[1, at, cut], half, ext_k)
                values_ref[head, at, :] = half_lanes(qkv_ref[2, at, cut], half, ext_k)
                whole = half_lanes(query, half, ext_ref[at, cut])
                queries_ref[head, step] = whole.astype(F32).T.astype(BF16)
                plain_ref[head, at, :] = half_lanes(query, half, zeros)
                plain_grads_ref[head, at, :] = half_lanes(grad, half, zeros)
                inner = jnp.sum(half_lanes(product, half, 0.0), axis=1, keepdims=True)
                extra = jnp.zeros((tile, 128), F32)
                for place, term in enumerate(three_terms(-inner)):
                    extra = jnp.where((lane & (DH - 1)) == SEGMENTS + place, term, extra)
                whole = half_lanes(grad.astype(F32), half, extra)
                grads_ref[head, step] = whole.T.astype(BF16)

    dk_ref[...] = jnp.zeros(dk_ref.shape, F32)
    dv_ref[...] = jnp.zeros(dv_ref.shape, F32)

    def pull(step, low, count):
        at = rows(step)
        window = pl.ds(pl.multiple_of(low * tile, tile), count * tile)
        for pair in range(pairs):
            probs, slopes, dq = [], [], []
            both = range(2 * pair, 2 * pair + 2)
            for head in both:
                weights = jnp.exp(mm(keys_ref[head, window, :], queries_ref[head, step]))
                flow = mm(values_ref[head, window, :], grads_ref[head, step])
                slope = (weights * flow).astype(BF16)
                probs.append(weights.astype(BF16))
                slopes.append(slope)
                dq.append(mm(turned_ref[pair, own_rows(head), window], slope))
            plain = jnp.concatenate([plain_ref[h, at, :] for h in both], axis=0)
            grads = jnp.concatenate([plain_grads_ref[h, at, :] for h in both], axis=0)
            cut = lanes(2 * pair)
            dv_ref[window, cut] += mm(jnp.concatenate(probs, axis=1), grads)
            dk_ref[window, cut] += mm(jnp.concatenate(slopes, axis=1), plain)
            dq_ref[at, cut] = jnp.concatenate(dq, axis=0).T

    for_spans(span_ref, tiles, pull)

    def finish(step, sums):
        cosine, sine = cos_ref[rows(step), :], sin_ref[rows(step), :]
        added = []
        for which, src in enumerate((dq_ref, dk_ref, dv_ref)):
            for pair in range(pairs):
                at = lanes(2 * pair)
                block = src[rows(step), at]
                if which < 2:
                    block = block * cosine - swap_halves(block) * sine
                low = block.astype(BF16)
                out_ref[which, rows(step), at] = low
                total = jnp.sum(low.astype(F32), axis=0, keepdims=True)
                added.append(sums[which * pairs + pair] + total)
        return tuple(added)

    zero = jnp.zeros((1, 128), F32)
    sums = lax.fori_loop(0, tiles, finish, (zero,) * (3 * pairs))
    sums = [jnp.concatenate(sums[w * pairs : (w + 1) * pairs], axis=1) for w in range(3)]
    sum_ref[...] = jnp.concatenate(sums + [jnp.zeros((5, pairs * 128), F32)], axis=0)


def attention_backward(
    spans, qkv, ext, attended, rest, grads, ext_k, cosine, sine, tile
):
    _, n, width = qkv.shape
    span = min(width, ATTENTION_LANES)
    wide = pl.BlockSpec((n, span), lambda i, *_: (0, i))
    three = pl.BlockSpec((3, n, span), lambda i, *_: (0, 0, i))
    tiles, pairs = n // tile, span // 128
    heads = pltpu.VMEM((2 * pairs, n, 128), BF16)
    turned = pltpu.VMEM((2 * pairs, tiles, 128, tile), BF16)
    return call(
        functools.partial(attention_backward_kernel, tile=tile), "attention_backward",
        (width // span,),
        [three, wide, wide, wide, wide, held((n, 128)), held((n, 128)), held((n, 128))],
        [three, pl.BlockSpec((8, span), lambda i, *_: (0, i))],
        [shaped(BF16, 3, n, width), shaped(F32, 8, width)],
        (spans, qkv, ext, attended, rest, grads, ext_k, cosine, sine), 0,
        prefetch=1,
        scratch=[
            heads, pltpu.VMEM((pairs, 128, n), BF16), heads, turned, heads, turned, heads,
        ] + [pltpu.VMEM((n, span), F32)] * 3,
    )


STRIP = 32


def token_sums(width, queries):
    token = lax.broadcasted_iota(jnp.int32, (width, queries), 0) // QLEN
    return token == lax.broadcasted_iota(jnp.int32, (width, queries), 1)


def score_kernel(low_ref, high_ref, doc_ref, query_ref, pick_ref, out_ref, sum_ref, total_ref):
    group = pl.program_id(0)
    docs, width = pick_ref.shape[1:]
    doc_rows = doc_ref.shape[0]
    strips = doc_rows // STRIP
    chunk = min(256, doc_rows)
    row = lax.broadcasted_iota(jnp.int32, (STRIP, width), 0)
    sum_ref[...] = jnp.zeros(sum_ref.shape, F32)

    def add_strip(sim, first, doc, pick):
        kept = jnp.where(row == pick - first, sim, 0.0)
        sum_ref[pl.ds(doc, 1)] += jnp.sum(kept.reshape(1, STRIP // 8, 8, width), axis=1)

    for start in range(0, doc_rows, chunk):
        sims = mm(doc_ref[start : start + chunk, :], query_ref[...], NT)
        for first in range(0, chunk, STRIP):
            place = group * strips + (start + first) // STRIP
            low, high = low_ref[place], high_ref[place]
            sim = sims[first : first + STRIP]
            add_strip(sim, start + first, low, pick_ref[0, pl.ds(low, 1), :])
            pick = jnp.where(high > low, pick_ref[0, pl.ds(high, 1), :], -1)
            add_strip(sim, start + first, high, pick)

    @pl.loop(0, strips)
    def _(strip):
        low, high = low_ref[group * strips + strip], high_ref[group * strips + strip]

        @pl.when(high > low + 1)
        def _():
            first = pl.multiple_of(strip * STRIP, STRIP)
            sim = mm(doc_ref[pl.ds(first, STRIP), :], query_ref[...], NT)

            @pl.loop(low + 1, high)
            def _(doc):
                add_strip(sim, first, doc, pick_ref[0, pl.ds(doc, 1), :])

    total_ref[group] = jnp.sum(sum_ref[...], axis=1)

    @pl.when(group == pl.num_programs(0) - 1)
    def _():
        spread = token_sums(width, out_ref.shape[1]).astype(F32).astype(BF16)
        total = jnp.concatenate([total_ref[g] for g in range(total_ref.shape[0])], axis=0)
        out_ref[...] = sum(mm(term.astype(BF16), spread) for term in three_terms(total))


def score_grad_kernel(
    low_ref, high_ref, doc_ref, query_ref, pick_ref, weight_ref, doc_out, query_out,
    sparse_ref, token_ref,
):
    group = pl.program_id(0)
    docs, width = pick_ref.shape[1:]
    doc_rows = doc_ref.shape[0]
    strips = doc_rows // STRIP
    chunk = min(256, doc_rows)
    row = lax.broadcasted_iota(jnp.int32, (STRIP, width), 0)

    def fill(held, first, doc, pick):
        return jnp.where(row == pick - first, token_ref[group, pl.ds(doc, 1), :], held)

    @pl.when(group == 0)
    def _():
        query_out[...] = jnp.zeros_like(query_out)
        spread = token_sums(width, weight_ref.shape[1]).astype(F32).astype(BF16)
        weights = mm(weight_ref[...].astype(BF16), spread, NT)
        for g in range(token_ref.shape[0]):
            token_ref[g] = weights[g * docs : (g + 1) * docs]

    total = None
    for start in range(0, doc_rows, chunk):
        for first in range(start, start + chunk, STRIP):
            place = group * strips + first // STRIP
            low, high = low_ref[place], high_ref[place]
            held = fill(jnp.zeros((STRIP, width), F32), first, low, pick_ref[0, pl.ds(low, 1), :])
            pick = jnp.where(high > low, pick_ref[0, pl.ds(high, 1), :], -1)
            sparse_ref[first : first + STRIP, :] = fill(held, first, high, pick).astype(BF16)
        sparse = sparse_ref[start : start + chunk, :]
        doc_out[start : start + chunk, :] = mm(sparse, query_ref[...])
        turned = doc_ref[start : start + chunk, :].astype(F32).T.astype(BF16)
        part = mm(turned, sparse)
        total = part if total is None else total + part
    query_out[...] += total

    @pl.loop(0, strips)
    def _(strip):
        low, high = low_ref[group * strips + strip], high_ref[group * strips + strip]

        @pl.when(high > low + 1)
        def _():
            first = pl.multiple_of(strip * STRIP, STRIP)
            held = lax.fori_loop(
                low + 1,
                high,
                lambda doc, held: fill(held, first, doc, pick_ref[0, pl.ds(doc, 1), :]),
                jnp.zeros((STRIP, width), F32),
            ).astype(BF16)
            doc_out[pl.ds(first, STRIP), :] += mm(held, query_ref[...])
            turned = doc_ref[pl.ds(first, STRIP), :].astype(F32).T.astype(BF16)
            query_out[...] += mm(turned, held)


def score_specs(doc_tile, query_tile, picks):
    groups, docs, width = picks.shape
    doc_rows = doc_tile.shape[0] // groups
    return (
        pl.BlockSpec((doc_rows, 128), lambda i, *_: (i, 0)),
        held(query_tile.shape),
        pl.BlockSpec((1, docs, width), lambda i, *_: (i, 0, 0)),
    )


def score_forward(lows, highs, doc_tile, query_tile, picks):
    groups, docs, width = picks.shape
    queries = width // QLEN
    doc_spec, query_spec, pick_spec = score_specs(doc_tile, query_tile, picks)
    return call(
        score_kernel, "score_forward", (groups,),
        [doc_spec, query_spec, pick_spec],
        [pl.BlockSpec((groups * docs, queries), lambda i, *_: (0, 0))],
        [shaped(F32, groups * docs, queries)],
        (lows, highs, doc_tile, query_tile, picks), 2 * doc_tile.shape[0] * width * 128,
        prefetch=2,
        scratch=[pltpu.VMEM((docs, 8, width), F32), pltpu.VMEM((groups, docs, width), F32)],
    )[0]


def score_backward(lows, highs, doc_tile, query_tile, picks, weights):
    groups, docs, width = picks.shape
    doc_spec, query_spec, pick_spec = score_specs(doc_tile, query_tile, picks)
    return call(
        score_grad_kernel, "score_backward", (groups,),
        [doc_spec, query_spec, pick_spec, held(weights.shape)],
        [doc_spec, pl.BlockSpec((128, width), lambda i, *_: (0, 0))],
        [shaped(F32, *doc_tile.shape), shaped(F32, 128, width)],
        (lows, highs, doc_tile, query_tile, picks, weights), 4 * doc_tile.shape[0] * width * 128,
        prefetch=2,
        scratch=[
            pltpu.VMEM((doc_tile.shape[0] // groups, width), BF16),
            pltpu.VMEM((groups, docs, width), F32),
        ],
    )


def rotary_tables(position):
    half_size = DH // 2
    frequency = jnp.exp(
        jnp.arange(half_size, dtype=F32) * (-2.0 * math.log(10000.0) / DH)
    )
    angles = position.astype(F32)[:, None] * frequency[None, :]
    cosine, sine = jnp.cos(angles), jnp.sin(angles)
    return (
        jnp.concatenate([cosine] * 4, axis=1),
        jnp.concatenate([-sine, sine, -sine, sine], axis=1),
    )


def on_device(
    tokens,
    doc_lengths,
    match_picks,
    labels,
    w_qkv,
    b_qkv,
    w_out,
    b_out,
    ln1_gain,
    ln1_bias,
    w_up,
    b_up,
    w_down,
    b_down,
    ln2_gain,
    ln2_bias,
    w_proj,
    log_scale,
):
    Order.last = ()
    C = lax.axis_size("cols")
    R = lax.axis_size("rows")
    c = lax.axis_index("cols")
    r = lax.axis_index("rows")
    width = tokens.shape[1]
    D = width * C
    Q = ROW_LEN // C
    DS = (tokens.shape[0] - ROW_LEN) // C
    n = Q + DS
    tile = math.gcd(256, math.gcd(Q, DS))

    def shift_cols(value, k):
        return lax.ppermute(value, "cols", [(i, (i + k) % C) for i in range(C)])

    def swap_rows(value, bit):
        return lax.ppermute(value, "rows", [(i, i ^ bit) for i in range(R)])

    def in_order(slots):
        if len(slots) == 1:
            return slots
        if len(slots) == 2:
            return [lax.select(c == 0, slots[0], slots[1]), lax.select(c == 0, slots[1], slots[0])]
        stacked = jnp.stack(slots)
        return [
            lax.dynamic_index_in_dim(stacked, (c - j) % C, 0, keepdims=False) for j in range(C)
        ]

    pack = [b_qkv.reshape(-1), b_up, b_out, ln1_gain, ln1_bias, b_down, ln2_gain, ln2_bias]
    ends = [0]
    for vector in pack:
        ends.append(ends[-1] + vector.shape[0])
    packed = jnp.concatenate(pack)

    def gather_pieces(pieces):
        return [lax.all_gather(piece, "rows", axis=0, tiled=True) for piece in pieces]

    late_weights = (w_out, w_up, w_down)
    late_pieces = [
        lax.dynamic_index_in_dim(w.reshape(R, -1, w.shape[1]), r, 0, keepdims=False)
        for w in late_weights
    ]
    if C == 2:
        x, qkv_other, proj_other, pack_other = start_up(
            R, (Q, DS, ROW_LEN), tokens, w_qkv, w_proj, packed.reshape(8, -1)
        )
        wqkv_slots = [w_qkv, qkv_other]
        wproj = jnp.concatenate(in_order([w_proj, proj_other]), axis=0)
        packs = [packed, pack_other.reshape(-1)]
    else:
        parts = jnp.concatenate(
            [tokens[:ROW_LEN].reshape(C, Q, width), tokens[ROW_LEN:].reshape(C, DS, width)], axis=1
        )

        def part(k):
            return lax.dynamic_index_in_dim(parts, (c + k) % C, 0, keepdims=False)

        x = jnp.concatenate(
            in_order([part(0)] + [shift_cols(part(k), k) for k in range(1, C)]), axis=1
        )

        def gather_slots(shard):
            flat = shard.reshape(-1, shard.shape[-1])
            piece = lax.dynamic_index_in_dim(
                flat.reshape(R, flat.shape[0] // R, flat.shape[1]), r, 0, keepdims=False
            )
            others = gather_pieces([shift_cols(piece, k) for k in range(1, C)])
            return [shard] + [other.reshape(shard.shape) for other in others]

        wqkv_slots = gather_slots(w_qkv)
        wproj = jnp.concatenate(
            in_order([w_proj] + [shift_cols(w_proj, k) for k in range(1, C)]), axis=0
        )
        packs = [packed] + [shift_cols(packed, k) for k in range(1, C)]

    ordered_packs = in_order(packs)

    def of_slot(which, k):
        return packs[k][ends[which] : ends[which + 1]]

    def whole(which):
        return jnp.concatenate([p[ends[which] : ends[which + 1]] for p in ordered_packs])

    bqkv_slots = [of_slot(0, k).reshape(b_qkv.shape) for k in range(C)]
    bup_slots = [of_slot(1, k)[None, :] for k in range(C)]
    bout, gain1, bias1, bdown, gain2, bias2 = [whole(which) for which in range(2, 8)]
    zero_row = jnp.zeros_like(bout)
    vectors = jnp.stack([bout, gain1, bias1, bdown, gain2, bias2, zero_row, zero_row])

    own_sizes = lax.dynamic_index_in_dim(
        lax.dynamic_index_in_dim(doc_lengths, r, 0, keepdims=False), c, 0, keepdims=False
    )
    own_ends = jnp.cumsum(own_sizes)
    places = jnp.arange(DS, dtype=jnp.int32)
    passed = places[:, None] >= own_ends[None, :]
    slot_id = jnp.sum(passed.astype(jnp.int32), axis=1)
    slot_begin = jnp.sum(jnp.where(passed, own_sizes[None, :], 0), axis=1)
    query_places = jnp.arange(Q, dtype=jnp.int32)
    position = jnp.concatenate([query_places % QLEN, places - slot_begin])
    cosine, sine = rotary_tables(position)
    segment = jnp.concatenate([(query_places // QLEN) % SEGMENTS, slot_id])
    lane = jnp.arange(128, dtype=jnp.int32)[None, :] % DH
    same = segment[:, None] == lane
    ext_k = (same | ((lane >= SEGMENTS) & (lane < SEGMENTS + 3))).astype(BF16)
    ext_q = jnp.where((lane < SEGMENTS) & ~same, -1e30, 0.0).astype(BF16)
    q_tiles, d_tiles = Q // tile, DS // tile
    steps = jnp.arange(q_tiles, dtype=jnp.int32)
    first_rows = jnp.arange(d_tiles, dtype=jnp.int32) * tile
    is_passed = first_rows[:, None] >= own_ends[None, :]
    low_rows = jnp.sum(jnp.where(is_passed, own_sizes[None, :], 0), axis=1)
    last_passed = (first_rows + tile - 1)[:, None] >= own_ends[None, :]
    high_rows = jnp.min(jnp.where(last_passed, DS, own_ends[None, :]), axis=1)
    spans = jnp.concatenate(
        [steps, q_tiles + low_rows // tile, steps + 1, q_tiles + (high_rows + tile - 1) // tile]
    ).astype(jnp.int32)

    queries_here, tile_docs, _ = match_picks.shape
    docs = own_sizes.shape[0]
    sizes = lax.dynamic_index_in_dim(doc_lengths, c, 1, keepdims=False)
    doc_ends = jnp.cumsum(sizes, axis=1)
    begins = doc_ends - sizes
    picks = jnp.transpose(match_picks, (1, 0, 2)).reshape(tile_docs, queries_here * QLEN)
    picks = begins.reshape(-1)[:, None] + picks % sizes.reshape(-1)[:, None]
    picks = picks.reshape(R, docs, queries_here * QLEN)
    strip_rows = (jnp.arange(DS // STRIP, dtype=jnp.int32) * STRIP)[None, :, None]
    lows = jnp.sum(doc_ends[:, None, :] <= strip_rows, axis=2).astype(jnp.int32).reshape(-1)
    highs = jnp.sum(begins[:, None, :] < strip_rows + STRIP, axis=2).astype(jnp.int32) - 1
    highs = highs.reshape(-1)

    qkv, attended, rests, exts = [], [], [], []
    for k in range(C):
        first = (picks, lows, highs) if k == 0 else ()
        qkv.append(project_qkv(x, wqkv_slots[k], bqkv_slots[k], cosine, sine, first))
        if k == 0:
            flat = jnp.concatenate([piece.reshape(-1, D) for piece in late_pieces])
            flat, _ = lax.optimization_barrier((flat, x))
            arrived = [shift_cols(flat, j) for j in range(1, C)]
            arrived = [pass_on(a) for a in arrived]
            ends_of = [0]
            for piece in late_pieces:
                ends_of.append(ends_of[-1] + piece.size // D)
            wout_slots, wup_slots, wdown_slots = (
                [own] + gather_pieces([
                    a[ends_of[j] : ends_of[j + 1]].reshape(late_pieces[j].shape) for a in arrived
                ])
                for j, own in enumerate(late_weights)
            )
            wout_slots, wup_slots, wdown_slots = (
                [slot.reshape(own.shape) for slot in slots_of]
                for slots_of, own in zip((wout_slots, wup_slots, wdown_slots), late_weights)
            )
        out, rest, ext = attention_forward(spans, qkv[k], ext_k, ext_q, tile)
        attended.append(out)
        rests.append(rest)
        exts.append(ext)
    normed_one, inverse_one, hidden_low, hidden_t = out_and_norm(x, vectors, attended, wout_slots)
    active, slopes = zip(*[up_and_gelu(hidden_low, wup_slots[k], bup_slots[k]) for k in range(C)])
    normed_two, inverse_two, output_low, unit, unit_low, unit_inverse = down_and_norm(
        normed_one, vectors, wproj, active, wdown_slots
    )

    doc_tile = gather_rows(R, unit_low[Q:]).reshape(R * DS, 128)
    query_tile = jnp.concatenate(
        in_order([unit_low[:Q]] + [shift_cols(unit_low[:Q], k) for k in range(1, C)]), axis=0
    )
    sims = score_forward(lows, highs, doc_tile, query_tile, picks)
    scores = sims.T

    scale = jnp.exp(log_scale[0])
    z = scale * scores
    row_top = jnp.max(z, axis=1)
    row_mass = jnp.sum(jnp.exp(z - row_top[:, None]), axis=1)
    is_label = (
        jnp.arange(tile_docs, dtype=jnp.int32)[None, :] == (labels - c * tile_docs)[:, None]
    )
    chosen = jnp.sum(jnp.where(is_label, z, 0.0), axis=1)
    own_stats = jnp.stack([row_top, row_mass, chosen])
    stats = jnp.stack([own_stats] + [shift_cols(own_stats, k) for k in range(1, C)])
    top_all = jnp.max(stats[:, 0], axis=0)
    mass_all = jnp.sum(stats[:, 1] * jnp.exp(stats[:, 0] - top_all), axis=0)
    log_total = top_all + jnp.log(mass_all)
    loss = log_total - jnp.sum(stats[:, 2], axis=0)
    dz = (jnp.exp(z - log_total[:, None]) - is_label.astype(F32)) / (queries_here * R)
    scale_part = jnp.sum(dz * z)
    dscores = (scale * dz).T
    doc_grad, query_grad_t = score_backward(lows, highs, doc_tile, query_tile, picks, dscores)
    query_parts = query_grad_t.T.reshape(C, Q, 128)

    def query_part(k):
        return lax.dynamic_index_in_dim(query_parts, (c + k) % C, 0, keepdims=False)

    query_grad = query_part(0)
    for k in range(1, C):
        query_grad = query_grad + shift_cols(query_part(k), k)

    doc_sum = scatter_rows(doc_grad.reshape(R, DS, 128))
    unit_grad = jnp.concatenate([query_grad, doc_sum], axis=0)

    core = r % 2
    slots_back = range(C - 1, -1, -1)
    share = D // R
    x_bit, *z_bits = [1 << b for b in range(1, R.bit_length() - 1)]

    def side_of(bit):
        return ((r // bit) % 2).astype(jnp.int32)

    def halves_of(left_t):
        return left_t.reshape(R // 2, 2, share, n)

    def rows_of(left, side):
        return lax.dynamic_index_in_dim(left, side, 1, keepdims=False).reshape(-1, n)

    def send_plain(left, right):
        part = mm(rows_of(left, 1 - core), right).astype(BF16)
        Order.last += (part,)
        return swap_rows(part, 1)

    def keep_plain(left, right, arrived, k):
        kept = mm(rows_of(left, core), right) + arrived.astype(F32)
        if k > 0:
            kept = kept.astype(BF16)
        Order.last += (kept,)
        return kept[None] if k == 0 else shift_cols(kept, C - k)[None]

    def next_fold(states, bit, inner):
        send, keep = fold(side_of(bit), [s[0] for s in states], [s[1] for s in states], inner)
        return keep, swap_rows(send, bit)

    def cols_state(kept):
        rest = kept[1]
        for other in kept[2:]:
            rest = rest.astype(F32) + other.astype(F32)
        return kept[0], rest

    embed_grad, resid_two_grad, branch, branch_t, head_sums = head_pull(
        unit_grad, unit, unit_inverse, wproj, normed_two, inverse_two, vectors
    )
    down_left, down_right = halves_of(branch_t), active
    pre_grads, up_sums, down_kept = [None] * C, [None] * C, [None] * C
    down_arrived = [None] * C
    for k in slots_back:
        down_arrived[k] = send_plain(down_left, down_right[k])
    for k in slots_back:
        pre_grads[k], up_sums[k] = up_pull(branch, wdown_slots[k], slopes[k])
        if k > 0:
            down_kept[k] = keep_plain(down_left, down_right[k], down_arrived[k], k)
    up_left, up_right = halves_of(hidden_t), pre_grads
    up_arrived, up_kept = [None] * C, [None] * C
    for k in slots_back:
        up_arrived[k] = send_plain(up_left, up_right[k])
    down_kept[0] = keep_plain(down_left, down_right[0], down_arrived[0], 0)
    for k in slots_back[:-1]:
        up_kept[k] = keep_plain(up_left, up_right[k], up_arrived[k], k)
    resid_one_grad, branch_one_t, hidden_sums, *attended_grads = hidden_pull(
        resid_two_grad, normed_one, inverse_one, vectors, pre_grads, wup_slots, wout_slots
    )
    up_kept[0] = keep_plain(up_left, up_right[0], up_arrived[0], 0)
    mixed_grads, mixed_sums = [None] * C, [None] * C
    def gather_small():
        proj_grad = mm(embed_grad, output_low, TN).reshape(R, -1, C, width)
        def cut(values, slot_rows):
            return values.reshape(slot_rows, R, -1)

        own_order = [(c - k) % C for k in range(C)]
        canonical = jnp.stack(
            [hidden_sums[0], hidden_sums[1], hidden_sums[2], head_sums[0], head_sums[1], head_sums[2]]
        ).reshape(6, C, R, -1)
        slots_small = []
        for k in range(C):
            rows = [mixed_sums[k][j].reshape(R, -1) for j in range(3)]
            rows.append(up_sums[k][0].reshape(R, -1))
            rows += [
                lax.dynamic_index_in_dim(canonical[j], own_order[k], 0, keepdims=False)
                for j in range(6)
            ]
            own_proj_grad = lax.dynamic_index_in_dim(proj_grad, own_order[k], 2, keepdims=False)
            rows.append(own_proj_grad.reshape(R, -1))
            rows.append(jnp.broadcast_to(scale_part, (R, 1)))
            slots_small.append(jnp.concatenate(rows, axis=1))
        return jnp.stack(slots_small, axis=1)

    def pull_attention(k):
        mixed_grads[k], mixed_sums[k] = attention_backward(
            spans, qkv[k], exts[k], attended[k], rests[k], attended_grads[k], ext_k, cosine, sine,
            tile,
        )

    for k in slots_back[:-1]:
        pull_attention(k)
    wide_state = next_fold([cols_state(down_kept), cols_state(up_kept)], x_bit, share)
    pull_attention(0)
    sent = [
        shift_cols(token_pull((c + k) % C, resid_one_grad, mixed_grads, wqkv_slots, BF16), k)
        for k in range(1, C)
    ]
    own_tokens = token_pull(c, resid_one_grad, mixed_grads, wqkv_slots, F32)
    late_grad, wide_grad = late_sums(
        R, C, halves_of(x.T), halves_of(branch_one_t), mixed_grads, attended, *wide_state
    )
    small = small_sum(R, C, gather_small())
    tokens_grad = assemble(c, Q, [own_tokens] + sent)
    qkv_grad, out_grad = late_grad[:3], late_grad[3]
    down_grad, up_grad = wide_grad
    one = D // (C * R)
    up_part = bup_slots[0].shape[1] // R
    bounds = [3 * one, 3 * one + up_part]
    for _ in range(6):
        bounds.append(bounds[-1] + one)
    pieces = [small[a:b] for a, b in zip(bounds[:-1], bounds[1:])]
    bup_out, bout_out, gain1_out, bias1_out, bdown_out, gain2_out, bias2_out = pieces
    return (
        scores,
        loss,
        tokens_grad,
        qkv_grad,
        small[: bounds[0]].reshape(3, one),
        out_grad.T,
        bout_out,
        gain1_out,
        bias1_out,
        up_grad,
        bup_out,
        down_grad.T,
        bdown_out,
        gain2_out,
        bias2_out,
        small[bounds[-1] : -1].reshape(-1, width).T,
        small[-1:],
    )


def solution(mesh):
    in_specs = (
        P("rows", "cols"),
        P(),
        P("rows", "cols", None),
        P("rows"),
        P(None, None, "cols"),
        P(None, "cols"),
        P("cols", None),
        P("cols"),
        P("cols"),
        P("cols"),
        P(None, "cols"),
        P("cols"),
        P("cols", None),
        P("cols"),
        P("cols"),
        P("cols"),
        P("cols", None),
        P(),
    )
    out_specs = (
        P("rows", "cols"),
        P("rows"),
        P("rows", "cols"),
        P(None, "rows", "cols"),
        P(None, ("cols", "rows")),
        P("cols", "rows"),
        P(("cols", "rows")),
        P(("cols", "rows")),
        P(("cols", "rows")),
        P("rows", "cols"),
        P(("cols", "rows")),
        P("cols", "rows"),
        P(("cols", "rows")),
        P(("cols", "rows")),
        P(("cols", "rows")),
        P("cols", "rows"),
        P(),
    )
    return jax.shard_map(
        on_device, mesh=mesh, in_specs=in_specs, out_specs=out_specs, check_vma=False
    )
```

```python
import functools
import math

import jax
import jax.numpy as jnp
from jax import lax
from jax.experimental import pallas as pl
from jax.experimental.pallas import tpu as pltpu
from jax.sharding import PartitionSpec as P

DH = 64
QLEN = 32
ROW_LEN = 1024
F32 = jnp.float32
BF16 = jnp.bfloat16
VMEM_LIMIT = 56 * 1024 * 1024
NT = (((1,), (1,)), ((), ()))
NN = (((1,), (0,)), ((), ()))
TN = (((0,), (0,)), ((), ()))


def mm(left, right, dims=NN):
    return lax.dot_general(left, right, dims, preferred_element_type=F32)


def row_step(rows):
    return 512 if rows % 512 == 0 else 128


def parts_of(step):
    size = 256 if step % 256 == 0 else 128
    return [slice(first, first + size) for first in range(0, step, size)]


def held(shape):
    return pl.BlockSpec(shape, lambda *_: (0,) * len(shape), pipeline_mode=pl.Buffered(1))


def shaped(dtype, *shape):
    return jax.ShapeDtypeStruct(shape, dtype)


class Order:
    last = ()


def call(
    body, name, grid, in_specs, out_specs, out_shape, operands, flops, scratch=(), prefetch=0, after=(),
    remote=None,
):
    count = len(operands)
    after = tuple(after) + Order.last

    def wrapped(*refs):
        body(*refs[:count], *refs[count + len(after) :])

    size = sum(math.prod(o.shape) * o.dtype.itemsize for o in list(operands) + list(out_shape))
    if flops == 0:
        size = 1024
    outs = pl.pallas_call(
        wrapped,
        grid_spec=pltpu.PrefetchScalarGridSpec(
            num_scalar_prefetch=prefetch,
            grid=grid,
            in_specs=list(in_specs) + [pl.BlockSpec(memory_space=pl.ANY)] * len(after),
            out_specs=out_specs,
            scratch_shapes=list(scratch),
        ),
        out_shape=out_shape,
        compiler_params=pltpu.CompilerParams(
            vmem_limit_bytes=VMEM_LIMIT, collective_id=remote, has_side_effects=remote is not None
        ),
        cost_estimate=pl.CostEstimate(flops=flops, bytes_accessed=size, transcendentals=0),
        name=name,
    )(*operands, *after)
    Order.last = (min(outs, key=lambda out: out.size * out.dtype.itemsize),)
    return outs


def row_spec(step, width):
    return pl.BlockSpec((step, width), lambda i, *_: (i, 0))


def column_spec(width, step):
    return pl.BlockSpec((width, step), lambda i, *_: (0, i))


MESH = pl.DeviceIdType.MESH
ANYWHERE = pl.BlockSpec(memory_space=pl.ANY)


def side_at(row, bit):
    return (row // bit) % 2


def across(row, bit):
    return row + bit * (1 - 2 * side_at(row, bit))


def flipped(row, bits):
    bit = 1
    while bit <= bits:
        if bits & bit:
            row = across(row, bit)
        bit *= 2
    return row


def greet(devices):
    barrier = pltpu.get_barrier_semaphore()
    for device in devices:
        pl.semaphore_signal(barrier, inc=1, device_id=device, device_id_type=MESH)
    pl.semaphore_wait(barrier, len(devices))


def send(source, target, sent, arrived, device):
    copy = pltpu.make_async_remote_copy(
        src_ref=source,
        dst_ref=target,
        send_sem=sent,
        recv_sem=arrived,
        device_id=device,
        device_id_type=MESH,
    )
    copy.start()
    return copy


def spread_order(count):
    pieces = sorted(range(count), key=lambda piece: (piece.bit_count(), -piece))
    order = []
    for piece in pieces:
        lowest = piece & -piece if piece else count
        bit = lowest // 2
        bits = []
        while bit:
            bits.append(bit)
            bit //= 2
        order.append((piece, bits))
    return order


def weights_kernel(rows, *refs):
    (qkv, proj, pack, qkv_o, proj_o, pack_o), (sent, arrived, wide_sent, wide_arrived) = refs[:6], refs[6:]
    r, c = lax.axis_index("rows"), lax.axis_index("cols")
    partner = {"cols": 1 - c}
    bits = [1 << b for b in range(rows.bit_length() - 1)]
    greet([partner] + [{"rows": across(r, bit)} for bit in bits])
    pairs = [(qkv.at[r], qkv_o.at[r]), (proj, proj_o), (pack, pack_o)]
    copies = [
        send(source, target, sent.at[place], arrived.at[place], partner)
        for place, (source, target) in enumerate(pairs)
    ]
    round_copies = {0: copies[0]}
    for piece, over in spread_order(rows):
        row = flipped(r, piece)
        round_copies[piece].wait_recv()
        for bit in over:
            round_copies[piece | bit] = send(
                qkv_o.at[row], qkv_o.at[row], wide_sent.at[piece | bit], wide_arrived.at[piece | bit],
                {"rows": across(r, bit)},
            )
    for copy in round_copies.values():
        copy.wait_send()
    for copy in copies[1:]:
        copy.wait()


def gather_weights(rows, qkv, proj, pack):
    pieces = qkv.reshape(rows, -1, qkv.shape[-1])
    operands = (pieces, proj, pack)
    qkv_o, proj_o, pack_o = call(
        functools.partial(weights_kernel, rows), "gather_weights", (1,),
        [ANYWHERE] * 3, [ANYWHERE] * 3, [shaped(o.dtype, *o.shape) for o in operands],
        operands, 0, remote=1,
        scratch=[
            pltpu.SemaphoreType.DMA((3,)), pltpu.SemaphoreType.DMA((3,)),
            pltpu.SemaphoreType.DMA((rows,)), pltpu.SemaphoreType.DMA((rows,)),
        ],
    )
    return qkv_o.reshape(qkv.shape), proj_o, pack_o


def gather_kernel(rows, own, out, own_sem, sent, arrived):
    r = lax.axis_index("rows")
    bits = [1 << b for b in range(rows.bit_length() - 1)]
    greet([{"rows": across(r, bit)} for bit in bits])
    local = pltpu.make_async_copy(own, out.at[r], own_sem)
    local.start()
    copies = {}
    size = own.shape[0] // PARTS
    for piece, over in spread_order(rows):
        row = flipped(r, piece)
        for part in range(PARTS):
            at = pl.ds(part * size, size)
            if piece:
                copies[piece, part].wait_recv()
            for bit in over:
                copies[piece | bit, part] = send(
                    out.at[row, at] if piece else own.at[at], out.at[row, at],
                    sent.at[piece | bit, part], arrived.at[piece | bit, part],
                    {"rows": across(r, bit)},
                )
    for copy in copies.values():
        copy.wait_send()
    local.wait()


PARTS = 2


def gather_rows(rows, own):
    return call(
        functools.partial(gather_kernel, rows), "gather_rows", (1,), [ANYWHERE], [ANYWHERE],
        [shaped(own.dtype, rows, *own.shape)], (own,), 0, remote=2,
        scratch=[
            pltpu.SemaphoreType.DMA, pltpu.SemaphoreType.DMA((rows, PARTS)),
            pltpu.SemaphoreType.DMA((rows, PARTS)),
        ],
    )[0]


def scatter_kernel(rows, parts, out, sent, arrived, *buffers):
    r = lax.axis_index("rows")
    bits = [1 << b for b in range(rows.bit_length() - 1)]
    greet([{"rows": across(r, bit)} for bit in bits])
    outgoing, incoming = buffers[: len(bits)], buffers[len(bits) :]
    size = parts.shape[1] // PARTS
    copies = {}

    def total(flips, levels, part):
        row, at = flipped(r, flips), pl.ds(part * size, size)
        value = parts[row, at]
        for level in range(levels):
            copies[level, flips >> (level + 1), part].wait_recv()
            value = value + incoming[level][row // (2 << level), at].astype(F32)
        return value

    for level, bit in enumerate(bits):
        count = rows // (2 << level)
        for turn in sorted(range(count), key=lambda f: tuple(-((f >> b) & 1) for b in range(8))):
            flips = (turn << (level + 1)) | bit
            place = flipped(r, flips) // (2 << level)
            for part in range(PARTS):
                at = pl.ds(part * size, size)
                outgoing[level][place, at] = total(flips, level, part).astype(BF16)
                name = rows - 2 * count + turn
                copies[level, turn, part] = send(
                    outgoing[level].at[place, at], incoming[level].at[place, at],
                    sent.at[name, part], arrived.at[name, part], {"rows": across(r, bit)},
                )
    for part in range(PARTS):
        out[part * size : (part + 1) * size, :] = total(0, len(bits), part)
    for copy in copies.values():
        copy.wait_send()


def scatter_rows(parts):
    rows, height, width = parts.shape
    levels = rows.bit_length() - 1
    buffers = [
        pltpu.VMEM((rows // (2 << level), height, width), BF16) for level in range(levels)
    ]
    return call(
        functools.partial(scatter_kernel, rows), "scatter_rows", (1,), [held(parts.shape)],
        [pl.BlockSpec((height, width), lambda *_: (0, 0))], [shaped(F32, height, width)],
        (parts,), 0, remote=3,
        scratch=[
            pltpu.SemaphoreType.DMA((rows, PARTS)), pltpu.SemaphoreType.DMA((rows, PARTS)),
        ] + buffers + buffers,
    )[0]


def small_sums(rows, cols, parts, out, *refs):
    bits = [1 << b for b in range(rows.bit_length() - 1)]
    sent, arrived = refs[:2]
    core_in, cols_in, totals = refs[2], refs[3], refs[4 : 4 + len(bits)]
    row_ins = refs[4 + len(bits) :]
    r, c = lax.axis_index("rows"), lax.axis_index("cols")
    others = [{"cols": (c + cols - k) % cols} for k in range(1, cols)]
    core = side_at(r, 1)
    copies = {}

    def first():
        copies["core"] = send(
            parts.at[:, 1 - core], core_in, sent.at[0], arrived.at[0], {"rows": across(r, 1)}
        )

    def second():
        copies["core"].wait()
        totals[0][...] = parts[:, core] + core_in[...]
        for k in range(1, cols):
            copies["cols", k] = send(
                totals[0].at[:, k], cols_in.at[k - 1], sent.at[k], arrived.at[k], others[k - 1]
            )

    def third():
        total = totals[0][:, 0]
        for k in range(1, cols):
            copies["cols", k].wait()
            total = total + cols_in[k - 1]
        pass_on(0, total)

    def pass_on(level, total):
        if level == len(bits) - 1:
            out[...] = total[0]
            return
        whole = totals[1 + level]
        whole[...] = total.reshape(whole.shape)
        copies["row", level] = send(
            whole.at[:, 1 - side_at(r, bits[1 + level])], row_ins[level],
            sent.at[cols + level], arrived.at[cols + level],
            {"rows": across(r, bits[1 + level])},
        )

    def later(level):
        copies["row", level].wait()
        pass_on(level + 1, totals[1 + level][:, side_at(r, bits[1 + level])] + row_ins[level][...])

    return [first, second, third] + [
        functools.partial(later, level) for level in range(len(bits) - 1)
    ]


def small_blocks(rows, cols, parts):
    length = parts.shape[2]
    width = -(-length // 1024) * 128
    parts = jnp.pad(parts, ((0, 0), (0, 0), (0, 8 * width - length)))
    parts = parts.reshape(rows // 2, 2, cols, 8, width)
    levels = rows.bit_length() - 1
    heights = [rows >> (level + 1) for level in range(1, levels)]
    scratch = [
        pltpu.SemaphoreType.DMA((cols + levels,)), pltpu.SemaphoreType.DMA((cols + levels,)),
        pltpu.VMEM((rows // 2, cols, 8, width), F32),
        pltpu.VMEM((cols - 1, rows // 2, 8, width), F32),
        pltpu.VMEM((rows // 2, cols, 8, width), F32),
    ]
    scratch += [pltpu.VMEM((height, 2, 8, width), F32) for height in heights]
    scratch += [pltpu.VMEM((height, 8, width), F32) for height in heights]
    return parts, scratch


def late_kernel(rows, cols, *refs):
    tokens_t, branch_t = refs[:2]
    far_rights, far_attended, refs = refs[2 : 2 + cols], refs[2 + cols : 2 + 2 * cols], refs[2 + 2 * cols :]
    (du_own, du_in, small, out, du_out, small_out), refs = refs[:6], refs[6:]
    (rights, right_sem), refs = refs[:2], refs[2:]
    (core_out, core_in, x_out, x_in, kept, cols_out, cols_in), refs = refs[:7], refs[7:]
    r, c = lax.axis_index("rows"), lax.axis_index("cols")
    x_bit, *z_bits = [1 << b for b in range(1, rows.bit_length() - 1)]
    levels = len(z_bits)
    z_out, z_in, z_kept = refs[:levels], refs[levels : 2 * levels], refs[2 * levels : 3 * levels]
    refs = refs[3 * levels :]
    du_z_out, du_z_in, du_kept = refs[:levels], refs[levels : 2 * levels], refs[2 * levels : 3 * levels]
    refs = refs[3 * levels :]
    (core_sem, x_sem, cols_sem, z_sem, du_sem), refs = refs[:5], refs[5:]
    small_steps = small_sums(rows, cols, small, small_out, *refs)
    share = out.shape[1]
    others = [{"cols": (c + cols - k) % cols} for k in range(1, cols)]
    core, x_side = side_at(r, 1), side_at(r, x_bit)
    greet([{"rows": across(r, bit)} for bit in [1, x_bit] + z_bits] + others)
    du_bits = z_bits[1:] + [x_bit]
    chunks = range(4)
    slots = range(cols - 1, -1, -1)
    copies = {}

    def halves(total, side, inner):
        pairs = total.reshape(-1, 2, inner, total.shape[1])
        near = jnp.where(side == 0, pairs[:, 0], pairs[:, 1]).reshape(-1, total.shape[1])
        far = jnp.where(side == 0, pairs[:, 1], pairs[:, 0]).reshape(-1, total.shape[1])
        return near, far

    def product(side, slot, chunk):
        left = (tokens_t if chunk < 3 else branch_t)[:, side]
        return mm(left.reshape(-1, left.shape[-1]), rights[slot, chunk])

    def load(slot, chunk):
        source = far_rights[slot].at[chunk] if chunk < 3 else far_attended[slot]
        return pltpu.make_async_copy(source, rights.at[slot, chunk], right_sem.at[slot, chunk])

    for chunk in chunks:
        for slot in slots:
            load(slot, chunk).start()

    def begin(chunk):
        for slot in slots:
            load(slot, chunk).wait()
            if chunk >= 2:
                copies["core", slot, chunk - 2].wait_send()
            core_out[slot, chunk % 2] = product(1 - core, slot, chunk).astype(BF16)
            copies["core", slot, chunk] = send(
                core_out.at[slot, chunk % 2], core_in.at[slot, chunk],
                core_sem.at[0, slot, chunk], core_sem.at[1, slot, chunk],
                {"rows": across(r, 1)},
            )

    def after_core(chunk):
        for slot in slots:
            total = product(core, slot, chunk)
            copies["core", slot, chunk].wait_recv()
            near, far = halves(total + core_in[slot, chunk].astype(F32), x_side, share)
            x_out[slot, chunk] = far.astype(BF16)
            kept[slot, chunk] = near
            copies["x", slot, chunk] = send(
                x_out.at[slot, chunk], x_in.at[slot, chunk], x_sem.at[0, slot, chunk],
                x_sem.at[1, slot, chunk], {"rows": across(r, x_bit)},
            )

    def after_x(chunk):
        for slot in slots:
            copies["x", slot, chunk].wait_recv()
            total = kept[slot, chunk] + x_in[slot, chunk].astype(F32)
            if slot == 0:
                kept[0, chunk] = total
            else:
                cols_out[slot - 1, chunk] = total.astype(BF16)
                copies["cols", slot, chunk] = send(
                    cols_out.at[slot - 1, chunk], cols_in.at[slot - 1, chunk],
                    cols_sem.at[0, slot - 1, chunk], cols_sem.at[1, slot - 1, chunk],
                    others[slot - 1],
                )

    def after_cols(chunk):
        total = kept[0, chunk]
        for slot in slots[:-1]:
            copies["cols", slot, chunk].wait_recv()
            total = total + cols_in[slot - 1, chunk].astype(F32)
        pass_z(chunk, 0, total)

    def pass_z(chunk, level, total):
        if level == levels:
            out[chunk] = total
            return
        bit = z_bits[level]
        near, far = halves(total, side_at(r, bit), share)
        z_out[level][chunk] = far.astype(BF16)
        z_kept[level][chunk] = near
        copies["z", level, chunk] = send(
            z_out[level].at[chunk], z_in[level].at[chunk], z_sem.at[0, level, chunk],
            z_sem.at[1, level, chunk], {"rows": across(r, bit)},
        )

    def after_z(chunk, level):
        copies["z", level, chunk].wait_recv()
        pass_z(chunk, level + 1, z_kept[level][chunk] + z_in[level][chunk].astype(F32))

    def pass_du(place, level, total):
        if level == levels:
            du_out[place] = total
            return
        bit = du_bits[level]
        near, far = halves(total, side_at(r, bit), share if bit == x_bit else 2 * share)
        du_z_out[level][place] = far.astype(BF16)
        du_kept[level][place] = near
        copies["du", level, place] = send(
            du_z_out[level].at[place], du_z_in[level].at[place], du_sem.at[0, level, place],
            du_sem.at[1, level, place], {"rows": across(r, bit)},
        )

    def after_du(place, level):
        copies["du", level, place].wait_recv()
        pass_du(place, level + 1, du_kept[level][place] + du_z_in[level][place].astype(F32))

    for place in range(2):
        pass_du(place, 0, du_own[place] + du_in[place].astype(F32))
    stages = [(0, begin), (1, after_core), (3, after_x), (4, after_cols)]
    stages += [(5 + level, functools.partial(after_z, level=level)) for level in range(levels)]
    for turn in range(len(chunks) + stages[-1][0]):
        for delay, stage in stages[::-1]:
            if 0 <= turn - delay < len(chunks):
                stage(turn - delay)
        if 3 <= turn < 3 + levels:
            for place in range(2):
                after_du(place, turn - 3)
        if turn >= 1 and small_steps:
            small_steps.pop(0)()
    for step in small_steps:
        step()
    for name, copy in copies.items():
        if name[0] != "core" or name[2] >= 2:
            copy.wait_send()


def late_sums(rows, cols, tokens_t, branch_t, rights, attended, du_own, du_in, small):
    share, n = tokens_t.shape[2:]
    width = attended[0].shape[1]
    wide = du_own.shape[2]
    half, quarter = rows // 2 * share, rows // 4 * share
    levels = rows.bit_length() - 3
    heights = [quarter >> (level + 1) for level in range(levels)]

    def vmem(dtype, *shape):
        return pltpu.VMEM(shape, dtype)

    def pair_of(*shape):
        return pltpu.SemaphoreType.DMA((2,) + shape)

    length = small.shape[2]
    small, small_scratch = small_blocks(rows, cols, small)
    operands = (tokens_t, branch_t, *rights, *attended, du_own, du_in, small)
    scratch = [
        vmem(BF16, cols, 4, n, width), pltpu.SemaphoreType.DMA((cols, 4)),
        vmem(BF16, cols, 2, half, width), vmem(BF16, cols, 4, half, width),
        vmem(BF16, cols, 4, quarter, width), vmem(BF16, cols, 4, quarter, width),
        vmem(F32, cols, 4, quarter, width),
        vmem(BF16, cols - 1, 4, quarter, width), vmem(BF16, cols - 1, 4, quarter, width),
    ]
    for count, size in ((4, width), (2, wide)):
        for dtype in (BF16, BF16, F32):
            scratch += [vmem(dtype, count, height, size) for height in heights]
    scratch += [
        pair_of(cols, 4), pair_of(cols, 4), pair_of(cols - 1, 4), pair_of(levels, 4),
        pair_of(levels, 2),
    ]
    def whole(*shape):
        return pl.BlockSpec(shape, lambda *_: (0,) * len(shape))

    late, wide_sum, small_sum = call(
        functools.partial(late_kernel, rows, cols), "late_sums", (1,),
        [held(tokens_t.shape), held(branch_t.shape)] + [ANYWHERE] * (2 * cols)
        + [held(du_own.shape), held(du_in.shape), held(small.shape)],
        [whole(4, share, width), whole(2, share, wide), whole(*small.shape[3:])],
        [
            shaped(F32, 4, share, width), shaped(F32, 2, share, wide), shaped(F32, *small.shape[3:])
        ],
        operands, 100_000_000_000, remote=5, scratch=scratch + small_scratch,
    )
    return late, wide_sum, small_sum.reshape(-1)[:length]


def swap_halves(block):
    lane = lax.broadcasted_iota(jnp.int32, block.shape, 1)
    return jnp.where((lane & 32) == 0, pltpu.roll(block, 96, 1), pltpu.roll(block, 32, 1))


def qkv_kernel(x_ref, w_ref, b_ref, cos_ref, sin_ref, out_ref):
    which = pl.program_id(0)
    bias = b_ref[pl.ds(which, 1), :]

    @pl.when(which < 2)
    def _():
        for at in parts_of(x_ref.shape[0]):
            mixed = mm(x_ref[at, :], w_ref[0]) + bias
            for first in range(0, mixed.shape[1], 128):
                block = mixed[:, first : first + 128]
                turned = block * cos_ref[at, :] + swap_halves(block) * sin_ref[at, :]
                out_ref[0, at, first : first + 128] = turned.astype(BF16)

    @pl.when(which == 2)
    def _():
        for at in parts_of(x_ref.shape[0]):
            out_ref[0, at, :] = (mm(x_ref[at, :], w_ref[0]) + bias).astype(BF16)


def project_qkv(x, weight, bias, cosine, sine, after=()):
    n, D = x.shape
    width = weight.shape[2]
    return call(
        qkv_kernel, "project_qkv", (3,),
        [
            held((n, D)), pl.BlockSpec((1, D, width), lambda j: (j, 0, 0)), held(bias.shape),
            held((n, 128)), held((n, 128)),
        ],
        [pl.BlockSpec((1, n, width), lambda j: (j, 0, 0))],
        [shaped(BF16, 3, n, width)],
        (x, weight, bias, cosine, sine), 6 * n * D * width, after=after,
    )[0]


def prepare_kernel(
    q_rows, sizes_ref, picks_ref, docs_ref, cos_ref, sin_ref, ext_k_ref, ext_q_ref, out_ref
):
    n = cos_ref.shape[0]
    size = math.gcd(256, math.gcd(q_rows, n))
    lane = lax.broadcasted_iota(jnp.int32, (size, 128), 1)
    frequency = jnp.exp((lane & (DH // 2 - 1)).astype(F32) * (-2.0 * math.log(10000.0) / DH))
    place_lane = lane & (DH - 1)
    for first in range(0, n, size):
        at = slice(first, first + size)
        row = lax.broadcasted_iota(jnp.int32, (size, 128), 0) + first
        if first < q_rows:
            position, segment = row & (QLEN - 1), (row // QLEN) & (SEGMENTS - 1)
        else:
            place = row - q_rows
            begin, segment, end = jnp.zeros_like(row), jnp.zeros_like(row), 0
            for doc in range(sizes_ref.shape[0]):
                end = end + sizes_ref[doc]
                passed = place >= end
                begin = jnp.where(passed, end, begin)
                segment = segment + passed.astype(jnp.int32)
            position = place - begin
        angles = position.astype(F32) * frequency
        sine = jnp.sin(angles)
        cos_ref[at, :] = jnp.cos(angles)
        sin_ref[at, :] = jnp.where((lane & (DH // 2)) == 0, -sine, sine)
        same = segment == place_lane
        ones = (place_lane >= SEGMENTS) & (place_lane < SEGMENTS + 3)
        ext_k_ref[at, :] = (same | ones).astype(F32).astype(BF16)
        apart = (place_lane < SEGMENTS) & jnp.logical_not(same)
        ext_q_ref[at, :] = jnp.where(apart, -1e30, 0.0).astype(BF16)
    queries = picks_ref.shape[0]
    begins, sizes = docs_ref[:, 0:1], docs_ref[:, 1:2]
    groups, docs = out_ref.shape[:2]
    for first in range(0, queries, 4):
        lanes = jnp.concatenate([picks_ref[first + j] for j in range(4)], axis=1)
        rows = begins + lax.rem(lanes, jnp.broadcast_to(sizes, lanes.shape))
        at = slice(first * QLEN, (first + 4) * QLEN)
        for group in range(groups):
            out_ref[group, :, at] = rows[group * docs : (group + 1) * docs]


def prepare(n, q_rows, own_sizes, match_picks, begins, sizes):
    groups, docs = sizes.shape
    width = match_picks.shape[0] * QLEN
    table = jnp.stack([begins.reshape(-1), sizes.reshape(-1)], axis=1)
    return call(
        functools.partial(prepare_kernel, q_rows), "prepare", (1,),
        [held(match_picks.shape), held(table.shape)],
        [pl.BlockSpec((n, 128), lambda *_: (0, 0))] * 4
        + [pl.BlockSpec((groups, docs, width), lambda *_: (0, 0, 0))],
        [
            shaped(F32, n, 128), shaped(F32, n, 128), shaped(BF16, n, 128), shaped(BF16, n, 128),
            shaped(jnp.int32, groups, docs, width),
        ],
        (own_sizes, match_picks, table), 0, prefetch=1,
    )


def normed_rows(residual):
    mean = jnp.mean(residual, axis=1, keepdims=True)
    centred = residual - mean
    inverse = lax.rsqrt(jnp.mean(centred * centred, axis=1, keepdims=True) + 1e-05)
    return centred * inverse, inverse


def norm_pull(grad_rows, normed, inverse, gain):
    spread = grad_rows * gain
    return inverse * (
        spread
        - jnp.mean(spread, axis=1, keepdims=True)
        - normed * jnp.mean(spread * normed, axis=1, keepdims=True)
    )


def column_sums(*arrays):
    rows = [jnp.sum(array, axis=0, keepdims=True) for array in arrays]
    rows.append(jnp.zeros((8 - len(rows), rows[0].shape[1]), F32))
    return jnp.concatenate(rows, axis=0)


def add_over_steps(ref, value):
    first = pl.program_id(0) == 0

    @pl.when(first)
    def _():
        ref[...] = value

    @pl.when(jnp.logical_not(first))
    def _():
        ref[...] += value


def out_norm_kernel(slots, *refs):
    x_ref, vec_ref = refs[:2]
    att_refs, w_refs = refs[2 : 2 + slots], refs[2 + slots : 2 + 2 * slots]
    normed_ref, inverse_ref, low_ref, turned_ref = refs[2 + 2 * slots :]
    for at in parts_of(x_ref.shape[0]):
        residual = x_ref[at, :].astype(F32) + vec_ref[0:1, :]
        for att_ref, w_ref in zip(att_refs, w_refs):
            residual = residual + mm(att_ref[at, :], w_ref[...])
        normed, inverse = normed_rows(residual)
        hidden = normed * vec_ref[1:2, :] + vec_ref[2:3, :]
        normed_ref[at, :] = normed
        inverse_ref[at, :] = inverse
        low_ref[at, :] = hidden.astype(BF16)
        turned_ref[:, at] = hidden.T.astype(BF16)


def out_and_norm(x, vectors, attended, weights):
    n, D = x.shape
    step = row_step(n)
    slots = len(attended)
    width = attended[0].shape[1]
    return call(
        functools.partial(out_norm_kernel, slots), "out_and_norm", (n // step,),
        [row_spec(step, D), held(vectors.shape)]
        + [row_spec(step, width)] * slots + [held((width, D))] * slots,
        [row_spec(step, D), row_spec(step, 1), row_spec(step, D), column_spec(D, step)],
        [shaped(F32, n, D), shaped(F32, n, 1), shaped(BF16, n, D), shaped(BF16, D, n)],
        (x, vectors, *attended, *weights), 2 * n * D * D,
    )


GELU_TERMS = (
    0.23532527933595032, 0.09138803439798156, 0.6495603483388861,
    -0.6354014529895687, 0.8866650885491606, -0.22753729931242958,
)


def gelu_parts(values):
    size = jnp.abs(values)
    part = pl.reciprocal(1.0 + (0.39 / math.sqrt(2.0)) * size)
    bell = jnp.exp(-0.5 * (values * values))
    series = 0.5 * GELU_TERMS[-1]
    for term in GELU_TERMS[-2::-1]:
        series = series * part + 0.5 * term
    tail = series * part * bell
    below = jnp.where(values >= 0.0, 1.0 - tail, tail)
    return values * below, below + values * bell * (1.0 / math.sqrt(2.0 * math.pi))


def up_kernel(x_ref, w_ref, b_ref, active_ref, slope_ref):
    width = w_ref.shape[1]
    chunk = min(256, width)
    for first in range(0, width, chunk):
        at = slice(first, first + chunk)
        active, slope = gelu_parts(mm(x_ref[...], w_ref[:, at]) + b_ref[:, at])
        active_ref[:, at] = active.astype(BF16)
        slope_ref[:, at] = slope


def up_and_gelu(x, weight, bias):
    n, D = x.shape
    width = weight.shape[1]
    step = row_step(n)
    return call(
        up_kernel, "up_and_gelu", (n // step,),
        [row_spec(step, D), held(weight.shape), held(bias.shape)],
        [row_spec(step, width)] * 2,
        [shaped(BF16, n, width), shaped(F32, n, width)],
        (x, weight, bias), 5 * n * D * width,
    )


def down_norm_kernel(slots, *refs):
    normed_ref, vec_ref, proj_ref = refs[:3]
    act_refs, w_refs = refs[3 : 3 + slots], refs[3 + slots : 3 + 2 * slots]
    normed_out, inverse_ref, low_ref, unit_ref, unit_low_ref, unit_inverse_ref = refs[3 + 2 * slots :]
    for at in parts_of(normed_ref.shape[0]):
        residual = normed_ref[at, :] * vec_ref[1:2, :] + vec_ref[2:3, :] + vec_ref[3:4, :]
        for act_ref, w_ref in zip(act_refs, w_refs):
            residual = residual + mm(act_ref[at, :], w_ref[...])
        normed, inverse = normed_rows(residual)
        normed_out[at, :] = normed
        inverse_ref[at, :] = inverse
        low = (normed * vec_ref[4:5, :] + vec_ref[5:6, :]).astype(BF16)
        low_ref[at, :] = low
        embedding = mm(low, proj_ref[...])
        unit_inverse = lax.rsqrt(jnp.sum(embedding * embedding, axis=1, keepdims=True) + 1e-06)
        unit = embedding * unit_inverse
        unit_ref[at, :] = unit
        unit_low_ref[at, :] = unit.astype(BF16)
        unit_inverse_ref[at, :] = unit_inverse


def down_and_norm(normed, vectors, proj, active, weights):
    n, D = normed.shape
    step = row_step(n)
    slots = len(active)
    width = active[0].shape[1]
    return call(
        functools.partial(down_norm_kernel, slots), "down_and_norm", (n // step,),
        [row_spec(step, D), held(vectors.shape), held(proj.shape)]
        + [row_spec(step, width)] * slots + [held((width, D))] * slots,
        [
            row_spec(step, D), row_spec(step, 1), row_spec(step, D),
            row_spec(step, 128), row_spec(step, 128), row_spec(step, 1),
        ],
        [
            shaped(F32, n, D), shaped(F32, n, 1), shaped(BF16, n, D),
            shaped(F32, n, 128), shaped(BF16, n, 128), shaped(F32, n, 1),
        ],
        (normed, vectors, proj, *active, *weights), 2 * n * D * width * slots,
    )


def head_pull_kernel(
    grad_ref, unit_ref, unit_inverse_ref, proj_ref, normed_ref, inverse_ref, vec_ref,
    embed_ref, residual_ref, low_ref, turned_ref, sum_ref,
):
    sums = []
    for at in parts_of(grad_ref.shape[0]):
        grad, unit = grad_ref[at, :], unit_ref[at, :]
        embed = grad - unit * jnp.sum(grad * unit, axis=1, keepdims=True)
        embed = (unit_inverse_ref[at, :] * embed).astype(BF16)
        embed_ref[at, :] = embed
        output_grad = mm(embed, proj_ref[...], NT)
        normed = normed_ref[at, :]
        residual = norm_pull(output_grad, normed, inverse_ref[at, :], vec_ref[4:5, :])
        residual_ref[at, :] = residual
        low_ref[at, :] = residual.astype(BF16)
        turned_ref[:, at] = residual.T.astype(BF16)
        sums.append(column_sums(residual, output_grad * normed, output_grad))
    add_over_steps(sum_ref, sum(sums))


def head_pull(unit_grad, unit, unit_inverse, proj, normed, inverse, vectors):
    n, D = normed.shape
    step = row_step(n)
    return call(
        head_pull_kernel, "head_pull", (n // step,),
        [
            row_spec(step, 128), row_spec(step, 128), row_spec(step, 1), held(proj.shape),
            row_spec(step, D), row_spec(step, 1), held(vectors.shape),
        ],
        [
            row_spec(step, 128), row_spec(step, D), row_spec(step, D),
            column_spec(D, step), pl.BlockSpec((8, D), lambda i: (0, 0)),
        ],
        [
            shaped(BF16, n, 128), shaped(F32, n, D), shaped(BF16, n, D),
            shaped(BF16, D, n), shaped(F32, 8, D),
        ],
        (unit_grad, unit, unit_inverse, proj, normed, inverse, vectors), 4 * n * D * 128,
    )


def up_pull_kernel(branch_ref, w_ref, slope_ref, out_ref, sum_ref):
    width = w_ref.shape[0]
    chunk = min(512, width)
    sums = []
    for first in range(0, width, chunk):
        at = slice(first, first + chunk)
        low = (mm(branch_ref[...], w_ref[at, :], NT) * slope_ref[:, at]).astype(BF16)
        out_ref[:, at] = low
        sums.append(column_sums(low.astype(F32)))
    add_over_steps(sum_ref, jnp.concatenate(sums, axis=1))


def up_pull(branch, weight, slope):
    n, D = branch.shape
    width = weight.shape[0]
    step = row_step(n)
    return call(
        up_pull_kernel, "up_pull", (n // step,),
        [row_spec(step, D), held(weight.shape), row_spec(step, width)],
        [row_spec(step, width), pl.BlockSpec((8, width), lambda i: (0, 0))],
        [shaped(BF16, n, width), shaped(F32, 8, width)],
        (branch, weight, slope), 2 * n * D * width,
    )


def hidden_pull_kernel(slots, *refs):
    residual_ref, normed_ref, inverse_ref, vec_ref = refs[:4]
    pre_refs, up_refs, out_refs = (refs[4 + j * slots : 4 + (j + 1) * slots] for j in range(3))
    rest = refs[4 + 3 * slots :]
    grad_ref, turned_ref, sum_ref = rest[:3]
    att_refs = rest[3:]
    sums = []
    for at in parts_of(residual_ref.shape[0]):
        hidden_grad = residual_ref[at, :]
        for pre_ref, up_ref in zip(pre_refs, up_refs):
            hidden_grad = hidden_grad + mm(pre_ref[at, :], up_ref[...], NT)
        normed = normed_ref[at, :]
        residual = norm_pull(hidden_grad, normed, inverse_ref[at, :], vec_ref[1:2, :])
        grad_ref[at, :] = residual
        low = residual.astype(BF16)
        turned_ref[:, at] = residual.T.astype(BF16)
        sums.append(column_sums(residual, hidden_grad * normed, hidden_grad))
        for att_ref, out_ref in zip(att_refs, out_refs):
            att_ref[at, :] = mm(low, out_ref[...], NT).astype(BF16)
    add_over_steps(sum_ref, sum(sums))


def hidden_pull(residual, normed, inverse, vectors, pre_grads, ups, outs):
    n, D = residual.shape
    step = row_step(n)
    slots = len(ups)
    wide, width = ups[0].shape[1], outs[0].shape[0]
    return call(
        functools.partial(hidden_pull_kernel, slots), "hidden_pull", (n // step,),
        [row_spec(step, D), row_spec(step, D), row_spec(step, 1), held(vectors.shape)]
        + [row_spec(step, wide)] * slots + [held((D, wide))] * slots
        + [held((width, D))] * slots,
        [row_spec(step, D), column_spec(D, step), pl.BlockSpec((8, D), lambda i: (0, 0))]
        + [row_spec(step, width)] * slots,
        [shaped(F32, n, D), shaped(BF16, D, n), shaped(F32, 8, D)]
        + [shaped(BF16, n, width)] * slots,
        (residual, normed, inverse, vectors, *pre_grads, *ups, *outs),
        0,
    )


def token_pull_kernel(slots, place_ref, *refs):
    residual_ref = refs[0]
    mixed_refs, w_refs = refs[1 : 1 + slots], refs[1 + slots : 1 + 2 * slots]
    out_ref = refs[-1]
    width = out_ref.shape[1]
    at = pl.ds(pl.multiple_of(place_ref[0] * width, width), width)
    total = residual_ref[...]
    for mixed_ref, w_ref in zip(mixed_refs, w_refs):
        for which in range(3):
            total = total + mm(mixed_ref[which], w_ref[which, at, :], NT)
    out_ref[...] = total.astype(out_ref.dtype)


def token_pull(place, residual, mixed_grads, weights, dtype):
    n, D = residual.shape
    step = row_step(n)
    slots = len(weights)
    width = weights[0].shape[2]
    return call(
        functools.partial(token_pull_kernel, slots), "token_pull", (n // step,),
        [pl.BlockSpec((step, width), lambda i, p: (i, p[0]))]
        + [pl.BlockSpec((3, step, width), lambda i, p: (0, i, 0))] * slots
        + [held((3, D, width))] * slots,
        [row_spec(step, width)],
        [shaped(dtype, n, width)],
        (place.reshape(1), residual, *mixed_grads, *weights), 0, prefetch=1,
    )[0]


def put_halves(total, inner, side, refs):
    pairs = total.reshape(-1, 2, inner, total.shape[1])
    keep = jnp.where(side == 0, pairs[:, 0], pairs[:, 1]).reshape(-1, total.shape[1])
    send = jnp.where(side == 0, pairs[:, 1], pairs[:, 0]).reshape(-1, total.shape[1])
    refs[0][0] = send.astype(BF16)
    refs[1][0] = keep


def grouped_index(starts, place, count):
    def index(j, i, *_):
        inside = (j >= starts[place]) & (j < starts[place + 1])
        row = jnp.clip(j - starts[place], 0, starts[place + 1] - starts[place] - 1)
        rest = jnp.where(j < starts[place], 0, count - 1)
        return row, 0, jnp.where(inside, i, rest)

    return index


def for_group(starts, body):
    if len(starts) == 2:
        body(0)
        return
    for place in range(len(starts) - 1):

        @pl.when((pl.program_id(0) >= starts[place]) & (pl.program_id(0) < starts[place + 1]))
        def _(place=place):
            body(place)


def join_kernel(slots, place_ref, *refs):
    out_ref, turned_ref = refs[-2:]
    width = refs[0].shape[1]
    for k in range(slots):
        at = pl.ds(pl.multiple_of((place_ref[0] + slots - k) % slots * width, width), width)
        out_ref[:, at] = refs[k][...]
        turned_ref[at, :] = refs[k][...].astype(F32).T.astype(BF16)


def join(c, slots):
    n, width = slots[0].shape
    D = width * len(slots)
    step = row_step(n)
    return call(
        functools.partial(join_kernel, len(slots)), "join", (n // step,),
        [row_spec(step, width)] * len(slots),
        [row_spec(step, D), pl.BlockSpec((D, step), lambda i, *_: (0, i))],
        [shaped(BF16, n, D), shaped(BF16, D, n)], (c.reshape(1), *slots), 0, prefetch=1,
    )


def assemble_kernel(place_ref, *refs):
    out_ref = refs[-1]
    slot = place_ref[1 + pl.program_id(0)]
    for k, ref in enumerate(refs[:-1]):

        @pl.when(slot == k)
        def _(ref=ref):
            out_ref[...] = ref[...].astype(F32)


def assemble(c, q_rows, slots):
    n, width = slots[0].shape
    count = len(slots)
    step = math.gcd(512, math.gcd(q_rows, n))
    q_steps, d_steps = q_rows // step, (n - q_rows) // step
    turns, owners = [], []
    for base, steps in ((0, q_steps), (q_steps, d_steps)):
        for owner in range(count):
            turns += [base + turn for turn in range(steps)]
            owners += [owner] * steps
    places = jnp.concatenate([c.reshape(1), (c - jnp.array(owners)) % count]).astype(jnp.int32)

    def turn_of(j, p):
        turn = jnp.where(j < count * q_steps, j % q_steps, q_steps + (j - count * q_steps) % d_steps)
        return turn, 0

    return call(
        assemble_kernel, "assemble", (len(turns),),
        [pl.BlockSpec((step, width), turn_of)] * count,
        [pl.BlockSpec((step, width), lambda j, p: (j, 0))],
        [shaped(F32, n * count, width)], (places, *slots), 0, prefetch=1,
    )[0]


def pass_on_kernel(in_ref, out_ref):
    out_ref[...] = in_ref[...]


def pass_on(array):
    spec = held(array.shape)
    return call(
        pass_on_kernel, "pass_on", (1,), [spec], [pl.BlockSpec(array.shape, lambda *_: (0,) * array.ndim)],
        [shaped(array.dtype, *array.shape)], (array,), 0,
    )[0]


def fold_kernel(starts, inner, place_ref, *refs):
    groups = len(starts) - 1

    def one_group(place):
        total = refs[place][0] + refs[groups + place][0].astype(F32)
        put_halves(total, inner, place_ref[0], refs[2 * groups :])

    for_group(starts, one_group)


def fold(side, owns, arrived, inner):
    _, rows, m = owns[0].shape
    chunk = min(1024, m)
    starts = [0]
    for own in owns:
        starts.append(starts[-1] + own.shape[0])

    def spec(size):
        return pl.BlockSpec((1, size, chunk), lambda j, i, p: (j, 0, i))

    half = rows // 2
    specs = [
        pl.BlockSpec((1, rows, chunk), grouped_index(starts, place, m // chunk))
        for place in range(len(owns))
    ]
    return call(
        functools.partial(fold_kernel, starts, inner), "fold", (starts[-1], m // chunk),
        specs + specs, [spec(half), spec(half)],
        [shaped(BF16, starts[-1], half, m), shaped(F32, starts[-1], half, m)],
        (side.reshape(1), *owns, *arrived), 0, prefetch=1,
    )


SEGMENTS = 8
ATTENTION_LANES = 128


def half_lanes(block, head, other):
    lane = lax.broadcasted_iota(jnp.int32, block.shape, 1)
    return jnp.where((lane >= DH) == (head == 1), block, other)


def scaled(block):
    return (block.astype(F32) * DH**-0.5).astype(BF16)


def three_terms(value):
    high = value.astype(BF16).astype(F32)
    middle = (value - high).astype(BF16).astype(F32)
    return high, middle, value - high - middle


def for_spans(span_ref, tiles, body):
    @pl.loop(0, tiles)
    def _(step):
        low, high = span_ref[step], span_ref[tiles + step]
        for count in range(1, tiles + 1):

            @pl.when(high - low == count)
            def _(count=count):
                body(step, low, count)


def attention_forward_kernel(
    span_ref, qkv_ref, ext_k_ref, ext_q_ref, out_ref, rest_ref, ext_ref,
    keys_ref, queries_ref, *, tile,
):
    n = ext_k_ref.shape[0]
    tiles = n // tile
    pairs = qkv_ref.shape[2] // 128

    def lanes(pair):
        return slice(pair * 128, pair * 128 + 128)

    for pair in range(pairs):
        query = scaled(qkv_ref[0, :, lanes(pair)])
        for half in range(2):
            keys_ref[2 * pair + half] = half_lanes(qkv_ref[1, :, lanes(pair)], half, ext_k_ref[...])
            queries_ref[2 * pair + half] = half_lanes(query, half, ext_q_ref[...])

    def attend(step, low, count):
        rows = pl.ds(pl.multiple_of(step * tile, tile), tile)
        window = pl.ds(pl.multiple_of(low * tile, tile), count * tile)
        lane = lax.broadcasted_iota(jnp.int32, (tile, 128), 1)
        for pair in range(pairs):
            at = lanes(pair)
            outs, extra = [], ext_q_ref[rows, :].astype(F32)
            for half in range(2):
                head = 2 * pair + half
                logits = mm(queries_ref[head, rows, :], keys_ref[head, window, :], NT)
                top = jnp.max(logits, axis=1, keepdims=True)
                weights = jnp.exp(logits - top)
                mass = jnp.sum(weights, axis=1, keepdims=True)
                probs = (weights * (1.0 / mass)).astype(BF16)
                outs.append(mm(probs, qkv_ref[2, window, at]))
                first = SEGMENTS + DH * (1 - half)
                for place, term in enumerate(three_terms(-(top + jnp.log(mass)))):
                    extra = jnp.where(lane == first + place, term, extra)
            out = jnp.where(lane < DH, outs[0], outs[1])
            out_ref[rows, at] = out.astype(BF16)
            rest_ref[rows, at] = (out - out.astype(BF16).astype(F32)).astype(BF16)
            ext_ref[rows, at] = extra.astype(BF16)

    for_spans(span_ref, tiles, attend)


def attention_forward(spans, qkv, ext_k, ext_q, tile):
    _, n, width = qkv.shape
    span = min(width, ATTENTION_LANES)
    wide = pl.BlockSpec((n, span), lambda i, *_: (0, i))
    heads = pltpu.VMEM((span // DH, n, 128), BF16)
    return call(
        functools.partial(attention_forward_kernel, tile=tile), "attention_forward",
        (width // span,),
        [pl.BlockSpec((3, n, span), lambda i, *_: (0, 0, i)), held((n, 128)), held((n, 128))],
        [wide, wide, wide],
        [shaped(BF16, n, width)] * 3,
        (spans, qkv, ext_k, ext_q), 0, prefetch=1, scratch=[heads, heads],
    )


def attention_backward_kernel(
    span_ref, qkv_ref, ext_ref, att_ref, rest_ref, grad_ref, ext_k_ref, cos_ref, sin_ref,
    out_ref, sum_ref,
    keys_ref, turned_ref, values_ref, queries_ref, plain_ref, grads_ref, plain_grads_ref,
    dq_ref, dk_ref, dv_ref, *, tile,
):
    n = ext_k_ref.shape[0]
    tiles = n // tile
    pairs = qkv_ref.shape[2] // 128
    heads = range(2 * pairs)

    def lanes(head):
        return slice(head // 2 * 128, head // 2 * 128 + 128)

    def own_rows(head):
        return slice(head % 2 * DH, head % 2 * DH + DH)

    def rows(step):
        return pl.ds(pl.multiple_of(step * tile, tile), tile)

    @pl.loop(0, tiles)
    def _(step):
        at = rows(step)
        zeros = jnp.zeros((tile, 128), BF16)
        lane = lax.broadcasted_iota(jnp.int32, (tile, 128), 1)
        ext_k = ext_k_ref[at, :]
        for pair in range(pairs):
            cut = lanes(2 * pair)
            grad = grad_ref[at, cut]
            out = att_ref[at, cut].astype(F32) + rest_ref[at, cut].astype(F32)
            product = grad.astype(F32) * out
            query = scaled(qkv_ref[0, at, cut])
            turned_ref[pair, :, at] = scaled(qkv_ref[1, at, cut]).astype(F32).T.astype(BF16)
            for half in range(2):
                head = 2 * pair + half
                keys_ref[head, at, :] = half_lanes(qkv_ref[1, at, cut], half, ext_k)
                values_ref[head, at, :] = half_lanes(qkv_ref[2, at, cut], half, ext_k)
                whole = half_lanes(query, half, ext_ref[at, cut])
                queries_ref[head, step] = whole.astype(F32).T.astype(BF16)
                plain_ref[head, at, :] = half_lanes(query, half, zeros)
                plain_grads_ref[head, at, :] = half_lanes(grad, half, zeros)
                inner = jnp.sum(half_lanes(product, half, 0.0), axis=1, keepdims=True)
                extra = jnp.zeros((tile, 128), F32)
                for place, term in enumerate(three_terms(-inner)):
                    extra = jnp.where((lane & (DH - 1)) == SEGMENTS + place, term, extra)
                whole = half_lanes(grad.astype(F32), half, extra)
                grads_ref[head, step] = whole.T.astype(BF16)

    dk_ref[...] = jnp.zeros(dk_ref.shape, F32)
    dv_ref[...] = jnp.zeros(dv_ref.shape, F32)

    def pull(step, low, count):
        at = rows(step)
        window = pl.ds(pl.multiple_of(low * tile, tile), count * tile)
        for pair in range(pairs):
            probs, slopes, dq = [], [], []
            both = range(2 * pair, 2 * pair + 2)
            for head in both:
                weights = jnp.exp(mm(keys_ref[head, window, :], queries_ref[head, step]))
                flow = mm(values_ref[head, window, :], grads_ref[head, step])
                slope = (weights * flow).astype(BF16)
                probs.append(weights.astype(BF16))
                slopes.append(slope)
                dq.append(mm(turned_ref[pair, own_rows(head), window], slope))
            plain = jnp.concatenate([plain_ref[h, at, :] for h in both], axis=0)
            grads = jnp.concatenate([plain_grads_ref[h, at, :] for h in both], axis=0)
            cut = lanes(2 * pair)
            dv_ref[window, cut] += mm(jnp.concatenate(probs, axis=1), grads)
            dk_ref[window, cut] += mm(jnp.concatenate(slopes, axis=1), plain)
            dq_ref[at, cut] = jnp.concatenate(dq, axis=0).T

    for_spans(span_ref, tiles, pull)

    def finish(step, sums):
        cosine, sine = cos_ref[rows(step), :], sin_ref[rows(step), :]
        added = []
        for which, src in enumerate((dq_ref, dk_ref, dv_ref)):
            for pair in range(pairs):
                at = lanes(2 * pair)
                block = src[rows(step), at]
                if which < 2:
                    block = block * cosine - swap_halves(block) * sine
                low = block.astype(BF16)
                out_ref[which, rows(step), at] = low
                total = jnp.sum(low.astype(F32), axis=0, keepdims=True)
                added.append(sums[which * pairs + pair] + total)
        return tuple(added)

    zero = jnp.zeros((1, 128), F32)
    sums = lax.fori_loop(0, tiles, finish, (zero,) * (3 * pairs))
    sums = [jnp.concatenate(sums[w * pairs : (w + 1) * pairs], axis=1) for w in range(3)]
    sum_ref[...] = jnp.concatenate(sums + [jnp.zeros((5, pairs * 128), F32)], axis=0)


def attention_backward(
    spans, qkv, ext, attended, rest, grads, ext_k, cosine, sine, tile
):
    _, n, width = qkv.shape
    span = min(width, ATTENTION_LANES)
    wide = pl.BlockSpec((n, span), lambda i, *_: (0, i))
    three = pl.BlockSpec((3, n, span), lambda i, *_: (0, 0, i))
    tiles, pairs = n // tile, span // 128
    heads = pltpu.VMEM((2 * pairs, n, 128), BF16)
    turned = pltpu.VMEM((2 * pairs, tiles, 128, tile), BF16)
    return call(
        functools.partial(attention_backward_kernel, tile=tile), "attention_backward",
        (width // span,),
        [three, wide, wide, wide, wide, held((n, 128)), held((n, 128)), held((n, 128))],
        [three, pl.BlockSpec((8, span), lambda i, *_: (0, i))],
        [shaped(BF16, 3, n, width), shaped(F32, 8, width)],
        (spans, qkv, ext, attended, rest, grads, ext_k, cosine, sine), 0,
        prefetch=1,
        scratch=[
            heads, pltpu.VMEM((pairs, 128, n), BF16), heads, turned, heads, turned, heads,
        ] + [pltpu.VMEM((n, span), F32)] * 3,
    )


STRIP = 32


def token_sums(width, queries):
    token = lax.broadcasted_iota(jnp.int32, (width, queries), 0) // QLEN
    return token == lax.broadcasted_iota(jnp.int32, (width, queries), 1)


def score_kernel(low_ref, high_ref, doc_ref, query_ref, pick_ref, out_ref, sum_ref, total_ref):
    group = pl.program_id(0)
    docs, width = pick_ref.shape[1:]
    doc_rows = doc_ref.shape[0]
    strips = doc_rows // STRIP
    chunk = min(256, doc_rows)
    row = lax.broadcasted_iota(jnp.int32, (STRIP, width), 0)
    sum_ref[...] = jnp.zeros(sum_ref.shape, F32)

    def add_strip(sim, first, doc, pick):
        kept = jnp.where(row == pick - first, sim, 0.0)
        sum_ref[pl.ds(doc, 1)] += jnp.sum(kept.reshape(1, STRIP // 8, 8, width), axis=1)

    for start in range(0, doc_rows, chunk):
        sims = mm(doc_ref[start : start + chunk, :], query_ref[...], NT)
        for first in range(0, chunk, STRIP):
            place = group * strips + (start + first) // STRIP
            low, high = low_ref[place], high_ref[place]
            sim = sims[first : first + STRIP]
            add_strip(sim, start + first, low, pick_ref[0, pl.ds(low, 1), :])
            pick = jnp.where(high > low, pick_ref[0, pl.ds(high, 1), :], -1)
            add_strip(sim, start + first, high, pick)

    @pl.loop(0, strips)
    def _(strip):
        low, high = low_ref[group * strips + strip], high_ref[group * strips + strip]

        @pl.when(high > low + 1)
        def _():
            first = pl.multiple_of(strip * STRIP, STRIP)
            sim = mm(doc_ref[pl.ds(first, STRIP), :], query_ref[...], NT)

            @pl.loop(low + 1, high)
            def _(doc):
                add_strip(sim, first, doc, pick_ref[0, pl.ds(doc, 1), :])

    total_ref[group] = jnp.sum(sum_ref[...], axis=1)

    @pl.when(group == pl.num_programs(0) - 1)
    def _():
        spread = token_sums(width, out_ref.shape[1]).astype(F32).astype(BF16)
        total = jnp.concatenate([total_ref[g] for g in range(total_ref.shape[0])], axis=0)
        out_ref[...] = sum(mm(term.astype(BF16), spread) for term in three_terms(total))


def score_grad_kernel(
    low_ref, high_ref, doc_ref, query_ref, pick_ref, weight_ref, doc_out, query_out,
    sparse_ref, token_ref,
):
    group = pl.program_id(0)
    docs, width = pick_ref.shape[1:]
    doc_rows = doc_ref.shape[0]
    strips = doc_rows // STRIP
    chunk = min(256, doc_rows)
    row = lax.broadcasted_iota(jnp.int32, (STRIP, width), 0)

    def fill(held, first, doc, pick):
        return jnp.where(row == pick - first, token_ref[group, pl.ds(doc, 1), :], held)

    @pl.when(group == 0)
    def _():
        query_out[...] = jnp.zeros_like(query_out)
        spread = token_sums(width, weight_ref.shape[1]).astype(F32).astype(BF16)
        weights = mm(weight_ref[...].astype(BF16), spread, NT)
        for g in range(token_ref.shape[0]):
            token_ref[g] = weights[g * docs : (g + 1) * docs]

    total = None
    for start in range(0, doc_rows, chunk):
        for first in range(start, start + chunk, STRIP):
            place = group * strips + first // STRIP
            low, high = low_ref[place], high_ref[place]
            held = fill(jnp.zeros((STRIP, width), F32), first, low, pick_ref[0, pl.ds(low, 1), :])
            pick = jnp.where(high > low, pick_ref[0, pl.ds(high, 1), :], -1)
            sparse_ref[first : first + STRIP, :] = fill(held, first, high, pick).astype(BF16)
        sparse = sparse_ref[start : start + chunk, :]
        doc_out[start : start + chunk, :] = mm(sparse, query_ref[...])
        turned = doc_ref[start : start + chunk, :].astype(F32).T.astype(BF16)
        part = mm(turned, sparse)
        total = part if total is None else total + part
    query_out[...] += total

    @pl.loop(0, strips)
    def _(strip):
        low, high = low_ref[group * strips + strip], high_ref[group * strips + strip]

        @pl.when(high > low + 1)
        def _():
            first = pl.multiple_of(strip * STRIP, STRIP)
            held = lax.fori_loop(
                low + 1,
                high,
                lambda doc, held: fill(held, first, doc, pick_ref[0, pl.ds(doc, 1), :]),
                jnp.zeros((STRIP, width), F32),
            ).astype(BF16)
            doc_out[pl.ds(first, STRIP), :] += mm(held, query_ref[...])
            turned = doc_ref[pl.ds(first, STRIP), :].astype(F32).T.astype(BF16)
            query_out[...] += mm(turned, held)


def score_specs(doc_tile, query_tile, picks):
    groups, docs, width = picks.shape
    doc_rows = doc_tile.shape[0] // groups
    return (
        pl.BlockSpec((doc_rows, 128), lambda i, *_: (i, 0)),
        held(query_tile.shape),
        pl.BlockSpec((1, docs, width), lambda i, *_: (i, 0, 0)),
    )


def score_forward(lows, highs, doc_tile, query_tile, picks):
    groups, docs, width = picks.shape
    queries = width // QLEN
    doc_spec, query_spec, pick_spec = score_specs(doc_tile, query_tile, picks)
    return call(
        score_kernel, "score_forward", (groups,),
        [doc_spec, query_spec, pick_spec],
        [pl.BlockSpec((groups * docs, queries), lambda i, *_: (0, 0))],
        [shaped(F32, groups * docs, queries)],
        (lows, highs, doc_tile, query_tile, picks), 2 * doc_tile.shape[0] * width * 128,
        prefetch=2,
        scratch=[pltpu.VMEM((docs, 8, width), F32), pltpu.VMEM((groups, docs, width), F32)],
    )[0]


def score_backward(lows, highs, doc_tile, query_tile, picks, weights):
    groups, docs, width = picks.shape
    doc_spec, query_spec, pick_spec = score_specs(doc_tile, query_tile, picks)
    return call(
        score_grad_kernel, "score_backward", (groups,),
        [doc_spec, query_spec, pick_spec, held(weights.shape)],
        [doc_spec, pl.BlockSpec((128, width), lambda i, *_: (0, 0))],
        [shaped(F32, *doc_tile.shape), shaped(F32, 128, width)],
        (lows, highs, doc_tile, query_tile, picks, weights), 4 * doc_tile.shape[0] * width * 128,
        prefetch=2,
        scratch=[
            pltpu.VMEM((doc_tile.shape[0] // groups, width), BF16),
            pltpu.VMEM((groups, docs, width), F32),
        ],
    )


def on_device(
    tokens,
    doc_lengths,
    match_picks,
    labels,
    w_qkv,
    b_qkv,
    w_out,
    b_out,
    ln1_gain,
    ln1_bias,
    w_up,
    b_up,
    w_down,
    b_down,
    ln2_gain,
    ln2_bias,
    w_proj,
    log_scale,
):
    Order.last = ()
    C = lax.axis_size("cols")
    R = lax.axis_size("rows")
    c = lax.axis_index("cols")
    r = lax.axis_index("rows")
    width = tokens.shape[1]
    D = width * C
    Q = ROW_LEN // C
    DS = (tokens.shape[0] - ROW_LEN) // C
    n = Q + DS
    tile = math.gcd(256, math.gcd(Q, DS))

    def shift_cols(value, k):
        return lax.ppermute(value, "cols", [(i, (i + k) % C) for i in range(C)])

    def swap_rows(value, bit):
        return lax.ppermute(value, "rows", [(i, i ^ bit) for i in range(R)])

    def in_order(slots):
        if len(slots) == 1:
            return slots
        if len(slots) == 2:
            return [lax.select(c == 0, slots[0], slots[1]), lax.select(c == 0, slots[1], slots[0])]
        stacked = jnp.stack(slots)
        return [
            lax.dynamic_index_in_dim(stacked, (c - j) % C, 0, keepdims=False) for j in range(C)
        ]

    pack = [b_qkv.reshape(-1), b_up, b_out, ln1_gain, ln1_bias, b_down, ln2_gain, ln2_bias]
    ends = [0]
    for vector in pack:
        ends.append(ends[-1] + vector.shape[0])
    packed = jnp.concatenate(pack)

    def gather_pieces(pieces):
        return [lax.all_gather(piece, "rows", axis=0, tiled=True) for piece in pieces]

    late_weights = (w_out, w_up, w_down)
    late_pieces = [
        lax.dynamic_index_in_dim(w.reshape(R, -1, w.shape[1]), r, 0, keepdims=False)
        for w in late_weights
    ]
    parts = jnp.concatenate(
        [tokens[:ROW_LEN].reshape(C, Q, width), tokens[ROW_LEN:].reshape(C, DS, width)], axis=1
    )

    def part(k):
        return lax.dynamic_index_in_dim(parts, (c + k) % C, 0, keepdims=False)

    token_slots = [part(0)] + [shift_cols(part(k), k) for k in range(1, C)]
    own_sizes = lax.dynamic_index_in_dim(
        lax.dynamic_index_in_dim(doc_lengths, r, 0, keepdims=False), c, 0, keepdims=False
    )
    sizes = lax.dynamic_index_in_dim(doc_lengths, c, 1, keepdims=False)
    doc_ends = jnp.cumsum(sizes, axis=1)
    begins = doc_ends - sizes
    cosine, sine, ext_k, ext_q, picks = prepare(n, Q, own_sizes, match_picks, begins, sizes)
    if C == 2:
        qkv_other, proj_other, pack_other = gather_weights(R, w_qkv, w_proj, packed.reshape(8, -1))
        wqkv_slots = [w_qkv, qkv_other]
        wproj = jnp.concatenate(in_order([w_proj, proj_other]), axis=0)
        packs = [packed, pack_other.reshape(-1)]
    else:

        def gather_slots(shard):
            flat = shard.reshape(-1, shard.shape[-1])
            piece = lax.dynamic_index_in_dim(
                flat.reshape(R, flat.shape[0] // R, flat.shape[1]), r, 0, keepdims=False
            )
            others = gather_pieces([shift_cols(piece, k) for k in range(1, C)])
            return [shard] + [other.reshape(shard.shape) for other in others]

        wqkv_slots = gather_slots(w_qkv)
        wproj = jnp.concatenate(
            in_order([w_proj] + [shift_cols(w_proj, k) for k in range(1, C)]), axis=0
        )
        packs = [packed] + [shift_cols(packed, k) for k in range(1, C)]
    x, x_t = join(c, token_slots)

    ordered_packs = in_order(packs)

    def of_slot(which, k):
        return packs[k][ends[which] : ends[which + 1]]

    def whole(which):
        return jnp.concatenate([p[ends[which] : ends[which + 1]] for p in ordered_packs])

    bqkv_slots = [of_slot(0, k).reshape(b_qkv.shape) for k in range(C)]
    bup_slots = [of_slot(1, k)[None, :] for k in range(C)]
    bout, gain1, bias1, bdown, gain2, bias2 = [whole(which) for which in range(2, 8)]
    zero_row = jnp.zeros_like(bout)
    vectors = jnp.stack([bout, gain1, bias1, bdown, gain2, bias2, zero_row, zero_row])

    own_ends = jnp.cumsum(own_sizes)
    share = D // R
    q_tiles, d_tiles = Q // tile, DS // tile
    steps = jnp.arange(q_tiles, dtype=jnp.int32)
    first_rows = jnp.arange(d_tiles, dtype=jnp.int32) * tile
    is_passed = first_rows[:, None] >= own_ends[None, :]
    low_rows = jnp.sum(jnp.where(is_passed, own_sizes[None, :], 0), axis=1)
    last_passed = (first_rows + tile - 1)[:, None] >= own_ends[None, :]
    high_rows = jnp.min(jnp.where(last_passed, DS, own_ends[None, :]), axis=1)
    spans = jnp.concatenate(
        [steps, q_tiles + low_rows // tile, steps + 1, q_tiles + (high_rows + tile - 1) // tile]
    ).astype(jnp.int32)

    queries_here, tile_docs, _ = match_picks.shape
    strip_rows = (jnp.arange(DS // STRIP, dtype=jnp.int32) * STRIP)[None, :, None]
    lows = jnp.sum(doc_ends[:, None, :] <= strip_rows, axis=2).astype(jnp.int32).reshape(-1)
    highs = jnp.sum(begins[:, None, :] < strip_rows + STRIP, axis=2).astype(jnp.int32) - 1
    highs = highs.reshape(-1)

    qkv, attended, rests, exts = [], [], [], []
    for k in range(C):
        first = (lows, highs) if k == 0 else ()
        qkv.append(project_qkv(x, wqkv_slots[k], bqkv_slots[k], cosine, sine, first))
        if k == 0:
            flat = jnp.concatenate([piece.reshape(-1, D) for piece in late_pieces])
            flat, _ = lax.optimization_barrier((flat, x))
            arrived = [shift_cols(flat, j) for j in range(1, C)]
            arrived = [pass_on(a) for a in arrived]
            ends_of = [0]
            for piece in late_pieces:
                ends_of.append(ends_of[-1] + piece.size // D)
            wout_slots, wup_slots, wdown_slots = (
                [own] + gather_pieces([
                    a[ends_of[j] : ends_of[j + 1]].reshape(late_pieces[j].shape) for a in arrived
                ])
                for j, own in enumerate(late_weights)
            )
            wout_slots, wup_slots, wdown_slots = (
                [slot.reshape(own.shape) for slot in slots_of]
                for slots_of, own in zip((wout_slots, wup_slots, wdown_slots), late_weights)
            )
        out, rest, ext = attention_forward(spans, qkv[k], ext_k, ext_q, tile)
        attended.append(out)
        rests.append(rest)
        exts.append(ext)
    normed_one, inverse_one, hidden_low, hidden_t = out_and_norm(x, vectors, attended, wout_slots)
    active, slopes = zip(*[up_and_gelu(hidden_low, wup_slots[k], bup_slots[k]) for k in range(C)])
    normed_two, inverse_two, output_low, unit, unit_low, unit_inverse = down_and_norm(
        normed_one, vectors, wproj, active, wdown_slots
    )

    doc_tile = gather_rows(R, unit_low[Q:]).reshape(R * DS, 128)
    query_tile = jnp.concatenate(
        in_order([unit_low[:Q]] + [shift_cols(unit_low[:Q], k) for k in range(1, C)]), axis=0
    )
    sims = score_forward(lows, highs, doc_tile, query_tile, picks)
    scores = sims.T

    scale = jnp.exp(log_scale[0])
    z = scale * scores
    row_top = jnp.max(z, axis=1)
    row_mass = jnp.sum(jnp.exp(z - row_top[:, None]), axis=1)
    is_label = (
        jnp.arange(tile_docs, dtype=jnp.int32)[None, :] == (labels - c * tile_docs)[:, None]
    )
    chosen = jnp.sum(jnp.where(is_label, z, 0.0), axis=1)
    own_stats = jnp.stack([row_top, row_mass, chosen])
    stats = jnp.stack([own_stats] + [shift_cols(own_stats, k) for k in range(1, C)])
    top_all = jnp.max(stats[:, 0], axis=0)
    mass_all = jnp.sum(stats[:, 1] * jnp.exp(stats[:, 0] - top_all), axis=0)
    log_total = top_all + jnp.log(mass_all)
    loss = log_total - jnp.sum(stats[:, 2], axis=0)
    dz = (jnp.exp(z - log_total[:, None]) - is_label.astype(F32)) / (queries_here * R)
    scale_part = jnp.sum(dz * z)
    dscores = (scale * dz).T
    doc_grad, query_grad_t = score_backward(lows, highs, doc_tile, query_tile, picks, dscores)
    query_parts = query_grad_t.T.reshape(C, Q, 128)

    def query_part(k):
        return lax.dynamic_index_in_dim(query_parts, (c + k) % C, 0, keepdims=False)

    query_grad = query_part(0)
    for k in range(1, C):
        query_grad = query_grad + shift_cols(query_part(k), k)

    doc_sum = scatter_rows(doc_grad.reshape(R, DS, 128))
    unit_grad = jnp.concatenate([query_grad, doc_sum], axis=0)

    core = r % 2
    slots_back = range(C - 1, -1, -1)
    share = D // R
    x_bit, *z_bits = [1 << b for b in range(1, R.bit_length() - 1)]

    def side_of(bit):
        return ((r // bit) % 2).astype(jnp.int32)

    def halves_of(left_t):
        return left_t.reshape(R // 2, 2, share, n)

    def rows_of(left, side):
        return lax.dynamic_index_in_dim(left, side, 1, keepdims=False).reshape(-1, n)

    def send_plain(left, right):
        part = mm(rows_of(left, 1 - core), right).astype(BF16)
        Order.last += (part,)
        return swap_rows(part, 1)

    def keep_plain(left, right, arrived, k):
        kept = mm(rows_of(left, core), right) + arrived.astype(F32)
        if k > 0:
            kept = kept.astype(BF16)
        Order.last += (kept,)
        return kept[None] if k == 0 else shift_cols(kept, C - k)[None]

    def next_fold(states, bit, inner):
        send, keep = fold(side_of(bit), [s[0] for s in states], [s[1] for s in states], inner)
        return keep, swap_rows(send, bit)

    def cols_state(kept):
        rest = kept[1]
        for other in kept[2:]:
            rest = rest.astype(F32) + other.astype(F32)
        return kept[0], rest

    embed_grad, resid_two_grad, branch, branch_t, head_sums = head_pull(
        unit_grad, unit, unit_inverse, wproj, normed_two, inverse_two, vectors
    )
    down_left, down_right = halves_of(branch_t), active
    pre_grads, up_sums, down_kept = [None] * C, [None] * C, [None] * C
    down_arrived = [None] * C
    for k in slots_back:
        down_arrived[k] = send_plain(down_left, down_right[k])
    for k in slots_back:
        pre_grads[k], up_sums[k] = up_pull(branch, wdown_slots[k], slopes[k])
        if k > 0:
            down_kept[k] = keep_plain(down_left, down_right[k], down_arrived[k], k)
    up_left, up_right = halves_of(hidden_t), pre_grads
    up_arrived, up_kept = [None] * C, [None] * C
    for k in slots_back:
        up_arrived[k] = send_plain(up_left, up_right[k])
    down_kept[0] = keep_plain(down_left, down_right[0], down_arrived[0], 0)
    for k in slots_back[:-1]:
        up_kept[k] = keep_plain(up_left, up_right[k], up_arrived[k], k)
    resid_one_grad, branch_one_t, hidden_sums, *attended_grads = hidden_pull(
        resid_two_grad, normed_one, inverse_one, vectors, pre_grads, wup_slots, wout_slots
    )
    up_kept[0] = keep_plain(up_left, up_right[0], up_arrived[0], 0)
    mixed_grads, mixed_sums = [None] * C, [None] * C
    def gather_small():
        proj_grad = mm(embed_grad, output_low, TN).reshape(R, -1, C, width)
        def cut(values, slot_rows):
            return values.reshape(slot_rows, R, -1)

        own_order = [(c - k) % C for k in range(C)]
        canonical = jnp.stack(
            [hidden_sums[0], hidden_sums[1], hidden_sums[2], head_sums[0], head_sums[1], head_sums[2]]
        ).reshape(6, C, R, -1)
        slots_small = []
        for k in range(C):
            rows = [mixed_sums[k][j].reshape(R, -1) for j in range(3)]
            rows.append(up_sums[k][0].reshape(R, -1))
            rows += [
                lax.dynamic_index_in_dim(canonical[j], own_order[k], 0, keepdims=False)
                for j in range(6)
            ]
            own_proj_grad = lax.dynamic_index_in_dim(proj_grad, own_order[k], 2, keepdims=False)
            rows.append(own_proj_grad.reshape(R, -1))
            rows.append(jnp.broadcast_to(scale_part, (R, 1)))
            slots_small.append(jnp.concatenate(rows, axis=1))
        return jnp.stack(slots_small, axis=1)

    def pull_attention(k):
        mixed_grads[k], mixed_sums[k] = attention_backward(
            spans, qkv[k], exts[k], attended[k], rests[k], attended_grads[k], ext_k, cosine, sine,
            tile,
        )

    for k in slots_back[:-1]:
        pull_attention(k)
    wide_state = next_fold([cols_state(down_kept), cols_state(up_kept)], z_bits[0], 2 * share)
    pull_attention(0)
    sent = [
        shift_cols(token_pull((c + k) % C, resid_one_grad, mixed_grads, wqkv_slots, BF16), k)
        for k in range(1, C)
    ]
    own_tokens = token_pull(c, resid_one_grad, mixed_grads, wqkv_slots, F32)
    late_grad, wide_grad, small = late_sums(
        R, C, halves_of(x_t), halves_of(branch_one_t), mixed_grads, attended, *wide_state,
        gather_small(),
    )
    tokens_grad = assemble(c, Q, [own_tokens] + sent)
    qkv_grad, out_grad = late_grad[:3], late_grad[3]
    down_grad, up_grad = wide_grad
    one = D // (C * R)
    up_part = bup_slots[0].shape[1] // R
    bounds = [3 * one, 3 * one + up_part]
    for _ in range(6):
        bounds.append(bounds[-1] + one)
    pieces = [small[a:b] for a, b in zip(bounds[:-1], bounds[1:])]
    bup_out, bout_out, gain1_out, bias1_out, bdown_out, gain2_out, bias2_out = pieces
    return (
        scores,
        loss,
        tokens_grad,
        qkv_grad,
        small[: bounds[0]].reshape(3, one),
        out_grad.T,
        bout_out,
        gain1_out,
        bias1_out,
        up_grad,
        bup_out,
        down_grad.T,
        bdown_out,
        gain2_out,
        bias2_out,
        small[bounds[-1] : -1].reshape(-1, width).T,
        small[-1:],
    )


def solution(mesh):
    in_specs = (
        P("rows", "cols"),
        P(),
        P("rows", "cols", None),
        P("rows"),
        P(None, None, "cols"),
        P(None, "cols"),
        P("cols", None),
        P("cols"),
        P("cols"),
        P("cols"),
        P(None, "cols"),
        P("cols"),
        P("cols", None),
        P("cols"),
        P("cols"),
        P("cols"),
        P("cols", None),
        P(),
    )
    out_specs = (
        P("rows", "cols"),
        P("rows"),
        P("rows", "cols"),
        P(None, "rows", "cols"),
        P(None, ("cols", "rows")),
        P("cols", "rows"),
        P(("cols", "rows")),
        P(("cols", "rows")),
        P(("cols", "rows")),
        P("rows", "cols"),
        P(("cols", "rows")),
        P("cols", "rows"),
        P(("cols", "rows")),
        P(("cols", "rows")),
        P(("cols", "rows")),
        P("cols", "rows"),
        P(),
    )
    return jax.shard_map(
        on_device, mesh=mesh, in_specs=in_specs, out_specs=out_specs, check_vma=False
    )
```

```python
import functools
import math

import jax
import jax.numpy as jnp
from jax import lax
from jax.experimental import pallas as pl
from jax.experimental.pallas import tpu as pltpu
from jax.sharding import PartitionSpec as P

DH = 64
QLEN = 32
ROW_LEN = 1024
F32 = jnp.float32
BF16 = jnp.bfloat16
VMEM_LIMIT = 56 * 1024 * 1024
NT = (((1,), (1,)), ((), ()))
NN = (((1,), (0,)), ((), ()))
TN = (((0,), (0,)), ((), ()))


def mm(left, right, dims=NN):
    return lax.dot_general(left, right, dims, preferred_element_type=F32)


def row_step(rows):
    return 512 if rows % 512 == 0 else 128


def parts_of(step):
    size = 256 if step % 256 == 0 else 128
    return [slice(first, first + size) for first in range(0, step, size)]


def held(shape):
    return pl.BlockSpec(shape, lambda *_: (0,) * len(shape), pipeline_mode=pl.Buffered(1))


def shaped(dtype, *shape):
    return jax.ShapeDtypeStruct(shape, dtype)


VMEM_SLACK = 16 * 1024 * 1024


class Order:
    last = ()


def call(
    body, name, grid, in_specs, out_specs, out_shape, operands, flops, scratch=(), prefetch=0, after=(),
    remote=None,
):
    count = len(operands)
    after = tuple(after) + Order.last

    def wrapped(*refs):
        body(*refs[:count], *refs[count + len(after) :])

    size = sum(math.prod(o.shape) * o.dtype.itemsize for o in list(operands) + list(out_shape))
    if flops == 0:
        size = 1024
    need = VMEM_SLACK
    for spec, array in zip(list(in_specs) + list(out_specs), list(operands)[prefetch:] + list(out_shape)):
        if spec.block_shape is not None:
            block = math.prod(spec.block_shape) * array.dtype.itemsize
            need += block if spec.pipeline_mode is not None else 2 * block
    for buffer in scratch:
        if getattr(buffer, "memory_space", None) == pltpu.VMEM:
            need += math.prod(buffer.shape) * jnp.dtype(buffer.dtype).itemsize
    outs = pl.pallas_call(
        wrapped,
        grid_spec=pltpu.PrefetchScalarGridSpec(
            num_scalar_prefetch=prefetch,
            grid=grid,
            in_specs=list(in_specs) + [pl.BlockSpec(memory_space=pl.ANY)] * len(after),
            out_specs=out_specs,
            scratch_shapes=list(scratch),
        ),
        out_shape=out_shape,
        compiler_params=pltpu.CompilerParams(
            vmem_limit_bytes=min(VMEM_LIMIT, need), collective_id=remote, has_side_effects=remote is not None
        ),
        cost_estimate=pl.CostEstimate(flops=flops, bytes_accessed=size, transcendentals=0),
        name=name,
    )(*operands, *after)
    Order.last = (min(outs, key=lambda out: out.size * out.dtype.itemsize),)
    return outs


def row_spec(step, width):
    return pl.BlockSpec((step, width), lambda i, *_: (i, 0))


def column_spec(width, step):
    return pl.BlockSpec((width, step), lambda i, *_: (0, i))


MESH = pl.DeviceIdType.MESH
ANYWHERE = pl.BlockSpec(memory_space=pl.ANY)


def side_at(row, bit):
    return (row // bit) % 2


def across(row, bit):
    return row + bit * (1 - 2 * side_at(row, bit))


def flipped(row, bits):
    bit = 1
    while bit <= bits:
        if bits & bit:
            row = across(row, bit)
        bit *= 2
    return row


def greet(devices):
    barrier = pltpu.get_barrier_semaphore()
    for device in devices:
        pl.semaphore_signal(barrier, inc=1, device_id=device, device_id_type=MESH)
    pl.semaphore_wait(barrier, len(devices))


def send(source, target, sent, arrived, device):
    copy = pltpu.make_async_remote_copy(
        src_ref=source,
        dst_ref=target,
        send_sem=sent,
        recv_sem=arrived,
        device_id=device,
        device_id_type=MESH,
    )
    copy.start()
    return copy


def spread_order(count):
    pieces = sorted(range(count), key=lambda piece: (piece.bit_count(), -piece))
    order = []
    for piece in pieces:
        lowest = piece & -piece if piece else count
        bit = lowest // 2
        bits = []
        while bit:
            bits.append(bit)
            bit //= 2
        order.append((piece, bits))
    return order


def gather_kernel(rows, own, out, own_sem, sent, arrived):
    r = lax.axis_index("rows")
    bits = [1 << b for b in range(rows.bit_length() - 1)]
    greet([{"rows": across(r, bit)} for bit in bits])
    local = pltpu.make_async_copy(own, out.at[r], own_sem)
    local.start()
    copies = {}
    size = own.shape[0] // PARTS
    for piece, over in spread_order(rows):
        row = flipped(r, piece)
        for part in range(PARTS):
            at = pl.ds(part * size, size)
            if piece:
                copies[piece, part].wait_recv()
            for bit in over:
                copies[piece | bit, part] = send(
                    out.at[row, at] if piece else own.at[at], out.at[row, at],
                    sent.at[piece | bit, part], arrived.at[piece | bit, part],
                    {"rows": across(r, bit)},
                )
    for copy in copies.values():
        copy.wait_send()
    local.wait()


PARTS = 2


def gather_rows(rows, own, remote):
    return call(
        functools.partial(gather_kernel, rows), "gather_rows", (1,), [ANYWHERE], [ANYWHERE],
        [shaped(own.dtype, rows, *own.shape)], (own,), 0, remote=remote,
        scratch=[
            pltpu.SemaphoreType.DMA, pltpu.SemaphoreType.DMA((rows, PARTS)),
            pltpu.SemaphoreType.DMA((rows, PARTS)),
        ],
    )[0]


def scatter_kernel(rows, parts, out, sent, arrived, *buffers):
    r = lax.axis_index("rows")
    bits = [1 << b for b in range(rows.bit_length() - 1)]
    greet([{"rows": across(r, bit)} for bit in bits])
    outgoing, incoming = buffers[: len(bits)], buffers[len(bits) :]
    size = parts.shape[1] // PARTS
    copies = {}

    def total(flips, levels, part):
        row, at = flipped(r, flips), pl.ds(part * size, size)
        value = parts[row, at]
        for level in range(levels):
            copies[level, flips >> (level + 1), part].wait_recv()
            value = value + incoming[level][row // (2 << level), at].astype(F32)
        return value

    for level, bit in enumerate(bits):
        count = rows // (2 << level)
        for turn in sorted(range(count), key=lambda f: tuple(-((f >> b) & 1) for b in range(8))):
            flips = (turn << (level + 1)) | bit
            place = flipped(r, flips) // (2 << level)
            for part in range(PARTS):
                at = pl.ds(part * size, size)
                outgoing[level][place, at] = total(flips, level, part).astype(BF16)
                name = rows - 2 * count + turn
                copies[level, turn, part] = send(
                    outgoing[level].at[place, at], incoming[level].at[place, at],
                    sent.at[name, part], arrived.at[name, part], {"rows": across(r, bit)},
                )
    for part in range(PARTS):
        out[part * size : (part + 1) * size, :] = total(0, len(bits), part)
    for copy in copies.values():
        copy.wait_send()


def scatter_rows(parts):
    rows, height, width = parts.shape
    levels = rows.bit_length() - 1
    buffers = [
        pltpu.VMEM((rows // (2 << level), height, width), BF16) for level in range(levels)
    ]
    return call(
        functools.partial(scatter_kernel, rows), "scatter_rows", (1,), [held(parts.shape)],
        [pl.BlockSpec((height, width), lambda *_: (0, 0))], [shaped(F32, height, width)],
        (parts,), 0, remote=3,
        scratch=[
            pltpu.SemaphoreType.DMA((rows, PARTS)), pltpu.SemaphoreType.DMA((rows, PARTS)),
        ] + buffers + buffers,
    )[0]


def small_sums(rows, cols, parts, out, *refs):
    bits = [1 << b for b in range(rows.bit_length() - 1)]
    sent, arrived = refs[:2]
    core_in, cols_in, totals = refs[2], refs[3], refs[4 : 4 + len(bits)]
    row_ins = refs[4 + len(bits) :]
    r, c = lax.axis_index("rows"), lax.axis_index("cols")
    others = [{"cols": (c + cols - k) % cols} for k in range(1, cols)]
    core = side_at(r, 1)
    copies = {}

    def first():
        copies["core"] = send(
            parts.at[:, 1 - core], core_in, sent.at[0], arrived.at[0], {"rows": across(r, 1)}
        )

    def second():
        copies["core"].wait()
        totals[0][...] = parts[:, core] + core_in[...]
        for k in range(1, cols):
            copies["cols", k] = send(
                totals[0].at[:, k], cols_in.at[k - 1], sent.at[k], arrived.at[k], others[k - 1]
            )

    def third():
        total = totals[0][:, 0]
        for k in range(1, cols):
            copies["cols", k].wait()
            total = total + cols_in[k - 1]
        pass_on(0, total)

    def pass_on(level, total):
        if level == len(bits) - 1:
            out[...] = total[0]
            return
        whole = totals[1 + level]
        whole[...] = total.reshape(whole.shape)
        copies["row", level] = send(
            whole.at[:, 1 - side_at(r, bits[1 + level])], row_ins[level],
            sent.at[cols + level], arrived.at[cols + level],
            {"rows": across(r, bits[1 + level])},
        )

    def later(level):
        copies["row", level].wait()
        pass_on(level + 1, totals[1 + level][:, side_at(r, bits[1 + level])] + row_ins[level][...])

    return [first, second, third] + [
        functools.partial(later, level) for level in range(len(bits) - 1)
    ]


def small_blocks(rows, cols, parts):
    length = parts.shape[2]
    width = -(-length // 1024) * 128
    parts = jnp.pad(parts, ((0, 0), (0, 0), (0, 8 * width - length)))
    parts = parts.reshape(rows // 2, 2, cols, 8, width)
    levels = rows.bit_length() - 1
    heights = [rows >> (level + 1) for level in range(1, levels)]
    scratch = [
        pltpu.SemaphoreType.DMA((cols + levels,)), pltpu.SemaphoreType.DMA((cols + levels,)),
        pltpu.VMEM((rows // 2, cols, 8, width), F32),
        pltpu.VMEM((cols - 1, rows // 2, 8, width), F32),
        pltpu.VMEM((rows // 2, cols, 8, width), F32),
    ]
    scratch += [pltpu.VMEM((height, 2, 8, width), F32) for height in heights]
    scratch += [pltpu.VMEM((height, 8, width), F32) for height in heights]
    return parts, scratch


def late_kernel(rows, cols, *refs):
    tokens_t, branch_t = refs[:2]
    far_rights, far_attended, refs = refs[2 : 2 + cols], refs[2 + cols : 2 + 2 * cols], refs[2 + 2 * cols :]
    (du_own, du_in, small, out, du_out, small_out), refs = refs[:6], refs[6:]
    (rights, right_sem), refs = refs[:2], refs[2:]
    (core_out, core_in, x_out, x_in, kept, cols_out, cols_in), refs = refs[:7], refs[7:]
    r, c = lax.axis_index("rows"), lax.axis_index("cols")
    x_bit, *z_bits = [1 << b for b in range(1, rows.bit_length() - 1)]
    levels = len(z_bits)
    z_out, z_in, z_kept = refs[:levels], refs[levels : 2 * levels], refs[2 * levels : 3 * levels]
    refs = refs[3 * levels :]
    du_z_out, du_z_in, du_kept = refs[:levels], refs[levels : 2 * levels], refs[2 * levels : 3 * levels]
    refs = refs[3 * levels :]
    (core_sem, x_sem, cols_sem, z_sem, du_sem), refs = refs[:5], refs[5:]
    small_steps = small_sums(rows, cols, small, small_out, *refs)
    share = out.shape[1]
    others = [{"cols": (c + cols - k) % cols} for k in range(1, cols)]
    core, x_side = side_at(r, 1), side_at(r, x_bit)
    greet([{"rows": across(r, bit)} for bit in [1, x_bit] + z_bits] + others)
    chunks = range(4)
    slots = range(cols - 1, -1, -1)
    copies = {}

    def halves(total, side, inner):
        pairs = total.reshape(-1, 2, inner, total.shape[1])
        near = jnp.where(side == 0, pairs[:, 0], pairs[:, 1]).reshape(-1, total.shape[1])
        far = jnp.where(side == 0, pairs[:, 1], pairs[:, 0]).reshape(-1, total.shape[1])
        return near, far

    def product(side, slot, chunk):
        left = (tokens_t if chunk < 3 else branch_t)[:, side]
        return mm(left.reshape(-1, left.shape[-1]), rights[slot, chunk])

    def load(slot, chunk):
        source = far_rights[slot].at[chunk] if chunk < 3 else far_attended[slot]
        return pltpu.make_async_copy(source, rights.at[slot, chunk], right_sem.at[slot, chunk])

    for chunk in chunks:
        for slot in slots:
            load(slot, chunk).start()

    def begin(chunk):
        for slot in slots:
            load(slot, chunk).wait()
            if chunk >= 2:
                copies["core", slot, chunk - 2].wait_send()
            core_out[slot, chunk % 2] = product(1 - core, slot, chunk).astype(BF16)
            copies["core", slot, chunk] = send(
                core_out.at[slot, chunk % 2], core_in.at[slot, chunk],
                core_sem.at[0, slot, chunk], core_sem.at[1, slot, chunk],
                {"rows": across(r, 1)},
            )

    def after_core(chunk):
        for slot in slots:
            total = product(core, slot, chunk)
            copies["core", slot, chunk].wait_recv()
            near, far = halves(total + core_in[slot, chunk].astype(F32), x_side, share)
            x_out[slot, chunk] = far.astype(BF16)
            kept[slot, chunk] = near
            copies["x", slot, chunk] = send(
                x_out.at[slot, chunk], x_in.at[slot, chunk], x_sem.at[0, slot, chunk],
                x_sem.at[1, slot, chunk], {"rows": across(r, x_bit)},
            )

    def after_x(chunk):
        for slot in slots:
            copies["x", slot, chunk].wait_recv()
            total = kept[slot, chunk] + x_in[slot, chunk].astype(F32)
            if slot == 0:
                kept[0, chunk] = total
            else:
                cols_out[slot - 1, chunk] = total.astype(BF16)
                copies["cols", slot, chunk] = send(
                    cols_out.at[slot - 1, chunk], cols_in.at[slot - 1, chunk],
                    cols_sem.at[0, slot - 1, chunk], cols_sem.at[1, slot - 1, chunk],
                    others[slot - 1],
                )

    def after_cols(chunk):
        total = kept[0, chunk]
        for slot in slots[:-1]:
            copies["cols", slot, chunk].wait_recv()
            total = total + cols_in[slot - 1, chunk].astype(F32)
        pass_z(chunk, 0, total)

    def pass_z(chunk, level, total):
        if level == levels:
            out[chunk] = total
            return
        bit = z_bits[level]
        near, far = halves(total, side_at(r, bit), share)
        z_out[level][chunk] = far.astype(BF16)
        z_kept[level][chunk] = near
        copies["z", level, chunk] = send(
            z_out[level].at[chunk], z_in[level].at[chunk], z_sem.at[0, level, chunk],
            z_sem.at[1, level, chunk], {"rows": across(r, bit)},
        )

    def after_z(chunk, level):
        copies["z", level, chunk].wait_recv()
        pass_z(chunk, level + 1, z_kept[level][chunk] + z_in[level][chunk].astype(F32))

    def pass_du(place, level, total):
        if level == levels:
            du_out[place] = total
            return
        bit = z_bits[level]
        near, far = halves(total, side_at(r, bit), share)
        du_z_out[level][place] = far.astype(BF16)
        du_kept[level][place] = near
        copies["du", level, place] = send(
            du_z_out[level].at[place], du_z_in[level].at[place], du_sem.at[0, level, place],
            du_sem.at[1, level, place], {"rows": across(r, bit)},
        )

    def after_du(place, level):
        copies["du", level, place].wait_recv()
        pass_du(place, level + 1, du_kept[level][place] + du_z_in[level][place].astype(F32))

    for place in range(2):
        pass_du(place, 0, du_own[place] + du_in[place].astype(F32))
    stages = [(0, begin), (1, after_core), (3, after_x), (4, after_cols)]
    stages += [(5 + level, functools.partial(after_z, level=level)) for level in range(levels)]
    for turn in range(len(chunks) + stages[-1][0]):
        for delay, stage in stages[::-1]:
            if 0 <= turn - delay < len(chunks):
                stage(turn - delay)
        if 3 <= turn < 3 + levels:
            for place in range(2):
                after_du(place, turn - 3)
        if turn >= 1 and small_steps:
            small_steps.pop(0)()
    for step in small_steps:
        step()
    for name, copy in copies.items():
        if name[0] != "core" or name[2] >= 2:
            copy.wait_send()


def late_sums(rows, cols, tokens_t, branch_t, rights, attended, du_own, du_in, small):
    share, n = tokens_t.shape[2:]
    width = attended[0].shape[1]
    wide = du_own.shape[2]
    half, quarter = rows // 2 * share, rows // 4 * share
    levels = rows.bit_length() - 3
    heights = [quarter >> (level + 1) for level in range(levels)]

    def vmem(dtype, *shape):
        return pltpu.VMEM(shape, dtype)

    def pair_of(*shape):
        return pltpu.SemaphoreType.DMA((2,) + shape)

    length = small.shape[2]
    small, small_scratch = small_blocks(rows, cols, small)
    operands = (tokens_t, branch_t, *rights, *attended, du_own, du_in, small)
    scratch = [
        vmem(BF16, cols, 4, n, width), pltpu.SemaphoreType.DMA((cols, 4)),
        vmem(BF16, cols, 2, half, width), vmem(BF16, cols, 4, half, width),
        vmem(BF16, cols, 4, quarter, width), vmem(BF16, cols, 4, quarter, width),
        vmem(F32, cols, 4, quarter, width),
        vmem(BF16, cols - 1, 4, quarter, width), vmem(BF16, cols - 1, 4, quarter, width),
    ]
    for count, size in ((4, width), (2, wide)):
        for dtype in (BF16, BF16, F32):
            scratch += [vmem(dtype, count, height, size) for height in heights]
    scratch += [
        pair_of(cols, 4), pair_of(cols, 4), pair_of(cols - 1, 4), pair_of(levels, 4),
        pair_of(levels, 2),
    ]
    def whole(*shape):
        return pl.BlockSpec(shape, lambda *_: (0,) * len(shape))

    late, wide_sum, small_sum = call(
        functools.partial(late_kernel, rows, cols), "late_sums", (1,),
        [held(tokens_t.shape), held(branch_t.shape)] + [ANYWHERE] * (2 * cols)
        + [held(du_own.shape), held(du_in.shape), held(small.shape)],
        [whole(4, share, width), whole(2, share, wide), whole(*small.shape[3:])],
        [
            shaped(F32, 4, share, width), shaped(F32, 2, share, wide), shaped(F32, *small.shape[3:])
        ],
        operands, 100_000_000_000, remote=5, scratch=scratch + small_scratch,
    )
    return late, wide_sum, small_sum.reshape(-1)[:length]


def swap_halves(block):
    lane = lax.broadcasted_iota(jnp.int32, block.shape, 1)
    return jnp.where((lane & 32) == 0, pltpu.roll(block, 96, 1), pltpu.roll(block, 32, 1))


def qkv_kernel(x_ref, w_ref, b_ref, cos_ref, sin_ref, out_ref):
    which = pl.program_id(0)
    bias = b_ref[pl.ds(which, 1), :]

    @pl.when(which < 2)
    def _():
        for at in parts_of(x_ref.shape[0]):
            mixed = mm(x_ref[at, :], w_ref[0]) + bias
            for first in range(0, mixed.shape[1], 128):
                block = mixed[:, first : first + 128]
                turned = block * cos_ref[at, :] + swap_halves(block) * sin_ref[at, :]
                out_ref[0, at, first : first + 128] = turned.astype(BF16)

    @pl.when(which == 2)
    def _():
        for at in parts_of(x_ref.shape[0]):
            out_ref[0, at, :] = (mm(x_ref[at, :], w_ref[0]) + bias).astype(BF16)


def project_qkv(x, weight, bias, cosine, sine, after=()):
    n, D = x.shape
    width = weight.shape[2]
    return call(
        qkv_kernel, "project_qkv", (3,),
        [
            held((n, D)), pl.BlockSpec((1, D, width), lambda j: (j, 0, 0)), held(bias.shape),
            held((n, 128)), held((n, 128)),
        ],
        [pl.BlockSpec((1, n, width), lambda j: (j, 0, 0))],
        [shaped(BF16, 3, n, width)],
        (x, weight, bias, cosine, sine), 6 * n * D * width, after=after,
    )[0]


def prepare_kernel(
    q_rows, sizes_ref, picks_ref, docs_ref, cos_ref, sin_ref, ext_k_ref, ext_q_ref, out_ref
):
    n = cos_ref.shape[0]
    size = math.gcd(256, math.gcd(q_rows, n))
    lane = lax.broadcasted_iota(jnp.int32, (size, 128), 1)
    frequency = jnp.exp((lane & (DH // 2 - 1)).astype(F32) * (-2.0 * math.log(10000.0) / DH))
    place_lane = lane & (DH - 1)
    for first in range(0, n, size):
        at = slice(first, first + size)
        row = lax.broadcasted_iota(jnp.int32, (size, 128), 0) + first
        if first < q_rows:
            position, segment = row & (QLEN - 1), (row // QLEN) & (SEGMENTS - 1)
        else:
            place = row - q_rows
            begin, segment, end = jnp.zeros_like(row), jnp.zeros_like(row), 0
            for doc in range(sizes_ref.shape[0]):
                end = end + sizes_ref[doc]
                passed = place >= end
                begin = jnp.where(passed, end, begin)
                segment = segment + passed.astype(jnp.int32)
            position = place - begin
        angles = position.astype(F32) * frequency
        sine = jnp.sin(angles)
        cos_ref[at, :] = jnp.cos(angles)
        sin_ref[at, :] = jnp.where((lane & (DH // 2)) == 0, -sine, sine)
        same = segment == place_lane
        ones = (place_lane >= SEGMENTS) & (place_lane < SEGMENTS + 3)
        ext_k_ref[at, :] = (same | ones).astype(F32).astype(BF16)
        apart = (place_lane < SEGMENTS) & jnp.logical_not(same)
        ext_q_ref[at, :] = jnp.where(apart, -1e30, 0.0).astype(BF16)
    queries = picks_ref.shape[0]
    begins, sizes = docs_ref[:, 0:1], docs_ref[:, 1:2]
    groups, docs = out_ref.shape[:2]
    for first in range(0, queries, 4):
        lanes = jnp.concatenate([picks_ref[first + j] for j in range(4)], axis=1)
        rows = begins + lax.rem(lanes, jnp.broadcast_to(sizes, lanes.shape))
        at = slice(first * QLEN, (first + 4) * QLEN)
        for group in range(groups):
            out_ref[group, :, at] = rows[group * docs : (group + 1) * docs]


def prepare(n, q_rows, own_sizes, match_picks, begins, sizes):
    groups, docs = sizes.shape
    width = match_picks.shape[0] * QLEN
    table = jnp.stack([begins.reshape(-1), sizes.reshape(-1)], axis=1)
    return call(
        functools.partial(prepare_kernel, q_rows), "prepare", (1,),
        [held(match_picks.shape), held(table.shape)],
        [pl.BlockSpec((n, 128), lambda *_: (0, 0))] * 4
        + [pl.BlockSpec((groups, docs, width), lambda *_: (0, 0, 0))],
        [
            shaped(F32, n, 128), shaped(F32, n, 128), shaped(BF16, n, 128), shaped(BF16, n, 128),
            shaped(jnp.int32, groups, docs, width),
        ],
        (own_sizes, match_picks, table), 0, prefetch=1,
    )


def normed_rows(residual):
    mean = jnp.mean(residual, axis=1, keepdims=True)
    centred = residual - mean
    inverse = lax.rsqrt(jnp.mean(centred * centred, axis=1, keepdims=True) + 1e-05)
    return centred * inverse, inverse


def norm_pull(grad_rows, normed, inverse, gain):
    spread = grad_rows * gain
    return inverse * (
        spread
        - jnp.mean(spread, axis=1, keepdims=True)
        - normed * jnp.mean(spread * normed, axis=1, keepdims=True)
    )


def column_sums(*arrays):
    rows = [jnp.sum(array, axis=0, keepdims=True) for array in arrays]
    rows.append(jnp.zeros((8 - len(rows), rows[0].shape[1]), F32))
    return jnp.concatenate(rows, axis=0)


def add_over_steps(ref, value):
    first = pl.program_id(0) == 0

    @pl.when(first)
    def _():
        ref[...] = value

    @pl.when(jnp.logical_not(first))
    def _():
        ref[...] += value


def out_norm_kernel(slots, *refs):
    x_ref, vec_ref = refs[:2]
    att_refs, w_refs = refs[2 : 2 + slots], refs[2 + slots : 2 + 2 * slots]
    normed_ref, inverse_ref, low_ref, turned_ref = refs[2 + 2 * slots :]
    for at in parts_of(x_ref.shape[0]):
        residual = x_ref[at, :].astype(F32) + vec_ref[0:1, :]
        for att_ref, w_ref in zip(att_refs, w_refs):
            residual = residual + mm(att_ref[at, :], w_ref[...])
        normed, inverse = normed_rows(residual)
        hidden = normed * vec_ref[1:2, :] + vec_ref[2:3, :]
        normed_ref[at, :] = normed
        inverse_ref[at, :] = inverse
        low_ref[at, :] = hidden.astype(BF16)
        turned_ref[:, at] = hidden.T.astype(BF16)


def out_and_norm(x, vectors, attended, weights):
    n, D = x.shape
    step = row_step(n)
    slots = len(attended)
    width = attended[0].shape[1]
    return call(
        functools.partial(out_norm_kernel, slots), "out_and_norm", (n // step,),
        [row_spec(step, D), held(vectors.shape)]
        + [row_spec(step, width)] * slots + [held((width, D))] * slots,
        [row_spec(step, D), row_spec(step, 1), row_spec(step, D), column_spec(D, step)],
        [shaped(F32, n, D), shaped(F32, n, 1), shaped(BF16, n, D), shaped(BF16, D, n)],
        (x, vectors, *attended, *weights), 2 * n * D * D,
    )


GELU_TERMS = (
    0.23532527933595032, 0.09138803439798156, 0.6495603483388861,
    -0.6354014529895687, 0.8866650885491606, -0.22753729931242958,
)


def gelu_parts(values):
    size = jnp.abs(values)
    part = pl.reciprocal(1.0 + (0.39 / math.sqrt(2.0)) * size)
    bell = jnp.exp(-0.5 * (values * values))
    series = 0.5 * GELU_TERMS[-1]
    for term in GELU_TERMS[-2::-1]:
        series = series * part + 0.5 * term
    tail = series * part * bell
    below = jnp.where(values >= 0.0, 1.0 - tail, tail)
    return values * below, below + values * bell * (1.0 / math.sqrt(2.0 * math.pi))


def up_kernel(x_ref, w_ref, b_ref, active_ref, slope_ref):
    width = w_ref.shape[1]
    chunk = min(256, width)
    for first in range(0, width, chunk):
        at = slice(first, first + chunk)
        active, slope = gelu_parts(mm(x_ref[...], w_ref[:, at]) + b_ref[:, at])
        active_ref[:, at] = active.astype(BF16)
        slope_ref[:, at] = slope


def up_and_gelu(x, weight, bias):
    n, D = x.shape
    width = weight.shape[1]
    step = row_step(n)
    return call(
        up_kernel, "up_and_gelu", (n // step,),
        [row_spec(step, D), held(weight.shape), held(bias.shape)],
        [row_spec(step, width)] * 2,
        [shaped(BF16, n, width), shaped(F32, n, width)],
        (x, weight, bias), 5 * n * D * width,
    )


def down_norm_kernel(slots, *refs):
    normed_ref, vec_ref, proj_ref = refs[:3]
    act_refs, w_refs = refs[3 : 3 + slots], refs[3 + slots : 3 + 2 * slots]
    normed_out, inverse_ref, low_ref, unit_ref, unit_low_ref, unit_inverse_ref = refs[3 + 2 * slots :]
    for at in parts_of(normed_ref.shape[0]):
        residual = normed_ref[at, :] * vec_ref[1:2, :] + vec_ref[2:3, :] + vec_ref[3:4, :]
        for act_ref, w_ref in zip(act_refs, w_refs):
            residual = residual + mm(act_ref[at, :], w_ref[...])
        normed, inverse = normed_rows(residual)
        normed_out[at, :] = normed
        inverse_ref[at, :] = inverse
        low = (normed * vec_ref[4:5, :] + vec_ref[5:6, :]).astype(BF16)
        low_ref[at, :] = low
        embedding = mm(low, proj_ref[...])
        unit_inverse = lax.rsqrt(jnp.sum(embedding * embedding, axis=1, keepdims=True) + 1e-06)
        unit = embedding * unit_inverse
        unit_ref[at, :] = unit
        unit_low_ref[at, :] = unit.astype(BF16)
        unit_inverse_ref[at, :] = unit_inverse


def down_and_norm(normed, vectors, proj, active, weights):
    n, D = normed.shape
    step = row_step(n)
    slots = len(active)
    width = active[0].shape[1]
    return call(
        functools.partial(down_norm_kernel, slots), "down_and_norm", (n // step,),
        [row_spec(step, D), held(vectors.shape), held(proj.shape)]
        + [row_spec(step, width)] * slots + [held((width, D))] * slots,
        [
            row_spec(step, D), row_spec(step, 1), row_spec(step, D),
            row_spec(step, 128), row_spec(step, 128), row_spec(step, 1),
        ],
        [
            shaped(F32, n, D), shaped(F32, n, 1), shaped(BF16, n, D),
            shaped(F32, n, 128), shaped(BF16, n, 128), shaped(F32, n, 1),
        ],
        (normed, vectors, proj, *active, *weights), 2 * n * D * width * slots,
    )


def head_pull_kernel(
    grad_ref, unit_ref, unit_inverse_ref, proj_ref, normed_ref, inverse_ref, vec_ref,
    embed_ref, residual_ref, low_ref, turned_ref, sum_ref,
):
    sums = []
    for at in parts_of(grad_ref.shape[0]):
        grad, unit = grad_ref[at, :], unit_ref[at, :]
        embed = grad - unit * jnp.sum(grad * unit, axis=1, keepdims=True)
        embed = (unit_inverse_ref[at, :] * embed).astype(BF16)
        embed_ref[at, :] = embed
        output_grad = mm(embed, proj_ref[...], NT)
        normed = normed_ref[at, :]
        residual = norm_pull(output_grad, normed, inverse_ref[at, :], vec_ref[4:5, :])
        residual_ref[at, :] = residual
        low_ref[at, :] = residual.astype(BF16)
        turned_ref[:, at] = residual.T.astype(BF16)
        sums.append(column_sums(residual, output_grad * normed, output_grad))
    add_over_steps(sum_ref, sum(sums))


def head_pull(unit_grad, unit, unit_inverse, proj, normed, inverse, vectors):
    n, D = normed.shape
    step = row_step(n)
    return call(
        head_pull_kernel, "head_pull", (n // step,),
        [
            row_spec(step, 128), row_spec(step, 128), row_spec(step, 1), held(proj.shape),
            row_spec(step, D), row_spec(step, 1), held(vectors.shape),
        ],
        [
            row_spec(step, 128), row_spec(step, D), row_spec(step, D),
            column_spec(D, step), pl.BlockSpec((8, D), lambda i: (0, 0)),
        ],
        [
            shaped(BF16, n, 128), shaped(F32, n, D), shaped(BF16, n, D),
            shaped(BF16, D, n), shaped(F32, 8, D),
        ],
        (unit_grad, unit, unit_inverse, proj, normed, inverse, vectors), 4 * n * D * 128,
    )


def up_pull_kernel(branch_ref, w_ref, slope_ref, out_ref, sum_ref):
    width = w_ref.shape[0]
    chunk = min(512, width)
    sums = []
    for first in range(0, width, chunk):
        at = slice(first, first + chunk)
        low = (mm(branch_ref[...], w_ref[at, :], NT) * slope_ref[:, at]).astype(BF16)
        out_ref[:, at] = low
        sums.append(column_sums(low.astype(F32)))
    add_over_steps(sum_ref, jnp.concatenate(sums, axis=1))


def up_pull(branch, weight, slope):
    n, D = branch.shape
    width = weight.shape[0]
    step = row_step(n)
    return call(
        up_pull_kernel, "up_pull", (n // step,),
        [row_spec(step, D), held(weight.shape), row_spec(step, width)],
        [row_spec(step, width), pl.BlockSpec((8, width), lambda i: (0, 0))],
        [shaped(BF16, n, width), shaped(F32, 8, width)],
        (branch, weight, slope), 2 * n * D * width,
    )


def hidden_pull_kernel(slots, *refs):
    residual_ref, normed_ref, inverse_ref, vec_ref = refs[:4]
    pre_refs, up_refs, out_refs = (refs[4 + j * slots : 4 + (j + 1) * slots] for j in range(3))
    rest = refs[4 + 3 * slots :]
    grad_ref, turned_ref, sum_ref = rest[:3]
    att_refs = rest[3:]
    sums = []
    for at in parts_of(residual_ref.shape[0]):
        hidden_grad = residual_ref[at, :]
        for pre_ref, up_ref in zip(pre_refs, up_refs):
            hidden_grad = hidden_grad + mm(pre_ref[at, :], up_ref[...], NT)
        normed = normed_ref[at, :]
        residual = norm_pull(hidden_grad, normed, inverse_ref[at, :], vec_ref[1:2, :])
        grad_ref[at, :] = residual
        low = residual.astype(BF16)
        turned_ref[:, at] = residual.T.astype(BF16)
        sums.append(column_sums(residual, hidden_grad * normed, hidden_grad))
        for att_ref, out_ref in zip(att_refs, out_refs):
            att_ref[at, :] = mm(low, out_ref[...], NT).astype(BF16)
    add_over_steps(sum_ref, sum(sums))


def hidden_pull(residual, normed, inverse, vectors, pre_grads, ups, outs):
    n, D = residual.shape
    step = row_step(n)
    slots = len(ups)
    wide, width = ups[0].shape[1], outs[0].shape[0]
    return call(
        functools.partial(hidden_pull_kernel, slots), "hidden_pull", (n // step,),
        [row_spec(step, D), row_spec(step, D), row_spec(step, 1), held(vectors.shape)]
        + [row_spec(step, wide)] * slots + [held((D, wide))] * slots
        + [held((width, D))] * slots,
        [row_spec(step, D), column_spec(D, step), pl.BlockSpec((8, D), lambda i: (0, 0))]
        + [row_spec(step, width)] * slots,
        [shaped(F32, n, D), shaped(BF16, D, n), shaped(F32, 8, D)]
        + [shaped(BF16, n, width)] * slots,
        (residual, normed, inverse, vectors, *pre_grads, *ups, *outs),
        0,
    )


def token_pull_kernel(slots, place_ref, *refs):
    residual_ref = refs[0]
    mixed_refs, w_refs = refs[1 : 1 + slots], refs[1 + slots : 1 + 2 * slots]
    out_ref = refs[-1]
    width = out_ref.shape[1]
    at = pl.ds(pl.multiple_of(place_ref[0] * width, width), width)
    total = residual_ref[...]
    for mixed_ref, w_ref in zip(mixed_refs, w_refs):
        for which in range(3):
            total = total + mm(mixed_ref[which], w_ref[which, at, :], NT)
    out_ref[...] = total.astype(out_ref.dtype)


def token_pull(place, residual, mixed_grads, weights, dtype):
    n, D = residual.shape
    step = row_step(n)
    slots = len(weights)
    width = weights[0].shape[2]
    return call(
        functools.partial(token_pull_kernel, slots), "token_pull", (n // step,),
        [pl.BlockSpec((step, width), lambda i, p: (i, p[0]))]
        + [pl.BlockSpec((3, step, width), lambda i, p: (0, i, 0))] * slots
        + [held((3, D, width))] * slots,
        [row_spec(step, width)],
        [shaped(dtype, n, width)],
        (place.reshape(1), residual, *mixed_grads, *weights), 0, prefetch=1,
    )[0]


def put_halves(total, inner, side, refs):
    pairs = total.reshape(-1, 2, inner, total.shape[1])
    keep = jnp.where(side == 0, pairs[:, 0], pairs[:, 1]).reshape(-1, total.shape[1])
    send = jnp.where(side == 0, pairs[:, 1], pairs[:, 0]).reshape(-1, total.shape[1])
    refs[0][0] = send.astype(BF16)
    refs[1][0] = keep


def grouped_index(starts, place, count):
    def index(j, i, *_):
        inside = (j >= starts[place]) & (j < starts[place + 1])
        row = jnp.clip(j - starts[place], 0, starts[place + 1] - starts[place] - 1)
        rest = jnp.where(j < starts[place], 0, count - 1)
        return row, 0, jnp.where(inside, i, rest)

    return index


def for_group(starts, body):
    if len(starts) == 2:
        body(0)
        return
    for place in range(len(starts) - 1):

        @pl.when((pl.program_id(0) >= starts[place]) & (pl.program_id(0) < starts[place + 1]))
        def _(place=place):
            body(place)


def join_kernel(slots, place_ref, *refs):
    out_ref = refs[-1]
    width = refs[0].shape[1]
    for k in range(slots):
        at = pl.ds(pl.multiple_of((place_ref[0] + slots - k) % slots * width, width), width)
        out_ref[:, at] = refs[k][...]


def join(c, slots):
    n, width = slots[0].shape
    D = width * len(slots)
    step = row_step(n)
    return call(
        functools.partial(join_kernel, len(slots)), "join", (n // step,),
        [row_spec(step, width)] * len(slots),
        [row_spec(step, D)], [shaped(BF16, n, D)], (c.reshape(1), *slots), 0, prefetch=1,
    )[0]


def assemble_kernel(place_ref, *refs):
    out_ref = refs[-1]
    slot = place_ref[1 + pl.program_id(0)]
    for k, ref in enumerate(refs[:-1]):

        @pl.when(slot == k)
        def _(ref=ref):
            out_ref[...] = ref[...].astype(F32)


def assemble(c, q_rows, slots):
    n, width = slots[0].shape
    count = len(slots)
    step = math.gcd(512, math.gcd(q_rows, n))
    q_steps, d_steps = q_rows // step, (n - q_rows) // step
    turns, owners = [], []
    for base, steps in ((0, q_steps), (q_steps, d_steps)):
        for owner in range(count):
            turns += [base + turn for turn in range(steps)]
            owners += [owner] * steps
    places = jnp.concatenate([c.reshape(1), (c - jnp.array(owners)) % count]).astype(jnp.int32)

    def turn_of(j, p):
        turn = jnp.where(j < count * q_steps, j % q_steps, q_steps + (j - count * q_steps) % d_steps)
        return turn, 0

    return call(
        assemble_kernel, "assemble", (len(turns),),
        [pl.BlockSpec((step, width), turn_of)] * count,
        [pl.BlockSpec((step, width), lambda j, p: (j, 0))],
        [shaped(F32, n * count, width)], (places, *slots), 0, prefetch=1,
    )[0]


def pass_on_kernel(in_ref, out_ref):
    out_ref[...] = in_ref[...]


def pass_on(array):
    spec = held(array.shape)
    return call(
        pass_on_kernel, "pass_on", (1,), [spec], [pl.BlockSpec(array.shape, lambda *_: (0,) * array.ndim)],
        [shaped(array.dtype, *array.shape)], (array,), 0,
    )[0]


def fold_kernel(starts, inner, place_ref, *refs):
    groups = len(starts) - 1

    def one_group(place):
        total = refs[place][0] + refs[groups + place][0].astype(F32)
        put_halves(total, inner, place_ref[0], refs[2 * groups :])

    for_group(starts, one_group)


def fold(side, owns, arrived, inner):
    _, rows, m = owns[0].shape
    chunk = min(1024, m)
    starts = [0]
    for own in owns:
        starts.append(starts[-1] + own.shape[0])

    def spec(size):
        return pl.BlockSpec((1, size, chunk), lambda j, i, p: (j, 0, i))

    half = rows // 2
    specs = [
        pl.BlockSpec((1, rows, chunk), grouped_index(starts, place, m // chunk))
        for place in range(len(owns))
    ]
    return call(
        functools.partial(fold_kernel, starts, inner), "fold", (starts[-1], m // chunk),
        specs + specs, [spec(half), spec(half)],
        [shaped(BF16, starts[-1], half, m), shaped(F32, starts[-1], half, m)],
        (side.reshape(1), *owns, *arrived), 0, prefetch=1,
    )


SEGMENTS = 8
ATTENTION_LANES = 128


def half_lanes(block, head, other):
    lane = lax.broadcasted_iota(jnp.int32, block.shape, 1)
    return jnp.where((lane >= DH) == (head == 1), block, other)


def scaled(block):
    return (block.astype(F32) * DH**-0.5).astype(BF16)


def three_terms(value):
    high = value.astype(BF16).astype(F32)
    middle = (value - high).astype(BF16).astype(F32)
    return high, middle, value - high - middle


def for_spans(span_ref, tiles, body):
    @pl.loop(0, tiles)
    def _(step):
        low, high = span_ref[step], span_ref[tiles + step]
        for count in range(1, tiles + 1):

            @pl.when(high - low == count)
            def _(count=count):
                body(step, low, count)


def attention_forward_kernel(
    span_ref, qkv_ref, ext_k_ref, ext_q_ref, out_ref, rest_ref, ext_ref,
    keys_ref, queries_ref, *, tile,
):
    n = ext_k_ref.shape[0]
    tiles = n // tile
    pairs = qkv_ref.shape[2] // 128

    def lanes(pair):
        return slice(pair * 128, pair * 128 + 128)

    for pair in range(pairs):
        query = scaled(qkv_ref[0, :, lanes(pair)])
        for half in range(2):
            keys_ref[2 * pair + half] = half_lanes(qkv_ref[1, :, lanes(pair)], half, ext_k_ref[...])
            queries_ref[2 * pair + half] = half_lanes(query, half, ext_q_ref[...])

    def attend(step, low, count):
        rows = pl.ds(pl.multiple_of(step * tile, tile), tile)
        window = pl.ds(pl.multiple_of(low * tile, tile), count * tile)
        lane = lax.broadcasted_iota(jnp.int32, (tile, 128), 1)
        for pair in range(pairs):
            at = lanes(pair)
            outs, extra = [], ext_q_ref[rows, :].astype(F32)
            for half in range(2):
                head = 2 * pair + half
                logits = mm(queries_ref[head, rows, :], keys_ref[head, window, :], NT)
                top = jnp.max(logits, axis=1, keepdims=True)
                weights = jnp.exp(logits - top)
                mass = jnp.sum(weights, axis=1, keepdims=True)
                probs = (weights * (1.0 / mass)).astype(BF16)
                outs.append(mm(probs, qkv_ref[2, window, at]))
                first = SEGMENTS + DH * (1 - half)
                for place, term in enumerate(three_terms(-(top + jnp.log(mass)))):
                    extra = jnp.where(lane == first + place, term, extra)
            out = jnp.where(lane < DH, outs[0], outs[1])
            out_ref[rows, at] = out.astype(BF16)
            rest_ref[rows, at] = (out - out.astype(BF16).astype(F32)).astype(BF16)
            ext_ref[rows, at] = extra.astype(BF16)

    for_spans(span_ref, tiles, attend)


def attention_forward(spans, qkv, ext_k, ext_q, tile):
    _, n, width = qkv.shape
    span = min(width, ATTENTION_LANES)
    wide = pl.BlockSpec((n, span), lambda i, *_: (0, i))
    heads = pltpu.VMEM((span // DH, n, 128), BF16)
    return call(
        functools.partial(attention_forward_kernel, tile=tile), "attention_forward",
        (width // span,),
        [pl.BlockSpec((3, n, span), lambda i, *_: (0, 0, i)), held((n, 128)), held((n, 128))],
        [wide, wide, wide],
        [shaped(BF16, n, width)] * 3,
        (spans, qkv, ext_k, ext_q), 0, prefetch=1, scratch=[heads, heads],
    )


def attention_backward_kernel(
    span_ref, qkv_ref, ext_ref, att_ref, rest_ref, grad_ref, ext_k_ref, cos_ref, sin_ref,
    out_ref, sum_ref,
    keys_ref, turned_ref, values_ref, queries_ref, plain_ref, grads_ref, plain_grads_ref,
    dq_ref, dk_ref, dv_ref, *, tile,
):
    n = ext_k_ref.shape[0]
    tiles = n // tile
    pairs = qkv_ref.shape[2] // 128
    heads = range(2 * pairs)

    def lanes(head):
        return slice(head // 2 * 128, head // 2 * 128 + 128)

    def own_rows(head):
        return slice(head % 2 * DH, head % 2 * DH + DH)

    def rows(step):
        return pl.ds(pl.multiple_of(step * tile, tile), tile)

    @pl.loop(0, tiles)
    def _(step):
        at = rows(step)
        zeros = jnp.zeros((tile, 128), BF16)
        lane = lax.broadcasted_iota(jnp.int32, (tile, 128), 1)
        ext_k = ext_k_ref[at, :]
        for pair in range(pairs):
            cut = lanes(2 * pair)
            grad = grad_ref[at, cut]
            out = att_ref[at, cut].astype(F32) + rest_ref[at, cut].astype(F32)
            product = grad.astype(F32) * out
            query = scaled(qkv_ref[0, at, cut])
            turned_ref[pair, :, at] = scaled(qkv_ref[1, at, cut]).astype(F32).T.astype(BF16)
            for half in range(2):
                head = 2 * pair + half
                keys_ref[head, at, :] = half_lanes(qkv_ref[1, at, cut], half, ext_k)
                values_ref[head, at, :] = half_lanes(qkv_ref[2, at, cut], half, ext_k)
                whole = half_lanes(query, half, ext_ref[at, cut])
                queries_ref[head, step] = whole.astype(F32).T.astype(BF16)
                plain_ref[head, at, :] = half_lanes(query, half, zeros)
                plain_grads_ref[head, at, :] = half_lanes(grad, half, zeros)
                inner = jnp.sum(half_lanes(product, half, 0.0), axis=1, keepdims=True)
                extra = jnp.zeros((tile, 128), F32)
                for place, term in enumerate(three_terms(-inner)):
                    extra = jnp.where((lane & (DH - 1)) == SEGMENTS + place, term, extra)
                whole = half_lanes(grad.astype(F32), half, extra)
                grads_ref[head, step] = whole.T.astype(BF16)

    dk_ref[...] = jnp.zeros(dk_ref.shape, F32)
    dv_ref[...] = jnp.zeros(dv_ref.shape, F32)

    def pull(step, low, count):
        at = rows(step)
        window = pl.ds(pl.multiple_of(low * tile, tile), count * tile)
        for pair in range(pairs):
            probs, slopes, dq = [], [], []
            both = range(2 * pair, 2 * pair + 2)
            for head in both:
                weights = jnp.exp(mm(keys_ref[head, window, :], queries_ref[head, step]))
                flow = mm(values_ref[head, window, :], grads_ref[head, step])
                slope = (weights * flow).astype(BF16)
                probs.append(weights.astype(BF16))
                slopes.append(slope)
                dq.append(mm(turned_ref[pair, own_rows(head), window], slope))
            plain = jnp.concatenate([plain_ref[h, at, :] for h in both], axis=0)
            grads = jnp.concatenate([plain_grads_ref[h, at, :] for h in both], axis=0)
            cut = lanes(2 * pair)
            dv_ref[window, cut] += mm(jnp.concatenate(probs, axis=1), grads)
            dk_ref[window, cut] += mm(jnp.concatenate(slopes, axis=1), plain)
            dq_ref[at, cut] = jnp.concatenate(dq, axis=0).T

    for_spans(span_ref, tiles, pull)

    def finish(step, sums):
        cosine, sine = cos_ref[rows(step), :], sin_ref[rows(step), :]
        added = []
        for which, src in enumerate((dq_ref, dk_ref, dv_ref)):
            for pair in range(pairs):
                at = lanes(2 * pair)
                block = src[rows(step), at]
                if which < 2:
                    block = block * cosine - swap_halves(block) * sine
                low = block.astype(BF16)
                out_ref[which, rows(step), at] = low
                total = jnp.sum(low.astype(F32), axis=0, keepdims=True)
                added.append(sums[which * pairs + pair] + total)
        return tuple(added)

    zero = jnp.zeros((1, 128), F32)
    sums = lax.fori_loop(0, tiles, finish, (zero,) * (3 * pairs))
    sums = [jnp.concatenate(sums[w * pairs : (w + 1) * pairs], axis=1) for w in range(3)]
    sum_ref[...] = jnp.concatenate(sums + [jnp.zeros((5, pairs * 128), F32)], axis=0)


def attention_backward(
    spans, qkv, ext, attended, rest, grads, ext_k, cosine, sine, tile
):
    _, n, width = qkv.shape
    span = min(width, ATTENTION_LANES)
    wide = pl.BlockSpec((n, span), lambda i, *_: (0, i))
    three = pl.BlockSpec((3, n, span), lambda i, *_: (0, 0, i))
    tiles, pairs = n // tile, span // 128
    heads = pltpu.VMEM((2 * pairs, n, 128), BF16)
    turned = pltpu.VMEM((2 * pairs, tiles, 128, tile), BF16)
    return call(
        functools.partial(attention_backward_kernel, tile=tile), "attention_backward",
        (width // span,),
        [three, wide, wide, wide, wide, held((n, 128)), held((n, 128)), held((n, 128))],
        [three, pl.BlockSpec((8, span), lambda i, *_: (0, i))],
        [shaped(BF16, 3, n, width), shaped(F32, 8, width)],
        (spans, qkv, ext, attended, rest, grads, ext_k, cosine, sine), 0,
        prefetch=1,
        scratch=[
            heads, pltpu.VMEM((pairs, 128, n), BF16), heads, turned, heads, turned, heads,
        ] + [pltpu.VMEM((n, span), F32)] * 3,
    )


STRIP = 32


def token_sums(width, queries):
    token = lax.broadcasted_iota(jnp.int32, (width, queries), 0) // QLEN
    return token == lax.broadcasted_iota(jnp.int32, (width, queries), 1)


def score_kernel(low_ref, high_ref, doc_ref, query_ref, pick_ref, out_ref, sum_ref, total_ref):
    group = pl.program_id(0)
    docs, width = pick_ref.shape[1:]
    doc_rows = doc_ref.shape[0]
    strips = doc_rows // STRIP
    chunk = min(256, doc_rows)
    row = lax.broadcasted_iota(jnp.int32, (STRIP, width), 0)
    sum_ref[...] = jnp.zeros(sum_ref.shape, F32)

    def add_strip(sim, first, doc, pick):
        kept = jnp.where(row == pick - first, sim, 0.0)
        sum_ref[pl.ds(doc, 1)] += jnp.sum(kept.reshape(1, STRIP // 8, 8, width), axis=1)

    for start in range(0, doc_rows, chunk):
        sims = mm(doc_ref[start : start + chunk, :], query_ref[...], NT)
        for first in range(0, chunk, STRIP):
            place = group * strips + (start + first) // STRIP
            low, high = low_ref[place], high_ref[place]
            sim = sims[first : first + STRIP]
            add_strip(sim, start + first, low, pick_ref[0, pl.ds(low, 1), :])
            pick = jnp.where(high > low, pick_ref[0, pl.ds(high, 1), :], -1)
            add_strip(sim, start + first, high, pick)

    @pl.loop(0, strips)
    def _(strip):
        low, high = low_ref[group * strips + strip], high_ref[group * strips + strip]

        @pl.when(high > low + 1)
        def _():
            first = pl.multiple_of(strip * STRIP, STRIP)
            sim = mm(doc_ref[pl.ds(first, STRIP), :], query_ref[...], NT)

            @pl.loop(low + 1, high)
            def _(doc):
                add_strip(sim, first, doc, pick_ref[0, pl.ds(doc, 1), :])

    total_ref[group] = jnp.sum(sum_ref[...], axis=1)

    @pl.when(group == pl.num_programs(0) - 1)
    def _():
        spread = token_sums(width, out_ref.shape[1]).astype(F32).astype(BF16)
        total = jnp.concatenate([total_ref[g] for g in range(total_ref.shape[0])], axis=0)
        out_ref[...] = sum(mm(term.astype(BF16), spread) for term in three_terms(total))


def score_grad_kernel(
    low_ref, high_ref, doc_ref, query_ref, pick_ref, weight_ref, doc_out, query_out,
    sparse_ref, token_ref,
):
    group = pl.program_id(0)
    docs, width = pick_ref.shape[1:]
    doc_rows = doc_ref.shape[0]
    strips = doc_rows // STRIP
    chunk = min(256, doc_rows)
    row = lax.broadcasted_iota(jnp.int32, (STRIP, width), 0)

    def fill(held, first, doc, pick):
        return jnp.where(row == pick - first, token_ref[group, pl.ds(doc, 1), :], held)

    @pl.when(group == 0)
    def _():
        query_out[...] = jnp.zeros_like(query_out)
        spread = token_sums(width, weight_ref.shape[1]).astype(F32).astype(BF16)
        weights = mm(weight_ref[...].astype(BF16), spread, NT)
        for g in range(token_ref.shape[0]):
            token_ref[g] = weights[g * docs : (g + 1) * docs]

    total = None
    for start in range(0, doc_rows, chunk):
        for first in range(start, start + chunk, STRIP):
            place = group * strips + first // STRIP
            low, high = low_ref[place], high_ref[place]
            held = fill(jnp.zeros((STRIP, width), F32), first, low, pick_ref[0, pl.ds(low, 1), :])
            pick = jnp.where(high > low, pick_ref[0, pl.ds(high, 1), :], -1)
            sparse_ref[first : first + STRIP, :] = fill(held, first, high, pick).astype(BF16)
        sparse = sparse_ref[start : start + chunk, :]
        doc_out[start : start + chunk, :] = mm(sparse, query_ref[...])
        turned = doc_ref[start : start + chunk, :].astype(F32).T.astype(BF16)
        part = mm(turned, sparse)
        total = part if total is None else total + part
    query_out[...] += total

    @pl.loop(0, strips)
    def _(strip):
        low, high = low_ref[group * strips + strip], high_ref[group * strips + strip]

        @pl.when(high > low + 1)
        def _():
            first = pl.multiple_of(strip * STRIP, STRIP)
            held = lax.fori_loop(
                low + 1,
                high,
                lambda doc, held: fill(held, first, doc, pick_ref[0, pl.ds(doc, 1), :]),
                jnp.zeros((STRIP, width), F32),
            ).astype(BF16)
            doc_out[pl.ds(first, STRIP), :] += mm(held, query_ref[...])
            turned = doc_ref[pl.ds(first, STRIP), :].astype(F32).T.astype(BF16)
            query_out[...] += mm(turned, held)


def score_specs(doc_tile, query_tile, picks):
    groups, docs, width = picks.shape
    doc_rows = doc_tile.shape[0] // groups
    return (
        pl.BlockSpec((doc_rows, 128), lambda i, *_: (i, 0)),
        held(query_tile.shape),
        pl.BlockSpec((1, docs, width), lambda i, *_: (i, 0, 0)),
    )


def score_forward(lows, highs, doc_tile, query_tile, picks):
    groups, docs, width = picks.shape
    queries = width // QLEN
    doc_spec, query_spec, pick_spec = score_specs(doc_tile, query_tile, picks)
    return call(
        score_kernel, "score_forward", (groups,),
        [doc_spec, query_spec, pick_spec],
        [pl.BlockSpec((groups * docs, queries), lambda i, *_: (0, 0))],
        [shaped(F32, groups * docs, queries)],
        (lows, highs, doc_tile, query_tile, picks), 2 * doc_tile.shape[0] * width * 128,
        prefetch=2,
        scratch=[pltpu.VMEM((docs, 8, width), F32), pltpu.VMEM((groups, docs, width), F32)],
    )[0]


def score_backward(lows, highs, doc_tile, query_tile, picks, weights):
    groups, docs, width = picks.shape
    doc_spec, query_spec, pick_spec = score_specs(doc_tile, query_tile, picks)
    return call(
        score_grad_kernel, "score_backward", (groups,),
        [doc_spec, query_spec, pick_spec, held(weights.shape)],
        [doc_spec, pl.BlockSpec((128, width), lambda i, *_: (0, 0))],
        [shaped(F32, *doc_tile.shape), shaped(F32, 128, width)],
        (lows, highs, doc_tile, query_tile, picks, weights), 4 * doc_tile.shape[0] * width * 128,
        prefetch=2,
        scratch=[
            pltpu.VMEM((doc_tile.shape[0] // groups, width), BF16),
            pltpu.VMEM((groups, docs, width), F32),
        ],
    )


def on_device(
    tokens,
    doc_lengths,
    match_picks,
    labels,
    w_qkv,
    b_qkv,
    w_out,
    b_out,
    ln1_gain,
    ln1_bias,
    w_up,
    b_up,
    w_down,
    b_down,
    ln2_gain,
    ln2_bias,
    w_proj,
    log_scale,
):
    Order.last = ()
    C = lax.axis_size("cols")
    R = lax.axis_size("rows")
    c = lax.axis_index("cols")
    r = lax.axis_index("rows")
    width = tokens.shape[1]
    D = width * C
    Q = ROW_LEN // C
    DS = (tokens.shape[0] - ROW_LEN) // C
    n = Q + DS
    tile = math.gcd(256, math.gcd(Q, DS))

    def shift_cols(value, k):
        return lax.ppermute(value, "cols", [(i, (i + k) % C) for i in range(C)])

    def swap_rows(value, bit):
        return lax.ppermute(value, "rows", [(i, i ^ bit) for i in range(R)])

    def in_order(slots):
        if len(slots) == 1:
            return slots
        if len(slots) == 2:
            return [lax.select(c == 0, slots[0], slots[1]), lax.select(c == 0, slots[1], slots[0])]
        stacked = jnp.stack(slots)
        return [
            lax.dynamic_index_in_dim(stacked, (c - j) % C, 0, keepdims=False) for j in range(C)
        ]

    pack = [b_qkv.reshape(-1), b_up, b_out, ln1_gain, ln1_bias, b_down, ln2_gain, ln2_bias]
    ends = [0]
    for vector in pack:
        ends.append(ends[-1] + vector.shape[0])
    packed = jnp.concatenate(pack)

    def gather_pieces(pieces):
        return [lax.all_gather(piece, "rows", axis=0, tiled=True) for piece in pieces]

    late_weights = (w_out, w_up, w_down)
    late_pieces = [
        lax.dynamic_index_in_dim(w.reshape(R, -1, w.shape[1]), r, 0, keepdims=False)
        for w in late_weights
    ]
    parts = jnp.concatenate(
        [tokens[:ROW_LEN].reshape(C, Q, width), tokens[ROW_LEN:].reshape(C, DS, width)], axis=1
    )

    def part(k):
        return lax.dynamic_index_in_dim(parts, (c + k) % C, 0, keepdims=False)

    qkv_piece = lax.dynamic_index_in_dim(
        w_qkv.reshape(R, -1, w_qkv.shape[2]), r, 0, keepdims=False
    )
    qkv_pieces = [shift_cols(qkv_piece, k) for k in range(1, C)]
    token_slots = [part(0)] + [shift_cols(part(k), k) for k in range(1, C)]
    own_sizes = lax.dynamic_index_in_dim(
        lax.dynamic_index_in_dim(doc_lengths, r, 0, keepdims=False), c, 0, keepdims=False
    )
    sizes = lax.dynamic_index_in_dim(doc_lengths, c, 1, keepdims=False)
    doc_ends = jnp.cumsum(sizes, axis=1)
    begins = doc_ends - sizes
    cosine, sine, ext_k, ext_q, picks = prepare(n, Q, own_sizes, match_picks, begins, sizes)
    wqkv_slots = [w_qkv]
    for k in range(1, C):
        if C == 2:
            other = gather_rows(R, qkv_pieces[k - 1], 1)
        else:
            other = lax.all_gather(qkv_pieces[k - 1], "rows", axis=0, tiled=True)
        wqkv_slots.append(other.reshape(w_qkv.shape))
    x = join(c, token_slots)
    behind, _ = lax.optimization_barrier(((w_proj, packed), x))
    wproj = jnp.concatenate(
        in_order([w_proj] + [shift_cols(behind[0], k) for k in range(1, C)]), axis=0
    )
    packs = [packed] + [shift_cols(behind[1], k) for k in range(1, C)]

    ordered_packs = in_order(packs)

    def of_slot(which, k):
        return packs[k][ends[which] : ends[which + 1]]

    def whole(which):
        return jnp.concatenate([p[ends[which] : ends[which + 1]] for p in ordered_packs])

    bqkv_slots = [of_slot(0, k).reshape(b_qkv.shape) for k in range(C)]
    bup_slots = [of_slot(1, k)[None, :] for k in range(C)]
    bout, gain1, bias1, bdown, gain2, bias2 = [whole(which) for which in range(2, 8)]
    zero_row = jnp.zeros_like(bout)
    vectors = jnp.stack([bout, gain1, bias1, bdown, gain2, bias2, zero_row, zero_row])

    own_ends = jnp.cumsum(own_sizes)
    share = D // R
    q_tiles, d_tiles = Q // tile, DS // tile
    steps = jnp.arange(q_tiles, dtype=jnp.int32)
    first_rows = jnp.arange(d_tiles, dtype=jnp.int32) * tile
    is_passed = first_rows[:, None] >= own_ends[None, :]
    low_rows = jnp.sum(jnp.where(is_passed, own_sizes[None, :], 0), axis=1)
    last_passed = (first_rows + tile - 1)[:, None] >= own_ends[None, :]
    high_rows = jnp.min(jnp.where(last_passed, DS, own_ends[None, :]), axis=1)
    spans = jnp.concatenate(
        [steps, q_tiles + low_rows // tile, steps + 1, q_tiles + (high_rows + tile - 1) // tile]
    ).astype(jnp.int32)

    queries_here, tile_docs, _ = match_picks.shape
    strip_rows = (jnp.arange(DS // STRIP, dtype=jnp.int32) * STRIP)[None, :, None]
    lows = jnp.sum(doc_ends[:, None, :] <= strip_rows, axis=2).astype(jnp.int32).reshape(-1)
    highs = jnp.sum(begins[:, None, :] < strip_rows + STRIP, axis=2).astype(jnp.int32) - 1
    highs = highs.reshape(-1)

    qkv, attended, rests, exts = [], [], [], []
    for k in range(C):
        first = (lows, highs) if k == 0 else ()
        qkv.append(project_qkv(x, wqkv_slots[k], bqkv_slots[k], cosine, sine, first))
        if k == 0:
            flat = jnp.concatenate([piece.reshape(-1, D) for piece in late_pieces])
            flat, _ = lax.optimization_barrier((flat, x))
            arrived = [shift_cols(flat, j) for j in range(1, C)]
            arrived = [pass_on(a) for a in arrived]
            ends_of = [0]
            for piece in late_pieces:
                ends_of.append(ends_of[-1] + piece.size // D)
            wout_slots, wup_slots, wdown_slots = (
                [own] + gather_pieces([
                    a[ends_of[j] : ends_of[j + 1]].reshape(late_pieces[j].shape) for a in arrived
                ])
                for j, own in enumerate(late_weights)
            )
            wout_slots, wup_slots, wdown_slots = (
                [slot.reshape(own.shape) for slot in slots_of]
                for slots_of, own in zip((wout_slots, wup_slots, wdown_slots), late_weights)
            )
        out, rest, ext = attention_forward(spans, qkv[k], ext_k, ext_q, tile)
        attended.append(out)
        rests.append(rest)
        exts.append(ext)
    normed_one, inverse_one, hidden_low, hidden_t = out_and_norm(x, vectors, attended, wout_slots)
    active, slopes = zip(*[up_and_gelu(hidden_low, wup_slots[k], bup_slots[k]) for k in range(C)])
    normed_two, inverse_two, output_low, unit, unit_low, unit_inverse = down_and_norm(
        normed_one, vectors, wproj, active, wdown_slots
    )

    doc_tile = gather_rows(R, unit_low[Q:], 2).reshape(R * DS, 128)
    query_tile = jnp.concatenate(
        in_order([unit_low[:Q]] + [shift_cols(unit_low[:Q], k) for k in range(1, C)]), axis=0
    )
    sims = score_forward(lows, highs, doc_tile, query_tile, picks)
    scores = sims.T

    scale = jnp.exp(log_scale[0])
    z = scale * scores
    row_top = jnp.max(z, axis=1)
    row_mass = jnp.sum(jnp.exp(z - row_top[:, None]), axis=1)
    is_label = (
        jnp.arange(tile_docs, dtype=jnp.int32)[None, :] == (labels - c * tile_docs)[:, None]
    )
    chosen = jnp.sum(jnp.where(is_label, z, 0.0), axis=1)
    own_stats = jnp.stack([row_top, row_mass, chosen])
    stats = jnp.stack([own_stats] + [shift_cols(own_stats, k) for k in range(1, C)])
    top_all = jnp.max(stats[:, 0], axis=0)
    mass_all = jnp.sum(stats[:, 1] * jnp.exp(stats[:, 0] - top_all), axis=0)
    log_total = top_all + jnp.log(mass_all)
    loss = log_total - jnp.sum(stats[:, 2], axis=0)
    dz = (jnp.exp(z - log_total[:, None]) - is_label.astype(F32)) / (queries_here * R)
    scale_part = jnp.sum(dz * z)
    dscores = (scale * dz).T
    doc_grad, query_grad_t = score_backward(lows, highs, doc_tile, query_tile, picks, dscores)
    query_parts = query_grad_t.T.reshape(C, Q, 128)

    def query_part(k):
        return lax.dynamic_index_in_dim(query_parts, (c + k) % C, 0, keepdims=False)

    query_grad = query_part(0)
    for k in range(1, C):
        query_grad = query_grad + shift_cols(query_part(k), k)

    doc_sum = scatter_rows(doc_grad.reshape(R, DS, 128))
    unit_grad = jnp.concatenate([query_grad, doc_sum], axis=0)

    core = r % 2
    slots_back = range(C - 1, -1, -1)
    share = D // R
    x_bit, *z_bits = [1 << b for b in range(1, R.bit_length() - 1)]

    def side_of(bit):
        return ((r // bit) % 2).astype(jnp.int32)

    def halves_of(left_t):
        return left_t.reshape(R // 2, 2, share, n)

    def rows_of(left, side):
        return lax.dynamic_index_in_dim(left, side, 1, keepdims=False).reshape(-1, n)

    def send_plain(left, right):
        part = mm(rows_of(left, 1 - core), right).astype(BF16)
        Order.last += (part,)
        return swap_rows(part, 1)

    def keep_plain(left, right, arrived, k):
        kept = mm(rows_of(left, core), right) + arrived.astype(F32)
        if k > 0:
            kept = kept.astype(BF16)
        Order.last += (kept,)
        return kept[None] if k == 0 else shift_cols(kept, C - k)[None]

    def next_fold(states, bit, inner):
        send, keep = fold(side_of(bit), [s[0] for s in states], [s[1] for s in states], inner)
        return keep, swap_rows(send, bit)

    def cols_state(kept):
        rest = kept[1]
        for other in kept[2:]:
            rest = rest.astype(F32) + other.astype(F32)
        return kept[0], rest

    embed_grad, resid_two_grad, branch, branch_t, head_sums = head_pull(
        unit_grad, unit, unit_inverse, wproj, normed_two, inverse_two, vectors
    )
    down_left, down_right = halves_of(branch_t), active
    pre_grads, up_sums, down_kept = [None] * C, [None] * C, [None] * C
    down_arrived = [None] * C
    for k in slots_back:
        down_arrived[k] = send_plain(down_left, down_right[k])
    for k in slots_back:
        pre_grads[k], up_sums[k] = up_pull(branch, wdown_slots[k], slopes[k])
        if k > 0:
            down_kept[k] = keep_plain(down_left, down_right[k], down_arrived[k], k)
    up_left, up_right = halves_of(hidden_t), pre_grads
    up_arrived, up_kept = [None] * C, [None] * C
    for k in slots_back:
        up_arrived[k] = send_plain(up_left, up_right[k])
    down_kept[0] = keep_plain(down_left, down_right[0], down_arrived[0], 0)
    for k in slots_back[:-1]:
        up_kept[k] = keep_plain(up_left, up_right[k], up_arrived[k], k)
    resid_one_grad, branch_one_t, hidden_sums, *attended_grads = hidden_pull(
        resid_two_grad, normed_one, inverse_one, vectors, pre_grads, wup_slots, wout_slots
    )
    up_kept[0] = keep_plain(up_left, up_right[0], up_arrived[0], 0)
    mixed_grads, mixed_sums = [None] * C, [None] * C
    def gather_small():
        proj_grad = mm(embed_grad, output_low, TN).reshape(R, -1, C, width)
        def cut(values, slot_rows):
            return values.reshape(slot_rows, R, -1)

        own_order = [(c - k) % C for k in range(C)]
        canonical = jnp.stack(
            [hidden_sums[0], hidden_sums[1], hidden_sums[2], head_sums[0], head_sums[1], head_sums[2]]
        ).reshape(6, C, R, -1)
        slots_small = []
        for k in range(C):
            rows = [mixed_sums[k][j].reshape(R, -1) for j in range(3)]
            rows.append(up_sums[k][0].reshape(R, -1))
            rows += [
                lax.dynamic_index_in_dim(canonical[j], own_order[k], 0, keepdims=False)
                for j in range(6)
            ]
            own_proj_grad = lax.dynamic_index_in_dim(proj_grad, own_order[k], 2, keepdims=False)
            rows.append(own_proj_grad.reshape(R, -1))
            rows.append(jnp.broadcast_to(scale_part, (R, 1)))
            slots_small.append(jnp.concatenate(rows, axis=1))
        return jnp.stack(slots_small, axis=1)

    def pull_attention(k):
        mixed_grads[k], mixed_sums[k] = attention_backward(
            spans, qkv[k], exts[k], attended[k], rests[k], attended_grads[k], ext_k, cosine, sine,
            tile,
        )

    for k in slots_back[:-1]:
        pull_attention(k)
    wide_state = next_fold([cols_state(down_kept), cols_state(up_kept)], x_bit, share)
    pull_attention(0)
    sent = [
        shift_cols(token_pull((c + k) % C, resid_one_grad, mixed_grads, wqkv_slots, BF16), k)
        for k in range(1, C)
    ]
    own_tokens = token_pull(c, resid_one_grad, mixed_grads, wqkv_slots, F32)
    late_grad, wide_grad, small = late_sums(
        R, C, halves_of(x.T), halves_of(branch_one_t), mixed_grads, attended, *wide_state,
        gather_small(),
    )
    tokens_grad = assemble(c, Q, [own_tokens] + sent)
    qkv_grad, out_grad = late_grad[:3], late_grad[3]
    down_grad, up_grad = wide_grad
    one = D // (C * R)
    up_part = bup_slots[0].shape[1] // R
    bounds = [3 * one, 3 * one + up_part]
    for _ in range(6):
        bounds.append(bounds[-1] + one)
    pieces = [small[a:b] for a, b in zip(bounds[:-1], bounds[1:])]
    bup_out, bout_out, gain1_out, bias1_out, bdown_out, gain2_out, bias2_out = pieces
    return (
        scores,
        loss,
        tokens_grad,
        qkv_grad,
        small[: bounds[0]].reshape(3, one),
        out_grad.T,
        bout_out,
        gain1_out,
        bias1_out,
        up_grad,
        bup_out,
        down_grad.T,
        bdown_out,
        gain2_out,
        bias2_out,
        small[bounds[-1] : -1].reshape(-1, width).T,
        small[-1:],
    )


def solution(mesh):
    in_specs = (
        P("rows", "cols"),
        P(),
        P("rows", "cols", None),
        P("rows"),
        P(None, None, "cols"),
        P(None, "cols"),
        P("cols", None),
        P("cols"),
        P("cols"),
        P("cols"),
        P(None, "cols"),
        P("cols"),
        P("cols", None),
        P("cols"),
        P("cols"),
        P("cols"),
        P("cols", None),
        P(),
    )
    out_specs = (
        P("rows", "cols"),
        P("rows"),
        P("rows", "cols"),
        P(None, "rows", "cols"),
        P(None, ("cols", "rows")),
        P("cols", "rows"),
        P(("cols", "rows")),
        P(("cols", "rows")),
        P(("cols", "rows")),
        P("rows", "cols"),
        P(("cols", "rows")),
        P("cols", "rows"),
        P(("cols", "rows")),
        P(("cols", "rows")),
        P(("cols", "rows")),
        P("cols", "rows"),
        P(),
    )
    return jax.shard_map(
        on_device, mesh=mesh, in_specs=in_specs, out_specs=out_specs, check_vma=False
    )
```

```python
import functools
import math

import jax
import jax.numpy as jnp
from jax import lax
from jax.experimental import pallas as pl
from jax.experimental.pallas import tpu as pltpu
from jax.sharding import PartitionSpec as P

DH = 64
QLEN = 32
ROW_LEN = 1024
F32 = jnp.float32
BF16 = jnp.bfloat16
VMEM_LIMIT = 56 * 1024 * 1024
NT = (((1,), (1,)), ((), ()))
NN = (((1,), (0,)), ((), ()))
TN = (((0,), (0,)), ((), ()))


def mm(left, right, dims=NN):
    return lax.dot_general(left, right, dims, preferred_element_type=F32)


def row_step(rows):
    return 512 if rows % 512 == 0 else 128


def parts_of(step):
    size = 256 if step % 256 == 0 else 128
    return [slice(first, first + size) for first in range(0, step, size)]


def held(shape):
    return pl.BlockSpec(shape, lambda *_: (0,) * len(shape), pipeline_mode=pl.Buffered(1))


def shaped(dtype, *shape):
    return jax.ShapeDtypeStruct(shape, dtype)


class Order:
    last = ()


def call(
    body, name, grid, in_specs, out_specs, out_shape, operands, flops, scratch=(), prefetch=0, after=(),
    remote=None,
):
    count = len(operands)
    after = tuple(after) + Order.last

    def wrapped(*refs):
        body(*refs[:count], *refs[count + len(after) :])

    size = sum(math.prod(o.shape) * o.dtype.itemsize for o in list(operands) + list(out_shape))
    if flops == 0:
        size = 1024
    outs = pl.pallas_call(
        wrapped,
        grid_spec=pltpu.PrefetchScalarGridSpec(
            num_scalar_prefetch=prefetch,
            grid=grid,
            in_specs=list(in_specs) + [pl.BlockSpec(memory_space=pl.ANY)] * len(after),
            out_specs=out_specs,
            scratch_shapes=list(scratch),
        ),
        out_shape=out_shape,
        compiler_params=pltpu.CompilerParams(
            vmem_limit_bytes=VMEM_LIMIT, collective_id=remote, has_side_effects=remote is not None
        ),
        cost_estimate=pl.CostEstimate(flops=flops, bytes_accessed=size, transcendentals=0),
        name=name,
    )(*operands, *after)
    Order.last = (min(outs, key=lambda out: out.size * out.dtype.itemsize),)
    return outs


def row_spec(step, width):
    return pl.BlockSpec((step, width), lambda i, *_: (i, 0))


def column_spec(width, step):
    return pl.BlockSpec((width, step), lambda i, *_: (0, i))


MESH = pl.DeviceIdType.MESH
ANYWHERE = pl.BlockSpec(memory_space=pl.ANY)


def side_at(row, bit):
    return (row // bit) % 2


def across(row, bit):
    return row + bit * (1 - 2 * side_at(row, bit))


def flipped(row, bits):
    bit = 1
    while bit <= bits:
        if bits & bit:
            row = across(row, bit)
        bit *= 2
    return row


def greet(devices):
    barrier = pltpu.get_barrier_semaphore()
    for device in devices:
        pl.semaphore_signal(barrier, inc=1, device_id=device, device_id_type=MESH)
    pl.semaphore_wait(barrier, len(devices))


def send(source, target, sent, arrived, device):
    copy = pltpu.make_async_remote_copy(
        src_ref=source,
        dst_ref=target,
        send_sem=sent,
        recv_sem=arrived,
        device_id=device,
        device_id_type=MESH,
    )
    copy.start()
    return copy


def spread_order(count):
    pieces = sorted(range(count), key=lambda piece: (piece.bit_count(), -piece))
    order = []
    for piece in pieces:
        lowest = piece & -piece if piece else count
        bit = lowest // 2
        bits = []
        while bit:
            bits.append(bit)
            bit //= 2
        order.append((piece, bits))
    return order


def gather_kernel(rows, own, out, own_sem, sent, arrived):
    r = lax.axis_index("rows")
    bits = [1 << b for b in range(rows.bit_length() - 1)]
    greet([{"rows": across(r, bit)} for bit in bits])
    local = pltpu.make_async_copy(own, out.at[r], own_sem)
    local.start()
    copies = {}
    size = own.shape[0] // PARTS
    for piece, over in spread_order(rows):
        row = flipped(r, piece)
        for part in range(PARTS):
            at = pl.ds(part * size, size)
            if piece:
                copies[piece, part].wait_recv()
            for bit in over:
                copies[piece | bit, part] = send(
                    out.at[row, at] if piece else own.at[at], out.at[row, at],
                    sent.at[piece | bit, part], arrived.at[piece | bit, part],
                    {"rows": across(r, bit)},
                )
    for copy in copies.values():
        copy.wait_send()
    local.wait()


PARTS = 2


def gather_rows(rows, own, remote):
    return call(
        functools.partial(gather_kernel, rows), "gather_rows", (1,), [ANYWHERE], [ANYWHERE],
        [shaped(own.dtype, rows, *own.shape)], (own,), 0, remote=remote,
        scratch=[
            pltpu.SemaphoreType.DMA, pltpu.SemaphoreType.DMA((rows, PARTS)),
            pltpu.SemaphoreType.DMA((rows, PARTS)),
        ],
    )[0]


def scatter_kernel(rows, parts, out, sent, arrived, *buffers):
    r = lax.axis_index("rows")
    bits = [1 << b for b in range(rows.bit_length() - 1)]
    greet([{"rows": across(r, bit)} for bit in bits])
    outgoing, incoming = buffers[: len(bits)], buffers[len(bits) :]
    size = parts.shape[1] // PARTS
    copies = {}

    def total(flips, levels, part):
        row, at = flipped(r, flips), pl.ds(part * size, size)
        value = parts[row, at]
        for level in range(levels):
            copies[level, flips >> (level + 1), part].wait_recv()
            value = value + incoming[level][row // (2 << level), at].astype(F32)
        return value

    for level, bit in enumerate(bits):
        count = rows // (2 << level)
        for turn in sorted(range(count), key=lambda f: tuple(-((f >> b) & 1) for b in range(8))):
            flips = (turn << (level + 1)) | bit
            place = flipped(r, flips) // (2 << level)
            for part in range(PARTS):
                at = pl.ds(part * size, size)
                outgoing[level][place, at] = total(flips, level, part).astype(BF16)
                name = rows - 2 * count + turn
                copies[level, turn, part] = send(
                    outgoing[level].at[place, at], incoming[level].at[place, at],
                    sent.at[name, part], arrived.at[name, part], {"rows": across(r, bit)},
                )
    for part in range(PARTS):
        out[part * size : (part + 1) * size, :] = total(0, len(bits), part)
    for copy in copies.values():
        copy.wait_send()


def scatter_rows(parts):
    rows, height, width = parts.shape
    levels = rows.bit_length() - 1
    buffers = [
        pltpu.VMEM((rows // (2 << level), height, width), BF16) for level in range(levels)
    ]
    return call(
        functools.partial(scatter_kernel, rows), "scatter_rows", (1,), [held(parts.shape)],
        [pl.BlockSpec((height, width), lambda *_: (0, 0))], [shaped(F32, height, width)],
        (parts,), 0, remote=3,
        scratch=[
            pltpu.SemaphoreType.DMA((rows, PARTS)), pltpu.SemaphoreType.DMA((rows, PARTS)),
        ] + buffers + buffers,
    )[0]


def small_sums(rows, cols, parts, out, *refs):
    bits = [1 << b for b in range(rows.bit_length() - 1)]
    sent, arrived = refs[:2]
    core_in, cols_in, totals = refs[2], refs[3], refs[4 : 4 + len(bits)]
    row_ins = refs[4 + len(bits) :]
    r, c = lax.axis_index("rows"), lax.axis_index("cols")
    others = [{"cols": (c + cols - k) % cols} for k in range(1, cols)]
    core = side_at(r, 1)
    copies = {}

    def first():
        copies["core"] = send(
            parts.at[:, 1 - core], core_in, sent.at[0], arrived.at[0], {"rows": across(r, 1)}
        )

    def second():
        copies["core"].wait()
        totals[0][...] = parts[:, core] + core_in[...]
        for k in range(1, cols):
            copies["cols", k] = send(
                totals[0].at[:, k], cols_in.at[k - 1], sent.at[k], arrived.at[k], others[k - 1]
            )

    def third():
        total = totals[0][:, 0]
        for k in range(1, cols):
            copies["cols", k].wait()
            total = total + cols_in[k - 1]
        pass_on(0, total)

    def pass_on(level, total):
        if level == len(bits) - 1:
            out[...] = total[0]
            return
        whole = totals[1 + level]
        whole[...] = total.reshape(whole.shape)
        copies["row", level] = send(
            whole.at[:, 1 - side_at(r, bits[1 + level])], row_ins[level],
            sent.at[cols + level], arrived.at[cols + level],
            {"rows": across(r, bits[1 + level])},
        )

    def later(level):
        copies["row", level].wait()
        pass_on(level + 1, totals[1 + level][:, side_at(r, bits[1 + level])] + row_ins[level][...])

    return [first, second, third] + [
        functools.partial(later, level) for level in range(len(bits) - 1)
    ]


def small_blocks(rows, cols, parts):
    length = parts.shape[2]
    width = -(-length // 1024) * 128
    parts = jnp.pad(parts, ((0, 0), (0, 0), (0, 8 * width - length)))
    parts = parts.reshape(rows // 2, 2, cols, 8, width)
    levels = rows.bit_length() - 1
    heights = [rows >> (level + 1) for level in range(1, levels)]
    scratch = [
        pltpu.SemaphoreType.DMA((cols + levels,)), pltpu.SemaphoreType.DMA((cols + levels,)),
        pltpu.VMEM((rows // 2, cols, 8, width), F32),
        pltpu.VMEM((cols - 1, rows // 2, 8, width), F32),
        pltpu.VMEM((rows // 2, cols, 8, width), F32),
    ]
    scratch += [pltpu.VMEM((height, 2, 8, width), F32) for height in heights]
    scratch += [pltpu.VMEM((height, 8, width), F32) for height in heights]
    return parts, scratch


def late_kernel(rows, cols, *refs):
    tokens_t, branch_t = refs[:2]
    far_rights, far_attended, refs = refs[2 : 2 + cols], refs[2 + cols : 2 + 2 * cols], refs[2 + 2 * cols :]
    (du_own, du_in, small, out, du_out, small_out), refs = refs[:6], refs[6:]
    (rights, right_sem), refs = refs[:2], refs[2:]
    (core_out, core_in, x_out, x_in, kept, cols_out, cols_in), refs = refs[:7], refs[7:]
    r, c = lax.axis_index("rows"), lax.axis_index("cols")
    x_bit, *z_bits = [1 << b for b in range(1, rows.bit_length() - 1)]
    levels = len(z_bits)
    z_out, z_in, z_kept = refs[:levels], refs[levels : 2 * levels], refs[2 * levels : 3 * levels]
    refs = refs[3 * levels :]
    du_z_out, du_z_in, du_kept = refs[:levels], refs[levels : 2 * levels], refs[2 * levels : 3 * levels]
    refs = refs[3 * levels :]
    (core_sem, x_sem, cols_sem, z_sem, du_sem), refs = refs[:5], refs[5:]
    small_steps = small_sums(rows, cols, small, small_out, *refs)
    share = out.shape[1]
    others = [{"cols": (c + cols - k) % cols} for k in range(1, cols)]
    core, x_side = side_at(r, 1), side_at(r, x_bit)
    greet([{"rows": across(r, bit)} for bit in [1, x_bit] + z_bits] + others)
    chunks = range(4)
    slots = range(cols - 1, -1, -1)
    copies = {}

    def halves(total, side, inner):
        pairs = total.reshape(-1, 2, inner, total.shape[1])
        near = jnp.where(side == 0, pairs[:, 0], pairs[:, 1]).reshape(-1, total.shape[1])
        far = jnp.where(side == 0, pairs[:, 1], pairs[:, 0]).reshape(-1, total.shape[1])
        return near, far

    def product(side, slot, chunk):
        left = (tokens_t if chunk < 3 else branch_t)[:, side]
        return mm(left.reshape(-1, left.shape[-1]), rights[slot, chunk])

    def load(slot, chunk):
        source = far_rights[slot].at[chunk] if chunk < 3 else far_attended[slot]
        return pltpu.make_async_copy(source, rights.at[slot, chunk], right_sem.at[slot, chunk])

    for chunk in chunks:
        for slot in slots:
            load(slot, chunk).start()

    def begin(chunk):
        for slot in slots:
            load(slot, chunk).wait()
            if chunk >= 2:
                copies["core", slot, chunk - 2].wait_send()
            core_out[slot, chunk % 2] = product(1 - core, slot, chunk).astype(BF16)
            copies["core", slot, chunk] = send(
                core_out.at[slot, chunk % 2], core_in.at[slot, chunk],
                core_sem.at[0, slot, chunk], core_sem.at[1, slot, chunk],
                {"rows": across(r, 1)},
            )

    def after_core(chunk):
        for slot in slots:
            total = product(core, slot, chunk)
            copies["core", slot, chunk].wait_recv()
            near, far = halves(total + core_in[slot, chunk].astype(F32), x_side, share)
            x_out[slot, chunk] = far.astype(BF16)
            kept[slot, chunk] = near
            copies["x", slot, chunk] = send(
                x_out.at[slot, chunk], x_in.at[slot, chunk], x_sem.at[0, slot, chunk],
                x_sem.at[1, slot, chunk], {"rows": across(r, x_bit)},
            )

    def after_x(chunk):
        for slot in slots:
            copies["x", slot, chunk].wait_recv()
            total = kept[slot, chunk] + x_in[slot, chunk].astype(F32)
            if slot == 0:
                kept[0, chunk] = total
            else:
                cols_out[slot - 1, chunk] = total.astype(BF16)
                copies["cols", slot, chunk] = send(
                    cols_out.at[slot - 1, chunk], cols_in.at[slot - 1, chunk],
                    cols_sem.at[0, slot - 1, chunk], cols_sem.at[1, slot - 1, chunk],
                    others[slot - 1],
                )

    def after_cols(chunk):
        total = kept[0, chunk]
        for slot in slots[:-1]:
            copies["cols", slot, chunk].wait_recv()
            total = total + cols_in[slot - 1, chunk].astype(F32)
        pass_z(chunk, 0, total)

    def pass_z(chunk, level, total):
        if level == levels:
            out[chunk] = total
            return
        bit = z_bits[level]
        near, far = halves(total, side_at(r, bit), share)
        z_out[level][chunk] = far.astype(BF16)
        z_kept[level][chunk] = near
        copies["z", level, chunk] = send(
            z_out[level].at[chunk], z_in[level].at[chunk], z_sem.at[0, level, chunk],
            z_sem.at[1, level, chunk], {"rows": across(r, bit)},
        )

    def after_z(chunk, level):
        copies["z", level, chunk].wait_recv()
        pass_z(chunk, level + 1, z_kept[level][chunk] + z_in[level][chunk].astype(F32))

    def pass_du(place, level, total):
        if level == levels:
            du_out[place] = total
            return
        bit = z_bits[level]
        near, far = halves(total, side_at(r, bit), share)
        du_z_out[level][place] = far.astype(BF16)
        du_kept[level][place] = near
        copies["du", level, place] = send(
            du_z_out[level].at[place], du_z_in[level].at[place], du_sem.at[0, level, place],
            du_sem.at[1, level, place], {"rows": across(r, bit)},
        )

    def after_du(place, level):
        copies["du", level, place].wait_recv()
        pass_du(place, level + 1, du_kept[level][place] + du_z_in[level][place].astype(F32))

    for place in range(2):
        pass_du(place, 0, du_own[place] + du_in[place].astype(F32))
    stages = [(0, begin), (1, after_core), (3, after_x), (4, after_cols)]
    stages += [(5 + level, functools.partial(after_z, level=level)) for level in range(levels)]
    for turn in range(len(chunks) + stages[-1][0]):
        for delay, stage in stages[::-1]:
            if 0 <= turn - delay < len(chunks):
                stage(turn - delay)
        if 3 <= turn < 3 + levels:
            for place in range(2):
                after_du(place, turn - 3)
        if turn >= 1 and small_steps:
            small_steps.pop(0)()
    for step in small_steps:
        step()
    for name, copy in copies.items():
        if name[0] != "core" or name[2] >= 2:
            copy.wait_send()


def late_sums(rows, cols, tokens_t, branch_t, rights, attended, du_own, du_in, small):
    share, n = tokens_t.shape[2:]
    width = attended[0].shape[1]
    wide = du_own.shape[2]
    half, quarter = rows // 2 * share, rows // 4 * share
    levels = rows.bit_length() - 3
    heights = [quarter >> (level + 1) for level in range(levels)]

    def vmem(dtype, *shape):
        return pltpu.VMEM(shape, dtype)

    def pair_of(*shape):
        return pltpu.SemaphoreType.DMA((2,) + shape)

    length = small.shape[2]
    small, small_scratch = small_blocks(rows, cols, small)
    operands = (tokens_t, branch_t, *rights, *attended, du_own, du_in, small)
    scratch = [
        vmem(BF16, cols, 4, n, width), pltpu.SemaphoreType.DMA((cols, 4)),
        vmem(BF16, cols, 2, half, width), vmem(BF16, cols, 4, half, width),
        vmem(BF16, cols, 4, quarter, width), vmem(BF16, cols, 4, quarter, width),
        vmem(F32, cols, 4, quarter, width),
        vmem(BF16, cols - 1, 4, quarter, width), vmem(BF16, cols - 1, 4, quarter, width),
    ]
    for count, size in ((4, width), (2, wide)):
        for dtype in (BF16, BF16, F32):
            scratch += [vmem(dtype, count, height, size) for height in heights]
    scratch += [
        pair_of(cols, 4), pair_of(cols, 4), pair_of(cols - 1, 4), pair_of(levels, 4),
        pair_of(levels, 2),
    ]
    def whole(*shape):
        return pl.BlockSpec(shape, lambda *_: (0,) * len(shape))

    late, wide_sum, small_sum = call(
        functools.partial(late_kernel, rows, cols), "late_sums", (1,),
        [held(tokens_t.shape), held(branch_t.shape)] + [ANYWHERE] * (2 * cols)
        + [held(du_own.shape), held(du_in.shape), held(small.shape)],
        [whole(4, share, width), whole(2, share, wide), whole(*small.shape[3:])],
        [
            shaped(F32, 4, share, width), shaped(F32, 2, share, wide), shaped(F32, *small.shape[3:])
        ],
        operands, 100_000_000_000, remote=5, scratch=scratch + small_scratch,
    )
    return late, wide_sum, small_sum.reshape(-1)[:length]


QKV_BIAS, UP_BIAS = 6, 9


def swap_halves(block):
    lane = lax.broadcasted_iota(jnp.int32, block.shape, 1)
    return jnp.where((lane & 32) == 0, pltpu.roll(block, 96, 1), pltpu.roll(block, 32, 1))


def qkv_kernel(x_ref, w_ref, b_ref, cos_ref, sin_ref, out_ref):
    which = pl.program_id(0)
    bias = b_ref[pl.ds(QKV_BIAS + which, 1), :]

    @pl.when(which < 2)
    def _():
        for at in parts_of(x_ref.shape[0]):
            mixed = mm(x_ref[at, :], w_ref[0]) + bias
            for first in range(0, mixed.shape[1], 128):
                block = mixed[:, first : first + 128]
                turned = block * cos_ref[at, :] + swap_halves(block) * sin_ref[at, :]
                out_ref[0, at, first : first + 128] = turned.astype(BF16)

    @pl.when(which == 2)
    def _():
        for at in parts_of(x_ref.shape[0]):
            out_ref[0, at, :] = (mm(x_ref[at, :], w_ref[0]) + bias).astype(BF16)


def project_qkv(x, weight, bias, cosine, sine, after=()):
    n, D = x.shape
    width = weight.shape[2]
    return call(
        qkv_kernel, "project_qkv", (3,),
        [
            held((n, D)), pl.BlockSpec((1, D, width), lambda j: (j, 0, 0)), held(bias.shape),
            held((n, 128)), held((n, 128)),
        ],
        [pl.BlockSpec((1, n, width), lambda j: (j, 0, 0))],
        [shaped(BF16, 3, n, width)],
        (x, weight, bias, cosine, sine), 6 * n * D * width, after=after,
    )[0]


def prepare_kernel(
    q_rows, sizes_ref, picks_ref, docs_ref, cos_ref, sin_ref, ext_k_ref, ext_q_ref, out_ref
):
    n = cos_ref.shape[0]
    size = math.gcd(256, math.gcd(q_rows, n))
    lane = lax.broadcasted_iota(jnp.int32, (size, 128), 1)
    frequency = jnp.exp((lane & (DH // 2 - 1)).astype(F32) * (-2.0 * math.log(10000.0) / DH))
    place_lane = lane & (DH - 1)
    for first in range(0, n, size):
        at = slice(first, first + size)
        row = lax.broadcasted_iota(jnp.int32, (size, 128), 0) + first
        if first < q_rows:
            position, segment = row & (QLEN - 1), (row // QLEN) & (SEGMENTS - 1)
        else:
            place = row - q_rows
            begin, segment, end = jnp.zeros_like(row), jnp.zeros_like(row), 0
            for doc in range(sizes_ref.shape[0]):
                end = end + sizes_ref[doc]
                passed = place >= end
                begin = jnp.where(passed, end, begin)
                segment = segment + passed.astype(jnp.int32)
            position = place - begin
        angles = position.astype(F32) * frequency
        sine = jnp.sin(angles)
        cos_ref[at, :] = jnp.cos(angles)
        sin_ref[at, :] = jnp.where((lane & (DH // 2)) == 0, -sine, sine)
        same = segment == place_lane
        ones = (place_lane >= SEGMENTS) & (place_lane < SEGMENTS + 3)
        ext_k_ref[at, :] = (same | ones).astype(F32).astype(BF16)
        apart = (place_lane < SEGMENTS) & jnp.logical_not(same)
        ext_q_ref[at, :] = jnp.where(apart, -1e30, 0.0).astype(BF16)
    queries = picks_ref.shape[0]
    begins, sizes = docs_ref[:, 0:1], docs_ref[:, 1:2]
    groups, docs = out_ref.shape[:2]
    for first in range(0, queries, 4):
        lanes = jnp.concatenate([picks_ref[first + j] for j in range(4)], axis=1)
        rows = begins + lax.rem(lanes, jnp.broadcast_to(sizes, lanes.shape))
        at = slice(first * QLEN, (first + 4) * QLEN)
        for group in range(groups):
            out_ref[group, :, at] = rows[group * docs : (group + 1) * docs]


def prepare(n, q_rows, own_sizes, match_picks, begins, sizes):
    groups, docs = sizes.shape
    width = match_picks.shape[0] * QLEN
    table = jnp.stack([begins.reshape(-1), sizes.reshape(-1)], axis=1)
    return call(
        functools.partial(prepare_kernel, q_rows), "prepare", (1,),
        [held(match_picks.shape), held(table.shape)],
        [pl.BlockSpec((n, 128), lambda *_: (0, 0))] * 4
        + [pl.BlockSpec((groups, docs, width), lambda *_: (0, 0, 0))],
        [
            shaped(F32, n, 128), shaped(F32, n, 128), shaped(BF16, n, 128), shaped(BF16, n, 128),
            shaped(jnp.int32, groups, docs, width),
        ],
        (own_sizes, match_picks, table), 0, prefetch=1,
    )


def normed_rows(residual):
    mean = jnp.mean(residual, axis=1, keepdims=True)
    centred = residual - mean
    inverse = lax.rsqrt(jnp.mean(centred * centred, axis=1, keepdims=True) + 1e-05)
    return centred * inverse, inverse


def norm_pull(grad_rows, normed, inverse, gain):
    spread = grad_rows * gain
    return inverse * (
        spread
        - jnp.mean(spread, axis=1, keepdims=True)
        - normed * jnp.mean(spread * normed, axis=1, keepdims=True)
    )


def column_sums(*arrays):
    rows = [jnp.sum(array, axis=0, keepdims=True) for array in arrays]
    rows.append(jnp.zeros((8 - len(rows), rows[0].shape[1]), F32))
    return jnp.concatenate(rows, axis=0)


def add_over_steps(ref, value):
    first = pl.program_id(0) == 0

    @pl.when(first)
    def _():
        ref[...] = value

    @pl.when(jnp.logical_not(first))
    def _():
        ref[...] += value


def out_norm_kernel(slots, *refs):
    x_ref, vec_ref = refs[:2]
    att_refs, w_refs = refs[2 : 2 + slots], refs[2 + slots : 2 + 2 * slots]
    normed_ref, inverse_ref, low_ref, turned_ref = refs[2 + 2 * slots :]
    for at in parts_of(x_ref.shape[0]):
        residual = x_ref[at, :].astype(F32) + vec_ref[0:1, :]
        for att_ref, w_ref in zip(att_refs, w_refs):
            residual = residual + mm(att_ref[at, :], w_ref[...])
        normed, inverse = normed_rows(residual)
        hidden = normed * vec_ref[1:2, :] + vec_ref[2:3, :]
        normed_ref[at, :] = normed
        inverse_ref[at, :] = inverse
        low_ref[at, :] = hidden.astype(BF16)
        turned_ref[:, at] = hidden.T.astype(BF16)


def out_and_norm(x, vectors, attended, weights):
    n, D = x.shape
    step = row_step(n)
    slots = len(attended)
    width = attended[0].shape[1]
    return call(
        functools.partial(out_norm_kernel, slots), "out_and_norm", (n // step,),
        [row_spec(step, D), held(vectors.shape)]
        + [row_spec(step, width)] * slots + [held((width, D))] * slots,
        [row_spec(step, D), row_spec(step, 1), row_spec(step, D), column_spec(D, step)],
        [shaped(F32, n, D), shaped(F32, n, 1), shaped(BF16, n, D), shaped(BF16, D, n)],
        (x, vectors, *attended, *weights), 2 * n * D * D,
    )


GELU_TERMS = (
    0.23532527933595032, 0.09138803439798156, 0.6495603483388861,
    -0.6354014529895687, 0.8866650885491606, -0.22753729931242958,
)


def gelu_parts(values):
    size = jnp.abs(values)
    part = pl.reciprocal(1.0 + (0.39 / math.sqrt(2.0)) * size)
    bell = jnp.exp(-0.5 * (values * values))
    series = 0.5 * GELU_TERMS[-1]
    for term in GELU_TERMS[-2::-1]:
        series = series * part + 0.5 * term
    tail = series * part * bell
    below = jnp.where(values >= 0.0, 1.0 - tail, tail)
    return values * below, below + values * bell * (1.0 / math.sqrt(2.0 * math.pi))


def up_kernel(x_ref, w_ref, b_ref, active_ref, slope_ref):
    width, part = w_ref.shape[1], b_ref.shape[1]
    chunk = min(256, part)
    for first in range(0, width, chunk):
        at = slice(first, first + chunk)
        row, lane = UP_BIAS + first // part, first % part
        bias = b_ref[row : row + 1, lane : lane + chunk]
        active, slope = gelu_parts(mm(x_ref[...], w_ref[:, at]) + bias)
        active_ref[:, at] = active.astype(BF16)
        slope_ref[:, at] = slope


def up_and_gelu(x, weight, bias):
    n, D = x.shape
    width = weight.shape[1]
    step = row_step(n)
    return call(
        up_kernel, "up_and_gelu", (n // step,),
        [row_spec(step, D), held(weight.shape), held(bias.shape)],
        [row_spec(step, width)] * 2,
        [shaped(BF16, n, width), shaped(F32, n, width)],
        (x, weight, bias), 5 * n * D * width,
    )


def down_norm_kernel(slots, *refs):
    normed_ref, vec_ref, proj_ref = refs[:3]
    act_refs, w_refs = refs[3 : 3 + slots], refs[3 + slots : 3 + 2 * slots]
    normed_out, inverse_ref, low_ref, unit_ref, unit_low_ref, unit_inverse_ref = refs[3 + 2 * slots :]
    for at in parts_of(normed_ref.shape[0]):
        residual = normed_ref[at, :] * vec_ref[1:2, :] + vec_ref[2:3, :] + vec_ref[3:4, :]
        for act_ref, w_ref in zip(act_refs, w_refs):
            residual = residual + mm(act_ref[at, :], w_ref[...])
        normed, inverse = normed_rows(residual)
        normed_out[at, :] = normed
        inverse_ref[at, :] = inverse
        low = (normed * vec_ref[4:5, :] + vec_ref[5:6, :]).astype(BF16)
        low_ref[at, :] = low
        embedding = mm(low, proj_ref[...])
        unit_inverse = lax.rsqrt(jnp.sum(embedding * embedding, axis=1, keepdims=True) + 1e-06)
        unit = embedding * unit_inverse
        unit_ref[at, :] = unit
        unit_low_ref[at, :] = unit.astype(BF16)
        unit_inverse_ref[at, :] = unit_inverse


def down_and_norm(normed, vectors, proj, active, weights):
    n, D = normed.shape
    step = row_step(n)
    slots = len(active)
    width = active[0].shape[1]
    return call(
        functools.partial(down_norm_kernel, slots), "down_and_norm", (n // step,),
        [row_spec(step, D), held(vectors.shape), held(proj.shape)]
        + [row_spec(step, width)] * slots + [held((width, D))] * slots,
        [
            row_spec(step, D), row_spec(step, 1), row_spec(step, D),
            row_spec(step, 128), row_spec(step, 128), row_spec(step, 1),
        ],
        [
            shaped(F32, n, D), shaped(F32, n, 1), shaped(BF16, n, D),
            shaped(F32, n, 128), shaped(BF16, n, 128), shaped(F32, n, 1),
        ],
        (normed, vectors, proj, *active, *weights), 2 * n * D * width * slots,
    )


def head_pull_kernel(
    grad_ref, unit_ref, unit_inverse_ref, proj_ref, normed_ref, inverse_ref, vec_ref,
    embed_ref, residual_ref, low_ref, turned_ref, sum_ref,
):
    sums = []
    for at in parts_of(grad_ref.shape[0]):
        grad, unit = grad_ref[at, :], unit_ref[at, :]
        embed = grad - unit * jnp.sum(grad * unit, axis=1, keepdims=True)
        embed = (unit_inverse_ref[at, :] * embed).astype(BF16)
        embed_ref[at, :] = embed
        output_grad = mm(embed, proj_ref[...], NT)
        normed = normed_ref[at, :]
        residual = norm_pull(output_grad, normed, inverse_ref[at, :], vec_ref[4:5, :])
        residual_ref[at, :] = residual
        low_ref[at, :] = residual.astype(BF16)
        turned_ref[:, at] = residual.T.astype(BF16)
        sums.append(column_sums(residual, output_grad * normed, output_grad))
    add_over_steps(sum_ref, sum(sums))


def head_pull(unit_grad, unit, unit_inverse, proj, normed, inverse, vectors):
    n, D = normed.shape
    step = row_step(n)
    return call(
        head_pull_kernel, "head_pull", (n // step,),
        [
            row_spec(step, 128), row_spec(step, 128), row_spec(step, 1), held(proj.shape),
            row_spec(step, D), row_spec(step, 1), held(vectors.shape),
        ],
        [
            row_spec(step, 128), row_spec(step, D), row_spec(step, D),
            column_spec(D, step), pl.BlockSpec((8, D), lambda i: (0, 0)),
        ],
        [
            shaped(BF16, n, 128), shaped(F32, n, D), shaped(BF16, n, D),
            shaped(BF16, D, n), shaped(F32, 8, D),
        ],
        (unit_grad, unit, unit_inverse, proj, normed, inverse, vectors), 4 * n * D * 128,
    )


def up_pull_kernel(branch_ref, w_ref, slope_ref, out_ref, sum_ref):
    width = w_ref.shape[0]
    chunk = min(512, width)
    sums = []
    for first in range(0, width, chunk):
        at = slice(first, first + chunk)
        low = (mm(branch_ref[...], w_ref[at, :], NT) * slope_ref[:, at]).astype(BF16)
        out_ref[:, at] = low
        sums.append(column_sums(low.astype(F32)))
    add_over_steps(sum_ref, jnp.concatenate(sums, axis=1))


def up_pull(branch, weight, slope):
    n, D = branch.shape
    width = weight.shape[0]
    step = row_step(n)
    return call(
        up_pull_kernel, "up_pull", (n // step,),
        [row_spec(step, D), held(weight.shape), row_spec(step, width)],
        [row_spec(step, width), pl.BlockSpec((8, width), lambda i: (0, 0))],
        [shaped(BF16, n, width), shaped(F32, 8, width)],
        (branch, weight, slope), 2 * n * D * width,
    )


def hidden_pull_kernel(slots, *refs):
    residual_ref, normed_ref, inverse_ref, vec_ref = refs[:4]
    pre_refs, up_refs, out_refs = (refs[4 + j * slots : 4 + (j + 1) * slots] for j in range(3))
    rest = refs[4 + 3 * slots :]
    grad_ref, turned_ref, sum_ref = rest[:3]
    att_refs = rest[3:]
    sums = []
    for at in parts_of(residual_ref.shape[0]):
        hidden_grad = residual_ref[at, :]
        for pre_ref, up_ref in zip(pre_refs, up_refs):
            hidden_grad = hidden_grad + mm(pre_ref[at, :], up_ref[...], NT)
        normed = normed_ref[at, :]
        residual = norm_pull(hidden_grad, normed, inverse_ref[at, :], vec_ref[1:2, :])
        grad_ref[at, :] = residual
        low = residual.astype(BF16)
        turned_ref[:, at] = residual.T.astype(BF16)
        sums.append(column_sums(residual, hidden_grad * normed, hidden_grad))
        for att_ref, out_ref in zip(att_refs, out_refs):
            att_ref[at, :] = mm(low, out_ref[...], NT).astype(BF16)
    add_over_steps(sum_ref, sum(sums))


def hidden_pull(residual, normed, inverse, vectors, pre_grads, ups, outs):
    n, D = residual.shape
    step = row_step(n)
    slots = len(ups)
    wide, width = ups[0].shape[1], outs[0].shape[0]
    return call(
        functools.partial(hidden_pull_kernel, slots), "hidden_pull", (n // step,),
        [row_spec(step, D), row_spec(step, D), row_spec(step, 1), held(vectors.shape)]
        + [row_spec(step, wide)] * slots + [held((D, wide))] * slots
        + [held((width, D))] * slots,
        [row_spec(step, D), column_spec(D, step), pl.BlockSpec((8, D), lambda i: (0, 0))]
        + [row_spec(step, width)] * slots,
        [shaped(F32, n, D), shaped(BF16, D, n), shaped(F32, 8, D)]
        + [shaped(BF16, n, width)] * slots,
        (residual, normed, inverse, vectors, *pre_grads, *ups, *outs),
        0,
    )


def token_pull_kernel(slots, place_ref, *refs):
    residual_ref = refs[0]
    mixed_refs, w_refs = refs[1 : 1 + slots], refs[1 + slots : 1 + 2 * slots]
    out_ref = refs[-1]
    width = out_ref.shape[1]
    at = pl.ds(pl.multiple_of(place_ref[0] * width, width), width)
    total = residual_ref[...]
    for mixed_ref, w_ref in zip(mixed_refs, w_refs):
        for which in range(3):
            total = total + mm(mixed_ref[which], w_ref[which, at, :], NT)
    out_ref[...] = total.astype(out_ref.dtype)


def token_pull(place, residual, mixed_grads, weights, dtype):
    n, D = residual.shape
    step = row_step(n)
    slots = len(weights)
    width = weights[0].shape[2]
    return call(
        functools.partial(token_pull_kernel, slots), "token_pull", (n // step,),
        [pl.BlockSpec((step, width), lambda i, p: (i, p[0]))]
        + [pl.BlockSpec((3, step, width), lambda i, p: (0, i, 0))] * slots
        + [held((3, D, width))] * slots,
        [row_spec(step, width)],
        [shaped(dtype, n, width)],
        (place.reshape(1), residual, *mixed_grads, *weights), 0, prefetch=1,
    )[0]


def put_halves(total, inner, side, refs):
    pairs = total.reshape(-1, 2, inner, total.shape[1])
    keep = jnp.where(side == 0, pairs[:, 0], pairs[:, 1]).reshape(-1, total.shape[1])
    send = jnp.where(side == 0, pairs[:, 1], pairs[:, 0]).reshape(-1, total.shape[1])
    refs[0][0] = send.astype(BF16)
    refs[1][0] = keep


def grouped_index(starts, place, count):
    def index(j, i, *_):
        inside = (j >= starts[place]) & (j < starts[place + 1])
        row = jnp.clip(j - starts[place], 0, starts[place + 1] - starts[place] - 1)
        rest = jnp.where(j < starts[place], 0, count - 1)
        return row, 0, jnp.where(inside, i, rest)

    return index


def for_group(starts, body):
    if len(starts) == 2:
        body(0)
        return
    for place in range(len(starts) - 1):

        @pl.when((pl.program_id(0) >= starts[place]) & (pl.program_id(0) < starts[place + 1]))
        def _(place=place):
            body(place)


def join_kernel(slots, place_ref, *refs):
    out_ref = refs[-1]
    width = refs[0].shape[1]
    for k in range(slots):
        at = pl.ds(pl.multiple_of((place_ref[0] + slots - k) % slots * width, width), width)
        out_ref[:, at] = refs[k][...]


def join(c, slots):
    n, width = slots[0].shape
    D = width * len(slots)
    step = row_step(n)
    return call(
        functools.partial(join_kernel, len(slots)), "join", (n // step,),
        [row_spec(step, width)] * len(slots),
        [row_spec(step, D)], [shaped(BF16, n, D)], (c.reshape(1), *slots), 0, prefetch=1,
    )[0]


def assemble_kernel(place_ref, *refs):
    out_ref = refs[-1]
    slot = place_ref[1 + pl.program_id(0)]
    for k, ref in enumerate(refs[:-1]):

        @pl.when(slot == k)
        def _(ref=ref):
            out_ref[...] = ref[...].astype(F32)


def assemble(c, q_rows, slots):
    n, width = slots[0].shape
    count = len(slots)
    step = math.gcd(512, math.gcd(q_rows, n))
    q_steps, d_steps = q_rows // step, (n - q_rows) // step
    turns, owners = [], []
    for base, steps in ((0, q_steps), (q_steps, d_steps)):
        for owner in range(count):
            turns += [base + turn for turn in range(steps)]
            owners += [owner] * steps
    places = jnp.concatenate([c.reshape(1), (c - jnp.array(owners)) % count]).astype(jnp.int32)

    def turn_of(j, p):
        turn = jnp.where(j < count * q_steps, j % q_steps, q_steps + (j - count * q_steps) % d_steps)
        return turn, 0

    return call(
        assemble_kernel, "assemble", (len(turns),),
        [pl.BlockSpec((step, width), turn_of)] * count,
        [pl.BlockSpec((step, width), lambda j, p: (j, 0))],
        [shaped(F32, n * count, width)], (places, *slots), 0, prefetch=1,
    )[0]


def pass_on_kernel(in_ref, out_ref):
    out_ref[...] = in_ref[...]


def pass_on(array):
    spec = held(array.shape)
    return call(
        pass_on_kernel, "pass_on", (1,), [spec], [pl.BlockSpec(array.shape, lambda *_: (0,) * array.ndim)],
        [shaped(array.dtype, *array.shape)], (array,), 0,
    )[0]


def fold_kernel(starts, inner, place_ref, *refs):
    groups = len(starts) - 1

    def one_group(place):
        total = refs[place][0] + refs[groups + place][0].astype(F32)
        put_halves(total, inner, place_ref[0], refs[2 * groups :])

    for_group(starts, one_group)


def fold(side, owns, arrived, inner):
    _, rows, m = owns[0].shape
    chunk = min(1024, m)
    starts = [0]
    for own in owns:
        starts.append(starts[-1] + own.shape[0])

    def spec(size):
        return pl.BlockSpec((1, size, chunk), lambda j, i, p: (j, 0, i))

    half = rows // 2
    specs = [
        pl.BlockSpec((1, rows, chunk), grouped_index(starts, place, m // chunk))
        for place in range(len(owns))
    ]
    return call(
        functools.partial(fold_kernel, starts, inner), "fold", (starts[-1], m // chunk),
        specs + specs, [spec(half), spec(half)],
        [shaped(BF16, starts[-1], half, m), shaped(F32, starts[-1], half, m)],
        (side.reshape(1), *owns, *arrived), 0, prefetch=1,
    )


SEGMENTS = 8
ATTENTION_LANES = 128


def half_lanes(block, head, other):
    lane = lax.broadcasted_iota(jnp.int32, block.shape, 1)
    return jnp.where((lane >= DH) == (head == 1), block, other)


def scaled(block):
    return (block.astype(F32) * DH**-0.5).astype(BF16)


def three_terms(value):
    high = value.astype(BF16).astype(F32)
    middle = (value - high).astype(BF16).astype(F32)
    return high, middle, value - high - middle


def for_spans(span_ref, tiles, body):
    @pl.loop(0, tiles)
    def _(step):
        low, high = span_ref[step], span_ref[tiles + step]
        for count in range(1, tiles + 1):

            @pl.when(high - low == count)
            def _(count=count):
                body(step, low, count)


def attention_forward_kernel(
    span_ref, qkv_ref, ext_k_ref, ext_q_ref, out_ref, rest_ref, ext_ref,
    keys_ref, queries_ref, *, tile,
):
    n = ext_k_ref.shape[0]
    tiles = n // tile
    pairs = qkv_ref.shape[2] // 128

    def lanes(pair):
        return slice(pair * 128, pair * 128 + 128)

    for pair in range(pairs):
        query = scaled(qkv_ref[0, :, lanes(pair)])
        for half in range(2):
            keys_ref[2 * pair + half] = half_lanes(qkv_ref[1, :, lanes(pair)], half, ext_k_ref[...])
            queries_ref[2 * pair + half] = half_lanes(query, half, ext_q_ref[...])

    def attend(step, low, count):
        rows = pl.ds(pl.multiple_of(step * tile, tile), tile)
        window = pl.ds(pl.multiple_of(low * tile, tile), count * tile)
        lane = lax.broadcasted_iota(jnp.int32, (tile, 128), 1)
        for pair in range(pairs):
            at = lanes(pair)
            outs, extra = [], ext_q_ref[rows, :].astype(F32)
            for half in range(2):
                head = 2 * pair + half
                logits = mm(queries_ref[head, rows, :], keys_ref[head, window, :], NT)
                top = jnp.max(logits, axis=1, keepdims=True)
                weights = jnp.exp(logits - top)
                mass = jnp.sum(weights, axis=1, keepdims=True)
                probs = (weights * (1.0 / mass)).astype(BF16)
                outs.append(mm(probs, qkv_ref[2, window, at]))
                first = SEGMENTS + DH * (1 - half)
                for place, term in enumerate(three_terms(-(top + jnp.log(mass)))):
                    extra = jnp.where(lane == first + place, term, extra)
            out = jnp.where(lane < DH, outs[0], outs[1])
            out_ref[rows, at] = out.astype(BF16)
            rest_ref[rows, at] = (out - out.astype(BF16).astype(F32)).astype(BF16)
            ext_ref[rows, at] = extra.astype(BF16)

    for_spans(span_ref, tiles, attend)


def attention_forward(spans, qkv, ext_k, ext_q, tile):
    _, n, width = qkv.shape
    span = min(width, ATTENTION_LANES)
    wide = pl.BlockSpec((n, span), lambda i, *_: (0, i))
    heads = pltpu.VMEM((span // DH, n, 128), BF16)
    return call(
        functools.partial(attention_forward_kernel, tile=tile), "attention_forward",
        (width // span,),
        [pl.BlockSpec((3, n, span), lambda i, *_: (0, 0, i)), held((n, 128)), held((n, 128))],
        [wide, wide, wide],
        [shaped(BF16, n, width)] * 3,
        (spans, qkv, ext_k, ext_q), 0, prefetch=1, scratch=[heads, heads],
    )


def attention_backward_kernel(
    span_ref, qkv_ref, ext_ref, att_ref, rest_ref, grad_ref, ext_k_ref, cos_ref, sin_ref,
    out_ref, sum_ref,
    keys_ref, turned_ref, values_ref, queries_ref, plain_ref, grads_ref, plain_grads_ref,
    dq_ref, dk_ref, dv_ref, *, tile,
):
    n = ext_k_ref.shape[0]
    tiles = n // tile
    pairs = qkv_ref.shape[2] // 128
    heads = range(2 * pairs)

    def lanes(head):
        return slice(head // 2 * 128, head // 2 * 128 + 128)

    def own_rows(head):
        return slice(head % 2 * DH, head % 2 * DH + DH)

    def rows(step):
        return pl.ds(pl.multiple_of(step * tile, tile), tile)

    @pl.loop(0, tiles)
    def _(step):
        at = rows(step)
        zeros = jnp.zeros((tile, 128), BF16)
        lane = lax.broadcasted_iota(jnp.int32, (tile, 128), 1)
        ext_k = ext_k_ref[at, :]
        for pair in range(pairs):
            cut = lanes(2 * pair)
            grad = grad_ref[at, cut]
            out = att_ref[at, cut].astype(F32) + rest_ref[at, cut].astype(F32)
            product = grad.astype(F32) * out
            query = scaled(qkv_ref[0, at, cut])
            turned_ref[pair, :, at] = scaled(qkv_ref[1, at, cut]).astype(F32).T.astype(BF16)
            for half in range(2):
                head = 2 * pair + half
                keys_ref[head, at, :] = half_lanes(qkv_ref[1, at, cut], half, ext_k)
                values_ref[head, at, :] = half_lanes(qkv_ref[2, at, cut], half, ext_k)
                whole = half_lanes(query, half, ext_ref[at, cut])
                queries_ref[head, step] = whole.astype(F32).T.astype(BF16)
                plain_ref[head, at, :] = half_lanes(query, half, zeros)
                plain_grads_ref[head, at, :] = half_lanes(grad, half, zeros)
                inner = jnp.sum(half_lanes(product, half, 0.0), axis=1, keepdims=True)
                extra = jnp.zeros((tile, 128), F32)
                for place, term in enumerate(three_terms(-inner)):
                    extra = jnp.where((lane & (DH - 1)) == SEGMENTS + place, term, extra)
                whole = half_lanes(grad.astype(F32), half, extra)
                grads_ref[head, step] = whole.T.astype(BF16)

    dk_ref[...] = jnp.zeros(dk_ref.shape, F32)
    dv_ref[...] = jnp.zeros(dv_ref.shape, F32)

    def pull(step, low, count):
        at = rows(step)
        window = pl.ds(pl.multiple_of(low * tile, tile), count * tile)
        for pair in range(pairs):
            probs, slopes, dq = [], [], []
            both = range(2 * pair, 2 * pair + 2)
            for head in both:
                weights = jnp.exp(mm(keys_ref[head, window, :], queries_ref[head, step]))
                flow = mm(values_ref[head, window, :], grads_ref[head, step])
                slope = (weights * flow).astype(BF16)
                probs.append(weights.astype(BF16))
                slopes.append(slope)
                dq.append(mm(turned_ref[pair, own_rows(head), window], slope))
            plain = jnp.concatenate([plain_ref[h, at, :] for h in both], axis=0)
            grads = jnp.concatenate([plain_grads_ref[h, at, :] for h in both], axis=0)
            cut = lanes(2 * pair)
            dv_ref[window, cut] += mm(jnp.concatenate(probs, axis=1), grads)
            dk_ref[window, cut] += mm(jnp.concatenate(slopes, axis=1), plain)
            dq_ref[at, cut] = jnp.concatenate(dq, axis=0).T

    for_spans(span_ref, tiles, pull)

    def finish(step, sums):
        cosine, sine = cos_ref[rows(step), :], sin_ref[rows(step), :]
        added = []
        for which, src in enumerate((dq_ref, dk_ref, dv_ref)):
            for pair in range(pairs):
                at = lanes(2 * pair)
                block = src[rows(step), at]
                if which < 2:
                    block = block * cosine - swap_halves(block) * sine
                low = block.astype(BF16)
                out_ref[which, rows(step), at] = low
                total = jnp.sum(low.astype(F32), axis=0, keepdims=True)
                added.append(sums[which * pairs + pair] + total)
        return tuple(added)

    zero = jnp.zeros((1, 128), F32)
    sums = lax.fori_loop(0, tiles, finish, (zero,) * (3 * pairs))
    sums = [jnp.concatenate(sums[w * pairs : (w + 1) * pairs], axis=1) for w in range(3)]
    sum_ref[...] = jnp.concatenate(sums + [jnp.zeros((5, pairs * 128), F32)], axis=0)


def attention_backward(
    spans, qkv, ext, attended, rest, grads, ext_k, cosine, sine, tile
):
    _, n, width = qkv.shape
    span = min(width, ATTENTION_LANES)
    wide = pl.BlockSpec((n, span), lambda i, *_: (0, i))
    three = pl.BlockSpec((3, n, span), lambda i, *_: (0, 0, i))
    tiles, pairs = n // tile, span // 128
    heads = pltpu.VMEM((2 * pairs, n, 128), BF16)
    turned = pltpu.VMEM((2 * pairs, tiles, 128, tile), BF16)
    return call(
        functools.partial(attention_backward_kernel, tile=tile), "attention_backward",
        (width // span,),
        [three, wide, wide, wide, wide, held((n, 128)), held((n, 128)), held((n, 128))],
        [three, pl.BlockSpec((8, span), lambda i, *_: (0, i))],
        [shaped(BF16, 3, n, width), shaped(F32, 8, width)],
        (spans, qkv, ext, attended, rest, grads, ext_k, cosine, sine), 0,
        prefetch=1,
        scratch=[
            heads, pltpu.VMEM((pairs, 128, n), BF16), heads, turned, heads, turned, heads,
        ] + [pltpu.VMEM((n, span), F32)] * 3,
    )


STRIP = 32


def token_sums(width, queries):
    token = lax.broadcasted_iota(jnp.int32, (width, queries), 0) // QLEN
    return token == lax.broadcasted_iota(jnp.int32, (width, queries), 1)


def score_kernel(low_ref, high_ref, doc_ref, query_ref, pick_ref, out_ref, sum_ref, total_ref):
    group = pl.program_id(0)
    docs, width = pick_ref.shape[1:]
    doc_rows = doc_ref.shape[0]
    strips = doc_rows // STRIP
    chunk = min(256, doc_rows)
    row = lax.broadcasted_iota(jnp.int32, (STRIP, width), 0)
    sum_ref[...] = jnp.zeros(sum_ref.shape, F32)

    def add_strip(sim, first, doc, pick):
        kept = jnp.where(row == pick - first, sim, 0.0)
        sum_ref[pl.ds(doc, 1)] += jnp.sum(kept.reshape(1, STRIP // 8, 8, width), axis=1)

    for start in range(0, doc_rows, chunk):
        sims = mm(doc_ref[start : start + chunk, :], query_ref[...], NT)
        for first in range(0, chunk, STRIP):
            place = group * strips + (start + first) // STRIP
            low, high = low_ref[place], high_ref[place]
            sim = sims[first : first + STRIP]
            add_strip(sim, start + first, low, pick_ref[0, pl.ds(low, 1), :])
            pick = jnp.where(high > low, pick_ref[0, pl.ds(high, 1), :], -1)
            add_strip(sim, start + first, high, pick)

    @pl.loop(0, strips)
    def _(strip):
        low, high = low_ref[group * strips + strip], high_ref[group * strips + strip]

        @pl.when(high > low + 1)
        def _():
            first = pl.multiple_of(strip * STRIP, STRIP)
            sim = mm(doc_ref[pl.ds(first, STRIP), :], query_ref[...], NT)

            @pl.loop(low + 1, high)
            def _(doc):
                add_strip(sim, first, doc, pick_ref[0, pl.ds(doc, 1), :])

    total_ref[group] = jnp.sum(sum_ref[...], axis=1)

    @pl.when(group == pl.num_programs(0) - 1)
    def _():
        spread = token_sums(width, out_ref.shape[1]).astype(F32).astype(BF16)
        total = jnp.concatenate([total_ref[g] for g in range(total_ref.shape[0])], axis=0)
        out_ref[...] = sum(mm(term.astype(BF16), spread) for term in three_terms(total))


def score_grad_kernel(
    low_ref, high_ref, doc_ref, query_ref, pick_ref, weight_ref, doc_out, query_out,
    sparse_ref, token_ref,
):
    group = pl.program_id(0)
    docs, width = pick_ref.shape[1:]
    doc_rows = doc_ref.shape[0]
    strips = doc_rows // STRIP
    chunk = min(256, doc_rows)
    row = lax.broadcasted_iota(jnp.int32, (STRIP, width), 0)

    def fill(held, first, doc, pick):
        return jnp.where(row == pick - first, token_ref[group, pl.ds(doc, 1), :], held)

    @pl.when(group == 0)
    def _():
        query_out[...] = jnp.zeros_like(query_out)
        spread = token_sums(width, weight_ref.shape[1]).astype(F32).astype(BF16)
        weights = mm(weight_ref[...].astype(BF16), spread, NT)
        for g in range(token_ref.shape[0]):
            token_ref[g] = weights[g * docs : (g + 1) * docs]

    total = None
    for start in range(0, doc_rows, chunk):
        for first in range(start, start + chunk, STRIP):
            place = group * strips + first // STRIP
            low, high = low_ref[place], high_ref[place]
            held = fill(jnp.zeros((STRIP, width), F32), first, low, pick_ref[0, pl.ds(low, 1), :])
            pick = jnp.where(high > low, pick_ref[0, pl.ds(high, 1), :], -1)
            sparse_ref[first : first + STRIP, :] = fill(held, first, high, pick).astype(BF16)
        sparse = sparse_ref[start : start + chunk, :]
        doc_out[start : start + chunk, :] = mm(sparse, query_ref[...])
        turned = doc_ref[start : start + chunk, :].astype(F32).T.astype(BF16)
        part = mm(turned, sparse)
        total = part if total is None else total + part
    query_out[...] += total

    @pl.loop(0, strips)
    def _(strip):
        low, high = low_ref[group * strips + strip], high_ref[group * strips + strip]

        @pl.when(high > low + 1)
        def _():
            first = pl.multiple_of(strip * STRIP, STRIP)
            held = lax.fori_loop(
                low + 1,
                high,
                lambda doc, held: fill(held, first, doc, pick_ref[0, pl.ds(doc, 1), :]),
                jnp.zeros((STRIP, width), F32),
            ).astype(BF16)
            doc_out[pl.ds(first, STRIP), :] += mm(held, query_ref[...])
            turned = doc_ref[pl.ds(first, STRIP), :].astype(F32).T.astype(BF16)
            query_out[...] += mm(turned, held)


def score_specs(doc_tile, query_tile, picks):
    groups, docs, width = picks.shape
    doc_rows = doc_tile.shape[0] // groups
    return (
        pl.BlockSpec((doc_rows, 128), lambda i, *_: (i, 0)),
        held(query_tile.shape),
        pl.BlockSpec((1, docs, width), lambda i, *_: (i, 0, 0)),
    )


def score_forward(lows, highs, doc_tile, query_tile, picks):
    groups, docs, width = picks.shape
    queries = width // QLEN
    doc_spec, query_spec, pick_spec = score_specs(doc_tile, query_tile, picks)
    return call(
        score_kernel, "score_forward", (groups,),
        [doc_spec, query_spec, pick_spec],
        [pl.BlockSpec((groups * docs, queries), lambda i, *_: (0, 0))],
        [shaped(F32, groups * docs, queries)],
        (lows, highs, doc_tile, query_tile, picks), 2 * doc_tile.shape[0] * width * 128,
        prefetch=2,
        scratch=[pltpu.VMEM((docs, 8, width), F32), pltpu.VMEM((groups, docs, width), F32)],
    )[0]


def score_backward(lows, highs, doc_tile, query_tile, picks, weights):
    groups, docs, width = picks.shape
    doc_spec, query_spec, pick_spec = score_specs(doc_tile, query_tile, picks)
    return call(
        score_grad_kernel, "score_backward", (groups,),
        [doc_spec, query_spec, pick_spec, held(weights.shape)],
        [doc_spec, pl.BlockSpec((128, width), lambda i, *_: (0, 0))],
        [shaped(F32, *doc_tile.shape), shaped(F32, 128, width)],
        (lows, highs, doc_tile, query_tile, picks, weights), 4 * doc_tile.shape[0] * width * 128,
        prefetch=2,
        scratch=[
            pltpu.VMEM((doc_tile.shape[0] // groups, width), BF16),
            pltpu.VMEM((groups, docs, width), F32),
        ],
    )


def on_device(
    tokens,
    doc_lengths,
    match_picks,
    labels,
    w_qkv,
    b_qkv,
    w_out,
    b_out,
    ln1_gain,
    ln1_bias,
    w_up,
    b_up,
    w_down,
    b_down,
    ln2_gain,
    ln2_bias,
    w_proj,
    log_scale,
):
    Order.last = ()
    C = lax.axis_size("cols")
    R = lax.axis_size("rows")
    c = lax.axis_index("cols")
    r = lax.axis_index("rows")
    width = tokens.shape[1]
    D = width * C
    Q = ROW_LEN // C
    DS = (tokens.shape[0] - ROW_LEN) // C
    n = Q + DS
    tile = math.gcd(256, math.gcd(Q, DS))

    def shift_cols(value, k):
        return lax.ppermute(value, "cols", [(i, (i + k) % C) for i in range(C)])

    def swap_rows(value, bit):
        return lax.ppermute(value, "rows", [(i, i ^ bit) for i in range(R)])

    def in_order(slots):
        if len(slots) == 1:
            return slots
        if len(slots) == 2:
            return [lax.select(c == 0, slots[0], slots[1]), lax.select(c == 0, slots[1], slots[0])]
        stacked = jnp.stack(slots)
        return [
            lax.dynamic_index_in_dim(stacked, (c - j) % C, 0, keepdims=False) for j in range(C)
        ]

    rows_in_order = [b_out, ln1_gain, ln1_bias, b_down, ln2_gain, ln2_bias]
    packed = jnp.concatenate(
        [jnp.stack(rows_in_order), b_qkv, b_up.reshape(-1, width)], axis=0
    )
    packed = jnp.pad(packed, ((0, 16 - packed.shape[0]), (0, 0)))

    def gather_pieces(pieces):
        return [lax.all_gather(piece, "rows", axis=0, tiled=True) for piece in pieces]

    late_weights = (w_out, w_up, w_down)
    late_pieces = [
        lax.dynamic_index_in_dim(w.reshape(R, -1, w.shape[1]), r, 0, keepdims=False)
        for w in late_weights
    ]
    parts = jnp.concatenate(
        [tokens[:ROW_LEN].reshape(C, Q, width), tokens[ROW_LEN:].reshape(C, DS, width)], axis=1
    )

    def part(k):
        return lax.dynamic_index_in_dim(parts, (c + k) % C, 0, keepdims=False)

    qkv_piece = lax.dynamic_index_in_dim(
        w_qkv.reshape(R, -1, w_qkv.shape[2]), r, 0, keepdims=False
    )
    qkv_pieces = [shift_cols(qkv_piece, k) for k in range(1, C)]
    token_slots = [part(0)] + [shift_cols(part(k), k) for k in range(1, C)]
    own_sizes = lax.dynamic_index_in_dim(
        lax.dynamic_index_in_dim(doc_lengths, r, 0, keepdims=False), c, 0, keepdims=False
    )
    sizes = lax.dynamic_index_in_dim(doc_lengths, c, 1, keepdims=False)
    doc_ends = jnp.cumsum(sizes, axis=1)
    begins = doc_ends - sizes
    cosine, sine, ext_k, ext_q, picks = prepare(n, Q, own_sizes, match_picks, begins, sizes)
    wqkv_slots = [w_qkv]
    for k in range(1, C):
        if C == 2:
            other = gather_rows(R, qkv_pieces[k - 1], 1)
        else:
            other = lax.all_gather(qkv_pieces[k - 1], "rows", axis=0, tiled=True)
        wqkv_slots.append(other.reshape(w_qkv.shape))
    x = join(c, token_slots)
    behind, _ = lax.optimization_barrier(((w_proj, packed), x))
    wproj = jnp.concatenate(
        in_order([w_proj] + [shift_cols(behind[0], k) for k in range(1, C)]), axis=0
    )
    packs = [packed] + [shift_cols(behind[1], k) for k in range(1, C)]

    vectors = jnp.concatenate([p[:8] for p in in_order(packs)], axis=1)

    own_ends = jnp.cumsum(own_sizes)
    share = D // R
    q_tiles, d_tiles = Q // tile, DS // tile
    steps = jnp.arange(q_tiles, dtype=jnp.int32)
    first_rows = jnp.arange(d_tiles, dtype=jnp.int32) * tile
    is_passed = first_rows[:, None] >= own_ends[None, :]
    low_rows = jnp.sum(jnp.where(is_passed, own_sizes[None, :], 0), axis=1)
    last_passed = (first_rows + tile - 1)[:, None] >= own_ends[None, :]
    high_rows = jnp.min(jnp.where(last_passed, DS, own_ends[None, :]), axis=1)
    spans = jnp.concatenate(
        [steps, q_tiles + low_rows // tile, steps + 1, q_tiles + (high_rows + tile - 1) // tile]
    ).astype(jnp.int32)

    queries_here, tile_docs, _ = match_picks.shape
    strip_rows = (jnp.arange(DS // STRIP, dtype=jnp.int32) * STRIP)[None, :, None]
    lows = jnp.sum(doc_ends[:, None, :] <= strip_rows, axis=2).astype(jnp.int32).reshape(-1)
    highs = jnp.sum(begins[:, None, :] < strip_rows + STRIP, axis=2).astype(jnp.int32) - 1
    highs = highs.reshape(-1)

    qkv, attended, rests, exts = [], [], [], []
    for k in range(C):
        first = (lows, highs) if k == 0 else ()
        qkv.append(project_qkv(x, wqkv_slots[k], packs[k], cosine, sine, first))
        if k == 0:
            flat = jnp.concatenate([piece.reshape(-1, D) for piece in late_pieces])
            flat, _ = lax.optimization_barrier((flat, x))
            arrived = [shift_cols(flat, j) for j in range(1, C)]
            arrived = [pass_on(a) for a in arrived]
            ends_of = [0]
            for piece in late_pieces:
                ends_of.append(ends_of[-1] + piece.size // D)
            wout_slots, wup_slots, wdown_slots = (
                [own] + gather_pieces([
                    a[ends_of[j] : ends_of[j + 1]].reshape(late_pieces[j].shape) for a in arrived
                ])
                for j, own in enumerate(late_weights)
            )
            wout_slots, wup_slots, wdown_slots = (
                [slot.reshape(own.shape) for slot in slots_of]
                for slots_of, own in zip((wout_slots, wup_slots, wdown_slots), late_weights)
            )
        out, rest, ext = attention_forward(spans, qkv[k], ext_k, ext_q, tile)
        attended.append(out)
        rests.append(rest)
        exts.append(ext)
    normed_one, inverse_one, hidden_low, hidden_t = out_and_norm(x, vectors, attended, wout_slots)
    active, slopes = zip(*[up_and_gelu(hidden_low, wup_slots[k], packs[k]) for k in range(C)])
    normed_two, inverse_two, output_low, unit, unit_low, unit_inverse = down_and_norm(
        normed_one, vectors, wproj, active, wdown_slots
    )

    doc_tile = gather_rows(R, unit_low[Q:], 2).reshape(R * DS, 128)
    query_tile = jnp.concatenate(
        in_order([unit_low[:Q]] + [shift_cols(unit_low[:Q], k) for k in range(1, C)]), axis=0
    )
    sims = score_forward(lows, highs, doc_tile, query_tile, picks)
    scores = sims.T

    scale = jnp.exp(log_scale[0])
    z = scale * scores
    row_top = jnp.max(z, axis=1)
    row_mass = jnp.sum(jnp.exp(z - row_top[:, None]), axis=1)
    is_label = (
        jnp.arange(tile_docs, dtype=jnp.int32)[None, :] == (labels - c * tile_docs)[:, None]
    )
    chosen = jnp.sum(jnp.where(is_label, z, 0.0), axis=1)
    own_stats = jnp.stack([row_top, row_mass, chosen])
    stats = jnp.stack([own_stats] + [shift_cols(own_stats, k) for k in range(1, C)])
    top_all = jnp.max(stats[:, 0], axis=0)
    mass_all = jnp.sum(stats[:, 1] * jnp.exp(stats[:, 0] - top_all), axis=0)
    log_total = top_all + jnp.log(mass_all)
    loss = log_total - jnp.sum(stats[:, 2], axis=0)
    dz = (jnp.exp(z - log_total[:, None]) - is_label.astype(F32)) / (queries_here * R)
    scale_part = jnp.sum(dz * z)
    dscores = (scale * dz).T
    doc_grad, query_grad_t = score_backward(lows, highs, doc_tile, query_tile, picks, dscores)
    query_parts = query_grad_t.T.reshape(C, Q, 128)

    def query_part(k):
        return lax.dynamic_index_in_dim(query_parts, (c + k) % C, 0, keepdims=False)

    query_grad = query_part(0)
    for k in range(1, C):
        query_grad = query_grad + shift_cols(query_part(k), k)

    doc_sum = scatter_rows(doc_grad.reshape(R, DS, 128))
    unit_grad = jnp.concatenate([query_grad, doc_sum], axis=0)

    core = r % 2
    slots_back = range(C - 1, -1, -1)
    share = D // R
    x_bit, *z_bits = [1 << b for b in range(1, R.bit_length() - 1)]

    def side_of(bit):
        return ((r // bit) % 2).astype(jnp.int32)

    def halves_of(left_t):
        return left_t.reshape(R // 2, 2, share, n)

    def rows_of(left, side):
        return lax.dynamic_index_in_dim(left, side, 1, keepdims=False).reshape(-1, n)

    def send_plain(left, right):
        part = mm(rows_of(left, 1 - core), right).astype(BF16)
        Order.last += (part,)
        return swap_rows(part, 1)

    def keep_plain(left, right, arrived, k):
        kept = mm(rows_of(left, core), right) + arrived.astype(F32)
        if k > 0:
            kept = kept.astype(BF16)
        Order.last += (kept,)
        return kept[None] if k == 0 else shift_cols(kept, C - k)[None]

    def next_fold(states, bit, inner):
        send, keep = fold(side_of(bit), [s[0] for s in states], [s[1] for s in states], inner)
        return keep, swap_rows(send, bit)

    def cols_state(kept):
        rest = kept[1]
        for other in kept[2:]:
            rest = rest.astype(F32) + other.astype(F32)
        return kept[0], rest

    embed_grad, resid_two_grad, branch, branch_t, head_sums = head_pull(
        unit_grad, unit, unit_inverse, wproj, normed_two, inverse_two, vectors
    )
    down_left, down_right = halves_of(branch_t), active
    pre_grads, up_sums, down_kept = [None] * C, [None] * C, [None] * C
    down_arrived = [None] * C
    for k in slots_back:
        down_arrived[k] = send_plain(down_left, down_right[k])
    for k in slots_back:
        pre_grads[k], up_sums[k] = up_pull(branch, wdown_slots[k], slopes[k])
        if k > 0:
            down_kept[k] = keep_plain(down_left, down_right[k], down_arrived[k], k)
    up_left, up_right = halves_of(hidden_t), pre_grads
    up_arrived, up_kept = [None] * C, [None] * C
    for k in slots_back:
        up_arrived[k] = send_plain(up_left, up_right[k])
    down_kept[0] = keep_plain(down_left, down_right[0], down_arrived[0], 0)
    for k in slots_back[:-1]:
        up_kept[k] = keep_plain(up_left, up_right[k], up_arrived[k], k)
    resid_one_grad, branch_one_t, hidden_sums, *attended_grads = hidden_pull(
        resid_two_grad, normed_one, inverse_one, vectors, pre_grads, wup_slots, wout_slots
    )
    up_kept[0] = keep_plain(up_left, up_right[0], up_arrived[0], 0)
    mixed_grads, mixed_sums = [None] * C, [None] * C
    def gather_small():
        proj_grad = mm(embed_grad, output_low, TN).reshape(R, -1, C, width)
        def cut(values, slot_rows):
            return values.reshape(slot_rows, R, -1)

        own_order = [(c - k) % C for k in range(C)]
        canonical = jnp.stack(
            [hidden_sums[0], hidden_sums[1], hidden_sums[2], head_sums[0], head_sums[1], head_sums[2]]
        ).reshape(6, C, R, -1)
        slots_small = []
        for k in range(C):
            rows = [mixed_sums[k][j].reshape(R, -1) for j in range(3)]
            rows.append(up_sums[k][0].reshape(R, -1))
            rows += [
                lax.dynamic_index_in_dim(canonical[j], own_order[k], 0, keepdims=False)
                for j in range(6)
            ]
            own_proj_grad = lax.dynamic_index_in_dim(proj_grad, own_order[k], 2, keepdims=False)
            rows.append(own_proj_grad.reshape(R, -1))
            rows.append(jnp.broadcast_to(scale_part, (R, 1)))
            slots_small.append(jnp.concatenate(rows, axis=1))
        return jnp.stack(slots_small, axis=1)

    def pull_attention(k):
        mixed_grads[k], mixed_sums[k] = attention_backward(
            spans, qkv[k], exts[k], attended[k], rests[k], attended_grads[k], ext_k, cosine, sine,
            tile,
        )

    for k in slots_back[:-1]:
        pull_attention(k)
    wide_state = next_fold([cols_state(down_kept), cols_state(up_kept)], x_bit, share)
    pull_attention(0)
    sent = [
        shift_cols(token_pull((c + k) % C, resid_one_grad, mixed_grads, wqkv_slots, BF16), k)
        for k in range(1, C)
    ]
    own_tokens = token_pull(c, resid_one_grad, mixed_grads, wqkv_slots, F32)
    late_grad, wide_grad, small = late_sums(
        R, C, halves_of(x.T), halves_of(branch_one_t), mixed_grads, attended, *wide_state,
        gather_small(),
    )
    tokens_grad = assemble(c, Q, [own_tokens] + sent)
    qkv_grad, out_grad = late_grad[:3], late_grad[3]
    down_grad, up_grad = wide_grad
    one = D // (C * R)
    up_part = b_up.shape[0] // R
    bounds = [3 * one, 3 * one + up_part]
    for _ in range(6):
        bounds.append(bounds[-1] + one)
    pieces = [small[a:b] for a, b in zip(bounds[:-1], bounds[1:])]
    bup_out, bout_out, gain1_out, bias1_out, bdown_out, gain2_out, bias2_out = pieces
    return (
        scores,
        loss,
        tokens_grad,
        qkv_grad,
        small[: bounds[0]].reshape(3, one),
        out_grad.T,
        bout_out,
        gain1_out,
        bias1_out,
        up_grad,
        bup_out,
        down_grad.T,
        bdown_out,
        gain2_out,
        bias2_out,
        small[bounds[-1] : -1].reshape(-1, width).T,
        small[-1:],
    )


def solution(mesh):
    in_specs = (
        P("rows", "cols"),
        P(),
        P("rows", "cols", None),
        P("rows"),
        P(None, None, "cols"),
        P(None, "cols"),
        P("cols", None),
        P("cols"),
        P("cols"),
        P("cols"),
        P(None, "cols"),
        P("cols"),
        P("cols", None),
        P("cols"),
        P("cols"),
        P("cols"),
        P("cols", None),
        P(),
    )
    out_specs = (
        P("rows", "cols"),
        P("rows"),
        P("rows", "cols"),
        P(None, "rows", "cols"),
        P(None, ("cols", "rows")),
        P("cols", "rows"),
        P(("cols", "rows")),
        P(("cols", "rows")),
        P(("cols", "rows")),
        P("rows", "cols"),
        P(("cols", "rows")),
        P("cols", "rows"),
        P(("cols", "rows")),
        P(("cols", "rows")),
        P(("cols", "rows")),
        P("cols", "rows"),
        P(),
    )
    return jax.shard_map(
        on_device, mesh=mesh, in_specs=in_specs, out_specs=out_specs, check_vma=False
    )
```

```python
import functools
import math

import jax
import jax.numpy as jnp
from jax import lax
from jax.experimental import pallas as pl
from jax.experimental.pallas import tpu as pltpu
from jax.sharding import PartitionSpec as P

DH = 64
QLEN = 32
ROW_LEN = 1024
F32 = jnp.float32
BF16 = jnp.bfloat16
VMEM_LIMIT = 56 * 1024 * 1024
NT = (((1,), (1,)), ((), ()))
NN = (((1,), (0,)), ((), ()))
TN = (((0,), (0,)), ((), ()))


def mm(left, right, dims=NN):
    return lax.dot_general(left, right, dims, preferred_element_type=F32)


def row_step(rows):
    return 512 if rows % 512 == 0 else 128


def parts_of(step):
    size = 256 if step % 256 == 0 else 128
    return [slice(first, first + size) for first in range(0, step, size)]


def held(shape):
    return pl.BlockSpec(shape, lambda *_: (0,) * len(shape), pipeline_mode=pl.Buffered(1))


def shaped(dtype, *shape):
    return jax.ShapeDtypeStruct(shape, dtype)


class Order:
    last = ()


def call(
    body, name, grid, in_specs, out_specs, out_shape, operands, flops, scratch=(), prefetch=0, after=(),
    remote=None,
):
    count = len(operands)
    after = tuple(after) + Order.last

    def wrapped(*refs):
        body(*refs[:count], *refs[count + len(after) :])

    size = sum(math.prod(o.shape) * o.dtype.itemsize for o in list(operands) + list(out_shape))
    if flops == 0:
        size = 1024
    outs = pl.pallas_call(
        wrapped,
        grid_spec=pltpu.PrefetchScalarGridSpec(
            num_scalar_prefetch=prefetch,
            grid=grid,
            in_specs=list(in_specs) + [pl.BlockSpec(memory_space=pl.ANY)] * len(after),
            out_specs=out_specs,
            scratch_shapes=list(scratch),
        ),
        out_shape=out_shape,
        compiler_params=pltpu.CompilerParams(
            vmem_limit_bytes=VMEM_LIMIT, collective_id=remote, has_side_effects=remote is not None
        ),
        cost_estimate=pl.CostEstimate(flops=flops, bytes_accessed=size, transcendentals=0),
        name=name,
    )(*operands, *after)
    Order.last = (min(outs, key=lambda out: out.size * out.dtype.itemsize),)
    return outs


def row_spec(step, width):
    return pl.BlockSpec((step, width), lambda i, *_: (i, 0))


def column_spec(width, step):
    return pl.BlockSpec((width, step), lambda i, *_: (0, i))


MESH = pl.DeviceIdType.MESH
ANYWHERE = pl.BlockSpec(memory_space=pl.ANY)


def side_at(row, bit):
    return (row // bit) % 2


def across(row, bit):
    return row + bit * (1 - 2 * side_at(row, bit))


def flipped(row, bits):
    bit = 1
    while bit <= bits:
        if bits & bit:
            row = across(row, bit)
        bit *= 2
    return row


def greet(devices):
    barrier = pltpu.get_barrier_semaphore()
    for device in devices:
        pl.semaphore_signal(barrier, inc=1, device_id=device, device_id_type=MESH)
    pl.semaphore_wait(barrier, len(devices))


def send(source, target, sent, arrived, device):
    copy = pltpu.make_async_remote_copy(
        src_ref=source,
        dst_ref=target,
        send_sem=sent,
        recv_sem=arrived,
        device_id=device,
        device_id_type=MESH,
    )
    copy.start()
    return copy


def spread_order(count):
    pieces = sorted(range(count), key=lambda piece: (piece.bit_count(), -piece))
    order = []
    for piece in pieces:
        lowest = piece & -piece if piece else count
        bit = lowest // 2
        bits = []
        while bit:
            bits.append(bit)
            bit //= 2
        order.append((piece, bits))
    return order


def gather_kernel(rows, own, out, own_sem, sent, arrived):
    r = lax.axis_index("rows")
    bits = [1 << b for b in range(rows.bit_length() - 1)]
    greet([{"rows": across(r, bit)} for bit in bits])
    local = pltpu.make_async_copy(own, out.at[r], own_sem)
    local.start()
    copies = {}
    size = own.shape[0] // PARTS
    for piece, over in spread_order(rows):
        row = flipped(r, piece)
        for part in range(PARTS):
            at = pl.ds(part * size, size)
            if piece:
                copies[piece, part].wait_recv()
            for bit in over:
                copies[piece | bit, part] = send(
                    out.at[row, at] if piece else own.at[at], out.at[row, at],
                    sent.at[piece | bit, part], arrived.at[piece | bit, part],
                    {"rows": across(r, bit)},
                )
    for copy in copies.values():
        copy.wait_send()
    local.wait()


PARTS = 2


def gather_rows(rows, own, remote):
    return call(
        functools.partial(gather_kernel, rows), "gather_rows", (1,), [ANYWHERE], [ANYWHERE],
        [shaped(own.dtype, rows, *own.shape)], (own,), 0, remote=remote,
        scratch=[
            pltpu.SemaphoreType.DMA, pltpu.SemaphoreType.DMA((rows, PARTS)),
            pltpu.SemaphoreType.DMA((rows, PARTS)),
        ],
    )[0]


def scatter_kernel(rows, parts, out, sent, arrived, *buffers):
    r = lax.axis_index("rows")
    bits = [1 << b for b in range(rows.bit_length() - 1)]
    greet([{"rows": across(r, bit)} for bit in bits])
    outgoing, incoming = buffers[: len(bits)], buffers[len(bits) :]
    size = parts.shape[1] // PARTS
    copies = {}

    def total(flips, levels, part):
        row, at = flipped(r, flips), pl.ds(part * size, size)
        value = parts[row, at]
        for level in range(levels):
            copies[level, flips >> (level + 1), part].wait_recv()
            value = value + incoming[level][row // (2 << level), at].astype(F32)
        return value

    for level, bit in enumerate(bits):
        count = rows // (2 << level)
        for turn in sorted(range(count), key=lambda f: tuple(-((f >> b) & 1) for b in range(8))):
            flips = (turn << (level + 1)) | bit
            place = flipped(r, flips) // (2 << level)
            for part in range(PARTS):
                at = pl.ds(part * size, size)
                outgoing[level][place, at] = total(flips, level, part).astype(BF16)
                name = rows - 2 * count + turn
                copies[level, turn, part] = send(
                    outgoing[level].at[place, at], incoming[level].at[place, at],
                    sent.at[name, part], arrived.at[name, part], {"rows": across(r, bit)},
                )
    for part in range(PARTS):
        out[part * size : (part + 1) * size, :] = total(0, len(bits), part)
    for copy in copies.values():
        copy.wait_send()


def scatter_rows(parts):
    rows, height, width = parts.shape
    levels = rows.bit_length() - 1
    buffers = [
        pltpu.VMEM((rows // (2 << level), height, width), BF16) for level in range(levels)
    ]
    return call(
        functools.partial(scatter_kernel, rows), "scatter_rows", (1,), [held(parts.shape)],
        [pl.BlockSpec((height, width), lambda *_: (0, 0))], [shaped(F32, height, width)],
        (parts,), 0, remote=3,
        scratch=[
            pltpu.SemaphoreType.DMA((rows, PARTS)), pltpu.SemaphoreType.DMA((rows, PARTS)),
        ] + buffers + buffers,
    )[0]


def small_sums(rows, cols, parts, out, *refs):
    bits = [1 << b for b in range(rows.bit_length() - 1)]
    sent, arrived = refs[:2]
    core_in, cols_in, totals = refs[2], refs[3], refs[4 : 4 + len(bits)]
    row_ins = refs[4 + len(bits) :]
    r, c = lax.axis_index("rows"), lax.axis_index("cols")
    others = [{"cols": (c + cols - k) % cols} for k in range(1, cols)]
    core = side_at(r, 1)
    copies = {}

    def first():
        copies["core"] = send(
            parts.at[:, 1 - core], core_in, sent.at[0], arrived.at[0], {"rows": across(r, 1)}
        )

    def second():
        copies["core"].wait()
        totals[0][...] = parts[:, core] + core_in[...]
        for k in range(1, cols):
            copies["cols", k] = send(
                totals[0].at[:, k], cols_in.at[k - 1], sent.at[k], arrived.at[k], others[k - 1]
            )

    def third():
        total = totals[0][:, 0]
        for k in range(1, cols):
            copies["cols", k].wait()
            total = total + cols_in[k - 1]
        pass_on(0, total)

    def pass_on(level, total):
        if level == len(bits) - 1:
            out[...] = total[0]
            return
        whole = totals[1 + level]
        whole[...] = total.reshape(whole.shape)
        copies["row", level] = send(
            whole.at[:, 1 - side_at(r, bits[1 + level])], row_ins[level],
            sent.at[cols + level], arrived.at[cols + level],
            {"rows": across(r, bits[1 + level])},
        )

    def later(level):
        copies["row", level].wait()
        pass_on(level + 1, totals[1 + level][:, side_at(r, bits[1 + level])] + row_ins[level][...])

    return [first, second, third] + [
        functools.partial(later, level) for level in range(len(bits) - 1)
    ]


def small_blocks(rows, cols, parts):
    length = parts.shape[2]
    width = -(-length // 1024) * 128
    parts = jnp.pad(parts, ((0, 0), (0, 0), (0, 8 * width - length)))
    parts = parts.reshape(rows // 2, 2, cols, 8, width)
    levels = rows.bit_length() - 1
    heights = [rows >> (level + 1) for level in range(1, levels)]
    scratch = [
        pltpu.SemaphoreType.DMA((cols + levels,)), pltpu.SemaphoreType.DMA((cols + levels,)),
        pltpu.VMEM((rows // 2, cols, 8, width), F32),
        pltpu.VMEM((cols - 1, rows // 2, 8, width), F32),
        pltpu.VMEM((rows // 2, cols, 8, width), F32),
    ]
    scratch += [pltpu.VMEM((height, 2, 8, width), F32) for height in heights]
    scratch += [pltpu.VMEM((height, 8, width), F32) for height in heights]
    return parts, scratch


def late_kernel(rows, cols, *refs):
    tokens_t, branch_t = refs[:2]
    far_rights, far_attended, refs = refs[2 : 2 + cols], refs[2 + cols : 2 + 2 * cols], refs[2 + 2 * cols :]
    (du_own, du_in, small, out, du_out, small_out), refs = refs[:6], refs[6:]
    (rights, right_sem), refs = refs[:2], refs[2:]
    (core_out, core_in, x_out, x_in, kept, cols_out, cols_in), refs = refs[:7], refs[7:]
    r, c = lax.axis_index("rows"), lax.axis_index("cols")
    x_bit, *z_bits = [1 << b for b in range(1, rows.bit_length() - 1)]
    levels = len(z_bits)
    z_out, z_in, z_kept = refs[:levels], refs[levels : 2 * levels], refs[2 * levels : 3 * levels]
    refs = refs[3 * levels :]
    du_z_out, du_z_in, du_kept = refs[:levels], refs[levels : 2 * levels], refs[2 * levels : 3 * levels]
    refs = refs[3 * levels :]
    (core_sem, x_sem, cols_sem, z_sem, du_sem), refs = refs[:5], refs[5:]
    small_steps = small_sums(rows, cols, small, small_out, *refs)
    share = out.shape[1]
    others = [{"cols": (c + cols - k) % cols} for k in range(1, cols)]
    core, x_side = side_at(r, 1), side_at(r, x_bit)
    greet([{"rows": across(r, bit)} for bit in [1, x_bit] + z_bits] + others)
    chunks = range(4)
    slots = range(cols - 1, -1, -1)
    copies = {}

    def halves(total, side, inner):
        pairs = total.reshape(-1, 2, inner, total.shape[1])
        near = jnp.where(side == 0, pairs[:, 0], pairs[:, 1]).reshape(-1, total.shape[1])
        far = jnp.where(side == 0, pairs[:, 1], pairs[:, 0]).reshape(-1, total.shape[1])
        return near, far

    def product(side, slot, chunk):
        left = (tokens_t if chunk < 3 else branch_t)[:, side]
        return mm(left.reshape(-1, left.shape[-1]), rights[slot, chunk])

    def load(slot, chunk):
        source = far_rights[slot].at[chunk] if chunk < 3 else far_attended[slot]
        return pltpu.make_async_copy(source, rights.at[slot, chunk], right_sem.at[slot, chunk])

    for chunk in chunks:
        for slot in slots:
            load(slot, chunk).start()

    def begin(chunk):
        for slot in slots:
            load(slot, chunk).wait()
            if chunk >= 2:
                copies["core", slot, chunk - 2].wait_send()
            core_out[slot, chunk % 2] = product(1 - core, slot, chunk).astype(BF16)
            copies["core", slot, chunk] = send(
                core_out.at[slot, chunk % 2], core_in.at[slot, chunk],
                core_sem.at[0, slot, chunk], core_sem.at[1, slot, chunk],
                {"rows": across(r, 1)},
            )

    def after_core(chunk):
        for slot in slots:
            total = product(core, slot, chunk)
            copies["core", slot, chunk].wait_recv()
            near, far = halves(total + core_in[slot, chunk].astype(F32), x_side, share)
            x_out[slot, chunk] = far.astype(BF16)
            kept[slot, chunk] = near
            copies["x", slot, chunk] = send(
                x_out.at[slot, chunk], x_in.at[slot, chunk], x_sem.at[0, slot, chunk],
                x_sem.at[1, slot, chunk], {"rows": across(r, x_bit)},
            )

    def after_x(chunk):
        for slot in slots:
            copies["x", slot, chunk].wait_recv()
            total = kept[slot, chunk] + x_in[slot, chunk].astype(F32)
            if slot == 0:
                kept[0, chunk] = total
            else:
                cols_out[slot - 1, chunk] = total.astype(BF16)
                copies["cols", slot, chunk] = send(
                    cols_out.at[slot - 1, chunk], cols_in.at[slot - 1, chunk],
                    cols_sem.at[0, slot - 1, chunk], cols_sem.at[1, slot - 1, chunk],
                    others[slot - 1],
                )

    def after_cols(chunk):
        total = kept[0, chunk]
        for slot in slots[:-1]:
            copies["cols", slot, chunk].wait_recv()
            total = total + cols_in[slot - 1, chunk].astype(F32)
        pass_z(chunk, 0, total)

    def pass_z(chunk, level, total):
        if level == levels:
            out[chunk] = total
            return
        bit = z_bits[level]
        near, far = halves(total, side_at(r, bit), share)
        z_out[level][chunk] = far.astype(BF16)
        z_kept[level][chunk] = near
        copies["z", level, chunk] = send(
            z_out[level].at[chunk], z_in[level].at[chunk], z_sem.at[0, level, chunk],
            z_sem.at[1, level, chunk], {"rows": across(r, bit)},
        )

    def after_z(chunk, level):
        copies["z", level, chunk].wait_recv()
        pass_z(chunk, level + 1, z_kept[level][chunk] + z_in[level][chunk].astype(F32))

    def pass_du(place, level, total):
        if level == levels:
            du_out[place] = total
            return
        bit = z_bits[level]
        near, far = halves(total, side_at(r, bit), share)
        du_z_out[level][place] = far.astype(BF16)
        du_kept[level][place] = near
        copies["du", level, place] = send(
            du_z_out[level].at[place], du_z_in[level].at[place], du_sem.at[0, level, place],
            du_sem.at[1, level, place], {"rows": across(r, bit)},
        )

    def after_du(place, level):
        copies["du", level, place].wait_recv()
        pass_du(place, level + 1, du_kept[level][place] + du_z_in[level][place].astype(F32))

    for place in range(2):
        pass_du(place, 0, du_own[place] + du_in[place].astype(F32))
    stages = [(0, begin), (1, after_core), (3, after_x), (4, after_cols)]
    stages += [(5 + level, functools.partial(after_z, level=level)) for level in range(levels)]
    for turn in range(len(chunks) + stages[-1][0]):
        for delay, stage in stages[::-1]:
            if 0 <= turn - delay < len(chunks):
                stage(turn - delay)
        if 3 <= turn < 3 + levels:
            for place in range(2):
                after_du(place, turn - 3)
        if turn >= 1 and small_steps:
            small_steps.pop(0)()
    for step in small_steps:
        step()
    for name, copy in copies.items():
        if name[0] != "core" or name[2] >= 2:
            copy.wait_send()


def late_sums(rows, cols, tokens_t, branch_t, rights, attended, du_own, du_in, small):
    share, n = tokens_t.shape[2:]
    width = attended[0].shape[1]
    wide = du_own.shape[2]
    half, quarter = rows // 2 * share, rows // 4 * share
    levels = rows.bit_length() - 3
    heights = [quarter >> (level + 1) for level in range(levels)]

    def vmem(dtype, *shape):
        return pltpu.VMEM(shape, dtype)

    def pair_of(*shape):
        return pltpu.SemaphoreType.DMA((2,) + shape)

    length = small.shape[2]
    small, small_scratch = small_blocks(rows, cols, small)
    operands = (tokens_t, branch_t, *rights, *attended, du_own, du_in, small)
    scratch = [
        vmem(BF16, cols, 4, n, width), pltpu.SemaphoreType.DMA((cols, 4)),
        vmem(BF16, cols, 2, half, width), vmem(BF16, cols, 4, half, width),
        vmem(BF16, cols, 4, quarter, width), vmem(BF16, cols, 4, quarter, width),
        vmem(F32, cols, 4, quarter, width),
        vmem(BF16, cols - 1, 4, quarter, width), vmem(BF16, cols - 1, 4, quarter, width),
    ]
    for count, size in ((4, width), (2, wide)):
        for dtype in (BF16, BF16, F32):
            scratch += [vmem(dtype, count, height, size) for height in heights]
    scratch += [
        pair_of(cols, 4), pair_of(cols, 4), pair_of(cols - 1, 4), pair_of(levels, 4),
        pair_of(levels, 2),
    ]
    def whole(*shape):
        return pl.BlockSpec(shape, lambda *_: (0,) * len(shape))

    late, wide_sum, small_sum = call(
        functools.partial(late_kernel, rows, cols), "late_sums", (1,),
        [held(tokens_t.shape), held(branch_t.shape)] + [ANYWHERE] * (2 * cols)
        + [held(du_own.shape), held(du_in.shape), held(small.shape)],
        [whole(4, share, width), whole(2, share, wide), whole(*small.shape[3:])],
        [
            shaped(F32, 4, share, width), shaped(F32, 2, share, wide), shaped(F32, *small.shape[3:])
        ],
        operands, 100_000_000_000, remote=5, scratch=scratch + small_scratch,
    )
    return late, wide_sum, small_sum.reshape(-1)[:length]


QKV_BIAS, UP_BIAS = 6, 9


def swap_halves(block):
    lane = lax.broadcasted_iota(jnp.int32, block.shape, 1)
    return jnp.where((lane & 32) == 0, pltpu.roll(block, 96, 1), pltpu.roll(block, 32, 1))


def qkv_kernel(slots, place_ref, *refs):
    x_refs, (w_ref, b_ref, cos_ref, sin_ref, out_ref) = refs[:slots], refs[slots:]
    which = pl.program_id(0)
    bias = b_ref[pl.ds(QKV_BIAS + which, 1), :]
    depth = x_refs[0].shape[1]

    def mixed_rows(at):
        total = bias
        for k, x_ref in enumerate(x_refs):
            place = (place_ref[0] + slots - k) % slots
            rows = pl.ds(pl.multiple_of(place * depth, depth), depth)
            total = total + mm(x_ref[at, :], w_ref[0, rows, :])
        return total

    @pl.when(which < 2)
    def _():
        for at in parts_of(out_ref.shape[1]):
            mixed = mixed_rows(at)
            for first in range(0, mixed.shape[1], 128):
                block = mixed[:, first : first + 128]
                turned = block * cos_ref[at, :] + swap_halves(block) * sin_ref[at, :]
                out_ref[0, at, first : first + 128] = turned.astype(BF16)

    @pl.when(which == 2)
    def _():
        for at in parts_of(out_ref.shape[1]):
            out_ref[0, at, :] = mixed_rows(at).astype(BF16)


def project_qkv(c, x_slots, weight, bias, cosine, sine, after=()):
    n = x_slots[0].shape[0]
    _, D, width = weight.shape
    return call(
        functools.partial(qkv_kernel, len(x_slots)), "project_qkv", (3,),
        [held(x.shape) for x in x_slots] + [
            pl.BlockSpec((1, D, width), lambda j, p: (j, 0, 0)), held(bias.shape),
            held((n, 128)), held((n, 128)),
        ],
        [pl.BlockSpec((1, n, width), lambda j, p: (j, 0, 0))],
        [shaped(BF16, 3, n, width)],
        (c.reshape(1), *x_slots, weight, bias, cosine, sine), 6 * n * D * width, after=after,
        prefetch=1,
    )[0]


def prepare_kernel(
    q_rows, sizes_ref, picks_ref, docs_ref, cos_ref, sin_ref, ext_k_ref, ext_q_ref, out_ref
):
    n = cos_ref.shape[0]
    size = math.gcd(256, math.gcd(q_rows, n))
    lane = lax.broadcasted_iota(jnp.int32, (size, 128), 1)
    frequency = jnp.exp((lane & (DH // 2 - 1)).astype(F32) * (-2.0 * math.log(10000.0) / DH))
    place_lane = lane & (DH - 1)
    for first in range(0, n, size):
        at = slice(first, first + size)
        row = lax.broadcasted_iota(jnp.int32, (size, 128), 0) + first
        if first < q_rows:
            position, segment = row & (QLEN - 1), (row // QLEN) & (SEGMENTS - 1)
        else:
            place = row - q_rows
            begin, segment, end = jnp.zeros_like(row), jnp.zeros_like(row), 0
            for doc in range(sizes_ref.shape[0]):
                end = end + sizes_ref[doc]
                passed = place >= end
                begin = jnp.where(passed, end, begin)
                segment = segment + passed.astype(jnp.int32)
            position = place - begin
        angles = position.astype(F32) * frequency
        sine = jnp.sin(angles)
        cos_ref[at, :] = jnp.cos(angles)
        sin_ref[at, :] = jnp.where((lane & (DH // 2)) == 0, -sine, sine)
        same = segment == place_lane
        ones = (place_lane >= SEGMENTS) & (place_lane < SEGMENTS + 3)
        ext_k_ref[at, :] = (same | ones).astype(F32).astype(BF16)
        apart = (place_lane < SEGMENTS) & jnp.logical_not(same)
        ext_q_ref[at, :] = jnp.where(apart, -1e30, 0.0).astype(BF16)
    queries = picks_ref.shape[0]
    begins, sizes = docs_ref[:, 0:1], docs_ref[:, 1:2]
    groups, docs = out_ref.shape[:2]
    for first in range(0, queries, 4):
        lanes = jnp.concatenate([picks_ref[first + j] for j in range(4)], axis=1)
        rows = begins + lax.rem(lanes, jnp.broadcast_to(sizes, lanes.shape))
        at = slice(first * QLEN, (first + 4) * QLEN)
        for group in range(groups):
            out_ref[group, :, at] = rows[group * docs : (group + 1) * docs]


def prepare(n, q_rows, own_sizes, match_picks, begins, sizes):
    groups, docs = sizes.shape
    width = match_picks.shape[0] * QLEN
    table = jnp.stack([begins.reshape(-1), sizes.reshape(-1)], axis=1)
    return call(
        functools.partial(prepare_kernel, q_rows), "prepare", (1,),
        [held(match_picks.shape), held(table.shape)],
        [pl.BlockSpec((n, 128), lambda *_: (0, 0))] * 4
        + [pl.BlockSpec((groups, docs, width), lambda *_: (0, 0, 0))],
        [
            shaped(F32, n, 128), shaped(F32, n, 128), shaped(BF16, n, 128), shaped(BF16, n, 128),
            shaped(jnp.int32, groups, docs, width),
        ],
        (own_sizes, match_picks, table), 0, prefetch=1,
    )


def normed_rows(residual):
    mean = jnp.mean(residual, axis=1, keepdims=True)
    centred = residual - mean
    inverse = lax.rsqrt(jnp.mean(centred * centred, axis=1, keepdims=True) + 1e-05)
    return centred * inverse, inverse


def norm_pull(grad_rows, normed, inverse, gain):
    spread = grad_rows * gain
    return inverse * (
        spread
        - jnp.mean(spread, axis=1, keepdims=True)
        - normed * jnp.mean(spread * normed, axis=1, keepdims=True)
    )


def column_sums(*arrays):
    rows = [jnp.sum(array, axis=0, keepdims=True) for array in arrays]
    rows.append(jnp.zeros((8 - len(rows), rows[0].shape[1]), F32))
    return jnp.concatenate(rows, axis=0)


def add_over_steps(ref, value):
    first = pl.program_id(0) == 0

    @pl.when(first)
    def _():
        ref[...] = value

    @pl.when(jnp.logical_not(first))
    def _():
        ref[...] += value


def out_norm_kernel(slots, *refs):
    x_ref, vec_ref = refs[:2]
    att_refs, w_refs = refs[2 : 2 + slots], refs[2 + slots : 2 + 2 * slots]
    normed_ref, inverse_ref, low_ref, turned_ref = refs[2 + 2 * slots :]
    for at in parts_of(x_ref.shape[0]):
        residual = x_ref[at, :].astype(F32) + vec_ref[0:1, :]
        for att_ref, w_ref in zip(att_refs, w_refs):
            residual = residual + mm(att_ref[at, :], w_ref[...])
        normed, inverse = normed_rows(residual)
        hidden = normed * vec_ref[1:2, :] + vec_ref[2:3, :]
        normed_ref[at, :] = normed
        inverse_ref[at, :] = inverse
        low_ref[at, :] = hidden.astype(BF16)
        turned_ref[:, at] = hidden.T.astype(BF16)


def out_and_norm(x, vectors, attended, weights):
    n, D = x.shape
    step = row_step(n)
    slots = len(attended)
    width = attended[0].shape[1]
    return call(
        functools.partial(out_norm_kernel, slots), "out_and_norm", (n // step,),
        [row_spec(step, D), held(vectors.shape)]
        + [row_spec(step, width)] * slots + [held((width, D))] * slots,
        [row_spec(step, D), row_spec(step, 1), row_spec(step, D), column_spec(D, step)],
        [shaped(F32, n, D), shaped(F32, n, 1), shaped(BF16, n, D), shaped(BF16, D, n)],
        (x, vectors, *attended, *weights), 2 * n * D * D,
    )


GELU_TERMS = (
    0.23532527933595032, 0.09138803439798156, 0.6495603483388861,
    -0.6354014529895687, 0.8866650885491606, -0.22753729931242958,
)


def gelu_parts(values):
    size = jnp.abs(values)
    part = pl.reciprocal(1.0 + (0.39 / math.sqrt(2.0)) * size)
    bell = jnp.exp(-0.5 * (values * values))
    series = 0.5 * GELU_TERMS[-1]
    for term in GELU_TERMS[-2::-1]:
        series = series * part + 0.5 * term
    tail = series * part * bell
    below = jnp.where(values >= 0.0, 1.0 - tail, tail)
    return values * below, below + values * bell * (1.0 / math.sqrt(2.0 * math.pi))


def up_kernel(x_ref, w_ref, b_ref, active_ref, slope_ref):
    width, part = w_ref.shape[1], b_ref.shape[1]
    chunk = min(256, part)
    for first in range(0, width, chunk):
        at = slice(first, first + chunk)
        row, lane = UP_BIAS + first // part, first % part
        bias = b_ref[row : row + 1, lane : lane + chunk]
        active, slope = gelu_parts(mm(x_ref[...], w_ref[:, at]) + bias)
        active_ref[:, at] = active.astype(BF16)
        slope_ref[:, at] = slope


def up_and_gelu(x, weight, bias):
    n, D = x.shape
    width = weight.shape[1]
    step = row_step(n)
    return call(
        up_kernel, "up_and_gelu", (n // step,),
        [row_spec(step, D), held(weight.shape), held(bias.shape)],
        [row_spec(step, width)] * 2,
        [shaped(BF16, n, width), shaped(F32, n, width)],
        (x, weight, bias), 5 * n * D * width,
    )


def down_norm_kernel(slots, *refs):
    normed_ref, vec_ref, proj_ref = refs[:3]
    act_refs, w_refs = refs[3 : 3 + slots], refs[3 + slots : 3 + 2 * slots]
    normed_out, inverse_ref, low_ref, unit_ref, unit_low_ref, unit_inverse_ref = refs[3 + 2 * slots :]
    for at in parts_of(normed_ref.shape[0]):
        residual = normed_ref[at, :] * vec_ref[1:2, :] + vec_ref[2:3, :] + vec_ref[3:4, :]
        for act_ref, w_ref in zip(act_refs, w_refs):
            residual = residual + mm(act_ref[at, :], w_ref[...])
        normed, inverse = normed_rows(residual)
        normed_out[at, :] = normed
        inverse_ref[at, :] = inverse
        low = (normed * vec_ref[4:5, :] + vec_ref[5:6, :]).astype(BF16)
        low_ref[at, :] = low
        embedding = mm(low, proj_ref[...])
        unit_inverse = lax.rsqrt(jnp.sum(embedding * embedding, axis=1, keepdims=True) + 1e-06)
        unit = embedding * unit_inverse
        unit_ref[at, :] = unit
        unit_low_ref[at, :] = unit.astype(BF16)
        unit_inverse_ref[at, :] = unit_inverse


def down_and_norm(normed, vectors, proj, active, weights):
    n, D = normed.shape
    step = row_step(n)
    slots = len(active)
    width = active[0].shape[1]
    return call(
        functools.partial(down_norm_kernel, slots), "down_and_norm", (n // step,),
        [row_spec(step, D), held(vectors.shape), held(proj.shape)]
        + [row_spec(step, width)] * slots + [held((width, D))] * slots,
        [
            row_spec(step, D), row_spec(step, 1), row_spec(step, D),
            row_spec(step, 128), row_spec(step, 128), row_spec(step, 1),
        ],
        [
            shaped(F32, n, D), shaped(F32, n, 1), shaped(BF16, n, D),
            shaped(F32, n, 128), shaped(BF16, n, 128), shaped(F32, n, 1),
        ],
        (normed, vectors, proj, *active, *weights), 2 * n * D * width * slots,
    )


def head_pull_kernel(
    grad_ref, unit_ref, unit_inverse_ref, proj_ref, normed_ref, inverse_ref, vec_ref,
    embed_ref, residual_ref, low_ref, turned_ref, sum_ref,
):
    sums = []
    for at in parts_of(grad_ref.shape[0]):
        grad, unit = grad_ref[at, :], unit_ref[at, :]
        embed = grad - unit * jnp.sum(grad * unit, axis=1, keepdims=True)
        embed = (unit_inverse_ref[at, :] * embed).astype(BF16)
        embed_ref[at, :] = embed
        output_grad = mm(embed, proj_ref[...], NT)
        normed = normed_ref[at, :]
        residual = norm_pull(output_grad, normed, inverse_ref[at, :], vec_ref[4:5, :])
        residual_ref[at, :] = residual
        low_ref[at, :] = residual.astype(BF16)
        turned_ref[:, at] = residual.T.astype(BF16)
        sums.append(column_sums(residual, output_grad * normed, output_grad))
    add_over_steps(sum_ref, sum(sums))


def head_pull(unit_grad, unit, unit_inverse, proj, normed, inverse, vectors):
    n, D = normed.shape
    step = row_step(n)
    return call(
        head_pull_kernel, "head_pull", (n // step,),
        [
            row_spec(step, 128), row_spec(step, 128), row_spec(step, 1), held(proj.shape),
            row_spec(step, D), row_spec(step, 1), held(vectors.shape),
        ],
        [
            row_spec(step, 128), row_spec(step, D), row_spec(step, D),
            column_spec(D, step), pl.BlockSpec((8, D), lambda i: (0, 0)),
        ],
        [
            shaped(BF16, n, 128), shaped(F32, n, D), shaped(BF16, n, D),
            shaped(BF16, D, n), shaped(F32, 8, D),
        ],
        (unit_grad, unit, unit_inverse, proj, normed, inverse, vectors), 4 * n * D * 128,
    )


def up_pull_kernel(branch_ref, w_ref, slope_ref, out_ref, sum_ref):
    width = w_ref.shape[0]
    chunk = min(512, width)
    sums = []
    for first in range(0, width, chunk):
        at = slice(first, first + chunk)
        low = (mm(branch_ref[...], w_ref[at, :], NT) * slope_ref[:, at]).astype(BF16)
        out_ref[:, at] = low
        sums.append(column_sums(low.astype(F32)))
    add_over_steps(sum_ref, jnp.concatenate(sums, axis=1))


def up_pull(branch, weight, slope):
    n, D = branch.shape
    width = weight.shape[0]
    step = row_step(n)
    return call(
        up_pull_kernel, "up_pull", (n // step,),
        [row_spec(step, D), held(weight.shape), row_spec(step, width)],
        [row_spec(step, width), pl.BlockSpec((8, width), lambda i: (0, 0))],
        [shaped(BF16, n, width), shaped(F32, 8, width)],
        (branch, weight, slope), 2 * n * D * width,
    )


def hidden_pull_kernel(slots, *refs):
    residual_ref, normed_ref, inverse_ref, vec_ref = refs[:4]
    pre_refs, up_refs, out_refs = (refs[4 + j * slots : 4 + (j + 1) * slots] for j in range(3))
    rest = refs[4 + 3 * slots :]
    grad_ref, turned_ref, sum_ref = rest[:3]
    att_refs = rest[3:]
    sums = []
    for at in parts_of(residual_ref.shape[0]):
        hidden_grad = residual_ref[at, :]
        for pre_ref, up_ref in zip(pre_refs, up_refs):
            hidden_grad = hidden_grad + mm(pre_ref[at, :], up_ref[...], NT)
        normed = normed_ref[at, :]
        residual = norm_pull(hidden_grad, normed, inverse_ref[at, :], vec_ref[1:2, :])
        grad_ref[at, :] = residual
        low = residual.astype(BF16)
        turned_ref[:, at] = residual.T.astype(BF16)
        sums.append(column_sums(residual, hidden_grad * normed, hidden_grad))
        for att_ref, out_ref in zip(att_refs, out_refs):
            att_ref[at, :] = mm(low, out_ref[...], NT).astype(BF16)
    add_over_steps(sum_ref, sum(sums))


def hidden_pull(residual, normed, inverse, vectors, pre_grads, ups, outs):
    n, D = residual.shape
    step = row_step(n)
    slots = len(ups)
    wide, width = ups[0].shape[1], outs[0].shape[0]
    return call(
        functools.partial(hidden_pull_kernel, slots), "hidden_pull", (n // step,),
        [row_spec(step, D), row_spec(step, D), row_spec(step, 1), held(vectors.shape)]
        + [row_spec(step, wide)] * slots + [held((D, wide))] * slots
        + [held((width, D))] * slots,
        [row_spec(step, D), column_spec(D, step), pl.BlockSpec((8, D), lambda i: (0, 0))]
        + [row_spec(step, width)] * slots,
        [shaped(F32, n, D), shaped(BF16, D, n), shaped(F32, 8, D)]
        + [shaped(BF16, n, width)] * slots,
        (residual, normed, inverse, vectors, *pre_grads, *ups, *outs),
        0,
    )


def token_pull_kernel(slots, place_ref, *refs):
    residual_ref = refs[0]
    mixed_refs, w_refs = refs[1 : 1 + slots], refs[1 + slots : 1 + 2 * slots]
    out_ref = refs[-1]
    width = out_ref.shape[1]
    at = pl.ds(pl.multiple_of(place_ref[0] * width, width), width)
    total = residual_ref[...]
    for mixed_ref, w_ref in zip(mixed_refs, w_refs):
        for which in range(3):
            total = total + mm(mixed_ref[which], w_ref[which, at, :], NT)
    out_ref[...] = total.astype(out_ref.dtype)


def token_pull(place, residual, mixed_grads, weights, dtype):
    n, D = residual.shape
    step = row_step(n)
    slots = len(weights)
    width = weights[0].shape[2]
    return call(
        functools.partial(token_pull_kernel, slots), "token_pull", (n // step,),
        [pl.BlockSpec((step, width), lambda i, p: (i, p[0]))]
        + [pl.BlockSpec((3, step, width), lambda i, p: (0, i, 0))] * slots
        + [held((3, D, width))] * slots,
        [row_spec(step, width)],
        [shaped(dtype, n, width)],
        (place.reshape(1), residual, *mixed_grads, *weights), 0, prefetch=1,
    )[0]


def put_halves(total, inner, side, refs):
    pairs = total.reshape(-1, 2, inner, total.shape[1])
    keep = jnp.where(side == 0, pairs[:, 0], pairs[:, 1]).reshape(-1, total.shape[1])
    send = jnp.where(side == 0, pairs[:, 1], pairs[:, 0]).reshape(-1, total.shape[1])
    refs[0][0] = send.astype(BF16)
    refs[1][0] = keep


def grouped_index(starts, place, count):
    def index(j, i, *_):
        inside = (j >= starts[place]) & (j < starts[place + 1])
        row = jnp.clip(j - starts[place], 0, starts[place + 1] - starts[place] - 1)
        rest = jnp.where(j < starts[place], 0, count - 1)
        return row, 0, jnp.where(inside, i, rest)

    return index


def for_group(starts, body):
    if len(starts) == 2:
        body(0)
        return
    for place in range(len(starts) - 1):

        @pl.when((pl.program_id(0) >= starts[place]) & (pl.program_id(0) < starts[place + 1]))
        def _(place=place):
            body(place)


def assemble_kernel(place_ref, *refs):
    out_ref = refs[-1]
    slot = place_ref[1 + pl.program_id(0)]
    for k, ref in enumerate(refs[:-1]):

        @pl.when(slot == k)
        def _(ref=ref):
            out_ref[...] = ref[...].astype(F32)


def assemble(c, q_rows, slots):
    n, width = slots[0].shape
    count = len(slots)
    step = math.gcd(512, math.gcd(q_rows, n))
    q_steps, d_steps = q_rows // step, (n - q_rows) // step
    turns, owners = [], []
    for base, steps in ((0, q_steps), (q_steps, d_steps)):
        for owner in range(count):
            turns += [base + turn for turn in range(steps)]
            owners += [owner] * steps
    places = jnp.concatenate([c.reshape(1), (c - jnp.array(owners)) % count]).astype(jnp.int32)

    def turn_of(j, p):
        turn = jnp.where(j < count * q_steps, j % q_steps, q_steps + (j - count * q_steps) % d_steps)
        return turn, 0

    return call(
        assemble_kernel, "assemble", (len(turns),),
        [pl.BlockSpec((step, width), turn_of)] * count,
        [pl.BlockSpec((step, width), lambda j, p: (j, 0))],
        [shaped(F32, n * count, width)], (places, *slots), 0, prefetch=1,
    )[0]


def pass_on_kernel(in_ref, out_ref):
    out_ref[...] = in_ref[...]


def pass_on(array, after=()):
    spec = held(array.shape)
    return call(
        pass_on_kernel, "pass_on", (1,), [spec], [pl.BlockSpec(array.shape, lambda *_: (0,) * array.ndim)],
        [shaped(array.dtype, *array.shape)], (array,), 0, after=after,
    )[0]


def fold_kernel(starts, inner, place_ref, *refs):
    groups = len(starts) - 1

    def one_group(place):
        total = refs[place][0] + refs[groups + place][0].astype(F32)
        put_halves(total, inner, place_ref[0], refs[2 * groups :])

    for_group(starts, one_group)


def fold(side, owns, arrived, inner):
    _, rows, m = owns[0].shape
    chunk = min(1024, m)
    starts = [0]
    for own in owns:
        starts.append(starts[-1] + own.shape[0])

    def spec(size):
        return pl.BlockSpec((1, size, chunk), lambda j, i, p: (j, 0, i))

    half = rows // 2
    specs = [
        pl.BlockSpec((1, rows, chunk), grouped_index(starts, place, m // chunk))
        for place in range(len(owns))
    ]
    return call(
        functools.partial(fold_kernel, starts, inner), "fold", (starts[-1], m // chunk),
        specs + specs, [spec(half), spec(half)],
        [shaped(BF16, starts[-1], half, m), shaped(F32, starts[-1], half, m)],
        (side.reshape(1), *owns, *arrived), 0, prefetch=1,
    )


SEGMENTS = 8
ATTENTION_LANES = 128


def half_lanes(block, head, other):
    lane = lax.broadcasted_iota(jnp.int32, block.shape, 1)
    return jnp.where((lane >= DH) == (head == 1), block, other)


def scaled(block):
    return (block.astype(F32) * DH**-0.5).astype(BF16)


def three_terms(value):
    high = value.astype(BF16).astype(F32)
    middle = (value - high).astype(BF16).astype(F32)
    return high, middle, value - high - middle


def for_spans(span_ref, tiles, body):
    @pl.loop(0, tiles)
    def _(step):
        low, high = span_ref[step], span_ref[tiles + step]
        for count in range(1, tiles + 1):

            @pl.when(high - low == count)
            def _(count=count):
                body(step, low, count)


def attention_forward_kernel(
    span_ref, qkv_ref, ext_k_ref, ext_q_ref, out_ref, rest_ref, ext_ref,
    keys_ref, queries_ref, *, tile,
):
    n = ext_k_ref.shape[0]
    tiles = n // tile
    pairs = qkv_ref.shape[2] // 128

    def lanes(pair):
        return slice(pair * 128, pair * 128 + 128)

    for pair in range(pairs):
        query = scaled(qkv_ref[0, :, lanes(pair)])
        for half in range(2):
            keys_ref[2 * pair + half] = half_lanes(qkv_ref[1, :, lanes(pair)], half, ext_k_ref[...])
            queries_ref[2 * pair + half] = half_lanes(query, half, ext_q_ref[...])

    def attend(step, low, count):
        rows = pl.ds(pl.multiple_of(step * tile, tile), tile)
        window = pl.ds(pl.multiple_of(low * tile, tile), count * tile)
        lane = lax.broadcasted_iota(jnp.int32, (tile, 128), 1)
        for pair in range(pairs):
            at = lanes(pair)
            outs, extra = [], ext_q_ref[rows, :].astype(F32)
            for half in range(2):
                head = 2 * pair + half
                logits = mm(queries_ref[head, rows, :], keys_ref[head, window, :], NT)
                top = jnp.max(logits, axis=1, keepdims=True)
                weights = jnp.exp(logits - top)
                mass = jnp.sum(weights, axis=1, keepdims=True)
                probs = (weights * (1.0 / mass)).astype(BF16)
                outs.append(mm(probs, qkv_ref[2, window, at]))
                first = SEGMENTS + DH * (1 - half)
                for place, term in enumerate(three_terms(-(top + jnp.log(mass)))):
                    extra = jnp.where(lane == first + place, term, extra)
            out = jnp.where(lane < DH, outs[0], outs[1])
            out_ref[rows, at] = out.astype(BF16)
            rest_ref[rows, at] = (out - out.astype(BF16).astype(F32)).astype(BF16)
            ext_ref[rows, at] = extra.astype(BF16)

    for_spans(span_ref, tiles, attend)


def attention_forward(spans, qkv, ext_k, ext_q, tile):
    _, n, width = qkv.shape
    span = min(width, ATTENTION_LANES)
    wide = pl.BlockSpec((n, span), lambda i, *_: (0, i))
    heads = pltpu.VMEM((span // DH, n, 128), BF16)
    return call(
        functools.partial(attention_forward_kernel, tile=tile), "attention_forward",
        (width // span,),
        [pl.BlockSpec((3, n, span), lambda i, *_: (0, 0, i)), held((n, 128)), held((n, 128))],
        [wide, wide, wide],
        [shaped(BF16, n, width)] * 3,
        (spans, qkv, ext_k, ext_q), 0, prefetch=1, scratch=[heads, heads],
    )


def attention_backward_kernel(
    span_ref, qkv_ref, ext_ref, att_ref, rest_ref, grad_ref, ext_k_ref, cos_ref, sin_ref,
    out_ref, sum_ref,
    keys_ref, turned_ref, values_ref, queries_ref, plain_ref, grads_ref, plain_grads_ref,
    dq_ref, dk_ref, dv_ref, *, tile,
):
    n = ext_k_ref.shape[0]
    tiles = n // tile
    pairs = qkv_ref.shape[2] // 128
    heads = range(2 * pairs)

    def lanes(head):
        return slice(head // 2 * 128, head // 2 * 128 + 128)

    def own_rows(head):
        return slice(head % 2 * DH, head % 2 * DH + DH)

    def rows(step):
        return pl.ds(pl.multiple_of(step * tile, tile), tile)

    @pl.loop(0, tiles)
    def _(step):
        at = rows(step)
        zeros = jnp.zeros((tile, 128), BF16)
        lane = lax.broadcasted_iota(jnp.int32, (tile, 128), 1)
        ext_k = ext_k_ref[at, :]
        for pair in range(pairs):
            cut = lanes(2 * pair)
            grad = grad_ref[at, cut]
            out = att_ref[at, cut].astype(F32) + rest_ref[at, cut].astype(F32)
            product = grad.astype(F32) * out
            query = scaled(qkv_ref[0, at, cut])
            turned_ref[pair, :, at] = scaled(qkv_ref[1, at, cut]).astype(F32).T.astype(BF16)
            for half in range(2):
                head = 2 * pair + half
                keys_ref[head, at, :] = half_lanes(qkv_ref[1, at, cut], half, ext_k)
                values_ref[head, at, :] = half_lanes(qkv_ref[2, at, cut], half, ext_k)
                whole = half_lanes(query, half, ext_ref[at, cut])
                queries_ref[head, step] = whole.astype(F32).T.astype(BF16)
                plain_ref[head, at, :] = half_lanes(query, half, zeros)
                plain_grads_ref[head, at, :] = half_lanes(grad, half, zeros)
                inner = jnp.sum(half_lanes(product, half, 0.0), axis=1, keepdims=True)
                extra = jnp.zeros((tile, 128), F32)
                for place, term in enumerate(three_terms(-inner)):
                    extra = jnp.where((lane & (DH - 1)) == SEGMENTS + place, term, extra)
                whole = half_lanes(grad.astype(F32), half, extra)
                grads_ref[head, step] = whole.T.astype(BF16)

    dk_ref[...] = jnp.zeros(dk_ref.shape, F32)
    dv_ref[...] = jnp.zeros(dv_ref.shape, F32)

    def pull(step, low, count):
        at = rows(step)
        window = pl.ds(pl.multiple_of(low * tile, tile), count * tile)
        for pair in range(pairs):
            probs, slopes, dq = [], [], []
            both = range(2 * pair, 2 * pair + 2)
            for head in both:
                weights = jnp.exp(mm(keys_ref[head, window, :], queries_ref[head, step]))
                flow = mm(values_ref[head, window, :], grads_ref[head, step])
                slope = (weights * flow).astype(BF16)
                probs.append(weights.astype(BF16))
                slopes.append(slope)
                dq.append(mm(turned_ref[pair, own_rows(head), window], slope))
            plain = jnp.concatenate([plain_ref[h, at, :] for h in both], axis=0)
            grads = jnp.concatenate([plain_grads_ref[h, at, :] for h in both], axis=0)
            cut = lanes(2 * pair)
            dv_ref[window, cut] += mm(jnp.concatenate(probs, axis=1), grads)
            dk_ref[window, cut] += mm(jnp.concatenate(slopes, axis=1), plain)
            dq_ref[at, cut] = jnp.concatenate(dq, axis=0).T

    for_spans(span_ref, tiles, pull)

    def finish(step, sums):
        cosine, sine = cos_ref[rows(step), :], sin_ref[rows(step), :]
        added = []
        for which, src in enumerate((dq_ref, dk_ref, dv_ref)):
            for pair in range(pairs):
                at = lanes(2 * pair)
                block = src[rows(step), at]
                if which < 2:
                    block = block * cosine - swap_halves(block) * sine
                low = block.astype(BF16)
                out_ref[which, rows(step), at] = low
                total = jnp.sum(low.astype(F32), axis=0, keepdims=True)
                added.append(sums[which * pairs + pair] + total)
        return tuple(added)

    zero = jnp.zeros((1, 128), F32)
    sums = lax.fori_loop(0, tiles, finish, (zero,) * (3 * pairs))
    sums = [jnp.concatenate(sums[w * pairs : (w + 1) * pairs], axis=1) for w in range(3)]
    sum_ref[...] = jnp.concatenate(sums + [jnp.zeros((5, pairs * 128), F32)], axis=0)


def attention_backward(
    spans, qkv, ext, attended, rest, grads, ext_k, cosine, sine, tile
):
    _, n, width = qkv.shape
    span = min(width, ATTENTION_LANES)
    wide = pl.BlockSpec((n, span), lambda i, *_: (0, i))
    three = pl.BlockSpec((3, n, span), lambda i, *_: (0, 0, i))
    tiles, pairs = n // tile, span // 128
    heads = pltpu.VMEM((2 * pairs, n, 128), BF16)
    turned = pltpu.VMEM((2 * pairs, tiles, 128, tile), BF16)
    return call(
        functools.partial(attention_backward_kernel, tile=tile), "attention_backward",
        (width // span,),
        [three, wide, wide, wide, wide, held((n, 128)), held((n, 128)), held((n, 128))],
        [three, pl.BlockSpec((8, span), lambda i, *_: (0, i))],
        [shaped(BF16, 3, n, width), shaped(F32, 8, width)],
        (spans, qkv, ext, attended, rest, grads, ext_k, cosine, sine), 0,
        prefetch=1,
        scratch=[
            heads, pltpu.VMEM((pairs, 128, n), BF16), heads, turned, heads, turned, heads,
        ] + [pltpu.VMEM((n, span), F32)] * 3,
    )


STRIP = 32


def token_sums(width, queries):
    token = lax.broadcasted_iota(jnp.int32, (width, queries), 0) // QLEN
    return token == lax.broadcasted_iota(jnp.int32, (width, queries), 1)


def score_kernel(low_ref, high_ref, doc_ref, query_ref, pick_ref, out_ref, sum_ref, total_ref):
    group = pl.program_id(0)
    docs, width = pick_ref.shape[1:]
    doc_rows = doc_ref.shape[0]
    strips = doc_rows // STRIP
    chunk = min(256, doc_rows)
    row = lax.broadcasted_iota(jnp.int32, (STRIP, width), 0)
    sum_ref[...] = jnp.zeros(sum_ref.shape, F32)

    def add_strip(sim, first, doc, pick):
        kept = jnp.where(row == pick - first, sim, 0.0)
        sum_ref[pl.ds(doc, 1)] += jnp.sum(kept.reshape(1, STRIP // 8, 8, width), axis=1)

    for start in range(0, doc_rows, chunk):
        sims = mm(doc_ref[start : start + chunk, :], query_ref[...], NT)
        for first in range(0, chunk, STRIP):
            place = group * strips + (start + first) // STRIP
            low, high = low_ref[place], high_ref[place]
            sim = sims[first : first + STRIP]
            add_strip(sim, start + first, low, pick_ref[0, pl.ds(low, 1), :])
            pick = jnp.where(high > low, pick_ref[0, pl.ds(high, 1), :], -1)
            add_strip(sim, start + first, high, pick)

    @pl.loop(0, strips)
    def _(strip):
        low, high = low_ref[group * strips + strip], high_ref[group * strips + strip]

        @pl.when(high > low + 1)
        def _():
            first = pl.multiple_of(strip * STRIP, STRIP)
            sim = mm(doc_ref[pl.ds(first, STRIP), :], query_ref[...], NT)

            @pl.loop(low + 1, high)
            def _(doc):
                add_strip(sim, first, doc, pick_ref[0, pl.ds(doc, 1), :])

    total_ref[group] = jnp.sum(sum_ref[...], axis=1)

    @pl.when(group == pl.num_programs(0) - 1)
    def _():
        spread = token_sums(width, out_ref.shape[1]).astype(F32).astype(BF16)
        total = jnp.concatenate([total_ref[g] for g in range(total_ref.shape[0])], axis=0)
        out_ref[...] = sum(mm(term.astype(BF16), spread) for term in three_terms(total))


def score_grad_kernel(
    low_ref, high_ref, doc_ref, query_ref, pick_ref, weight_ref, doc_out, query_out,
    sparse_ref, token_ref,
):
    group = pl.program_id(0)
    docs, width = pick_ref.shape[1:]
    doc_rows = doc_ref.shape[0]
    strips = doc_rows // STRIP
    chunk = min(256, doc_rows)
    row = lax.broadcasted_iota(jnp.int32, (STRIP, width), 0)

    def fill(held, first, doc, pick):
        return jnp.where(row == pick - first, token_ref[group, pl.ds(doc, 1), :], held)

    @pl.when(group == 0)
    def _():
        query_out[...] = jnp.zeros_like(query_out)
        spread = token_sums(width, weight_ref.shape[1]).astype(F32).astype(BF16)
        weights = mm(weight_ref[...].astype(BF16), spread, NT)
        for g in range(token_ref.shape[0]):
            token_ref[g] = weights[g * docs : (g + 1) * docs]

    total = None
    for start in range(0, doc_rows, chunk):
        for first in range(start, start + chunk, STRIP):
            place = group * strips + first // STRIP
            low, high = low_ref[place], high_ref[place]
            held = fill(jnp.zeros((STRIP, width), F32), first, low, pick_ref[0, pl.ds(low, 1), :])
            pick = jnp.where(high > low, pick_ref[0, pl.ds(high, 1), :], -1)
            sparse_ref[first : first + STRIP, :] = fill(held, first, high, pick).astype(BF16)
        sparse = sparse_ref[start : start + chunk, :]
        doc_out[start : start + chunk, :] = mm(sparse, query_ref[...])
        turned = doc_ref[start : start + chunk, :].astype(F32).T.astype(BF16)
        part = mm(turned, sparse)
        total = part if total is None else total + part
    query_out[...] += total

    @pl.loop(0, strips)
    def _(strip):
        low, high = low_ref[group * strips + strip], high_ref[group * strips + strip]

        @pl.when(high > low + 1)
        def _():
            first = pl.multiple_of(strip * STRIP, STRIP)
            held = lax.fori_loop(
                low + 1,
                high,
                lambda doc, held: fill(held, first, doc, pick_ref[0, pl.ds(doc, 1), :]),
                jnp.zeros((STRIP, width), F32),
            ).astype(BF16)
            doc_out[pl.ds(first, STRIP), :] += mm(held, query_ref[...])
            turned = doc_ref[pl.ds(first, STRIP), :].astype(F32).T.astype(BF16)
            query_out[...] += mm(turned, held)


def score_specs(doc_tile, query_tile, picks):
    groups, docs, width = picks.shape
    doc_rows = doc_tile.shape[0] // groups
    return (
        pl.BlockSpec((doc_rows, 128), lambda i, *_: (i, 0)),
        held(query_tile.shape),
        pl.BlockSpec((1, docs, width), lambda i, *_: (i, 0, 0)),
    )


def score_forward(lows, highs, doc_tile, query_tile, picks):
    groups, docs, width = picks.shape
    queries = width // QLEN
    doc_spec, query_spec, pick_spec = score_specs(doc_tile, query_tile, picks)
    return call(
        score_kernel, "score_forward", (groups,),
        [doc_spec, query_spec, pick_spec],
        [pl.BlockSpec((groups * docs, queries), lambda i, *_: (0, 0))],
        [shaped(F32, groups * docs, queries)],
        (lows, highs, doc_tile, query_tile, picks), 2 * doc_tile.shape[0] * width * 128,
        prefetch=2,
        scratch=[pltpu.VMEM((docs, 8, width), F32), pltpu.VMEM((groups, docs, width), F32)],
    )[0]


def score_backward(lows, highs, doc_tile, query_tile, picks, weights):
    groups, docs, width = picks.shape
    doc_spec, query_spec, pick_spec = score_specs(doc_tile, query_tile, picks)
    return call(
        score_grad_kernel, "score_backward", (groups,),
        [doc_spec, query_spec, pick_spec, held(weights.shape)],
        [doc_spec, pl.BlockSpec((128, width), lambda i, *_: (0, 0))],
        [shaped(F32, *doc_tile.shape), shaped(F32, 128, width)],
        (lows, highs, doc_tile, query_tile, picks, weights), 4 * doc_tile.shape[0] * width * 128,
        prefetch=2,
        scratch=[
            pltpu.VMEM((doc_tile.shape[0] // groups, width), BF16),
            pltpu.VMEM((groups, docs, width), F32),
        ],
    )


def on_device(
    tokens,
    doc_lengths,
    match_picks,
    labels,
    w_qkv,
    b_qkv,
    w_out,
    b_out,
    ln1_gain,
    ln1_bias,
    w_up,
    b_up,
    w_down,
    b_down,
    ln2_gain,
    ln2_bias,
    w_proj,
    log_scale,
):
    Order.last = ()
    C = lax.axis_size("cols")
    R = lax.axis_size("rows")
    c = lax.axis_index("cols")
    r = lax.axis_index("rows")
    width = tokens.shape[1]
    D = width * C
    Q = ROW_LEN // C
    DS = (tokens.shape[0] - ROW_LEN) // C
    n = Q + DS
    tile = math.gcd(256, math.gcd(Q, DS))

    def shift_cols(value, k):
        return lax.ppermute(value, "cols", [(i, (i + k) % C) for i in range(C)])

    def swap_rows(value, bit):
        return lax.ppermute(value, "rows", [(i, i ^ bit) for i in range(R)])

    def in_order(slots):
        if len(slots) == 1:
            return slots
        if len(slots) == 2:
            return [lax.select(c == 0, slots[0], slots[1]), lax.select(c == 0, slots[1], slots[0])]
        stacked = jnp.stack(slots)
        return [
            lax.dynamic_index_in_dim(stacked, (c - j) % C, 0, keepdims=False) for j in range(C)
        ]

    rows_in_order = [b_out, ln1_gain, ln1_bias, b_down, ln2_gain, ln2_bias]
    packed = jnp.concatenate(
        [jnp.stack(rows_in_order), b_qkv, b_up.reshape(-1, width)], axis=0
    )
    packed = jnp.pad(packed, ((0, 16 - packed.shape[0]), (0, 0)))

    def gather_pieces(pieces):
        return [lax.all_gather(piece, "rows", axis=0, tiled=True) for piece in pieces]

    late_weights = (w_out, w_up, w_down)
    late_pieces = [
        lax.dynamic_index_in_dim(w.reshape(R, -1, w.shape[1]), r, 0, keepdims=False)
        for w in late_weights
    ]
    parts = jnp.concatenate(
        [tokens[:ROW_LEN].reshape(C, Q, width), tokens[ROW_LEN:].reshape(C, DS, width)], axis=1
    )

    def part(k):
        return lax.dynamic_index_in_dim(parts, (c + k) % C, 0, keepdims=False)

    qkv_piece = lax.dynamic_index_in_dim(
        w_qkv.reshape(R, -1, w_qkv.shape[2]), r, 0, keepdims=False
    )
    qkv_pieces = [shift_cols(qkv_piece, k) for k in range(1, C)]
    token_slots = [part(0)] + [shift_cols(part(k), k) for k in range(1, C)]
    own_sizes = lax.dynamic_index_in_dim(
        lax.dynamic_index_in_dim(doc_lengths, r, 0, keepdims=False), c, 0, keepdims=False
    )
    sizes = lax.dynamic_index_in_dim(doc_lengths, c, 1, keepdims=False)
    doc_ends = jnp.cumsum(sizes, axis=1)
    begins = doc_ends - sizes
    cosine, sine, ext_k, ext_q, picks = prepare(n, Q, own_sizes, match_picks, begins, sizes)
    wqkv_slots = [w_qkv] + [
        lax.all_gather(piece, "rows", axis=0, tiled=True).reshape(w_qkv.shape)
        for piece in qkv_pieces
    ]
    x = jnp.concatenate(in_order(token_slots), axis=1)
    flat = pass_on(
        jnp.concatenate([piece.reshape(-1, D) for piece in late_pieces]), token_slots[1:]
    )
    behind, _ = lax.optimization_barrier(((w_proj, packed), flat))
    wproj = jnp.concatenate(
        in_order([w_proj] + [shift_cols(behind[0], k) for k in range(1, C)]), axis=0
    )
    packs = [packed] + [shift_cols(behind[1], k) for k in range(1, C)]

    vectors = jnp.concatenate([p[:8] for p in in_order(packs)], axis=1)

    own_ends = jnp.cumsum(own_sizes)
    share = D // R
    q_tiles, d_tiles = Q // tile, DS // tile
    steps = jnp.arange(q_tiles, dtype=jnp.int32)
    first_rows = jnp.arange(d_tiles, dtype=jnp.int32) * tile
    is_passed = first_rows[:, None] >= own_ends[None, :]
    low_rows = jnp.sum(jnp.where(is_passed, own_sizes[None, :], 0), axis=1)
    last_passed = (first_rows + tile - 1)[:, None] >= own_ends[None, :]
    high_rows = jnp.min(jnp.where(last_passed, DS, own_ends[None, :]), axis=1)
    spans = jnp.concatenate(
        [steps, q_tiles + low_rows // tile, steps + 1, q_tiles + (high_rows + tile - 1) // tile]
    ).astype(jnp.int32)

    queries_here, tile_docs, _ = match_picks.shape
    strip_rows = (jnp.arange(DS // STRIP, dtype=jnp.int32) * STRIP)[None, :, None]
    lows = jnp.sum(doc_ends[:, None, :] <= strip_rows, axis=2).astype(jnp.int32).reshape(-1)
    highs = jnp.sum(begins[:, None, :] < strip_rows + STRIP, axis=2).astype(jnp.int32) - 1
    highs = highs.reshape(-1)

    qkv, attended, rests, exts = [], [], [], []
    for k in range(C):
        first = (lows, highs) if k == 0 else ()
        qkv.append(project_qkv(c, token_slots, wqkv_slots[k], packs[k], cosine, sine, first))
        if k == 0:
            arrived = [shift_cols(flat, j) for j in range(1, C)]
            arrived = [pass_on(a) for a in arrived]
            ends_of = [0]
            for piece in late_pieces:
                ends_of.append(ends_of[-1] + piece.size // D)
            wout_slots, wup_slots, wdown_slots = (
                [own] + gather_pieces([
                    a[ends_of[j] : ends_of[j + 1]].reshape(late_pieces[j].shape) for a in arrived
                ])
                for j, own in enumerate(late_weights)
            )
            wout_slots, wup_slots, wdown_slots = (
                [slot.reshape(own.shape) for slot in slots_of]
                for slots_of, own in zip((wout_slots, wup_slots, wdown_slots), late_weights)
            )
        out, rest, ext = attention_forward(spans, qkv[k], ext_k, ext_q, tile)
        attended.append(out)
        rests.append(rest)
        exts.append(ext)
    normed_one, inverse_one, hidden_low, hidden_t = out_and_norm(x, vectors, attended, wout_slots)
    active, slopes = zip(*[up_and_gelu(hidden_low, wup_slots[k], packs[k]) for k in range(C)])
    normed_two, inverse_two, output_low, unit, unit_low, unit_inverse = down_and_norm(
        normed_one, vectors, wproj, active, wdown_slots
    )

    doc_tile = gather_rows(R, unit_low[Q:], 2).reshape(R * DS, 128)
    query_tile = jnp.concatenate(
        in_order([unit_low[:Q]] + [shift_cols(unit_low[:Q], k) for k in range(1, C)]), axis=0
    )
    sims = score_forward(lows, highs, doc_tile, query_tile, picks)
    scores = sims.T

    scale = jnp.exp(log_scale[0])
    z = scale * scores
    row_top = jnp.max(z, axis=1)
    row_mass = jnp.sum(jnp.exp(z - row_top[:, None]), axis=1)
    is_label = (
        jnp.arange(tile_docs, dtype=jnp.int32)[None, :] == (labels - c * tile_docs)[:, None]
    )
    chosen = jnp.sum(jnp.where(is_label, z, 0.0), axis=1)
    own_stats = jnp.stack([row_top, row_mass, chosen])
    stats = jnp.stack([own_stats] + [shift_cols(own_stats, k) for k in range(1, C)])
    top_all = jnp.max(stats[:, 0], axis=0)
    mass_all = jnp.sum(stats[:, 1] * jnp.exp(stats[:, 0] - top_all), axis=0)
    log_total = top_all + jnp.log(mass_all)
    loss = log_total - jnp.sum(stats[:, 2], axis=0)
    dz = (jnp.exp(z - log_total[:, None]) - is_label.astype(F32)) / (queries_here * R)
    scale_part = jnp.sum(dz * z)
    dscores = (scale * dz).T
    doc_grad, query_grad_t = score_backward(lows, highs, doc_tile, query_tile, picks, dscores)
    query_parts = query_grad_t.T.reshape(C, Q, 128)

    def query_part(k):
        return lax.dynamic_index_in_dim(query_parts, (c + k) % C, 0, keepdims=False)

    query_grad = query_part(0)
    for k in range(1, C):
        query_grad = query_grad + shift_cols(query_part(k), k)

    doc_sum = scatter_rows(doc_grad.reshape(R, DS, 128))
    unit_grad = jnp.concatenate([query_grad, doc_sum], axis=0)

    core = r % 2
    slots_back = range(C - 1, -1, -1)
    share = D // R
    x_bit, *z_bits = [1 << b for b in range(1, R.bit_length() - 1)]

    def side_of(bit):
        return ((r // bit) % 2).astype(jnp.int32)

    def halves_of(left_t):
        return left_t.reshape(R // 2, 2, share, n)

    def rows_of(left, side):
        return lax.dynamic_index_in_dim(left, side, 1, keepdims=False).reshape(-1, n)

    def send_plain(left, right):
        part = mm(rows_of(left, 1 - core), right).astype(BF16)
        Order.last += (part,)
        return swap_rows(part, 1)

    def keep_plain(left, right, arrived, k):
        kept = mm(rows_of(left, core), right) + arrived.astype(F32)
        if k > 0:
            kept = kept.astype(BF16)
        Order.last += (kept,)
        return kept[None] if k == 0 else shift_cols(kept, C - k)[None]

    def next_fold(states, bit, inner):
        send, keep = fold(side_of(bit), [s[0] for s in states], [s[1] for s in states], inner)
        return keep, swap_rows(send, bit)

    def cols_state(kept):
        rest = kept[1]
        for other in kept[2:]:
            rest = rest.astype(F32) + other.astype(F32)
        return kept[0], rest

    embed_grad, resid_two_grad, branch, branch_t, head_sums = head_pull(
        unit_grad, unit, unit_inverse, wproj, normed_two, inverse_two, vectors
    )
    down_left, down_right = halves_of(branch_t), active
    pre_grads, up_sums, down_kept = [None] * C, [None] * C, [None] * C
    down_arrived = [None] * C
    for k in slots_back:
        down_arrived[k] = send_plain(down_left, down_right[k])
    for k in slots_back:
        pre_grads[k], up_sums[k] = up_pull(branch, wdown_slots[k], slopes[k])
        if k > 0:
            down_kept[k] = keep_plain(down_left, down_right[k], down_arrived[k], k)
    up_left, up_right = halves_of(hidden_t), pre_grads
    up_arrived, up_kept = [None] * C, [None] * C
    for k in slots_back:
        up_arrived[k] = send_plain(up_left, up_right[k])
    down_kept[0] = keep_plain(down_left, down_right[0], down_arrived[0], 0)
    for k in slots_back[:-1]:
        up_kept[k] = keep_plain(up_left, up_right[k], up_arrived[k], k)
    resid_one_grad, branch_one_t, hidden_sums, *attended_grads = hidden_pull(
        resid_two_grad, normed_one, inverse_one, vectors, pre_grads, wup_slots, wout_slots
    )
    up_kept[0] = keep_plain(up_left, up_right[0], up_arrived[0], 0)
    mixed_grads, mixed_sums = [None] * C, [None] * C
    def gather_small():
        proj_grad = mm(embed_grad, output_low, TN).reshape(R, -1, C, width)
        def cut(values, slot_rows):
            return values.reshape(slot_rows, R, -1)

        own_order = [(c - k) % C for k in range(C)]
        canonical = jnp.stack(
            [hidden_sums[0], hidden_sums[1], hidden_sums[2], head_sums[0], head_sums[1], head_sums[2]]
        ).reshape(6, C, R, -1)
        slots_small = []
        for k in range(C):
            rows = [mixed_sums[k][j].reshape(R, -1) for j in range(3)]
            rows.append(up_sums[k][0].reshape(R, -1))
            rows += [
                lax.dynamic_index_in_dim(canonical[j], own_order[k], 0, keepdims=False)
                for j in range(6)
            ]
            own_proj_grad = lax.dynamic_index_in_dim(proj_grad, own_order[k], 2, keepdims=False)
            rows.append(own_proj_grad.reshape(R, -1))
            rows.append(jnp.broadcast_to(scale_part, (R, 1)))
            slots_small.append(jnp.concatenate(rows, axis=1))
        return jnp.stack(slots_small, axis=1)

    def pull_attention(k):
        mixed_grads[k], mixed_sums[k] = attention_backward(
            spans, qkv[k], exts[k], attended[k], rests[k], attended_grads[k], ext_k, cosine, sine,
            tile,
        )

    for k in slots_back[:-1]:
        pull_attention(k)
    wide_state = next_fold([cols_state(down_kept), cols_state(up_kept)], x_bit, share)
    pull_attention(0)
    sent = [
        shift_cols(token_pull((c + k) % C, resid_one_grad, mixed_grads, wqkv_slots, BF16), k)
        for k in range(1, C)
    ]
    own_tokens = token_pull(c, resid_one_grad, mixed_grads, wqkv_slots, F32)
    late_grad, wide_grad, small = late_sums(
        R, C, halves_of(x.T), halves_of(branch_one_t), mixed_grads, attended, *wide_state,
        gather_small(),
    )
    tokens_grad = assemble(c, Q, [own_tokens] + sent)
    qkv_grad, out_grad = late_grad[:3], late_grad[3]
    down_grad, up_grad = wide_grad
    one = D // (C * R)
    up_part = b_up.shape[0] // R
    bounds = [3 * one, 3 * one + up_part]
    for _ in range(6):
        bounds.append(bounds[-1] + one)
    pieces = [small[a:b] for a, b in zip(bounds[:-1], bounds[1:])]
    bup_out, bout_out, gain1_out, bias1_out, bdown_out, gain2_out, bias2_out = pieces
    return (
        scores,
        loss,
        tokens_grad,
        qkv_grad,
        small[: bounds[0]].reshape(3, one),
        out_grad.T,
        bout_out,
        gain1_out,
        bias1_out,
        up_grad,
        bup_out,
        down_grad.T,
        bdown_out,
        gain2_out,
        bias2_out,
        small[bounds[-1] : -1].reshape(-1, width).T,
        small[-1:],
    )


def solution(mesh):
    in_specs = (
        P("rows", "cols"),
        P(),
        P("rows", "cols", None),
        P("rows"),
        P(None, None, "cols"),
        P(None, "cols"),
        P("cols", None),
        P("cols"),
        P("cols"),
        P("cols"),
        P(None, "cols"),
        P("cols"),
        P("cols", None),
        P("cols"),
        P("cols"),
        P("cols"),
        P("cols", None),
        P(),
    )
    out_specs = (
        P("rows", "cols"),
        P("rows"),
        P("rows", "cols"),
        P(None, "rows", "cols"),
        P(None, ("cols", "rows")),
        P("cols", "rows"),
        P(("cols", "rows")),
        P(("cols", "rows")),
        P(("cols", "rows")),
        P("rows", "cols"),
        P(("cols", "rows")),
        P("cols", "rows"),
        P(("cols", "rows")),
        P(("cols", "rows")),
        P(("cols", "rows")),
        P("cols", "rows"),
        P(),
    )
    return jax.shard_map(
        on_device, mesh=mesh, in_specs=in_specs, out_specs=out_specs, check_vma=False
    )
```
